32 devices in a mesh: head: 4 (over y, x), blk: 8 (over z, core).
Axes of the slice: x: 2, y: 2, z: 4, core: 2. Of those that a mesh axis runs over, the one named last changes fastest.
Arguments:
- stream: bfloat16 [2, 32, 128, 512], P(None, ('head', 'blk')), may hold values from -6 to 6
- accumulator: bfloat16 [2, 32, 128, 512], P(None, ('head', 'blk')), may hold values from -12 to 12
- upstream: bfloat16 [2, 32, 128, 512], P(None, ('head', 'blk')), may hold values from -6 to 6
- segment_ids: int32 [2, 32, 128], P(None, ('head', 'blk')), may hold values from 0 to 3, as said below
- w_query: bfloat16 [512, 512], P(('head', 'blk')), may hold values from -0.5 to 0.5
- w_key: bfloat16 [512, 512], P(('head', 'blk')), may hold values from -0.25 to 0.25
- w_value: bfloat16 [512, 512], P(('head', 'blk')), may hold values from -0.25 to 0.25
- w_out: bfloat16 [512, 512], P(('head', 'blk')), may hold values from -1 to 1
- w_up: bfloat16 [512, 2048], P(('head', 'blk')), may hold values from -0.25 to 0.25
- b_up: bfloat16 [2048], P(('head', 'blk')), may hold values from -1.796875 to 1.796875
- w_down: bfloat16 [2048, 512], P(('head', 'blk')), may hold values from -0.125 to 0.125
- b_down: bfloat16 [512], P(('head', 'blk')), may hold values from -1.796875 to 1.796875
- gain_attn: bfloat16 [512], P(('head', 'blk')), may hold values from 0.5 to 1.5
- bias_attn: bfloat16 [512], P(('head', 'blk')), may hold values from -1.796875 to 1.796875
- gain_ffn: bfloat16 [512], P(('head', 'blk')), may hold values from 0.5 to 1.5
- bias_ffn: bfloat16 [512], P(('head', 'blk')), may hold values from -1.796875 to 1.796875
- gain_final: bfloat16 [512], P(('head', 'blk')), may hold values from 0.5 to 1.5
- bias_final: bfloat16 [512], P(('head', 'blk')), may hold values from -1.796875 to 1.796875
Outputs:
- layer_out: bfloat16 [2, 32, 128, 512], P(None, ('head', 'blk'))
- grad_stream: float32 [2, 32, 128, 512], P(None, ('head', 'blk'))
- grad_accum: float32 [2, 32, 128, 512], P(None, ('head', 'blk'))
- grad_w_query: float32 [512, 512], P(('head', 'blk'))
- grad_w_key: float32 [512, 512], P(('head', 'blk'))
- grad_w_value: float32 [512, 512], P(('head', 'blk'))
- grad_w_out: float32 [512, 512], P(('head', 'blk'))
- grad_w_up: float32 [512, 2048], P(('head', 'blk'))
- grad_b_up: float32 [2048], P(('head', 'blk'))
- grad_w_down: float32 [2048, 512], P(('head', 'blk'))
- grad_b_down: float32 [512], P(('head', 'blk'))
- grad_gain_attn: float32 [512], P(('head', 'blk'))
- grad_bias_attn: float32 [512], P(('head', 'blk'))
- grad_gain_ffn: float32 [512], P(('head', 'blk'))
- grad_bias_ffn: float32 [512], P(('head', 'blk'))
- grad_gain_final: float32 [512], P(('head', 'blk'))
- grad_bias_final: float32 [512], P(('head', 'blk'))
The draws below stay inside these ranges and needn't reach their ends.
Inputs may be any that keep to these rules, and one draw needn't show every extreme that they name: `segment_ids`: entry [m, d, c] belongs to position c * 32 + d of sequence m. Along a sequence's positions the numbers start at 0 and never fall, rising by one at each new document; every sequence holds exactly (3546) // 1100 + 1 documents; each document is a run of consecutive positions, the first one of at least 825, each but the last of at most 1650.
All inputs are finite; a program needn't handle non-finite values.
Results may differ from the reference program's by a relative error of at most 0.015.
The reference program's roundings to bfloat16 on the way count: a program that leaves them out, or rounds other values in their place, can miss the bound.
Values may be sent and summed in bfloat16 or wider, within the bound.
A program may use at most 256 MiB of HBM per device.

```python
import math
import jax
import jax.numpy as jnp
from jax import lax

D = 512
HEADS = 8
DH = 64
FF = 2048
MB = 2
DOC_SPAN = 1100
TOK_DEV = 128
SHARDS = 32
LENGTH = 4096


def draw_segment_ids(key, part):
    key = jax.random.fold_in(key, 11)
    bound_count = (LENGTH - DOC_SPAN // 2) // DOC_SPAN
    quarter = DOC_SPAN // 4
    offsets = jax.random.randint(key, (MB, bound_count), -quarter, quarter + 1).astype(jnp.int32)
    slots = (jnp.arange(bound_count, dtype=jnp.int32) + 1) * DOC_SPAN
    doc_ends = (slots[None, :] + offsets).astype(jnp.int32)
    positions = jnp.arange(LENGTH, dtype=jnp.int32)
    doc_ids = jnp.sum((positions[None, :, None] >= doc_ends[:, None, :]).astype(jnp.int32), axis=2).astype(jnp.int32)
    return doc_ids.reshape(MB, TOK_DEV, SHARDS).transpose(0, 2, 1)


def steps_of(rng, extent, cuts, low, largest):
    factor_of, own = 1.0, jax.random.fold_in(rng, 6)
    for position, blocks in cuts:
        heights = jnp.exp(jax.random.uniform(jax.random.fold_in(own, position), (blocks,), jnp.float32, low / len(cuts), largest / len(cuts)))
        factor_of = factor_of * jnp.repeat(heights, extent[position] // blocks).reshape([-1 if axis == position else 1 for axis in range(len(extent))])
    return factor_of


def scatter_about(key, extent, width, bound, pieces=(), kind=jnp.bfloat16):
    array = width * jax.random.normal(key, extent, jnp.float32)
    if pieces:
        array = array * steps_of(key, extent, pieces, -0.22, 0.18)
    return jnp.clip(array, -bound, bound).astype(kind)


def setup_inputs(seed: int = 0) -> dict:
    streams_of = jax.random.split(jax.random.key(seed), 19)
    return {
        "stream": scatter_about(streams_of[0], (MB, SHARDS, TOK_DEV, D), 1.0, 6.0, ((1, 32),)),
        "accumulator": scatter_about(streams_of[1], (MB, SHARDS, TOK_DEV, D), 2.0, 12.0, ((1, 32),)),
        "upstream": scatter_about(streams_of[2], (MB, SHARDS, TOK_DEV, D), 1.0, 6.0, ((1, 32),)),
        "segment_ids": draw_segment_ids(jax.random.fold_in(streams_of[18], 71), 0),
        "w_query": scatter_about(streams_of[4], (D, D), (D // 4) ** -0.5, 0.5, ((0, 32),)),
        "w_key": scatter_about(streams_of[5], (D, D), D ** -0.5, 0.25, ((0, 32),)),
        "w_value": scatter_about(streams_of[6], (D, D), D ** -0.5, 0.25, ((0, 32),)),
        "w_out": scatter_about(streams_of[7], (D, D), (D // 16) ** -0.5, 1.0, ((0, 32),)),
        "w_up": scatter_about(streams_of[8], (D, FF), D ** -0.5, 0.25, ((0, 32),)),
        "b_up": scatter_about(streams_of[9], (FF,), 0.3, 1.796875, ((0, 32),)),
        "w_down": scatter_about(streams_of[10], (FF, D), FF ** -0.5, 0.125, ((0, 32),)),
        "b_down": scatter_about(streams_of[11], (D,), 0.3, 1.796875, ((0, 32),)),
        "gain_attn": jnp.clip(1.0 + 0.1 * jax.random.normal(streams_of[12], (D,), jnp.float32), 0.5, 1.5).astype(jnp.bfloat16),
        "bias_attn": scatter_about(streams_of[13], (D,), 0.3, 1.796875, ((0, 32),)),
        "gain_ffn": jnp.clip(1.0 + 0.1 * jax.random.normal(streams_of[14], (D,), jnp.float32), 0.5, 1.5).astype(jnp.bfloat16),
        "bias_ffn": scatter_about(streams_of[15], (D,), 0.3, 1.796875, ((0, 32),)),
        "gain_final": jnp.clip(1.0 + 0.1 * jax.random.normal(streams_of[16], (D,), jnp.float32), 0.5, 1.5).astype(jnp.bfloat16),
        "bias_final": scatter_about(streams_of[17], (D,), 0.3, 1.796875, ((0, 32),)),
    }


@jax.custom_vjp
def low(v):
    return lax.optimization_barrier(v.astype(jnp.bfloat16)).astype(jnp.float32)

@jax.custom_vjp
def low_back(v):
    return v

def low_keep(v):
    return (low(v), None)

def low_pass(kept, grad):
    return (grad,)

def back_keep(v):
    return (v, None)

def back_low(kept, grad):
    return (low(grad),)
low.defvjp(low_keep, low_pass)
low_back.defvjp(back_keep, back_low)
EPSILON = 1e-05
HIGHEST = lax.Precision.HIGHEST

def matmul(left, right):
    return jnp.dot(left, right, precision=HIGHEST, preferred_element_type=jnp.float32)

def rounded(values):
    return low_back(low(values))

def layer_norm(inputs, norm_gain, norm_bias):
    average = lax.optimization_barrier(jnp.mean(inputs, axis=-1, keepdims=True))
    centered = inputs - average
    variance = lax.optimization_barrier(jnp.mean(centered * centered, axis=-1, keepdims=True))
    return centered * lax.rsqrt(variance + EPSILON) * norm_gain + norm_bias

def attention(queries, key_rows, value_rows, seg_ids):
    length = queries.shape[0]
    block_len = math.gcd(length, 512)
    scaling = DH ** (-0.5)

    def one_block(inputs):
        query_part, seg_part = inputs
        raw_scores = jnp.einsum('qhd,khd->hqk', query_part, key_rows, precision=HIGHEST)
        scores = low_back(raw_scores) * scaling
        allowed = seg_part[:, None] == seg_ids[None, :]
        scores = jnp.where(allowed[None], scores, -1e+30)
        attn_prob = low(jax.nn.softmax(scores, axis=-1))
        return jnp.einsum('hqk,khd->qhd', attn_prob, value_rows, precision=HIGHEST)
    parts = (queries.reshape(length // block_len, block_len, HEADS, DH), seg_ids.reshape(length // block_len, block_len))
    return lax.map(jax.checkpoint(one_block), parts).reshape(length, HEADS * DH)

def forward(params, stream, accum, seg_ids):
    q_weight, k_weight, v_weight, o_weight, up_weight, up_bias, down_weight, down_bias, gain_one, shift_one, gain_two, shift_two, gain_three, shift_three = params
    results = []
    for micro_step in range(MB):
        inputs = stream[micro_step].reshape(-1, D)
        carried = accum[micro_step].reshape(-1, D)
        segs = seg_ids[micro_step].reshape(-1)
        length = inputs.shape[0]
        queries = rounded(matmul(inputs, q_weight)).reshape(length, HEADS, DH)
        key_rows = rounded(matmul(inputs, k_weight)).reshape(length, HEADS, DH)
        value_rows = rounded(matmul(inputs, v_weight)).reshape(length, HEADS, DH)
        mixed = rounded(attention(queries, key_rows, value_rows, segs))
        branch = low_back(matmul(mixed, o_weight))
        first = layer_norm(inputs + branch, gain_one, shift_one)
        hidden_pre = low_back(matmul(low(first), up_weight)) + up_bias
        hidden = low(jax.nn.gelu(hidden_pre, approximate=False))
        feed = low_back(matmul(hidden, down_weight)) + down_bias
        second = layer_norm(first + feed, gain_two, shift_two)
        summed = carried + branch + feed
        results.append(second + layer_norm(summed, gain_three, shift_three))
    return jnp.stack(results).reshape(stream.shape)

def reference(stream, accumulator, upstream, segment_ids, w_query, w_key, w_value, w_out, w_up, b_up, w_down, b_down, gain_attn, bias_attn, gain_ffn, bias_ffn, gain_final, bias_final):
    params = tuple((member.astype(jnp.float32) for member in (w_query, w_key, w_value, w_out, w_up, b_up, w_down, b_down, gain_attn, bias_attn, gain_ffn, bias_ffn, gain_final, bias_final)))

    def run(param_set, stream_wide, accum_wide):
        return forward(param_set, stream_wide, accum_wide, segment_ids)
    output, pullback = jax.vjp(run, params, stream.astype(jnp.float32), accumulator.astype(jnp.float32))
    param_grads, stream_grad, accum_grad = pullback(upstream.astype(jnp.float32))
    return (output.astype(jnp.bfloat16), stream_grad, accum_grad, param_grads[0], param_grads[1], param_grads[2], param_grads[3], param_grads[4], param_grads[5], param_grads[6], param_grads[7], param_grads[8], param_grads[9], param_grads[10], param_grads[11], param_grads[12], param_grads[13])
```

```python
import functools
import math

import jax
import jax.numpy as jnp
from jax import lax
from jax.experimental import pallas as pl
from jax.experimental.pallas import tpu as pltpu
from jax.sharding import PartitionSpec as P

DH = 64
f32, bf16 = jnp.float32, jnp.bfloat16
MESH = pl.DeviceIdType.MESH
FAR = -1e30


EPSILON = 1e-05


def norm_forward(inputs, norm_gain, norm_bias):
    average = jnp.mean(inputs, axis=-1, keepdims=True)
    centered = inputs - average
    inv_std = lax.rsqrt(jnp.mean(centered * centered, axis=-1, keepdims=True) + EPSILON)
    normed = centered * inv_std
    return (normed * norm_gain + norm_bias, normed, inv_std)


def norm_backward(gradient, normed, inv_std, norm_gain):
    scaled = gradient * norm_gain
    projected = (
        scaled
        - jnp.mean(scaled, axis=-1, keepdims=True)
        - normed * jnp.mean(scaled * normed, axis=-1, keepdims=True)
    )
    return (inv_std * projected, jnp.sum(gradient * normed, axis=0), jnp.sum(gradient, axis=0))


def smooth_gate(pre_act):
    return jax.nn.gelu(pre_act, approximate=False)


def split_rows(length):
    block_len = math.gcd(length, 512)
    return (length // block_len, block_len)


def block_scores(queries, query_seg, key_rows, key_seg, scaling):
    scores = (
        jnp.einsum("sgd,kgd->sgk", queries, key_rows, preferred_element_type=jnp.float32) * scaling
    )
    allowed = query_seg[:, None, None] == key_seg[None, None, :]
    return (scores, allowed)


def block_grads(
    queries, query_seg, grad_rows, log_total, row_delta, key_rows, value_rows, key_seg, scaling
):
    scores, allowed = block_scores(queries, query_seg, key_rows, key_seg, scaling)
    attn_prob = jnp.where(allowed, jnp.exp(scores - log_total[:, :, None]), 0.0)
    prob_grad = jnp.einsum(
        "sgd,kgd->sgk", grad_rows, value_rows, preferred_element_type=jnp.float32
    )
    score_grad = (attn_prob * (prob_grad - row_delta[:, :, None]) * scaling).astype(jnp.bfloat16)
    return (attn_prob.astype(jnp.bfloat16), score_grad)


def key_blocks(key_rows, value_rows, key_seg, groups):
    block_num, block_len = split_rows(key_rows.shape[0])
    return (
        key_rows.reshape(block_num, block_len, groups, -1),
        value_rows.reshape(block_num, block_len, groups, -1),
        key_seg.reshape(block_num, block_len),
    )


def attend_fold(queries, query_seg, scaling, carried, portion):
    key_rows, value_rows, key_seg = portion

    def step(running, blocks):
        key_part, value_part, seg_part = blocks
        old_max, old_total, weighted = running
        scores, allowed = block_scores(queries, query_seg, key_part, seg_part, scaling)
        row_max = jnp.maximum(old_max, jnp.max(jnp.where(allowed, scores, -1e30), axis=2))
        exp_scores = jnp.where(allowed, jnp.exp(scores - row_max[:, :, None]), 0.0)
        rescale = jnp.exp(old_max - row_max)
        new_total = old_total * rescale + jnp.sum(exp_scores, axis=2)
        weighted = weighted * rescale[:, :, None] + jnp.einsum(
            "sgk,kgd->sgd",
            exp_scores.astype(jnp.bfloat16),
            value_part,
            preferred_element_type=jnp.float32,
        )
        return ((row_max, new_total, weighted), None)

    running, unused = lax.scan(
        step, carried, key_blocks(key_rows, value_rows, key_seg, queries.shape[1])
    )
    return running


def local(
    stream,
    accumulator,
    upstream,
    segment_ids,
    w_query,
    w_key,
    w_value,
    w_out,
    w_up,
    b_up,
    w_down,
    b_down,
    gain_attn,
    bias_attn,
    gain_ffn,
    bias_ffn,
    gain_final,
    bias_final,
):
    heads_axis = lax.axis_size("head")
    micro = stream.shape[0]
    tokens = stream.shape[2]
    width = stream.shape[3]
    group_width = width // heads_axis
    groups = group_width // DH
    scaling = DH ** (-0.5)
    f32 = jnp.float32
    bf16 = jnp.bfloat16
    out_list = []
    stream_grads = []
    accum_grads = []
    grad_totals = None
    for micro_step in range(micro):
        (
            q_weight,
            k_weight,
            v_weight,
            o_weight,
            up_weight,
            up_bias,
            down_weight,
            down_bias,
            gain_one,
            shift_one,
            gain_two,
            shift_two,
            gain_three,
            shift_three,
        ) = (
            lax.all_gather(w_query, ("head", "blk"), axis=0, tiled=True),
            lax.all_gather(w_key, ("head", "blk"), axis=0, tiled=True),
            lax.all_gather(w_value, ("head", "blk"), axis=0, tiled=True),
            lax.all_gather(w_out, ("head", "blk"), axis=0, tiled=True),
            lax.all_gather(w_up, ("head", "blk"), axis=0, tiled=True),
            lax.all_gather(b_up, ("head", "blk"), axis=0, tiled=True),
            lax.all_gather(w_down, ("head", "blk"), axis=0, tiled=True),
            lax.all_gather(b_down, ("head", "blk"), axis=0, tiled=True),
            lax.all_gather(gain_attn, ("head", "blk"), axis=0, tiled=True),
            lax.all_gather(bias_attn, ("head", "blk"), axis=0, tiled=True),
            lax.all_gather(gain_ffn, ("head", "blk"), axis=0, tiled=True),
            lax.all_gather(bias_ffn, ("head", "blk"), axis=0, tiled=True),
            lax.all_gather(gain_final, ("head", "blk"), axis=0, tiled=True),
            lax.all_gather(bias_final, ("head", "blk"), axis=0, tiled=True),
        )
        inputs = stream[micro_step, 0]
        input_wide = inputs.astype(f32)
        carried = accumulator[micro_step, 0].astype(f32)
        segs = segment_ids[micro_step, 0]
        projections = jnp.stack(
            [
                jnp.dot(inputs, q_weight, preferred_element_type=f32),
                jnp.dot(inputs, k_weight, preferred_element_type=f32),
                jnp.dot(inputs, v_weight, preferred_element_type=f32),
            ]
        ).astype(bf16)
        projections = projections.reshape(3, tokens, heads_axis, group_width)
        seg_wide = jnp.broadcast_to(segs[None, :, None, None], (1, tokens, heads_axis, 1))
        regrouped, seg_group = (
            lax.all_to_all(projections, "head", split_axis=2, concat_axis=1, tiled=True),
            lax.all_to_all(seg_wide, "head", split_axis=2, concat_axis=1, tiled=True),
        )
        rows = regrouped.shape[1]
        query_loc = regrouped[0, :, 0]
        key_loc = regrouped[1, :, 0]
        value_loc = regrouped[2, :, 0]
        seg_loc = seg_group[0, :, 0, 0]
        queries3 = query_loc.reshape(rows, groups, DH)
        start_state = (
            jnp.full((rows, groups), -1e30, f32),
            jnp.zeros((rows, groups), f32),
            jnp.zeros((rows, groups, DH), f32),
        )
        row_max, row_total, weighted = attend_fold(
            queries3,
            seg_loc,
            scaling,
            start_state,
            (
                lax.all_gather(key_loc, "blk", axis=0, tiled=True),
                lax.all_gather(value_loc, "blk", axis=0, tiled=True),
                lax.all_gather(seg_loc, "blk", axis=0, tiled=True),
            ),
        )
        attn_out = weighted / row_total[:, :, None]
        log_total = row_max + jnp.log(row_total)
        attn_send = attn_out.astype(bf16).reshape(rows, 1, group_width)
        mixed = lax.all_to_all(attn_send, "head", split_axis=0, concat_axis=1, tiled=True).reshape(
            tokens, width
        )
        branch = jnp.dot(mixed, o_weight, preferred_element_type=f32)
        first, normed_one, inv_one = norm_forward(
            input_wide + branch, gain_one.astype(f32), shift_one.astype(f32)
        )
        first_low = first.astype(bf16)
        hidden_pre = jnp.dot(first_low, up_weight, preferred_element_type=f32) + up_bias.astype(f32)
        hidden_act, gate_pull = jax.vjp(smooth_gate, hidden_pre)
        hidden = hidden_act.astype(bf16)
        feed = jnp.dot(hidden, down_weight, preferred_element_type=f32) + down_bias.astype(f32)
        second, normed_two, inv_two = norm_forward(
            first + feed, gain_two.astype(f32), shift_two.astype(f32)
        )
        final, normed_three, inv_three = norm_forward(
            carried + branch + feed, gain_three.astype(f32), shift_three.astype(f32)
        )
        out_list.append((second + final).astype(bf16))
        cotangent = upstream[micro_step, 0].astype(f32)
        accum_grad, gain3_grad, shift3_grad = norm_backward(
            cotangent, normed_three, inv_three, gain_three.astype(f32)
        )
        second_grad, gain2_grad, shift2_grad = norm_backward(
            cotangent, normed_two, inv_two, gain_two.astype(f32)
        )
        feed_grad = second_grad + accum_grad
        feed_low = feed_grad.astype(bf16)
        down_grad = jnp.dot(hidden.T, feed_low, preferred_element_type=f32)
        (hidden_grad,) = gate_pull(jnp.dot(feed_low, down_weight.T, preferred_element_type=f32))
        hidden_low = hidden_grad.astype(bf16)
        up_grad = jnp.dot(first_low.T, hidden_low, preferred_element_type=f32)
        first_grad = second_grad + jnp.dot(hidden_low, up_weight.T, preferred_element_type=f32)
        resid_grad, gain1_grad, shift1_grad = norm_backward(
            first_grad, normed_one, inv_one, gain_one.astype(f32)
        )
        branch_low = (resid_grad + accum_grad).astype(bf16)
        out_wgrad = jnp.dot(mixed.T, branch_low, preferred_element_type=f32)
        mixed_grad = jnp.dot(branch_low, o_weight.T, preferred_element_type=f32).astype(bf16)
        mixed_grad = mixed_grad.reshape(tokens, heads_axis, group_width)
        grad_group = lax.all_to_all(mixed_grad, "head", split_axis=1, concat_axis=0, tiled=True)
        grad_loc = grad_group[:, 0]
        grad3 = grad_loc.reshape(rows, groups, DH)
        row_delta = jnp.sum(grad3.astype(f32) * attn_out, axis=2)
        whole_keys, whole_values, whole_seg = (
            lax.all_gather(key_loc, "blk", axis=0, tiled=True),
            lax.all_gather(value_loc, "blk", axis=0, tiled=True),
            lax.all_gather(seg_loc, "blk", axis=0, tiled=True),
        )

        def backward_step(running, blocks):
            key_part, value_part, seg_part = blocks
            attn_prob, score_grad = block_grads(
                queries3,
                seg_loc,
                grad3,
                log_total,
                row_delta,
                key_part,
                value_part,
                seg_part,
                scaling,
            )
            running = running + jnp.einsum(
                "sgk,kgd->sgd", score_grad, key_part, preferred_element_type=f32
            )
            key_term = jnp.einsum("sgk,sgd->kgd", score_grad, queries3, preferred_element_type=f32)
            value_term = jnp.einsum("sgk,sgd->kgd", attn_prob, grad3, preferred_element_type=f32)
            return (running, (key_term, value_term))

        query_grad, (key_terms, value_terms) = lax.scan(
            backward_step,
            jnp.zeros((rows, groups, DH), f32),
            key_blocks(whole_keys, whole_values, whole_seg, groups),
        )
        key_grad, value_grad = (
            lax.psum_scatter(
                key_terms.reshape(-1, group_width), "blk", scatter_dimension=0, tiled=True
            ),
            lax.psum_scatter(
                value_terms.reshape(-1, group_width), "blk", scatter_dimension=0, tiled=True
            ),
        )
        grad_stack = jnp.stack(
            [query_grad.reshape(rows, group_width), key_grad, value_grad]
        ).astype(bf16)
        grad_stack = grad_stack.reshape(3, rows, 1, group_width)
        returned = lax.all_to_all(
            grad_stack, "head", split_axis=1, concat_axis=2, tiled=True
        ).reshape(3, tokens, width)
        query_wgrad = jnp.dot(inputs.T, returned[0], preferred_element_type=f32)
        key_wgrad = jnp.dot(inputs.T, returned[1], preferred_element_type=f32)
        value_wgrad = jnp.dot(inputs.T, returned[2], preferred_element_type=f32)
        input_grad = (
            resid_grad
            + jnp.dot(returned[0], q_weight.T, preferred_element_type=f32)
            + jnp.dot(returned[1], k_weight.T, preferred_element_type=f32)
            + jnp.dot(returned[2], v_weight.T, preferred_element_type=f32)
        )
        stream_grads.append(input_grad)
        accum_grads.append(accum_grad)
        step_grads = (
            query_wgrad,
            key_wgrad,
            value_wgrad,
            out_wgrad,
            up_grad,
            jnp.sum(hidden_grad, axis=0),
            down_grad,
            jnp.sum(feed_grad, axis=0),
            gain1_grad,
            shift1_grad,
            gain2_grad,
            shift2_grad,
            gain3_grad,
            shift3_grad,
        )
        if grad_totals is None:
            grad_totals = step_grads
        else:
            grad_totals = tuple((older + newer for older, newer in zip(grad_totals, step_grads)))
    summed = lax.psum_scatter(grad_totals, ("head", "blk"), scatter_dimension=0, tiled=True)
    layer_out = jnp.stack(out_list)[:, None]
    grad_stream = jnp.stack(stream_grads)[:, None]
    grad_accum = jnp.stack(accum_grads)[:, None]
    return (
        layer_out,
        grad_stream,
        grad_accum,
        summed[0],
        summed[1],
        summed[2],
        summed[3],
        summed[4],
        summed[5],
        summed[6],
        summed[7],
        summed[8],
        summed[9],
        summed[10],
        summed[11],
        summed[12],
        summed[13],
    )


def dot_t(a, b):
    return lax.dot_general(a, b, (((1,), (1,)), ((), ())), preferred_element_type=f32)

def dot_n(a, b):
    return lax.dot_general(a, b, (((1,), (0,)), ((), ())), preferred_element_type=f32)

def dot_0(a, b):
    return lax.dot_general(a, b, (((0,), (0,)), ((), ())), preferred_element_type=f32)

def lanes(shape):
    return lax.broadcasted_iota(jnp.int32, shape, len(shape) - 1)

def query_marks(seg_row):
    wide = jnp.broadcast_to(seg_row, (128, seg_row.shape[1])).T
    return (wide == lanes(wide.shape)).astype(f32).astype(bf16)

def half_lanes(tile, half):
    wide = tile.astype(f32)
    if half:
        wide = pltpu.roll(wide, 64, 1)
    return jnp.where(lanes(wide.shape) < 64, wide, 0.0).astype(bf16)

def attn_fwd_kernel(bounds, q_ref, kv_ref, seg_q_ref, seg_k_ref, o_ref, of_ref, lse_ref, kv2_ref, vo_ref):
    chunks, keys = seg_k_ref.shape
    log_scale = math.log2(math.e) * DH ** (-0.5)

    def prepare(t, c):
        rows = pl.ds(pl.multiple_of(t * keys, keys), keys)
        kv = kv_ref[rows, :]
        wide = jnp.broadcast_to(seg_k_ref[pl.ds(t, 1), :], (128, keys)).T
        kv2_ref[rows, 0:128] = kv
        kv2_ref[rows, 128:256] = jnp.where(wide == lanes(wide.shape), 0.0, FAR).astype(bf16)
        vo_ref[rows, :] = jnp.where(lanes(kv.shape) < 64, 1.0, kv.astype(f32)).astype(bf16)
        return c

    lax.fori_loop(0, chunks, prepare, 0)

    def tile(j, c):
        q_tile = q_ref[j]
        rows = q_tile.shape[0]
        outs = []
        for half in range(2):
            i = half * (chunks // 2) + j
            left = half_lanes(q_tile, half)
            left = jnp.concatenate([left, query_marks(seg_q_ref[pl.ds(i, 1), :])], axis=1)
            low, high = bounds[0, i], bounds[1, i]
            first = lax.fori_loop(0, chunks, lambda t, n: n + jnp.where(bounds[1, t] < low, 1, 0), 0)
            last = lax.fori_loop(0, chunks, lambda t, n: n + jnp.where(bounds[0, t] <= high, 1, 0), 0)

            def step(t, carry):
                top, acc = carry
                at = pl.ds(pl.multiple_of(t * keys, keys), keys)
                s = dot_t(left, kv2_ref[at, :])
                new = jnp.maximum(top, jnp.max(s, axis=1, keepdims=True))
                p = jnp.exp2((s - new) * log_scale)
                acc = acc * jnp.exp2((top - new) * log_scale) + dot_n(p.astype(bf16), vo_ref[at, :])
                return new, acc

            top, acc = lax.fori_loop(
                first, last, step, (jnp.full((rows, 1), FAR, f32), jnp.zeros((rows, 128), f32))
            )
            total = pltpu.roll(acc, 64, 1)
            outs.append(acc / total)
            lse = jnp.broadcast_to(top * log_scale, acc.shape) + jnp.log2(acc)
            lse_ref[pl.ds(i, 1), :] = lse.T[0:1, :]
        o = jnp.where(lanes(outs[0].shape) < 64, pltpu.roll(outs[0], 64, 1), outs[1])
        of_ref[j] = o
        o_ref[j] = o.astype(bf16)
        return c

    lax.fori_loop(0, chunks // 2, tile, 0)

def attn_fwd(bounds, q, kv, seg_q, seg_k):
    chunks, keys = seg_k.shape
    vm = pl.BlockSpec(memory_space=pltpu.VMEM)
    return pl.pallas_call(
        attn_fwd_kernel,
        out_shape=(
            jax.ShapeDtypeStruct(q.shape, bf16),
            jax.ShapeDtypeStruct(q.shape, f32),
            jax.ShapeDtypeStruct(seg_q.shape, f32),
            jax.ShapeDtypeStruct((chunks * keys, 256), bf16),
        ),
        in_specs=[pl.BlockSpec(memory_space=pltpu.SMEM), vm, vm, vm, vm],
        out_specs=(vm, vm, vm, vm),
        scratch_shapes=[pltpu.VMEM((chunks * keys, 128), bf16)],
        compiler_params=pltpu.CompilerParams(vmem_limit_bytes=56 << 20),
        name="attn_fwd",
    )(bounds, q, kv, seg_q, seg_k)

def attn_bwd_kernel(bounds, q_ref, do_ref, of_ref, lse_ref, kv2_ref, seg_q_ref, dq_ref, dkv_ref):
    chunks = seg_q_ref.shape[0]
    keys = kv2_ref.shape[0] // chunks
    log_scale = math.log2(math.e) * DH ** (-0.5)
    dkv_ref[...] = jnp.zeros_like(dkv_ref)

    def tile(j, c):
        q_tile, do_tile = q_ref[j], do_ref[j]
        rows = q_tile.shape[0]
        prod = do_tile.astype(f32) * of_ref[j]
        prod = prod.T
        dqs = []
        for half in range(2):
            i = half * (chunks // 2) + j
            left = half_lanes(q_tile, half)
            grad = do_tile.astype(f32)
            if not half:
                grad = pltpu.roll(grad, 64, 1)
            grad = jnp.where(lanes(grad.shape) < 64, 0.0, grad).astype(bf16)
            delta = jnp.sum(prod[64 * half:64 * half + 64], axis=0, keepdims=True)
            lse = lse_ref[pl.ds(i, 1), :]
            both = jnp.concatenate([left, grad], axis=0)
            marks = query_marks(seg_q_ref[pl.ds(i, 1), :])
            right = jnp.concatenate([both, jnp.concatenate([marks, jnp.zeros_like(marks)], axis=0)], axis=1)
            low, high = bounds[0, i], bounds[1, i]
            first = lax.fori_loop(0, chunks, lambda t, n: n + jnp.where(bounds[1, t] < low, 1, 0), 0)
            last = lax.fori_loop(0, chunks, lambda t, n: n + jnp.where(bounds[0, t] <= high, 1, 0), 0)

            def step(t, dq):
                at = pl.ds(pl.multiple_of(t * keys, keys), keys)
                kv2 = kv2_ref[at, :]
                sdp = dot_t(kv2, right)
                p = jnp.exp2(sdp[:, :rows] * log_scale - lse)
                ds = (p * (sdp[:, rows:] - delta)).astype(bf16)
                dkv_ref[at, :] += dot_n(jnp.concatenate([ds, p.astype(bf16)], axis=1), both)
                return dq + dot_0(ds, kv2[:, 0:128])

            dqs.append(lax.fori_loop(first, last, step, jnp.zeros((rows, 128), f32)))
        dq = jnp.where(lanes(dqs[0].shape) < 64, dqs[0], pltpu.roll(dqs[1], 64, 1))
        dq_ref[j] = (dq * DH ** (-0.5)).astype(bf16)
        return c

    lax.fori_loop(0, chunks // 2, tile, 0)
    dkv = dkv_ref[...]
    dkv_ref[...] = jnp.where(lanes(dkv.shape) < 64, dkv * DH ** (-0.5), dkv)

def attn_bwd(bounds, q, do, of, lse, kv2, seg_q):
    vm = pl.BlockSpec(memory_space=pltpu.VMEM)
    return pl.pallas_call(
        attn_bwd_kernel,
        out_shape=(
            jax.ShapeDtypeStruct(q.shape, bf16),
            jax.ShapeDtypeStruct((kv2.shape[0], 128), f32),
        ),
        in_specs=[pl.BlockSpec(memory_space=pltpu.SMEM), vm, vm, vm, vm, vm, vm],
        out_specs=(vm, vm),
        compiler_params=pltpu.CompilerParams(vmem_limit_bytes=56 << 20),
        name="attn_bwd",
    )(bounds, q, do, of, lse, kv2, seg_q)


class Spot:
    def __init__(self, nb):
        self.nb, self.nz = nb, nb // 2
        self.h, b = lax.axis_index("head"), lax.axis_index("blk")
        self.z, self.c = b // 2, lax.rem(b, 2)
        self.near = (self.h + 1 - 2 * lax.rem(self.h, 2), lax.rem(self.h + 2, 4))
        self.diag = 3 - self.h
        self.me = self.h * nb + b

    def index(self, h, z, c):
        return h * self.nb + z * 2 + c

    def ahead(self, k):
        return lax.rem(self.z + k, self.nz)


def remote(src, dst, send, recv, h, b):
    return pltpu.make_async_remote_copy(
        src_ref=src,
        dst_ref=dst,
        send_sem=send,
        recv_sem=recv,
        device_id={"head": h, "blk": b},
        device_id_type=MESH,
    )


def each(count, body, start=0):
    def run(i, c):
        body(i)
        return c

    lax.fori_loop(start, count, run, 0)


def greet_all(n, nb, me):
    barrier = pltpu.get_barrier_semaphore()

    def signal(i):
        t = lax.rem(me + i, n)
        pl.semaphore_signal(
            barrier, inc=1, device_id={"head": t // nb, "blk": lax.rem(t, nb)}, device_id_type=MESH
        )

    each(n, signal, 1)
    pl.semaphore_wait(barrier, n - 1)


class Gather:
    def __init__(self, spot, shard, full, send, recv, local):
        self.s, self.shard, self.full, self.local = spot, shard, full, local
        self.send, self.recv = send, recv
        self.half = shard.shape[-1] // 2

    def copy(self, src, dst, k, h, z, c, recv_k=None):
        recv_k = k if recv_k is None else recv_k
        return remote(src, dst, self.send.at[k], self.recv.at[recv_k], h, z * 2 + c)

    def to_z(self, z):
        s = self.s
        return self.copy(self.shard, self.full.at[s.me], z, s.h, z, s.c, s.z)

    def from_z(self, z):
        s = self.s
        slot = self.full.at[s.index(s.h, z, s.c)]
        return self.copy(slot, slot, z, s.h, z, s.c)

    def near(self, w, z, own=False):
        s = self.s
        slot = self.full.at[s.index(s.h, z, s.c)]
        return self.copy(self.shard if own else slot, slot, (1 + w) * s.nz + z, s.near[w], s.z, s.c)

    def from_near(self, w, z):
        s = self.s
        slot = self.full.at[s.index(s.near[w], z, s.c)]
        return self.copy(slot, slot, (1 + w) * s.nz + z, s.near[w], s.z, s.c)

    def lanes(self, slot, w):
        return slot.at[:, pl.ds(w * self.half, self.half)]

    def onward(self, w, z):
        s = self.s
        slot = self.lanes(self.full.at[s.index(s.near[w], z, s.c)], w)
        return self.copy(slot, slot, (3 + w) * s.nz + z, s.near[1 - w], s.z, s.c)

    def from_onward(self, w, z):
        s = self.s
        slot = self.lanes(self.full.at[s.index(s.diag, z, s.c)], w)
        return self.copy(slot, slot, (3 + w) * s.nz + z, s.near[1 - w], s.z, s.c)

    def twin(self, h, z, own=False):
        s = self.s
        slot = self.full.at[s.index(h, z, s.c)]
        return self.copy(self.shard if own else slot, slot, 5 * s.nz + h * s.nz + z, s.h, s.z, 1 - s.c)

    def from_twin(self, h, z):
        s = self.s
        slot = self.full.at[s.index(h, z, 1 - s.c)]
        return self.copy(slot, slot, 5 * s.nz + h * s.nz + z, s.h, s.z, 1 - s.c)

    def begin(self):
        s = self.s
        self.own = pltpu.make_async_copy(self.shard, self.full.at[s.me], self.local)
        self.own.start()
        each(s.nz, lambda k: self.to_z(s.ahead(k)).start(), 1)
        self.near(0, s.z, True).start()
        self.near(1, s.z, True).start()
        self.twin(s.h, s.z, True).start()

    def spread(self):
        s = self.s

        def go(k):
            z = s.ahead(k)
            self.from_z(z).wait_recv()
            self.near(0, z).start()
            self.near(1, z).start()
            self.twin(s.h, z).start()

        each(s.nz, go, 1)

    def cross(self):
        s = self.s

        def go(k):
            z = s.ahead(k)
            for w in range(2):
                self.from_near(w, z).wait_recv()
                self.onward(w, z).start()
                self.twin(s.near[w], z).start()

        each(s.nz, go)

    def last(self):
        s = self.s

        def go(k):
            z = s.ahead(k)
            for w in range(2):
                self.from_onward(w, z).wait_recv()
            self.twin(s.diag, z).start()

        each(s.nz, go)

    def arrive(self):
        s = self.s
        each(4, lambda h: each(s.nz, lambda z: self.from_twin(h, z).wait_recv()))
        self.own.wait()

    def sent(self):
        s = self.s
        each(s.nz, lambda k: self.to_z(s.ahead(k)).wait_send(), 1)

        def go(z):
            for w in range(2):
                self.near(w, z).wait_send()
                self.onward(w, z).wait_send()
            each(4, lambda h: self.twin(h, z).wait_send())

        each(s.nz, go)


class Scatter:
    def __init__(self, spot, part, twin, diag, near, line, send, recv):
        self.s, self.part, self.t, self.d, self.n, self.l = spot, part, twin, diag, near, line
        self.send, self.recv = send, recv
        self.half = part.shape[-1] // 2

    def copy(self, src, dst, k, h, z, c, recv_k=None):
        recv_k = k if recv_k is None else recv_k
        return remote(src, dst, self.send.at[k], self.recv.at[recv_k], h, z * 2 + c)

    def mine(self, h, z):
        return self.s.index(h, z, self.s.c)

    def lanes(self, w):
        return pl.ds(w * self.half, self.half)

    def to_twin(self, h, z):
        s = self.s
        src = self.part.at[s.index(h, z, 1 - s.c)]
        return self.copy(src, self.t.at[h, z], h * s.nz + z, s.h, s.z, 1 - s.c)

    def to_diag(self, w, z):
        s = self.s
        src = self.part.at[self.mine(s.diag, z), :, self.lanes(w)]
        return self.copy(src, self.d.at[w, z], (4 + w) * s.nz + z, s.near[w], s.z, s.c)

    def to_near(self, w, z):
        s = self.s
        src = self.part.at[self.mine(s.near[w], z)]
        return self.copy(src, self.n.at[w, z], (6 + w) * s.nz + z, s.near[w], s.z, s.c)

    def to_line(self, z):
        s = self.s
        src = self.part.at[self.mine(s.h, z)]
        return self.copy(src, self.l.at[s.z], 8 * s.nz + z, s.h, z, s.c, 8 * s.nz + s.z)

    def from_line(self, z):
        s = self.s
        src = self.part.at[self.mine(s.h, z)]
        return self.copy(src, self.l.at[z], 8 * s.nz + z, s.h, z, s.c)

    def begin(self):
        each(4, lambda h: each(self.s.nz, lambda z: self.to_twin(h, z).start()))

    def pair(self, h, z):
        self.to_twin(h, z).wait_recv()
        return self.part[self.mine(h, z)].astype(f32) + self.t[h, z].astype(f32)

    def keep(self, h, z, value):
        self.part[self.mine(h, z)] = value.astype(self.part.dtype)

    def first(self):
        s = self.s

        def go(k):
            z = s.ahead(k)
            self.keep(s.diag, z, self.pair(s.diag, z))
            for w in range(2):
                self.to_diag(w, z).start()

        each(s.nz + 1, go, 1)

    def second(self):
        s = self.s

        def go(k):
            z = s.ahead(k)
            for w in range(2):
                value = self.pair(s.near[w], z)
                self.to_diag(1 - w, z).wait_recv()
                other = self.d[1 - w, z].astype(f32)
                if w == 0:
                    value = jnp.concatenate([value[:, : self.half], value[:, self.half :] + other], axis=1)
                else:
                    value = jnp.concatenate([value[:, : self.half] + other, value[:, self.half :]], axis=1)
                self.keep(s.near[w], z, value)
                self.to_near(w, z).start()

        each(s.nz + 1, go, 1)

    def joined(self, z):
        value = self.pair(self.s.h, z)
        for w in range(2):
            self.to_near(w, z).wait_recv()
            value = value + self.n[w, z].astype(f32)
        return value

    def third(self):
        s = self.s

        def go(k):
            z = s.ahead(k)
            self.keep(s.h, z, self.joined(z))
            self.to_line(z).start()

        each(s.nz, go, 1)

    def total(self):
        s = self.s
        value = self.joined(s.z)

        def go(k, value):
            z = s.ahead(k)
            self.from_line(z).wait_recv()
            return value + self.l[z].astype(f32)

        return lax.fori_loop(1, s.nz, go, value)

    def sent(self):
        s = self.s

        def go(z):
            each(4, lambda h: self.to_twin(h, z).wait_send())
            for w in range(2):
                self.to_diag(w, z).wait_send()
                self.to_near(w, z).wait_send()

        each(s.nz, go)
        each(s.nz, lambda k: self.to_line(s.ahead(k)).wait_send(), 1)


class Exchange:
    def __init__(self, spot, src, dst, send, recv, local):
        self.s, self.src, self.dst, self.send, self.recv, self.local = spot, src, dst, send, recv, local
        self.g = spot.me // 2

    def copy(self, i, back=False):
        s = self.s
        to = lax.rem(self.g + i, 16)
        t = to * 2 + s.c
        src = self.src(to)
        dst = self.dst(lax.rem(self.g + 16 - i, 16)) if back else self.dst(self.g)
        return remote(src, dst, self.send.at[i], self.recv.at[i], t // s.nb, lax.rem(t, s.nb))

    def own(self):
        return pltpu.make_async_copy(self.src(self.g), self.dst(self.g), self.local)

    def begin(self):
        self.own().start()
        each(16, lambda i: self.copy(i).start(), 1)

    def arrive(self, i):
        self.copy(i, True).wait_recv()

    def end(self):
        each(16, self.arrive, 1)
        self.sent()

    def sent(self):
        self.own().wait()
        each(16, lambda i: self.copy(i).wait_send(), 1)


def weave(left, right):
    kind = left.dtype
    left, right = left.astype(f32), right.astype(f32)
    low = lanes(left.shape) < 64
    first = jnp.where(low, left, pltpu.roll(right, 64, 1)).astype(kind)
    second = jnp.where(low, pltpu.roll(left, 64, 1), right).astype(kind)
    return first, second


def any_specs(count):
    return [pl.BlockSpec(memory_space=pl.ANY)] * count


def vmem_specs(count):
    return [pl.BlockSpec(memory_space=pltpu.VMEM)] * count


def project_kernel(
    n, nb, x_ref, wq_ref, wk_ref, wv_ref, wo_ref, wu_ref, wd_ref, vec_ref,
    q_out, kv_out, wa_out, wb_out, wd_out, vec_out,
    sa, sb, wa, kv_send, q_send, ag_send, ag_recv, ag_local, ex_send, ex_recv, ex_local,
    tw_send, tw_recv, out_sem,
):
    s = Spot(nb)
    greet_all(n, nb, s.me)
    for t in range(4):
        tile = slice(128 * t, 128 * t + 128)
        first, second = weave(wk_ref[:, tile], wv_ref[:, tile])
        sa[:, 256 * t:256 * t + 128] = first
        sa[:, 256 * t + 128:256 * t + 256] = second
    sa[:, 1024:1536] = wq_ref[...]
    sb[:, 0:512] = wo_ref[...]
    sb[:, 512:2560] = wu_ref[...]
    jobs = [
        Gather(s, shard, full, ag_send.at[k], ag_recv.at[k], ag_local.at[k])
        for k, (shard, full) in enumerate(((sa, wa), (sb, wb_out), (wd_ref, wd_out), (vec_ref, vec_out)))
    ]
    jobs[0].begin()
    jobs[0].spread()
    jobs[0].cross()
    jobs[0].last()
    for job in jobs[1:]:
        job.begin()
    jobs[0].arrive()
    keep = pltpu.make_async_copy(wa, wa_out, out_sem)
    keep.start()
    qkv = dot_n(x_ref[...], wa[...].reshape(512, 1536)).astype(bf16)
    for m in range(2):
        rows = slice(128 * m, 128 * m + 128)
        for h in range(8):
            kv_send[8 * m + h] = qkv[rows, 128 * h:128 * h + 128].reshape(8, 16, 128)
        for t in range(4):
            tile = qkv[rows, 1024 + 128 * t:1152 + 128 * t]
            first, second = weave(tile[0:64], tile[64:128])
            q_send[8 * m + 2 * t] = first.reshape(4, 16, 128)
            q_send[8 * m + 2 * t + 1] = second.reshape(4, 16, 128)
    kv_ex = Exchange(
        s, lambda p: kv_send.at[p], lambda g: kv_out.at[:, g, s.c], ex_send.at[0], ex_recv.at[0], ex_local.at[0]
    )
    q_ex = Exchange(s, lambda p: q_send.at[p], lambda g: q_out.at[:, g], ex_send.at[1], ex_recv.at[1], ex_local.at[1])
    kv_ex.begin()
    q_ex.begin()
    for job in jobs[1:]:
        job.spread()
    for job in jobs[1:]:
        job.cross()

    def twin(g, c):
        slot = kv_out.at[:, g, c]
        return remote(slot, slot, tw_send.at[g], tw_recv.at[g], s.h, s.z * 2 + 1 - s.c)

    kv_ex.own().wait()
    twin(kv_ex.g, s.c).start()

    def forward(i):
        kv_ex.arrive(i)
        twin(lax.rem(kv_ex.g + 16 - i, 16), s.c).start()

    each(16, forward, 1)
    for job in jobs[1:]:
        job.last()
    for job in jobs[1:]:
        job.arrive()
    each(16, lambda g: twin(g, 1 - s.c).wait_recv())
    each(16, lambda g: twin(g, s.c).wait_send())
    each(16, lambda i: kv_ex.copy(i).wait_send(), 1)
    q_ex.end()
    for job in jobs:
        job.sent()
    keep.wait()


def project(n, nb, x, wq, wk, wv, wo, wu, wd, vec):
    dma = pltpu.SemaphoreType.DMA
    nz = nb // 2
    return pl.pallas_call(
        functools.partial(project_kernel, n, nb),
        out_shape=(
            jax.ShapeDtypeStruct((4, 16, 16, 128), bf16),
            jax.ShapeDtypeStruct((8, 16, 2, 16, 128), bf16),
            jax.ShapeDtypeStruct((n, 16, 1536), bf16),
            jax.ShapeDtypeStruct((n, 16, 2560), bf16),
            jax.ShapeDtypeStruct((n, 64, 512), bf16),
            jax.ShapeDtypeStruct((n, 8, 256), f32),
        ),
        in_specs=vmem_specs(8),
        out_specs=any_specs(6),
        scratch_shapes=[
            pltpu.VMEM((16, 1536), bf16),
            pltpu.VMEM((16, 2560), bf16),
            pltpu.VMEM((n, 16, 1536), bf16),
            pltpu.VMEM((16, 8, 16, 128), bf16),
            pltpu.VMEM((16, 4, 16, 128), bf16),
            dma((4, 9 * nz)),
            dma((4, 9 * nz)),
            dma((4,)),
            dma((2, 16)),
            dma((2, 16)),
            dma((2,)),
            dma((16,)),
            dma((16,)),
            dma,
        ],
        compiler_params=pltpu.CompilerParams(
            collective_id=1, has_side_effects=True, vmem_limit_bytes=40 << 20
        ),
        name="project",
    )(x, wq, wk, wv, wo, wu, wd, vec)


def row_norm(v):
    mean = jnp.mean(v, axis=-1, keepdims=True)
    mid = v - mean
    inv = lax.rsqrt(jnp.mean(mid * mid, axis=-1, keepdims=True) + EPSILON)
    return mid * inv, inv


def row_norm_back(grad, normed, inv, gain):
    part = grad * gain
    return inv * (
        part
        - jnp.mean(part, axis=-1, keepdims=True)
        - normed * jnp.mean(part * normed, axis=-1, keepdims=True)
    )


def column_sum(v):
    return jnp.sum(v, axis=0, keepdims=True)


def middle_kernel(
    n, nb, o_ref, x_ref, y_ref, g_ref, wb_hbm, wd_hbm, par_ref, bup_ref,
    do_out, out_ref, dacc_ref, dz1_ref, x1_ref, dur_ref, h_ref, dfr_ref, omix_ref, dar_ref, pg_ref, bg_ref,
    wb, wd, o_recv, do_send, slope, ex_send, ex_recv, ex_local, in_sem,
):
    s = Spot(nb)
    load_b = pltpu.make_async_copy(wb_hbm, wb, in_sem.at[0])
    load_d = pltpu.make_async_copy(wd_hbm, wd, in_sem.at[1])
    load_b.start()
    load_d.start()
    greet_all(n, nb, s.me)
    o_ex = Exchange(
        s, lambda p: o_ref.at[:, p], lambda g: o_recv.at[g], ex_send.at[0], ex_recv.at[0], ex_local.at[0]
    )
    o_ex.begin()
    load_b.wait()
    load_d.wait()
    o_ex.end()
    for m in range(2):
        for t in range(4):
            first, second = weave(
                o_recv[8 * m + 2 * t].reshape(64, 128), o_recv[8 * m + 2 * t + 1].reshape(64, 128)
            )
            omix_ref[128 * m:128 * m + 64, 128 * t:128 * t + 128] = first
            omix_ref[128 * m + 64:128 * m + 128, 128 * t:128 * t + 128] = second
    gain1, bias1 = par_ref[1:2], par_ref[2:3]
    gain2, bias2 = par_ref[3:4], par_ref[4:5]
    gain3, bias3 = par_ref[5:6], par_ref[6:7]
    w_out = wb[:, :, 0:512].reshape(512, 512)
    a = dot_n(omix_ref[...], w_out)
    n1, r1 = row_norm(x_ref[...].astype(f32) + a)
    x1 = n1 * gain1 + bias1
    x1r = x1.astype(bf16)
    x1_ref[...] = x1r
    feed = jnp.zeros_like(x1)
    for t in range(4):
        cols = slice(512 * t, 512 * t + 512)
        u = dot_n(x1r, wb[:, :, 512 + 512 * t:1024 + 512 * t].reshape(512, 512)) + bup_ref[:, cols]
        phi = 0.5 * (1.0 + lax.erf(u * (0.5**0.5)))
        hid = (u * phi).astype(bf16)
        slope[:, cols] = phi + u * jnp.exp(-0.5 * u * u) * ((2.0 * math.pi) ** -0.5)
        h_ref[:, cols] = hid
        feed = feed + dot_n(hid, wd[8 * t:8 * t + 8].reshape(512, 512))
    feed = feed + par_ref[0:1]
    n2, r2 = row_norm(x1 + feed)
    n3, r3 = row_norm(y_ref[...].astype(f32) + a + feed)
    out_ref[...] = (n2 * gain2 + bias2 + (n3 * gain3 + bias3)).astype(bf16)
    g = g_ref[...].astype(f32)
    dacc = row_norm_back(g, n3, r3, gain3)
    dacc_ref[...] = dacc
    dz2 = row_norm_back(g, n2, r2, gain2)
    df = dz2 + dacc
    dfr = df.astype(bf16)
    dfr_ref[...] = dfr
    dx1 = dz2
    for t in range(4):
        cols = slice(512 * t, 512 * t + 512)
        du = dot_t(dfr, wd[8 * t:8 * t + 8].reshape(512, 512)) * slope[:, cols]
        bg_ref[:, cols] = column_sum(du)
        dur = du.astype(bf16)
        dur_ref[:, cols] = dur
        dx1 = dx1 + dot_t(dur, wb[:, :, 512 + 512 * t:1024 + 512 * t].reshape(512, 512))
    dz1 = row_norm_back(dx1, n1, r1, gain1)
    dz1_ref[...] = dz1
    dar = (dz1 + dacc).astype(bf16)
    dar_ref[...] = dar
    do = dot_t(dar, w_out).astype(bf16)
    for m in range(2):
        for t in range(4):
            tile = do[128 * m:128 * m + 128, 128 * t:128 * t + 128]
            first, second = weave(tile[0:64], tile[64:128])
            do_send[8 * m + 2 * t] = first.reshape(4, 16, 128)
            do_send[8 * m + 2 * t + 1] = second.reshape(4, 16, 128)
    do_ex = Exchange(
        s, lambda p: do_send.at[p], lambda g: do_out.at[:, g], ex_send.at[1], ex_recv.at[1], ex_local.at[1]
    )
    do_ex.begin()
    pg_ref[0:1] = column_sum(df)
    pg_ref[1:2] = column_sum(dx1 * n1)
    pg_ref[2:3] = column_sum(dx1)
    pg_ref[3:4] = column_sum(g * n2)
    pg_ref[4:5] = column_sum(g)
    pg_ref[5:6] = column_sum(g * n3)
    pg_ref[6:7] = column_sum(g)
    pg_ref[7:8] = jnp.zeros((1, 512), f32)
    do_ex.end()


def middle(n, nb, o, x, y, g, wb, wd, par, bup):
    dma = pltpu.SemaphoreType.DMA
    rows = x.shape[0]

    def wide(width, kind):
        return jax.ShapeDtypeStruct((rows, width), kind)

    return pl.pallas_call(
        functools.partial(middle_kernel, n, nb),
        out_shape=(
            jax.ShapeDtypeStruct((4, 16, 16, 128), bf16),
            wide(512, bf16), wide(512, f32), wide(512, f32), wide(512, bf16), wide(2048, bf16),
            wide(2048, bf16), wide(512, bf16), wide(512, bf16), wide(512, bf16),
            jax.ShapeDtypeStruct((8, 512), f32),
            jax.ShapeDtypeStruct((1, 2048), f32),
        ),
        in_specs=vmem_specs(4) + any_specs(2) + vmem_specs(2),
        out_specs=any_specs(1) + vmem_specs(11),
        scratch_shapes=[
            pltpu.VMEM(wb.shape, bf16),
            pltpu.VMEM(wd.shape, bf16),
            pltpu.VMEM((16, 4, 16, 128), bf16),
            pltpu.VMEM((16, 4, 16, 128), bf16),
            pltpu.VMEM((rows, 2048), f32),
            dma((2, 16)),
            dma((2, 16)),
            dma((2,)),
            dma((2,)),
        ],
        compiler_params=pltpu.CompilerParams(
            collective_id=2, has_side_effects=True, vmem_limit_bytes=50 << 20
        ),
        name="middle",
    )(o, x, y, g, wb, wd, par, bup)


def finish_kernel(
    n, nb, dq_ref, dkv_ref, x_ref, dz1_ref, x1_ref, dur_ref, h_ref, dfr_ref, omix_ref, dar_ref, gv_ref, wa_ref,
    gx_ref, gq_ref, gk_ref, gv_out, go_ref, gu_ref, gd_ref, gvec_ref,
    pa, ta, da, na, la, pb, tb, db, nb_, lb, pd, td, dd, nd, ld, pv, tv, dv, nv, lv,
    twin_buf, dkv_send, dkv_recv, dq_recv, dqkv, rs_send, rs_recv, ex_send, ex_recv, ex_local, tw_send, tw_recv,
):
    s = Spot(nb)
    greet_all(n, nb, s.me)
    swap = remote(dkv_ref.at[:, :, 1 - s.c], twin_buf, tw_send, tw_recv, s.h, s.z * 2 + 1 - s.c)
    swap.start()
    jobs = [
        Scatter(s, *bufs, rs_send.at[k], rs_recv.at[k])
        for k, bufs in enumerate(
            ((pb, tb, db, nb_, lb), (pd, td, dd, nd, ld), (pv, tv, dv, nv, lv), (pa, ta, da, na, la))
        )
    ]
    pv[...] = gv_ref[...]
    jobs[2].begin()
    pb[:, :, 0:512] = dot_0(omix_ref[...], dar_ref[...]).astype(bf16).reshape(n, 16, 512)
    for t in range(4):
        cols = slice(512 * t, 512 * t + 512)
        pb[:, :, 512 + 512 * t:1024 + 512 * t] = (
            dot_0(x1_ref[...], dur_ref[:, cols]).astype(bf16).reshape(n, 16, 512)
        )
    jobs[0].begin()
    for t in range(4):
        cols = slice(512 * t, 512 * t + 512)
        pd[8 * t:8 * t + 8] = dot_0(h_ref[:, cols], dfr_ref[...]).astype(bf16).reshape(8, 64, 512)
    jobs[1].begin()
    swap.wait()

    def add(g):
        dkv_send[g] = (dkv_ref[:, g, s.c] + twin_buf[:, g]).astype(bf16)

    each(16, add)
    kv_ex = Exchange(
        s, lambda p: dkv_send.at[p], lambda g: dkv_recv.at[g], ex_send.at[0], ex_recv.at[0], ex_local.at[0]
    )
    q_ex = Exchange(s, lambda p: dq_ref.at[:, p], lambda g: dq_recv.at[g], ex_send.at[1], ex_recv.at[1], ex_local.at[1])
    kv_ex.begin()
    q_ex.begin()
    for job in jobs[:3]:
        job.first()
    for job in jobs[:3]:
        job.second()
    for job in jobs[:3]:
        job.third()
    kv_ex.end()
    q_ex.end()
    for m in range(2):
        rows = slice(128 * m, 128 * m + 128)
        for h in range(8):
            dqkv[rows, 128 * h:128 * h + 128] = dkv_recv[8 * m + h].reshape(128, 128)
        for t in range(4):
            first, second = weave(
                dq_recv[8 * m + 2 * t].reshape(64, 128), dq_recv[8 * m + 2 * t + 1].reshape(64, 128)
            )
            dqkv[128 * m:128 * m + 64, 1024 + 128 * t:1152 + 128 * t] = first
            dqkv[128 * m + 64:128 * m + 128, 1024 + 128 * t:1152 + 128 * t] = second
    for t in range(3):
        cols = slice(512 * t, 512 * t + 512)
        pa[:, :, cols] = dot_0(x_ref[...], dqkv[:, cols]).astype(bf16).reshape(n, 16, 512)
    jobs[3].begin()
    gx_ref[...] = dz1_ref[...] + dot_t(dqkv[...], wa_ref[...].reshape(512, 1536))
    total = jobs[0].total()
    go_ref[...] = total[:, 0:512]
    gu_ref[...] = total[:, 512:2560]
    gd_ref[...] = jobs[1].total()
    gvec_ref[...] = jobs[2].total()
    jobs[3].first()
    jobs[3].second()
    jobs[3].third()
    total = jobs[3].total()
    gq_ref[...] = total[:, 1024:1536]
    for t in range(4):
        first, second = weave(total[:, 256 * t:256 * t + 128], total[:, 256 * t + 128:256 * t + 256])
        gk_ref[:, 128 * t:128 * t + 128] = first
        gv_out[:, 128 * t:128 * t + 128] = second
    for job in jobs:
        job.sent()


def finish(n, nb, dq, dkv, x, dz1, x1, dur, hid, dfr, omix, dar, gvec, wa):
    dma = pltpu.SemaphoreType.DMA
    nz = nb // 2
    rows = x.shape[0]

    def buffers(depth, width, kind):
        return [
            pltpu.VMEM((n, depth, width), kind),
            pltpu.VMEM((4, nz, depth, width), kind),
            pltpu.VMEM((2, nz, depth, width // 2), kind),
            pltpu.VMEM((2, nz, depth, width), kind),
            pltpu.VMEM((nz, depth, width), kind),
        ]

    def wide(height, width):
        return jax.ShapeDtypeStruct((height, width), f32)

    return pl.pallas_call(
        functools.partial(finish_kernel, n, nb),
        out_shape=(
            wide(rows, 512), wide(16, 512), wide(16, 512), wide(16, 512), wide(16, 512), wide(16, 2048),
            wide(64, 512), wide(8, 256),
        ),
        in_specs=vmem_specs(12),
        out_specs=vmem_specs(8),
        scratch_shapes=[
            *buffers(16, 1536, bf16),
            *buffers(16, 2560, bf16),
            *buffers(64, 512, bf16),
            *buffers(8, 256, f32),
            pltpu.VMEM((8, 16, 16, 128), f32),
            pltpu.VMEM((16, 8, 16, 128), bf16),
            pltpu.VMEM((16, 8, 16, 128), bf16),
            pltpu.VMEM((16, 4, 16, 128), bf16),
            pltpu.VMEM((rows, 1536), bf16),
            dma((4, 9 * nz)),
            dma((4, 9 * nz)),
            dma((2, 16)),
            dma((2, 16)),
            dma((2,)),
            dma,
            dma,
        ],
        compiler_params=pltpu.CompilerParams(
            collective_id=3, has_side_effects=True, vmem_limit_bytes=58 << 20
        ),
        name="finish",
    )(dq, dkv, x, dz1, x1, dur, hid, dfr, omix, dar, gvec, wa)


def by_pairs(
    stream, accumulator, upstream, segment_ids, w_query, w_key, w_value, w_out, w_up, b_up, w_down, b_down,
    gain_attn, bias_attn, gain_ffn, bias_ffn, gain_final, bias_final,
):
    nb = lax.axis_size("blk")
    n = 4 * nb
    x = stream.reshape(256, 512)
    y = accumulator.reshape(256, 512)
    g = upstream.reshape(256, 512)
    small = (b_down, gain_attn, bias_attn, gain_ffn, bias_ffn, gain_final, bias_final)
    row = jnp.concatenate([b_up.astype(f32), *(v.astype(f32) for v in small), jnp.zeros((80,), f32)])
    seg_row = segment_ids.astype(f32).reshape(256)
    vec = jnp.concatenate([row[None], seg_row[None], jnp.zeros((6, 256), f32)], axis=0)
    q, kv, wa, wb, wd, vecs = project(n, nb, x, w_query, w_key, w_value, w_out, w_up, w_down, vec)
    bup = vecs[:, 0, 0:64].reshape(1, 2048)
    par = jnp.pad(vecs[:, 0, 64:176].reshape(n, 7, 16).transpose(1, 0, 2).reshape(7, 512), ((0, 1), (0, 0)))
    me = lax.axis_index("head") * nb + lax.axis_index("blk")
    pair = me // 2
    seg = vecs[:, 1].reshape(n, 2, 8, 16).astype(jnp.int32)
    seg = lax.dynamic_index_in_dim(seg, pair // 8, 1, False)
    seg_k = seg.transpose(1, 0, 2).reshape(8, 16 * n)
    seg_q = lax.dynamic_index_in_dim(seg.reshape(n // 2, 2, 8, 16), lax.rem(me, 2), 1, False)
    seg_q = seg_q.transpose(1, 0, 2).reshape(8, 8 * n)
    bounds = jnp.stack([seg_k[:, 0], seg_k[:, -1]])
    o, of, lse, kv2 = attn_fwd(bounds, q.reshape(4, 256, 128), kv.reshape(4096, 128), seg_q, seg_k)
    do, out, dacc, dz1, x1, dur, hid, dfr, omix, dar, pg, bg = middle(
        n, nb, o.reshape(4, 16, 16, 128), x, y, g, wb, wd, par, bup
    )
    gvec = jnp.concatenate(
        [bg.reshape(n, 64), pg[0:7].reshape(7, n, 16).transpose(1, 0, 2).reshape(n, 112), jnp.zeros((n, 80), f32)], axis=1
    )
    gvec = jnp.pad(gvec[:, None], ((0, 0), (0, 7), (0, 0)))
    dq, dkv = attn_bwd(bounds, q.reshape(4, 256, 128), do.reshape(4, 256, 128), of, lse, kv2, seg_q)
    gx, gq, gk, gv, go, gu, gd, gs = finish(
        n, nb, dq.reshape(4, 16, 16, 128), dkv.reshape(8, 16, 2, 16, 128), x, dz1, x1, dur, hid, dfr, omix, dar, gvec, wa
    )
    gs = gs[0]
    smalls = [gs[64 + 16 * k:80 + 16 * k] for k in range(7)]
    return (
        out.reshape(stream.shape), gx.reshape(stream.shape), dacc.reshape(stream.shape),
        gq, gk, gv, go, gu, gs[0:64], gd, *smalls,
    )


def pairs_fit(mesh, shape):
    return mesh.shape["head"] == 4 and mesh.shape["blk"] == 8 and shape == (2, 32, 128, 512)


def solution(mesh):
    def step(*args):
        return run(by_pairs if pairs_fit(mesh, args[0].shape) else local, mesh)(*args)

    return step


def run(body, mesh):
    return jax.shard_map(
        body,
        mesh=mesh,
        in_specs=(
            P(None, ("head", "blk"), None, None),
            P(None, ("head", "blk"), None, None),
            P(None, ("head", "blk"), None, None),
            P(None, ("head", "blk"), None),
            P(("head", "blk"), None),
            P(("head", "blk"), None),
            P(("head", "blk"), None),
            P(("head", "blk"), None),
            P(("head", "blk"), None),
            P(("head", "blk")),
            P(("head", "blk"), None),
            P(("head", "blk")),
            P(("head", "blk")),
            P(("head", "blk")),
            P(("head", "blk")),
            P(("head", "blk")),
            P(("head", "blk")),
            P(("head", "blk")),
        ),
        out_specs=(
            P(None, ("head", "blk"), None, None),
            P(None, ("head", "blk"), None, None),
            P(None, ("head", "blk"), None, None),
            P(("head", "blk"), None),
            P(("head", "blk"), None),
            P(("head", "blk"), None),
            P(("head", "blk"), None),
            P(("head", "blk"), None),
            P(("head", "blk")),
            P(("head", "blk"), None),
            P(("head", "blk")),
            P(("head", "blk")),
            P(("head", "blk")),
            P(("head", "blk")),
            P(("head", "blk")),
            P(("head", "blk")),
            P(("head", "blk")),
        ),
        check_vma=False,
    )
```

```python
import functools
import math

import jax
import jax.numpy as jnp
from jax import lax
from jax.experimental import pallas as pl
from jax.experimental.pallas import tpu as pltpu
from jax.sharding import PartitionSpec as P

DH = 64
f32, bf16 = jnp.float32, jnp.bfloat16
MESH = pl.DeviceIdType.MESH
FAR = -1e30
VMEM_BYTES = 60 << 20


EPSILON = 1e-05


def norm_forward(inputs, norm_gain, norm_bias):
    average = jnp.mean(inputs, axis=-1, keepdims=True)
    centered = inputs - average
    inv_std = lax.rsqrt(jnp.mean(centered * centered, axis=-1, keepdims=True) + EPSILON)
    normed = centered * inv_std
    return (normed * norm_gain + norm_bias, normed, inv_std)


def norm_backward(gradient, normed, inv_std, norm_gain):
    scaled = gradient * norm_gain
    projected = (
        scaled
        - jnp.mean(scaled, axis=-1, keepdims=True)
        - normed * jnp.mean(scaled * normed, axis=-1, keepdims=True)
    )
    return (inv_std * projected, jnp.sum(gradient * normed, axis=0), jnp.sum(gradient, axis=0))


def smooth_gate(pre_act):
    return jax.nn.gelu(pre_act, approximate=False)


def split_rows(length):
    block_len = math.gcd(length, 512)
    return (length // block_len, block_len)


def block_scores(queries, query_seg, key_rows, key_seg, scaling):
    scores = (
        jnp.einsum("sgd,kgd->sgk", queries, key_rows, preferred_element_type=jnp.float32) * scaling
    )
    allowed = query_seg[:, None, None] == key_seg[None, None, :]
    return (scores, allowed)


def block_grads(
    queries, query_seg, grad_rows, log_total, row_delta, key_rows, value_rows, key_seg, scaling
):
    scores, allowed = block_scores(queries, query_seg, key_rows, key_seg, scaling)
    attn_prob = jnp.where(allowed, jnp.exp(scores - log_total[:, :, None]), 0.0)
    prob_grad = jnp.einsum(
        "sgd,kgd->sgk", grad_rows, value_rows, preferred_element_type=jnp.float32
    )
    score_grad = (attn_prob * (prob_grad - row_delta[:, :, None]) * scaling).astype(jnp.bfloat16)
    return (attn_prob.astype(jnp.bfloat16), score_grad)


def key_blocks(key_rows, value_rows, key_seg, groups):
    block_num, block_len = split_rows(key_rows.shape[0])
    return (
        key_rows.reshape(block_num, block_len, groups, -1),
        value_rows.reshape(block_num, block_len, groups, -1),
        key_seg.reshape(block_num, block_len),
    )


def attend_fold(queries, query_seg, scaling, carried, portion):
    key_rows, value_rows, key_seg = portion

    def step(running, blocks):
        key_part, value_part, seg_part = blocks
        old_max, old_total, weighted = running
        scores, allowed = block_scores(queries, query_seg, key_part, seg_part, scaling)
        row_max = jnp.maximum(old_max, jnp.max(jnp.where(allowed, scores, -1e30), axis=2))
        exp_scores = jnp.where(allowed, jnp.exp(scores - row_max[:, :, None]), 0.0)
        rescale = jnp.exp(old_max - row_max)
        new_total = old_total * rescale + jnp.sum(exp_scores, axis=2)
        weighted = weighted * rescale[:, :, None] + jnp.einsum(
            "sgk,kgd->sgd",
            exp_scores.astype(jnp.bfloat16),
            value_part,
            preferred_element_type=jnp.float32,
        )
        return ((row_max, new_total, weighted), None)

    running, unused = lax.scan(
        step, carried, key_blocks(key_rows, value_rows, key_seg, queries.shape[1])
    )
    return running


def local(
    stream,
    accumulator,
    upstream,
    segment_ids,
    w_query,
    w_key,
    w_value,
    w_out,
    w_up,
    b_up,
    w_down,
    b_down,
    gain_attn,
    bias_attn,
    gain_ffn,
    bias_ffn,
    gain_final,
    bias_final,
):
    heads_axis = lax.axis_size("head")
    micro = stream.shape[0]
    tokens = stream.shape[2]
    width = stream.shape[3]
    group_width = width // heads_axis
    groups = group_width // DH
    scaling = DH ** (-0.5)
    f32 = jnp.float32
    bf16 = jnp.bfloat16
    out_list = []
    stream_grads = []
    accum_grads = []
    grad_totals = None
    for micro_step in range(micro):
        (
            q_weight,
            k_weight,
            v_weight,
            o_weight,
            up_weight,
            up_bias,
            down_weight,
            down_bias,
            gain_one,
            shift_one,
            gain_two,
            shift_two,
            gain_three,
            shift_three,
        ) = (
            lax.all_gather(w_query, ("head", "blk"), axis=0, tiled=True),
            lax.all_gather(w_key, ("head", "blk"), axis=0, tiled=True),
            lax.all_gather(w_value, ("head", "blk"), axis=0, tiled=True),
            lax.all_gather(w_out, ("head", "blk"), axis=0, tiled=True),
            lax.all_gather(w_up, ("head", "blk"), axis=0, tiled=True),
            lax.all_gather(b_up, ("head", "blk"), axis=0, tiled=True),
            lax.all_gather(w_down, ("head", "blk"), axis=0, tiled=True),
            lax.all_gather(b_down, ("head", "blk"), axis=0, tiled=True),
            lax.all_gather(gain_attn, ("head", "blk"), axis=0, tiled=True),
            lax.all_gather(bias_attn, ("head", "blk"), axis=0, tiled=True),
            lax.all_gather(gain_ffn, ("head", "blk"), axis=0, tiled=True),
            lax.all_gather(bias_ffn, ("head", "blk"), axis=0, tiled=True),
            lax.all_gather(gain_final, ("head", "blk"), axis=0, tiled=True),
            lax.all_gather(bias_final, ("head", "blk"), axis=0, tiled=True),
        )
        inputs = stream[micro_step, 0]
        input_wide = inputs.astype(f32)
        carried = accumulator[micro_step, 0].astype(f32)
        segs = segment_ids[micro_step, 0]
        projections = jnp.stack(
            [
                jnp.dot(inputs, q_weight, preferred_element_type=f32),
                jnp.dot(inputs, k_weight, preferred_element_type=f32),
                jnp.dot(inputs, v_weight, preferred_element_type=f32),
            ]
        ).astype(bf16)
        projections = projections.reshape(3, tokens, heads_axis, group_width)
        seg_wide = jnp.broadcast_to(segs[None, :, None, None], (1, tokens, heads_axis, 1))
        regrouped, seg_group = (
            lax.all_to_all(projections, "head", split_axis=2, concat_axis=1, tiled=True),
            lax.all_to_all(seg_wide, "head", split_axis=2, concat_axis=1, tiled=True),
        )
        rows = regrouped.shape[1]
        query_loc = regrouped[0, :, 0]
        key_loc = regrouped[1, :, 0]
        value_loc = regrouped[2, :, 0]
        seg_loc = seg_group[0, :, 0, 0]
        queries3 = query_loc.reshape(rows, groups, DH)
        start_state = (
            jnp.full((rows, groups), -1e30, f32),
            jnp.zeros((rows, groups), f32),
            jnp.zeros((rows, groups, DH), f32),
        )
        row_max, row_total, weighted = attend_fold(
            queries3,
            seg_loc,
            scaling,
            start_state,
            (
                lax.all_gather(key_loc, "blk", axis=0, tiled=True),
                lax.all_gather(value_loc, "blk", axis=0, tiled=True),
                lax.all_gather(seg_loc, "blk", axis=0, tiled=True),
            ),
        )
        attn_out = weighted / row_total[:, :, None]
        log_total = row_max + jnp.log(row_total)
        attn_send = attn_out.astype(bf16).reshape(rows, 1, group_width)
        mixed = lax.all_to_all(attn_send, "head", split_axis=0, concat_axis=1, tiled=True).reshape(
            tokens, width
        )
        branch = jnp.dot(mixed, o_weight, preferred_element_type=f32)
        first, normed_one, inv_one = norm_forward(
            input_wide + branch, gain_one.astype(f32), shift_one.astype(f32)
        )
        first_low = first.astype(bf16)
        hidden_pre = jnp.dot(first_low, up_weight, preferred_element_type=f32) + up_bias.astype(f32)
        hidden_act, gate_pull = jax.vjp(smooth_gate, hidden_pre)
        hidden = hidden_act.astype(bf16)
        feed = jnp.dot(hidden, down_weight, preferred_element_type=f32) + down_bias.astype(f32)
        second, normed_two, inv_two = norm_forward(
            first + feed, gain_two.astype(f32), shift_two.astype(f32)
        )
        final, normed_three, inv_three = norm_forward(
            carried + branch + feed, gain_three.astype(f32), shift_three.astype(f32)
        )
        out_list.append((second + final).astype(bf16))
        cotangent = upstream[micro_step, 0].astype(f32)
        accum_grad, gain3_grad, shift3_grad = norm_backward(
            cotangent, normed_three, inv_three, gain_three.astype(f32)
        )
        second_grad, gain2_grad, shift2_grad = norm_backward(
            cotangent, normed_two, inv_two, gain_two.astype(f32)
        )
        feed_grad = second_grad + accum_grad
        feed_low = feed_grad.astype(bf16)
        down_grad = jnp.dot(hidden.T, feed_low, preferred_element_type=f32)
        (hidden_grad,) = gate_pull(jnp.dot(feed_low, down_weight.T, preferred_element_type=f32))
        hidden_low = hidden_grad.astype(bf16)
        up_grad = jnp.dot(first_low.T, hidden_low, preferred_element_type=f32)
        first_grad = second_grad + jnp.dot(hidden_low, up_weight.T, preferred_element_type=f32)
        resid_grad, gain1_grad, shift1_grad = norm_backward(
            first_grad, normed_one, inv_one, gain_one.astype(f32)
        )
        branch_low = (resid_grad + accum_grad).astype(bf16)
        out_wgrad = jnp.dot(mixed.T, branch_low, preferred_element_type=f32)
        mixed_grad = jnp.dot(branch_low, o_weight.T, preferred_element_type=f32).astype(bf16)
        mixed_grad = mixed_grad.reshape(tokens, heads_axis, group_width)
        grad_group = lax.all_to_all(mixed_grad, "head", split_axis=1, concat_axis=0, tiled=True)
        grad_loc = grad_group[:, 0]
        grad3 = grad_loc.reshape(rows, groups, DH)
        row_delta = jnp.sum(grad3.astype(f32) * attn_out, axis=2)
        whole_keys, whole_values, whole_seg = (
            lax.all_gather(key_loc, "blk", axis=0, tiled=True),
            lax.all_gather(value_loc, "blk", axis=0, tiled=True),
            lax.all_gather(seg_loc, "blk", axis=0, tiled=True),
        )

        def backward_step(running, blocks):
            key_part, value_part, seg_part = blocks
            attn_prob, score_grad = block_grads(
                queries3,
                seg_loc,
                grad3,
                log_total,
                row_delta,
                key_part,
                value_part,
                seg_part,
                scaling,
            )
            running = running + jnp.einsum(
                "sgk,kgd->sgd", score_grad, key_part, preferred_element_type=f32
            )
            key_term = jnp.einsum("sgk,sgd->kgd", score_grad, queries3, preferred_element_type=f32)
            value_term = jnp.einsum("sgk,sgd->kgd", attn_prob, grad3, preferred_element_type=f32)
            return (running, (key_term, value_term))

        query_grad, (key_terms, value_terms) = lax.scan(
            backward_step,
            jnp.zeros((rows, groups, DH), f32),
            key_blocks(whole_keys, whole_values, whole_seg, groups),
        )
        key_grad, value_grad = (
            lax.psum_scatter(
                key_terms.reshape(-1, group_width), "blk", scatter_dimension=0, tiled=True
            ),
            lax.psum_scatter(
                value_terms.reshape(-1, group_width), "blk", scatter_dimension=0, tiled=True
            ),
        )
        grad_stack = jnp.stack(
            [query_grad.reshape(rows, group_width), key_grad, value_grad]
        ).astype(bf16)
        grad_stack = grad_stack.reshape(3, rows, 1, group_width)
        returned = lax.all_to_all(
            grad_stack, "head", split_axis=1, concat_axis=2, tiled=True
        ).reshape(3, tokens, width)
        query_wgrad = jnp.dot(inputs.T, returned[0], preferred_element_type=f32)
        key_wgrad = jnp.dot(inputs.T, returned[1], preferred_element_type=f32)
        value_wgrad = jnp.dot(inputs.T, returned[2], preferred_element_type=f32)
        input_grad = (
            resid_grad
            + jnp.dot(returned[0], q_weight.T, preferred_element_type=f32)
            + jnp.dot(returned[1], k_weight.T, preferred_element_type=f32)
            + jnp.dot(returned[2], v_weight.T, preferred_element_type=f32)
        )
        stream_grads.append(input_grad)
        accum_grads.append(accum_grad)
        step_grads = (
            query_wgrad,
            key_wgrad,
            value_wgrad,
            out_wgrad,
            up_grad,
            jnp.sum(hidden_grad, axis=0),
            down_grad,
            jnp.sum(feed_grad, axis=0),
            gain1_grad,
            shift1_grad,
            gain2_grad,
            shift2_grad,
            gain3_grad,
            shift3_grad,
        )
        if grad_totals is None:
            grad_totals = step_grads
        else:
            grad_totals = tuple((older + newer for older, newer in zip(grad_totals, step_grads)))
    summed = lax.psum_scatter(grad_totals, ("head", "blk"), scatter_dimension=0, tiled=True)
    layer_out = jnp.stack(out_list)[:, None]
    grad_stream = jnp.stack(stream_grads)[:, None]
    grad_accum = jnp.stack(accum_grads)[:, None]
    return (
        layer_out,
        grad_stream,
        grad_accum,
        summed[0],
        summed[1],
        summed[2],
        summed[3],
        summed[4],
        summed[5],
        summed[6],
        summed[7],
        summed[8],
        summed[9],
        summed[10],
        summed[11],
        summed[12],
        summed[13],
    )


def dot_t(a, b):
    return lax.dot_general(a, b, (((1,), (1,)), ((), ())), preferred_element_type=f32)

def dot_n(a, b):
    return lax.dot_general(a, b, (((1,), (0,)), ((), ())), preferred_element_type=f32)

def dot_0(a, b):
    return lax.dot_general(a, b, (((0,), (0,)), ((), ())), preferred_element_type=f32)

def lanes(shape):
    return lax.broadcasted_iota(jnp.int32, shape, len(shape) - 1)

def query_marks(seg_row):
    wide = jnp.broadcast_to(seg_row, (128, seg_row.shape[1])).T
    return (wide == lanes(wide.shape)).astype(f32).astype(bf16)

def half_lanes(tile, half):
    wide = tile.astype(f32)
    if half:
        wide = pltpu.roll(wide, 64, 1)
    return jnp.where(lanes(wide.shape) < 64, wide, 0.0).astype(bf16)

def attn_fwd_kernel(
    q_hbm, kv_hbm, seg_q_hbm, seg_k_hbm, o_hbm, of_hbm, lse_hbm, kv2_hbm,
    q_ref, kv_ref, seg_q_ref, seg_k_ref, bounds, o_ref, of_ref, lse_ref, kv2_ref, vo_ref, in_sem, out_sem,
):
    loads = copies(
        [(seg_q_hbm, seg_q_ref), (seg_k_hbm, seg_k_ref), (seg_k_hbm, bounds), (kv_hbm, kv_ref), (q_hbm, q_ref)], in_sem
    )
    wait_all(loads)
    chunks, keys = seg_k_ref.shape
    log_scale = math.log2(math.e) * DH ** (-0.5)

    def prepare(t, c):
        rows = pl.ds(pl.multiple_of(t * keys, keys), keys)
        kv = kv_ref[rows, :]
        wide = jnp.broadcast_to(seg_k_ref[pl.ds(t, 1), :], (128, keys)).T
        kv2_ref[rows, 0:128] = kv
        kv2_ref[rows, 128:256] = jnp.where(wide == lanes(wide.shape), 0.0, FAR).astype(bf16)
        vo_ref[rows, :] = jnp.where(lanes(kv.shape) < 64, 1.0, kv.astype(f32)).astype(bf16)
        return c

    lax.fori_loop(0, chunks, prepare, 0)
    stores = copies([(kv2_ref, kv2_hbm)], out_sem)

    def tile(j, c):
        q_tile = q_ref[j]
        rows = q_tile.shape[0]
        outs = []
        for half in range(2):
            i = half * (chunks // 2) + j
            left = half_lanes(q_tile, half)
            left = jnp.concatenate([left, query_marks(seg_q_ref[pl.ds(i, 1), :])], axis=1)
            low, high = bounds[i, 0], bounds[i, keys - 1]
            first = lax.fori_loop(0, chunks, lambda t, n: n + jnp.where(bounds[t, keys - 1] < low, 1, 0), 0)
            last = lax.fori_loop(0, chunks, lambda t, n: n + jnp.where(bounds[t, 0] <= high, 1, 0), 0)

            def step(t, carry):
                top, acc = carry
                at = pl.ds(pl.multiple_of(t * keys, keys), keys)
                s = dot_t(left, kv2_ref[at, :])
                new = jnp.maximum(top, jnp.max(s, axis=1, keepdims=True))
                p = jnp.exp2((s - new) * log_scale)
                acc = acc * jnp.exp2((top - new) * log_scale) + dot_n(p.astype(bf16), vo_ref[at, :])
                return new, acc

            top, acc = lax.fori_loop(
                first, last, step, (jnp.full((rows, 1), FAR, f32), jnp.zeros((rows, 128), f32))
            )
            total = pltpu.roll(acc, 64, 1)
            outs.append(acc / total)
            lse = jnp.broadcast_to(top * log_scale, acc.shape) + jnp.log2(acc)
            lse_ref[pl.ds(i, 1), :] = lse.T[0:1, :]
        o = jnp.where(lanes(outs[0].shape) < 64, pltpu.roll(outs[0], 64, 1), outs[1])
        of_ref[j] = o
        o_ref[j] = o.astype(bf16)
        return c

    lax.fori_loop(0, chunks // 2, tile, 0)
    stores += copies([(o_ref, o_hbm), (of_ref, of_hbm), (lse_ref, lse_hbm)], out_sem.at[pl.ds(1, 3)])
    wait_all(stores)


def attn_fwd(q, kv, seg_q, seg_k):
    chunks, keys = seg_k.shape
    dma = pltpu.SemaphoreType.DMA
    shapes = ((q.shape, bf16), (q.shape, f32), (seg_q.shape, f32), ((chunks * keys, 256), bf16))
    return pl.pallas_call(
        attn_fwd_kernel,
        out_shape=[jax.ShapeDtypeStruct(shape, kind) for shape, kind in shapes],
        in_specs=any_specs(4),
        out_specs=any_specs(4),
        scratch_shapes=[
            *[pltpu.VMEM(a.shape, a.dtype) for a in (q, kv, seg_q, seg_k)],
            pltpu.SMEM(seg_k.shape, jnp.int32),
            *[pltpu.VMEM(shape, kind) for shape, kind in shapes],
            pltpu.VMEM((chunks * keys, 128), bf16),
            dma((5,)),
            dma((4,)),
        ],
        compiler_params=pltpu.CompilerParams(vmem_limit_bytes=VMEM_BYTES),
        name="attn_fwd",
    )(q, kv, seg_q, seg_k)


def attn_bwd_kernel(
    q_hbm, do_hbm, of_hbm, lse_hbm, kv2_hbm, seg_q_hbm, seg_k_hbm, pass1, pass2, dq_hbm, dkv_hbm, out1, out2,
    q_ref, do_ref, of_ref, lse_ref, kv2_ref, seg_q_ref, bounds, dq_ref, dkv_ref, hold1, hold2, in_sem, out_sem,
):
    loads = copies(
        [
            (q_hbm, q_ref), (do_hbm, do_ref), (of_hbm, of_ref), (lse_hbm, lse_ref), (kv2_hbm, kv2_ref),
            (seg_q_hbm, seg_q_ref), (seg_k_hbm, bounds),
            (pass1, hold1), (pass2, hold2),
        ],
        in_sem,
    )
    dkv_ref[...] = jnp.zeros_like(dkv_ref)
    wait_all(loads)
    stores = copies([(hold1, out1), (hold2, out2)], out_sem)
    chunks, keys = bounds.shape
    log_scale = math.log2(math.e) * DH ** (-0.5)

    def tile(j, c):
        q_tile, do_tile = q_ref[j], do_ref[j]
        rows = q_tile.shape[0]
        prod = do_tile.astype(f32) * of_ref[j]
        prod = prod.T
        dqs = []
        for half in range(2):
            i = half * (chunks // 2) + j
            left = half_lanes(q_tile, half)
            grad = do_tile.astype(f32)
            if not half:
                grad = pltpu.roll(grad, 64, 1)
            grad = jnp.where(lanes(grad.shape) < 64, 0.0, grad).astype(bf16)
            delta = jnp.sum(prod[64 * half:64 * half + 64], axis=0, keepdims=True)
            lse = lse_ref[pl.ds(i, 1), :]
            both = jnp.concatenate([left, grad], axis=0)
            marks = query_marks(seg_q_ref[pl.ds(i, 1), :])
            right = jnp.concatenate([both, jnp.concatenate([marks, jnp.zeros_like(marks)], axis=0)], axis=1)
            low, high = bounds[i, 0], bounds[i, keys - 1]
            first = lax.fori_loop(0, chunks, lambda t, n: n + jnp.where(bounds[t, keys - 1] < low, 1, 0), 0)
            last = lax.fori_loop(0, chunks, lambda t, n: n + jnp.where(bounds[t, 0] <= high, 1, 0), 0)

            def step(t, dq):
                at = pl.ds(pl.multiple_of(t * keys, keys), keys)
                kv2 = kv2_ref[at, :]
                sdp = dot_t(kv2, right)
                p = jnp.exp2(sdp[:, :rows] * log_scale - lse)
                ds = (p * (sdp[:, rows:] - delta)).astype(bf16)
                dkv_ref[at, :] += dot_n(jnp.concatenate([ds, p.astype(bf16)], axis=1), both)
                return dq + dot_0(ds, kv2[:, 0:128])

            dqs.append(lax.fori_loop(first, last, step, jnp.zeros((rows, 128), f32)))
        dq = jnp.where(lanes(dqs[0].shape) < 64, dqs[0], pltpu.roll(dqs[1], 64, 1))
        dq_ref[j] = (dq * DH ** (-0.5)).astype(bf16)
        return c

    lax.fori_loop(0, chunks // 2, tile, 0)
    dkv = dkv_ref[...]
    dkv_ref[...] = jnp.where(lanes(dkv.shape) < 64, dkv * DH ** (-0.5), dkv)
    stores += copies([(dq_ref, dq_hbm), (dkv_ref, dkv_hbm)], out_sem.at[pl.ds(2, 2)])
    wait_all(stores)


def attn_bwd(q, do, of, lse, kv2, seg_q, seg_k, pass1, pass2):
    dma = pltpu.SemaphoreType.DMA
    shapes = ((q.shape, bf16), ((kv2.shape[0], 128), f32))
    return pl.pallas_call(
        attn_bwd_kernel,
        out_shape=[jax.ShapeDtypeStruct(shape, kind) for shape, kind in shapes]
        + [jax.ShapeDtypeStruct(a.shape, a.dtype) for a in (pass1, pass2)],
        in_specs=any_specs(9),
        out_specs=any_specs(4),
        scratch_shapes=[
            *[pltpu.VMEM(a.shape, a.dtype) for a in (q, do, of, lse, kv2, seg_q)],
            pltpu.SMEM(seg_k.shape, jnp.int32),
            *[pltpu.VMEM(shape, kind) for shape, kind in shapes],
            *[pltpu.VMEM(a.shape, a.dtype) for a in (pass1, pass2)],
            dma((9,)),
            dma((4,)),
        ],
        compiler_params=pltpu.CompilerParams(vmem_limit_bytes=VMEM_BYTES),
        name="attn_bwd",
    )(q, do, of, lse, kv2, seg_q, seg_k, pass1, pass2)


class Spot:
    def __init__(self, nb):
        self.nb, self.nz = nb, nb // 2
        self.h, b = lax.axis_index("head"), lax.axis_index("blk")
        self.z, self.c = b // 2, lax.rem(b, 2)
        self.near = (self.h + 1 - 2 * lax.rem(self.h, 2), lax.rem(self.h + 2, 4))
        self.diag = 3 - self.h
        self.me = self.h * nb + b

    def index(self, h, z, c):
        return h * self.nb + z * 2 + c

    def ahead(self, k):
        return lax.rem(self.z + k, self.nz)


def remote(src, dst, send, recv, h, b):
    return pltpu.make_async_remote_copy(
        src_ref=src,
        dst_ref=dst,
        send_sem=send,
        recv_sem=recv,
        device_id={"head": h, "blk": b},
        device_id_type=MESH,
    )


def each(count, body, start=0):
    def run(i, c):
        body(i)
        return c

    lax.fori_loop(start, count, run, 0)


def greet_all(n, nb, me):
    barrier = pltpu.get_barrier_semaphore()

    def signal(i):
        t = lax.rem(me + i, n)
        pl.semaphore_signal(
            barrier, inc=1, device_id={"head": t // nb, "blk": lax.rem(t, nb)}, device_id_type=MESH
        )

    each(n, signal, 1)
    pl.semaphore_wait(barrier, n - 1)


def halves(shape):
    rows, width = shape
    if width > 128:
        return [(slice(None), slice(w * width // 2, (w + 1) * width // 2)) for w in range(2)]
    return [(slice(w * rows // 2, (w + 1) * rows // 2), slice(None)) for w in range(2)]


class Gather:
    def __init__(self, spot, shard, full, send, recv, local):
        self.s, self.shard, self.full, self.local = spot, shard, full, local
        self.send, self.recv = send, recv
        self.cut = halves(shard.shape)

    def copy(self, src, dst, k, h, z, c, recv_k=None):
        recv_k = k if recv_k is None else recv_k
        return remote(src, dst, self.send.at[k], self.recv.at[recv_k], h, z * 2 + c)

    def to_z(self, z):
        s = self.s
        return self.copy(self.shard, self.full.at[s.me], z, s.h, z, s.c, s.z)

    def from_z(self, z):
        s = self.s
        slot = self.full.at[s.index(s.h, z, s.c)]
        return self.copy(slot, slot, z, s.h, z, s.c)

    def near(self, w, z, own=False):
        s = self.s
        slot = self.full.at[s.index(s.h, z, s.c)]
        return self.copy(self.shard if own else slot, slot, (1 + w) * s.nz + z, s.near[w], s.z, s.c)

    def from_near(self, w, z):
        s = self.s
        slot = self.full.at[s.index(s.near[w], z, s.c)]
        return self.copy(slot, slot, (1 + w) * s.nz + z, s.near[w], s.z, s.c)

    def lanes(self, slot, w):
        return slot.at[self.cut[w]]

    def onward(self, w, z):
        s = self.s
        slot = self.lanes(self.full.at[s.index(s.near[w], z, s.c)], w)
        return self.copy(slot, slot, (3 + w) * s.nz + z, s.near[1 - w], s.z, s.c)

    def from_onward(self, w, z):
        s = self.s
        slot = self.lanes(self.full.at[s.index(s.diag, z, s.c)], w)
        return self.copy(slot, slot, (3 + w) * s.nz + z, s.near[1 - w], s.z, s.c)

    def twin(self, h, z, own=False):
        s = self.s
        slot = self.full.at[s.index(h, z, s.c)]
        return self.copy(self.shard if own else slot, slot, 5 * s.nz + h * s.nz + z, s.h, s.z, 1 - s.c)

    def from_twin(self, h, z):
        s = self.s
        slot = self.full.at[s.index(h, z, 1 - s.c)]
        return self.copy(slot, slot, 5 * s.nz + h * s.nz + z, s.h, s.z, 1 - s.c)

    def begin(self):
        s = self.s
        self.own = pltpu.make_async_copy(self.shard, self.full.at[s.me], self.local)
        self.own.start()
        each(s.nz, lambda k: self.to_z(s.ahead(k)).start(), 1)
        self.near(0, s.z, True).start()
        self.near(1, s.z, True).start()
        self.twin(s.h, s.z, True).start()

    def spread(self):
        s = self.s

        def go(k):
            z = s.ahead(k)
            self.from_z(z).wait_recv()
            self.near(0, z).start()
            self.near(1, z).start()
            self.twin(s.h, z).start()

        each(s.nz, go, 1)

    def cross(self):
        s = self.s

        def go(k):
            z = s.ahead(k)
            for w in range(2):
                self.from_near(w, z).wait_recv()
                self.onward(w, z).start()
                self.twin(s.near[w], z).start()

        each(s.nz, go)

    def last(self):
        s = self.s

        def go(k):
            z = s.ahead(k)
            for w in range(2):
                self.from_onward(w, z).wait_recv()
            self.twin(s.diag, z).start()

        each(s.nz, go)

    def arrive(self):
        s = self.s
        each(4, lambda h: each(s.nz, lambda z: self.from_twin(h, z).wait_recv()))
        self.own.wait()

    def sent(self):
        s = self.s
        each(s.nz, lambda k: self.to_z(s.ahead(k)).wait_send(), 1)

        def go(z):
            for w in range(2):
                self.near(w, z).wait_send()
                self.onward(w, z).wait_send()
            each(4, lambda h: self.twin(h, z).wait_send())

        each(s.nz, go)


class Scatter:
    def __init__(self, spot, part, twin, diag, near, line, send, recv):
        self.s, self.part, self.t, self.d, self.n, self.l = spot, part, twin, diag, near, line
        self.send, self.recv = send, recv
        self.cut = halves(part.shape[1:])
        self.axis = 1 if self.cut[0][0] == slice(None) else 0

    def copy(self, src, dst, k, h, z, c, recv_k=None):
        recv_k = k if recv_k is None else recv_k
        return remote(src, dst, self.send.at[k], self.recv.at[recv_k], h, z * 2 + c)

    def mine(self, h, z):
        return self.s.index(h, z, self.s.c)

    def to_twin(self, h, z):
        s = self.s
        src = self.part.at[s.index(h, z, 1 - s.c)]
        return self.copy(src, self.t.at[h, z], h * s.nz + z, s.h, s.z, 1 - s.c)

    def to_diag(self, w, z):
        s = self.s
        src = self.part.at[self.mine(s.diag, z)].at[self.cut[w]]
        return self.copy(src, self.d.at[w, z], (4 + w) * s.nz + z, s.near[w], s.z, s.c)

    def to_near(self, w, z):
        s = self.s
        src = self.part.at[self.mine(s.near[w], z)]
        return self.copy(src, self.n.at[w, z], (6 + w) * s.nz + z, s.near[w], s.z, s.c)

    def to_line(self, z):
        s = self.s
        src = self.part.at[self.mine(s.h, z)]
        return self.copy(src, self.l.at[s.z], 8 * s.nz + z, s.h, z, s.c, 8 * s.nz + s.z)

    def from_line(self, z):
        s = self.s
        src = self.part.at[self.mine(s.h, z)]
        return self.copy(src, self.l.at[z], 8 * s.nz + z, s.h, z, s.c)

    def begin(self):
        each(4, lambda h: each(self.s.nz, lambda z: self.to_twin(h, z).start()))

    def pair(self, h, z):
        self.to_twin(h, z).wait_recv()
        return self.part[self.mine(h, z)].astype(f32) + self.t[h, z].astype(f32)

    def keep(self, h, z, value):
        self.part[self.mine(h, z)] = value.astype(self.part.dtype)

    def first(self):
        s = self.s

        def go(k):
            z = s.ahead(k)
            self.keep(s.diag, z, self.pair(s.diag, z))
            for w in range(2):
                self.to_diag(w, z).start()

        each(s.nz + 1, go, 1)

    def second(self):
        s = self.s

        def go(k):
            z = s.ahead(k)
            for w in range(2):
                value = self.pair(s.near[w], z)
                self.to_diag(1 - w, z).wait_recv()
                other = self.d[1 - w, z].astype(f32)
                pieces = [value[cut] for cut in self.cut]
                pieces[1 - w] = pieces[1 - w] + other
                value = jnp.concatenate(pieces, axis=self.axis)
                self.keep(s.near[w], z, value)
                self.to_near(w, z).start()

        each(s.nz + 1, go, 1)

    def joined(self, z):
        value = self.pair(self.s.h, z)
        for w in range(2):
            self.to_near(w, z).wait_recv()
            value = value + self.n[w, z].astype(f32)
        return value

    def third(self):
        s = self.s

        def go(k):
            z = s.ahead(k)
            self.keep(s.h, z, self.joined(z))
            self.to_line(z).start()

        each(s.nz, go, 1)

    def total(self):
        s = self.s
        value = self.joined(s.z)

        def go(k, value):
            z = s.ahead(k)
            self.from_line(z).wait_recv()
            return value + self.l[z].astype(f32)

        return lax.fori_loop(1, s.nz, go, value)

    def sent(self):
        s = self.s

        def go(z):
            each(4, lambda h: self.to_twin(h, z).wait_send())
            for w in range(2):
                self.to_diag(w, z).wait_send()
                self.to_near(w, z).wait_send()

        each(s.nz, go)
        each(s.nz, lambda k: self.to_line(s.ahead(k)).wait_send(), 1)


class Exchange:
    def __init__(self, spot, src, dst, send, recv, local):
        self.s, self.src, self.dst, self.send, self.recv, self.local = spot, src, dst, send, recv, local
        self.g = spot.me // 2

    def copy(self, i, back=False):
        s = self.s
        to = lax.rem(self.g + i, 16)
        t = to * 2 + s.c
        src = self.src(to)
        dst = self.dst(lax.rem(self.g + 16 - i, 16)) if back else self.dst(self.g)
        return remote(src, dst, self.send.at[i], self.recv.at[i], t // s.nb, lax.rem(t, s.nb))

    def own(self):
        return pltpu.make_async_copy(self.src(self.g), self.dst(self.g), self.local)

    def begin(self):
        self.own().start()
        each(16, lambda i: self.copy(i).start(), 1)

    def arrive(self, i):
        self.copy(i, True).wait_recv()

    def end(self):
        each(16, self.arrive, 1)
        self.sent()

    def sent(self):
        self.own().wait()
        each(16, lambda i: self.copy(i).wait_send(), 1)


def weave(left, right):
    kind = left.dtype
    left, right = left.astype(f32), right.astype(f32)
    low = lanes(left.shape) < 64
    first = jnp.where(low, left, pltpu.roll(right, 64, 1)).astype(kind)
    second = jnp.where(low, pltpu.roll(left, 64, 1), right).astype(kind)
    return first, second


def any_specs(count):
    return [pl.BlockSpec(memory_space=pl.ANY)] * count


def copies(pairs, sems):
    jobs = [pltpu.make_async_copy(src, dst, sems.at[k]) for k, (src, dst) in enumerate(pairs)]
    for job in jobs:
        job.start()
    return jobs


def wait_all(jobs):
    for job in jobs:
        job.wait()


def rows_of(shape):
    return lax.broadcasted_iota(jnp.int32, shape, 0)


def spread_row(block, width, each_lane):
    count = block.shape[0]
    pick = (rows_of((128, width)) == lax.rem(lanes((128, width)), each_lane)).astype(f32).astype(bf16)
    wide = dot_n(block.astype(bf16), pick)
    return column_sum(jnp.where(rows_of((count, width)) == lanes((count, width)) // each_lane, wide, 0.0))


def gather_row(row, count, each_lane):
    width = row.shape[1]
    wide = jnp.where(rows_of((count, width)) == lanes((count, width)) // each_lane, row, 0.0)
    pick = (lanes((width, 128)) == lax.rem(rows_of((width, 128)), each_lane)).astype(f32)
    return lax.dot_general(
        wide, pick, (((1,), (0,)), ((), ())), precision=lax.Precision.HIGHEST, preferred_element_type=f32
    )


def project_kernel(n, nb, *refs):
    x_hbm, wq_hbm, wk_hbm, wv_hbm, wo_hbm, wu_hbm, wd_hbm, seg_hbm = refs[:8]
    smalls = refs[8:16]
    q_out, kv_out, wa_out, wb_out, wd_out, par_out, bup_out, segk_out, segq_out = refs[16:25]
    (
        x, wq, wk, wv, wo, wu, wd, seg, *small, bup_small, vec, vecs, sa, sb, wa, kv_send, q_send, par, bup, segk, segq,
        in_sem, out_sem, ag_send, ag_recv, ag_local, ex_send, ex_recv, ex_local, tw_send, tw_recv,
    ) = refs[25:]
    s = Spot(nb)
    loads = copies(
        [(wq_hbm, wq), (wk_hbm, wk), (wv_hbm, wv), (seg_hbm, seg), (smalls[0], bup_small)]
        + [(smalls[k], small[k - 1]) for k in range(1, 8)]
        + [(wo_hbm, wo), (wu_hbm, wu), (wd_hbm, wd), (x_hbm, x)],
        in_sem,
    )
    greet_all(n, nb, s.me)
    wait_all(loads[:12])
    for t in range(4):
        tile = slice(128 * t, 128 * t + 128)
        first, second = weave(wk[:, tile], wv[:, tile])
        sa[:, 256 * t:256 * t + 128] = first
        sa[:, 256 * t + 128:256 * t + 256] = second
    sa[:, 1024:1536] = wq[...]
    vec[...] = jnp.zeros_like(vec)
    vec[0:1, 0:64] = bup_small[...].astype(f32).reshape(1, 64)
    for k in range(7):
        vec[k + 1:k + 2, 0:16] = small[k][...].astype(f32).reshape(1, 16)
    vec[8:10, :] = seg[...].astype(f32)
    jobs = [
        Gather(s, shard, full, ag_send.at[k], ag_recv.at[k], ag_local.at[k])
        for k, (shard, full) in enumerate(((sa, wa), (vec, vecs), (sb, wb_out), (wd, wd_out)))
    ]
    for job in jobs[:2]:
        job.begin()
    wait_all(loads[12:])
    sb[:, 0:512] = wo[...]
    sb[:, 512:2560] = wu[...]
    for job in jobs[:2]:
        job.spread()
    for job in jobs[:2]:
        job.cross()
    for job in jobs[:2]:
        job.last()
    for job in jobs[2:]:
        job.begin()
    for job in jobs[:2]:
        job.arrive()
    outs = copies([(wa, wa_out)], out_sem)
    qkv = dot_n(x[...], wa[...].reshape(512, 1536)).astype(bf16)
    for m in range(2):
        rows = slice(128 * m, 128 * m + 128)
        for h in range(8):
            kv_send[8 * m + h] = qkv[rows, 128 * h:128 * h + 128].reshape(8, 16, 128)
        for t in range(4):
            tile = qkv[rows, 1024 + 128 * t:1152 + 128 * t]
            first, second = weave(tile[0:64], tile[64:128])
            q_send[8 * m + 2 * t] = first.reshape(4, 16, 128)
            q_send[8 * m + 2 * t + 1] = second.reshape(4, 16, 128)
    kv_ex = Exchange(
        s, lambda p: kv_send.at[p], lambda g: kv_out.at[:, g, s.c], ex_send.at[0], ex_recv.at[0], ex_local.at[0]
    )
    q_ex = Exchange(s, lambda p: q_send.at[p], lambda g: q_out.at[:, g], ex_send.at[1], ex_recv.at[1], ex_local.at[1])
    kv_ex.begin()
    q_ex.begin()
    for job in jobs[2:]:
        job.spread()
    bup[...] = spread_row(vecs[:, 0, :], 2048, 64)
    for k in range(7):
        par[k:k + 1, :] = spread_row(vecs[:, k + 1, :], 512, 16)
    par[7:8, :] = jnp.zeros((1, 512), f32)
    ids = jnp.where(kv_ex.g < 8, vecs[:, 8, :], vecs[:, 9, :]).astype(bf16)
    for i in range(8):
        pick = (rows_of((128, 512)) == 16 * i + lax.rem(lanes((128, 512)), 16)).astype(f32).astype(bf16)
        wide = dot_n(ids, pick)
        source = rows_of((n, 512))
        row = jnp.where(source == lanes((n, 512)) // 16, wide, 0.0)
        segk[i:i + 1, :] = column_sum(row).astype(jnp.int32)
        source = rows_of((n, 256))
        own = (source // 2 == lanes((n, 256)) // 16) & (lax.rem(source, 2) == s.c)
        segq[i:i + 1, :] = column_sum(jnp.where(own, wide[:, 0:256], 0.0)).astype(jnp.int32)
    outs += copies([(par, par_out), (bup, bup_out), (segk, segk_out), (segq, segq_out)], out_sem.at[pl.ds(1, 4)])
    for job in jobs[2:]:
        job.cross()

    def twin(g, c):
        slot = kv_out.at[:, g, c]
        return remote(slot, slot, tw_send.at[g], tw_recv.at[g], s.h, s.z * 2 + 1 - s.c)

    kv_ex.own().wait()
    twin(kv_ex.g, s.c).start()

    def forward(i):
        kv_ex.arrive(i)
        twin(lax.rem(kv_ex.g + 16 - i, 16), s.c).start()

    each(16, forward, 1)
    for job in jobs[2:]:
        job.last()
    for job in jobs[2:]:
        job.arrive()
    each(16, lambda g: twin(g, 1 - s.c).wait_recv())
    each(16, lambda g: twin(g, s.c).wait_send())
    each(16, lambda i: kv_ex.copy(i).wait_send(), 1)
    q_ex.end()
    for job in jobs:
        job.sent()
    wait_all(outs)


def project(n, nb, x, wq, wk, wv, wo, wu, wd, seg, smalls):
    dma = pltpu.SemaphoreType.DMA
    nz = nb // 2
    return pl.pallas_call(
        functools.partial(project_kernel, n, nb),
        out_shape=(
            jax.ShapeDtypeStruct((4, 16, 16, 128), bf16),
            jax.ShapeDtypeStruct((8, 16, 2, 16, 128), bf16),
            jax.ShapeDtypeStruct((n, 16, 1536), bf16),
            jax.ShapeDtypeStruct((n, 16, 2560), bf16),
            jax.ShapeDtypeStruct((n, 64, 512), bf16),
            jax.ShapeDtypeStruct((8, 512), f32),
            jax.ShapeDtypeStruct((1, 2048), f32),
            jax.ShapeDtypeStruct((8, 512), jnp.int32),
            jax.ShapeDtypeStruct((8, 256), jnp.int32),
        ),
        in_specs=any_specs(16),
        out_specs=any_specs(9),
        scratch_shapes=[
            pltpu.VMEM(x.shape, bf16),
            pltpu.VMEM((16, 512), bf16),
            pltpu.VMEM((16, 512), bf16),
            pltpu.VMEM((16, 512), bf16),
            pltpu.VMEM((16, 512), bf16),
            pltpu.VMEM((16, 2048), bf16),
            pltpu.VMEM((64, 512), bf16),
            pltpu.VMEM((2, 128), jnp.int32),
            *[pltpu.VMEM((16,), bf16)] * 7,
            pltpu.VMEM((64,), bf16),
            pltpu.VMEM((16, 128), f32),
            pltpu.VMEM((n, 16, 128), f32),
            pltpu.VMEM((16, 1536), bf16),
            pltpu.VMEM((16, 2560), bf16),
            pltpu.VMEM((n, 16, 1536), bf16),
            pltpu.VMEM((16, 8, 16, 128), bf16),
            pltpu.VMEM((16, 4, 16, 128), bf16),
            pltpu.VMEM((8, 512), f32),
            pltpu.VMEM((1, 2048), f32),
            pltpu.VMEM((8, 512), jnp.int32),
            pltpu.VMEM((8, 256), jnp.int32),
            dma((16,)),
            dma((5,)),
            dma((4, 9 * nz)),
            dma((4, 9 * nz)),
            dma((4,)),
            dma((2, 16)),
            dma((2, 16)),
            dma((2,)),
            dma((16,)),
            dma((16,)),
        ],
        compiler_params=pltpu.CompilerParams(
            collective_id=1, has_side_effects=True, vmem_limit_bytes=VMEM_BYTES
        ),
        name="project",
    )(x, wq, wk, wv, wo, wu, wd, seg, *smalls)


def row_norm(v):
    mean = jnp.mean(v, axis=-1, keepdims=True)
    mid = v - mean
    inv = lax.rsqrt(jnp.mean(mid * mid, axis=-1, keepdims=True) + EPSILON)
    return mid * inv, inv


def row_norm_back(grad, normed, inv, gain):
    part = grad * gain
    return inv * (
        part
        - jnp.mean(part, axis=-1, keepdims=True)
        - normed * jnp.mean(part * normed, axis=-1, keepdims=True)
    )


def column_sum(v):
    return jnp.sum(v, axis=0, keepdims=True)


def middle_kernel(n, nb, *refs):
    o_hbm, x_hbm, y_hbm, g_hbm, wb_hbm, wd_hbm, par_hbm, bup_hbm = refs[:8]
    outs_hbm = refs[9:20]
    do_out = refs[8]
    (
        o_in, x, y, g_in, wb, wd, par, bup, o_recv, do_send, slope,
        out, dacc_ref, dz1_ref, x1_ref, dur_ref, hid_ref, dfr_ref, omix, dar_ref, gvec, bias_up,
        in_sem, out_sem, ex_send, ex_recv, ex_local,
    ) = refs[20:]
    s = Spot(nb)
    loads = copies(
        [(o_hbm, o_in), (x_hbm, x), (y_hbm, y), (g_hbm, g_in), (par_hbm, par), (bup_hbm, bup), (wb_hbm, wb), (wd_hbm, wd)],
        in_sem,
    )
    greet_all(n, nb, s.me)
    loads[0].wait()
    o_ex = Exchange(
        s, lambda p: o_in.at[:, p], lambda g: o_recv.at[g], ex_send.at[0], ex_recv.at[0], ex_local.at[0]
    )
    o_ex.begin()
    wait_all(loads[1:])
    o_ex.end()
    for m in range(2):
        for t in range(4):
            first, second = weave(
                o_recv[8 * m + 2 * t].reshape(64, 128), o_recv[8 * m + 2 * t + 1].reshape(64, 128)
            )
            omix[128 * m:128 * m + 64, 128 * t:128 * t + 128] = first
            omix[128 * m + 64:128 * m + 128, 128 * t:128 * t + 128] = second
    gain1, bias1 = par[1:2], par[2:3]
    gain2, bias2 = par[3:4], par[4:5]
    gain3, bias3 = par[5:6], par[6:7]
    w_out = wb[:, :, 0:512].reshape(512, 512)
    a = dot_n(omix[...], w_out)
    n1, r1 = row_norm(x[...].astype(f32) + a)
    x1 = n1 * gain1 + bias1
    x1r = x1.astype(bf16)
    x1_ref[...] = x1r
    feed = jnp.zeros_like(x1)
    for t in range(4):
        cols = slice(512 * t, 512 * t + 512)
        u = dot_n(x1r, wb[:, :, 512 + 512 * t:1024 + 512 * t].reshape(512, 512)) + bup[:, cols]
        phi = 0.5 * (1.0 + lax.erf(u * (0.5**0.5)))
        hid = (u * phi).astype(bf16)
        slope[:, cols] = phi + u * jnp.exp(-0.5 * u * u) * ((2.0 * math.pi) ** -0.5)
        hid_ref[:, cols] = hid
        feed = feed + dot_n(hid, wd[8 * t:8 * t + 8].reshape(512, 512))
    feed = feed + par[0:1]
    n2, r2 = row_norm(x1 + feed)
    n3, r3 = row_norm(y[...].astype(f32) + a + feed)
    out[...] = (n2 * gain2 + bias2 + (n3 * gain3 + bias3)).astype(bf16)
    g = g_in[...].astype(f32)
    dacc = row_norm_back(g, n3, r3, gain3)
    dacc_ref[...] = dacc
    dz2 = row_norm_back(g, n2, r2, gain2)
    df = dz2 + dacc
    dfr = df.astype(bf16)
    dfr_ref[...] = dfr
    dx1 = dz2
    for t in range(4):
        cols = slice(512 * t, 512 * t + 512)
        du = dot_t(dfr, wd[8 * t:8 * t + 8].reshape(512, 512)) * slope[:, cols]
        bias_up[:, cols] = column_sum(du)
        dur = du.astype(bf16)
        dur_ref[:, cols] = dur
        dx1 = dx1 + dot_t(dur, wb[:, :, 512 + 512 * t:1024 + 512 * t].reshape(512, 512))
    dz1 = row_norm_back(dx1, n1, r1, gain1)
    dz1_ref[...] = dz1
    dar = (dz1 + dacc).astype(bf16)
    dar_ref[...] = dar
    do = dot_t(dar, w_out).astype(bf16)
    for m in range(2):
        for t in range(4):
            tile = do[128 * m:128 * m + 128, 128 * t:128 * t + 128]
            first, second = weave(tile[0:64], tile[64:128])
            do_send[8 * m + 2 * t] = first.reshape(4, 16, 128)
            do_send[8 * m + 2 * t + 1] = second.reshape(4, 16, 128)
    do_ex = Exchange(
        s, lambda p: do_send.at[p], lambda g: do_out.at[:, g], ex_send.at[1], ex_recv.at[1], ex_local.at[1]
    )
    do_ex.begin()
    stores = copies(
        zip((out, dacc_ref, dz1_ref, x1_ref, dur_ref, hid_ref, dfr_ref, omix, dar_ref), outs_hbm[:9]), out_sem
    )
    sum_g = column_sum(g)
    sums = (
        column_sum(df), column_sum(dx1 * n1), column_sum(dx1), column_sum(g * n2), sum_g, column_sum(g * n3), sum_g
    )
    gvec[...] = jnp.zeros_like(gvec)
    gvec[:, 0, :] = gather_row(bias_up[...], n, 64)
    for k in range(7):
        gvec[:, k + 1, :] = gather_row(sums[k], n, 16)
    stores += copies([(gvec, outs_hbm[9])], out_sem.at[pl.ds(9, 1)])
    do_ex.end()
    wait_all(stores)


def middle(n, nb, o, x, y, g, wb, wd, par, bup):
    dma = pltpu.SemaphoreType.DMA
    rows = x.shape[0]
    saved = [
        ((rows, 512), bf16), ((rows, 512), f32), ((rows, 512), f32), ((rows, 512), bf16), ((rows, 2048), bf16),
        ((rows, 2048), bf16), ((rows, 512), bf16), ((rows, 512), bf16), ((rows, 512), bf16), ((n, 16, 128), f32),
    ]
    return pl.pallas_call(
        functools.partial(middle_kernel, n, nb),
        out_shape=[jax.ShapeDtypeStruct((4, 16, 16, 128), bf16)]
        + [jax.ShapeDtypeStruct(shape, kind) for shape, kind in saved]
        + [jax.ShapeDtypeStruct((8, 128), f32)],
        in_specs=any_specs(8),
        out_specs=any_specs(12),
        scratch_shapes=[
            pltpu.VMEM(o.shape, bf16),
            pltpu.VMEM(x.shape, bf16),
            pltpu.VMEM(x.shape, bf16),
            pltpu.VMEM(x.shape, bf16),
            pltpu.VMEM(wb.shape, bf16),
            pltpu.VMEM(wd.shape, bf16),
            pltpu.VMEM(par.shape, f32),
            pltpu.VMEM(bup.shape, f32),
            pltpu.VMEM((16, 4, 16, 128), bf16),
            pltpu.VMEM((16, 4, 16, 128), bf16),
            pltpu.VMEM((rows, 2048), f32),
            *[pltpu.VMEM(shape, kind) for shape, kind in saved],
            pltpu.VMEM((1, 2048), f32),
            dma((8,)),
            dma((10,)),
            dma((2, 16)),
            dma((2, 16)),
            dma((2,)),
        ],
        compiler_params=pltpu.CompilerParams(
            collective_id=2, has_side_effects=True, vmem_limit_bytes=VMEM_BYTES
        ),
        name="middle",
    )(o, x, y, g, wb, wd, par, bup)[:11]


def finish_kernel(n, nb, *refs):
    ins = refs[:12]
    outs = refs[12:20]
    (
        dq, dkv, x, dz1, x1, dur, hid, dfr, omix, dar, gvec, wa,
        pa, ta, da, na, la, pb, tb, db, nb_, lb, pd, td, dd, nd, ld, tv, dv, nv, lv,
        twin_buf, dkv_send, dkv_recv, dq_recv, dqkv, gx, gq, gk, gv, go, gu, gd, gs,
        in_sem, out_sem, rs_send, rs_recv, ex_send, ex_recv, ex_local, tw_send, tw_recv,
    ) = refs[20:]
    s = Spot(nb)
    order = (1, 10, 8, 9, 4, 5, 6, 7, 0, 2, 3, 11)
    local = (dq, dkv, x, dz1, x1, dur, hid, dfr, omix, dar, gvec, wa)
    loads = copies([(ins[k], local[k]) for k in order], in_sem)
    greet_all(n, nb, s.me)
    swap = remote(ins[1].at[:, :, 1 - s.c], twin_buf, tw_send, tw_recv, s.h, s.z * 2 + 1 - s.c)
    swap.start()
    jobs = [
        Scatter(s, *bufs, rs_send.at[k], rs_recv.at[k])
        for k, bufs in enumerate(
            ((pb, tb, db, nb_, lb), (pd, td, dd, nd, ld), (gvec, tv, dv, nv, lv), (pa, ta, da, na, la))
        )
    ]
    wait_all(loads[:6])
    jobs[2].begin()
    pb[:, :, 0:512] = dot_0(omix[...], dar[...]).astype(bf16).reshape(n, 16, 512)
    for t in range(4):
        cols = slice(512 * t, 512 * t + 512)
        pb[:, :, 512 + 512 * t:1024 + 512 * t] = dot_0(x1[...], dur[:, cols]).astype(bf16).reshape(n, 16, 512)
    jobs[0].begin()
    wait_all(loads[6:])
    for t in range(4):
        cols = slice(512 * t, 512 * t + 512)
        pd[8 * t:8 * t + 8] = dot_0(hid[:, cols], dfr[...]).astype(bf16).reshape(8, 64, 512)
    jobs[1].begin()
    swap.wait()

    def add(g):
        dkv_send[g] = (dkv[:, g, s.c] + twin_buf[:, g]).astype(bf16)

    each(16, add)
    kv_ex = Exchange(
        s, lambda p: dkv_send.at[p], lambda g: dkv_recv.at[g], ex_send.at[0], ex_recv.at[0], ex_local.at[0]
    )
    q_ex = Exchange(s, lambda p: dq.at[:, p], lambda g: dq_recv.at[g], ex_send.at[1], ex_recv.at[1], ex_local.at[1])
    kv_ex.begin()
    q_ex.begin()
    for job in jobs[:3]:
        job.first()
    for job in jobs[:3]:
        job.second()
    for job in jobs[:3]:
        job.third()
    kv_ex.end()
    q_ex.end()
    for m in range(2):
        rows = slice(128 * m, 128 * m + 128)
        for h in range(8):
            dqkv[rows, 128 * h:128 * h + 128] = dkv_recv[8 * m + h].reshape(128, 128)
        for t in range(4):
            first, second = weave(
                dq_recv[8 * m + 2 * t].reshape(64, 128), dq_recv[8 * m + 2 * t + 1].reshape(64, 128)
            )
            dqkv[128 * m:128 * m + 64, 1024 + 128 * t:1152 + 128 * t] = first
            dqkv[128 * m + 64:128 * m + 128, 1024 + 128 * t:1152 + 128 * t] = second
    for t in range(3):
        cols = slice(512 * t, 512 * t + 512)
        pa[:, :, cols] = dot_0(x[...], dqkv[:, cols]).astype(bf16).reshape(n, 16, 512)
    jobs[3].begin()
    gx[...] = dz1[...] + dot_t(dqkv[...], wa[...].reshape(512, 1536))
    stores = copies([(gx, outs[0])], out_sem)
    total = jobs[0].total()
    go[...] = total[:, 0:512]
    gu[...] = total[:, 512:2560]
    gd[...] = jobs[1].total()
    gs[...] = jobs[2].total()
    stores += copies(zip((go, gu, gd, gs), outs[4:8]), out_sem.at[pl.ds(1, 4)])
    jobs[3].first()
    jobs[3].second()
    jobs[3].third()
    total = jobs[3].total()
    gq[...] = total[:, 1024:1536]
    for t in range(4):
        first, second = weave(total[:, 256 * t:256 * t + 128], total[:, 256 * t + 128:256 * t + 256])
        gk[:, 128 * t:128 * t + 128] = first
        gv[:, 128 * t:128 * t + 128] = second
    stores += copies(zip((gq, gk, gv), outs[1:4]), out_sem.at[pl.ds(5, 3)])
    for job in jobs:
        job.sent()
    wait_all(stores)


def finish(n, nb, dq, dkv, x, dz1, x1, dur, hid, dfr, omix, dar, gvec, wa):
    dma = pltpu.SemaphoreType.DMA
    nz = nb // 2
    rows = x.shape[0]

    def buffers(depth, width, kind):
        return [
            pltpu.VMEM((n, depth, width), kind),
            pltpu.VMEM((4, nz, depth, width), kind),
            pltpu.VMEM((2, nz, depth, width // 2), kind),
            pltpu.VMEM((2, nz, depth, width), kind),
            pltpu.VMEM((nz, depth, width), kind),
        ]

    args = (dq, dkv, x, dz1, x1, dur, hid, dfr, omix, dar, gvec, wa)
    shapes = ((rows, 512), (16, 512), (16, 512), (16, 512), (16, 512), (16, 2048), (64, 512), (16, 128))
    return pl.pallas_call(
        functools.partial(finish_kernel, n, nb),
        out_shape=[jax.ShapeDtypeStruct(shape, f32) for shape in shapes],
        in_specs=any_specs(12),
        out_specs=any_specs(8),
        scratch_shapes=[
            *[pltpu.VMEM(arg.shape, arg.dtype) for arg in args],
            *buffers(16, 1536, bf16),
            *buffers(16, 2560, bf16),
            *buffers(64, 512, bf16),
            *buffers(16, 128, f32)[1:2],
            pltpu.VMEM((2, nz, 8, 128), f32),
            *buffers(16, 128, f32)[3:],
            pltpu.VMEM((8, 16, 16, 128), f32),
            pltpu.VMEM((16, 8, 16, 128), bf16),
            pltpu.VMEM((16, 8, 16, 128), bf16),
            pltpu.VMEM((16, 4, 16, 128), bf16),
            pltpu.VMEM((rows, 1536), bf16),
            *[pltpu.VMEM(shape, f32) for shape in shapes],
            dma((12,)),
            dma((8,)),
            dma((4, 9 * nz)),
            dma((4, 9 * nz)),
            dma((2, 16)),
            dma((2, 16)),
            dma((2,)),
            dma,
            dma,
        ],
        compiler_params=pltpu.CompilerParams(
            collective_id=3, has_side_effects=True, vmem_limit_bytes=VMEM_BYTES
        ),
        name="finish",
    )(*args)


def deliver_kernel(count, *refs):
    ins, outs = refs[:count], refs[count:2 * count + 7]
    stage, lines, (in_sem, sems) = refs[2 * count + 7:3 * count + 7], refs[3 * count + 7:3 * count + 15], refs[-2:]
    loads = copies(zip(ins, stage), in_sem)
    jobs = []
    for k in range(count - 1):
        loads[k].wait()
        jobs += copies([(stage[k], outs[k])], sems.at[pl.ds(k, 1)])
    loads[-1].wait()
    vec = stage[-1]
    lines[0][...] = vec[0:1, 0:64].reshape(64)
    for k in range(1, 8):
        lines[k][...] = vec[k:k + 1, 0:16].reshape(16)
    jobs += copies(zip(lines, outs[count - 1:]), sems.at[pl.ds(count - 1, 8)])
    wait_all(jobs)


def deliver(arrays, vec):
    count = len(arrays) + 1
    lines = [(64,)] + [(16,)] * 7
    return pl.pallas_call(
        functools.partial(deliver_kernel, count),
        out_shape=[jax.ShapeDtypeStruct(a.shape, a.dtype) for a in arrays]
        + [jax.ShapeDtypeStruct(shape, f32) for shape in lines],
        in_specs=any_specs(count),
        out_specs=any_specs(count + 7),
        scratch_shapes=[
            *[pltpu.VMEM(a.shape, a.dtype) for a in (*arrays, vec)],
            *[pltpu.VMEM(shape, f32) for shape in lines],
            pltpu.SemaphoreType.DMA((count,)),
            pltpu.SemaphoreType.DMA((count + 7,)),
        ],
        compiler_params=pltpu.CompilerParams(vmem_limit_bytes=VMEM_BYTES),
        name="deliver",
    )(*arrays, vec)


def by_pairs(
    stream, accumulator, upstream, segment_ids, w_query, w_key, w_value, w_out, w_up, b_up, w_down, b_down,
    gain_attn, bias_attn, gain_ffn, bias_ffn, gain_final, bias_final,
):
    nb = lax.axis_size("blk")
    n = 4 * nb
    x = stream.reshape(256, 512)
    y = accumulator.reshape(256, 512)
    g = upstream.reshape(256, 512)
    smalls = (b_up, b_down, gain_attn, bias_attn, gain_ffn, bias_ffn, gain_final, bias_final)
    q, kv, wa, wb, wd, par, bup, seg_k, seg_q = project(
        n, nb, x, w_query, w_key, w_value, w_out, w_up, w_down, segment_ids.reshape(2, 128), smalls
    )
    o, of, lse, kv2 = attn_fwd(q.reshape(4, 256, 128), kv.reshape(4096, 128), seg_q, seg_k)
    do, out, dacc, dz1, x1, dur, hid, dfr, omix, dar, gvec = middle(
        n, nb, o.reshape(4, 16, 16, 128), x, y, g, wb, wd, par, bup
    )
    dq, dkv, out, dacc = attn_bwd(q.reshape(4, 256, 128), do.reshape(4, 256, 128), of, lse, kv2, seg_q, seg_k, out, dacc)
    gx, gq, gk, gv, go, gu, gd, gs = finish(
        n, nb, dq.reshape(4, 16, 16, 128), dkv.reshape(8, 16, 2, 16, 128), x, dz1, x1, dur, hid, dfr, omix, dar, gvec, wa
    )
    gx, gq, gk, gv, go, gu, gd, gbu, *small_grads = deliver((gx, gq, gk, gv, go, gu, gd), gs)
    return (
        out.reshape(stream.shape), gx.reshape(stream.shape), dacc.reshape(stream.shape),
        gq, gk, gv, go, gu, gbu, gd, *small_grads,
    )


def pairs_fit(mesh, shape):
    return mesh.shape["head"] == 4 and mesh.shape["blk"] == 8 and shape == (2, 32, 128, 512)


def solution(mesh):
    def step(*args):
        return run(by_pairs if pairs_fit(mesh, args[0].shape) else local, mesh)(*args)

    return step


def run(body, mesh):
    return jax.shard_map(
        body,
        mesh=mesh,
        in_specs=(
            P(None, ("head", "blk"), None, None),
            P(None, ("head", "blk"), None, None),
            P(None, ("head", "blk"), None, None),
            P(None, ("head", "blk"), None),
            P(("head", "blk"), None),
            P(("head", "blk"), None),
            P(("head", "blk"), None),
            P(("head", "blk"), None),
            P(("head", "blk"), None),
            P(("head", "blk")),
            P(("head", "blk"), None),
            P(("head", "blk")),
            P(("head", "blk")),
            P(("head", "blk")),
            P(("head", "blk")),
            P(("head", "blk")),
            P(("head", "blk")),
            P(("head", "blk")),
        ),
        out_specs=(
            P(None, ("head", "blk"), None, None),
            P(None, ("head", "blk"), None, None),
            P(None, ("head", "blk"), None, None),
            P(("head", "blk"), None),
            P(("head", "blk"), None),
            P(("head", "blk"), None),
            P(("head", "blk"), None),
            P(("head", "blk"), None),
            P(("head", "blk")),
            P(("head", "blk"), None),
            P(("head", "blk")),
            P(("head", "blk")),
            P(("head", "blk")),
            P(("head", "blk")),
            P(("head", "blk")),
            P(("head", "blk")),
            P(("head", "blk")),
        ),
        check_vma=False,
    )
```

```python
import functools
import math

import jax
import jax.numpy as jnp
from jax import lax
from jax.experimental import pallas as pl
from jax.experimental.pallas import tpu as pltpu
from jax.sharding import PartitionSpec as P

DH = 64
f32, bf16 = jnp.float32, jnp.bfloat16
MESH = pl.DeviceIdType.MESH
FAR = -1e30
VMEM_BYTES = 60 << 20


EPSILON = 1e-05


def norm_forward(inputs, norm_gain, norm_bias):
    average = jnp.mean(inputs, axis=-1, keepdims=True)
    centered = inputs - average
    inv_std = lax.rsqrt(jnp.mean(centered * centered, axis=-1, keepdims=True) + EPSILON)
    normed = centered * inv_std
    return (normed * norm_gain + norm_bias, normed, inv_std)


def norm_backward(gradient, normed, inv_std, norm_gain):
    scaled = gradient * norm_gain
    projected = (
        scaled
        - jnp.mean(scaled, axis=-1, keepdims=True)
        - normed * jnp.mean(scaled * normed, axis=-1, keepdims=True)
    )
    return (inv_std * projected, jnp.sum(gradient * normed, axis=0), jnp.sum(gradient, axis=0))


def smooth_gate(pre_act):
    return jax.nn.gelu(pre_act, approximate=False)


def split_rows(length):
    block_len = math.gcd(length, 512)
    return (length // block_len, block_len)


def block_scores(queries, query_seg, key_rows, key_seg, scaling):
    scores = (
        jnp.einsum("sgd,kgd->sgk", queries, key_rows, preferred_element_type=jnp.float32) * scaling
    )
    allowed = query_seg[:, None, None] == key_seg[None, None, :]
    return (scores, allowed)


def block_grads(
    queries, query_seg, grad_rows, log_total, row_delta, key_rows, value_rows, key_seg, scaling
):
    scores, allowed = block_scores(queries, query_seg, key_rows, key_seg, scaling)
    attn_prob = jnp.where(allowed, jnp.exp(scores - log_total[:, :, None]), 0.0)
    prob_grad = jnp.einsum(
        "sgd,kgd->sgk", grad_rows, value_rows, preferred_element_type=jnp.float32
    )
    score_grad = (attn_prob * (prob_grad - row_delta[:, :, None]) * scaling).astype(jnp.bfloat16)
    return (attn_prob.astype(jnp.bfloat16), score_grad)


def key_blocks(key_rows, value_rows, key_seg, groups):
    block_num, block_len = split_rows(key_rows.shape[0])
    return (
        key_rows.reshape(block_num, block_len, groups, -1),
        value_rows.reshape(block_num, block_len, groups, -1),
        key_seg.reshape(block_num, block_len),
    )


def attend_fold(queries, query_seg, scaling, carried, portion):
    key_rows, value_rows, key_seg = portion

    def step(running, blocks):
        key_part, value_part, seg_part = blocks
        old_max, old_total, weighted = running
        scores, allowed = block_scores(queries, query_seg, key_part, seg_part, scaling)
        row_max = jnp.maximum(old_max, jnp.max(jnp.where(allowed, scores, -1e30), axis=2))
        exp_scores = jnp.where(allowed, jnp.exp(scores - row_max[:, :, None]), 0.0)
        rescale = jnp.exp(old_max - row_max)
        new_total = old_total * rescale + jnp.sum(exp_scores, axis=2)
        weighted = weighted * rescale[:, :, None] + jnp.einsum(
            "sgk,kgd->sgd",
            exp_scores.astype(jnp.bfloat16),
            value_part,
            preferred_element_type=jnp.float32,
        )
        return ((row_max, new_total, weighted), None)

    running, unused = lax.scan(
        step, carried, key_blocks(key_rows, value_rows, key_seg, queries.shape[1])
    )
    return running


def local(
    stream,
    accumulator,
    upstream,
    segment_ids,
    w_query,
    w_key,
    w_value,
    w_out,
    w_up,
    b_up,
    w_down,
    b_down,
    gain_attn,
    bias_attn,
    gain_ffn,
    bias_ffn,
    gain_final,
    bias_final,
):
    heads_axis = lax.axis_size("head")
    micro = stream.shape[0]
    tokens = stream.shape[2]
    width = stream.shape[3]
    group_width = width // heads_axis
    groups = group_width // DH
    scaling = DH ** (-0.5)
    f32 = jnp.float32
    bf16 = jnp.bfloat16
    out_list = []
    stream_grads = []
    accum_grads = []
    grad_totals = None
    for micro_step in range(micro):
        (
            q_weight,
            k_weight,
            v_weight,
            o_weight,
            up_weight,
            up_bias,
            down_weight,
            down_bias,
            gain_one,
            shift_one,
            gain_two,
            shift_two,
            gain_three,
            shift_three,
        ) = (
            lax.all_gather(w_query, ("head", "blk"), axis=0, tiled=True),
            lax.all_gather(w_key, ("head", "blk"), axis=0, tiled=True),
            lax.all_gather(w_value, ("head", "blk"), axis=0, tiled=True),
            lax.all_gather(w_out, ("head", "blk"), axis=0, tiled=True),
            lax.all_gather(w_up, ("head", "blk"), axis=0, tiled=True),
            lax.all_gather(b_up, ("head", "blk"), axis=0, tiled=True),
            lax.all_gather(w_down, ("head", "blk"), axis=0, tiled=True),
            lax.all_gather(b_down, ("head", "blk"), axis=0, tiled=True),
            lax.all_gather(gain_attn, ("head", "blk"), axis=0, tiled=True),
            lax.all_gather(bias_attn, ("head", "blk"), axis=0, tiled=True),
            lax.all_gather(gain_ffn, ("head", "blk"), axis=0, tiled=True),
            lax.all_gather(bias_ffn, ("head", "blk"), axis=0, tiled=True),
            lax.all_gather(gain_final, ("head", "blk"), axis=0, tiled=True),
            lax.all_gather(bias_final, ("head", "blk"), axis=0, tiled=True),
        )
        inputs = stream[micro_step, 0]
        input_wide = inputs.astype(f32)
        carried = accumulator[micro_step, 0].astype(f32)
        segs = segment_ids[micro_step, 0]
        projections = jnp.stack(
            [
                jnp.dot(inputs, q_weight, preferred_element_type=f32),
                jnp.dot(inputs, k_weight, preferred_element_type=f32),
                jnp.dot(inputs, v_weight, preferred_element_type=f32),
            ]
        ).astype(bf16)
        projections = projections.reshape(3, tokens, heads_axis, group_width)
        seg_wide = jnp.broadcast_to(segs[None, :, None, None], (1, tokens, heads_axis, 1))
        regrouped, seg_group = (
            lax.all_to_all(projections, "head", split_axis=2, concat_axis=1, tiled=True),
            lax.all_to_all(seg_wide, "head", split_axis=2, concat_axis=1, tiled=True),
        )
        rows = regrouped.shape[1]
        query_loc = regrouped[0, :, 0]
        key_loc = regrouped[1, :, 0]
        value_loc = regrouped[2, :, 0]
        seg_loc = seg_group[0, :, 0, 0]
        queries3 = query_loc.reshape(rows, groups, DH)
        start_state = (
            jnp.full((rows, groups), -1e30, f32),
            jnp.zeros((rows, groups), f32),
            jnp.zeros((rows, groups, DH), f32),
        )
        row_max, row_total, weighted = attend_fold(
            queries3,
            seg_loc,
            scaling,
            start_state,
            (
                lax.all_gather(key_loc, "blk", axis=0, tiled=True),
                lax.all_gather(value_loc, "blk", axis=0, tiled=True),
                lax.all_gather(seg_loc, "blk", axis=0, tiled=True),
            ),
        )
        attn_out = weighted / row_total[:, :, None]
        log_total = row_max + jnp.log(row_total)
        attn_send = attn_out.astype(bf16).reshape(rows, 1, group_width)
        mixed = lax.all_to_all(attn_send, "head", split_axis=0, concat_axis=1, tiled=True).reshape(
            tokens, width
        )
        branch = jnp.dot(mixed, o_weight, preferred_element_type=f32)
        first, normed_one, inv_one = norm_forward(
            input_wide + branch, gain_one.astype(f32), shift_one.astype(f32)
        )
        first_low = first.astype(bf16)
        hidden_pre = jnp.dot(first_low, up_weight, preferred_element_type=f32) + up_bias.astype(f32)
        hidden_act, gate_pull = jax.vjp(smooth_gate, hidden_pre)
        hidden = hidden_act.astype(bf16)
        feed = jnp.dot(hidden, down_weight, preferred_element_type=f32) + down_bias.astype(f32)
        second, normed_two, inv_two = norm_forward(
            first + feed, gain_two.astype(f32), shift_two.astype(f32)
        )
        final, normed_three, inv_three = norm_forward(
            carried + branch + feed, gain_three.astype(f32), shift_three.astype(f32)
        )
        out_list.append((second + final).astype(bf16))
        cotangent = upstream[micro_step, 0].astype(f32)
        accum_grad, gain3_grad, shift3_grad = norm_backward(
            cotangent, normed_three, inv_three, gain_three.astype(f32)
        )
        second_grad, gain2_grad, shift2_grad = norm_backward(
            cotangent, normed_two, inv_two, gain_two.astype(f32)
        )
        feed_grad = second_grad + accum_grad
        feed_low = feed_grad.astype(bf16)
        down_grad = jnp.dot(hidden.T, feed_low, preferred_element_type=f32)
        (hidden_grad,) = gate_pull(jnp.dot(feed_low, down_weight.T, preferred_element_type=f32))
        hidden_low = hidden_grad.astype(bf16)
        up_grad = jnp.dot(first_low.T, hidden_low, preferred_element_type=f32)
        first_grad = second_grad + jnp.dot(hidden_low, up_weight.T, preferred_element_type=f32)
        resid_grad, gain1_grad, shift1_grad = norm_backward(
            first_grad, normed_one, inv_one, gain_one.astype(f32)
        )
        branch_low = (resid_grad + accum_grad).astype(bf16)
        out_wgrad = jnp.dot(mixed.T, branch_low, preferred_element_type=f32)
        mixed_grad = jnp.dot(branch_low, o_weight.T, preferred_element_type=f32).astype(bf16)
        mixed_grad = mixed_grad.reshape(tokens, heads_axis, group_width)
        grad_group = lax.all_to_all(mixed_grad, "head", split_axis=1, concat_axis=0, tiled=True)
        grad_loc = grad_group[:, 0]
        grad3 = grad_loc.reshape(rows, groups, DH)
        row_delta = jnp.sum(grad3.astype(f32) * attn_out, axis=2)
        whole_keys, whole_values, whole_seg = (
            lax.all_gather(key_loc, "blk", axis=0, tiled=True),
            lax.all_gather(value_loc, "blk", axis=0, tiled=True),
            lax.all_gather(seg_loc, "blk", axis=0, tiled=True),
        )

        def backward_step(running, blocks):
            key_part, value_part, seg_part = blocks
            attn_prob, score_grad = block_grads(
                queries3,
                seg_loc,
                grad3,
                log_total,
                row_delta,
                key_part,
                value_part,
                seg_part,
                scaling,
            )
            running = running + jnp.einsum(
                "sgk,kgd->sgd", score_grad, key_part, preferred_element_type=f32
            )
            key_term = jnp.einsum("sgk,sgd->kgd", score_grad, queries3, preferred_element_type=f32)
            value_term = jnp.einsum("sgk,sgd->kgd", attn_prob, grad3, preferred_element_type=f32)
            return (running, (key_term, value_term))

        query_grad, (key_terms, value_terms) = lax.scan(
            backward_step,
            jnp.zeros((rows, groups, DH), f32),
            key_blocks(whole_keys, whole_values, whole_seg, groups),
        )
        key_grad, value_grad = (
            lax.psum_scatter(
                key_terms.reshape(-1, group_width), "blk", scatter_dimension=0, tiled=True
            ),
            lax.psum_scatter(
                value_terms.reshape(-1, group_width), "blk", scatter_dimension=0, tiled=True
            ),
        )
        grad_stack = jnp.stack(
            [query_grad.reshape(rows, group_width), key_grad, value_grad]
        ).astype(bf16)
        grad_stack = grad_stack.reshape(3, rows, 1, group_width)
        returned = lax.all_to_all(
            grad_stack, "head", split_axis=1, concat_axis=2, tiled=True
        ).reshape(3, tokens, width)
        query_wgrad = jnp.dot(inputs.T, returned[0], preferred_element_type=f32)
        key_wgrad = jnp.dot(inputs.T, returned[1], preferred_element_type=f32)
        value_wgrad = jnp.dot(inputs.T, returned[2], preferred_element_type=f32)
        input_grad = (
            resid_grad
            + jnp.dot(returned[0], q_weight.T, preferred_element_type=f32)
            + jnp.dot(returned[1], k_weight.T, preferred_element_type=f32)
            + jnp.dot(returned[2], v_weight.T, preferred_element_type=f32)
        )
        stream_grads.append(input_grad)
        accum_grads.append(accum_grad)
        step_grads = (
            query_wgrad,
            key_wgrad,
            value_wgrad,
            out_wgrad,
            up_grad,
            jnp.sum(hidden_grad, axis=0),
            down_grad,
            jnp.sum(feed_grad, axis=0),
            gain1_grad,
            shift1_grad,
            gain2_grad,
            shift2_grad,
            gain3_grad,
            shift3_grad,
        )
        if grad_totals is None:
            grad_totals = step_grads
        else:
            grad_totals = tuple((older + newer for older, newer in zip(grad_totals, step_grads)))
    summed = lax.psum_scatter(grad_totals, ("head", "blk"), scatter_dimension=0, tiled=True)
    layer_out = jnp.stack(out_list)[:, None]
    grad_stream = jnp.stack(stream_grads)[:, None]
    grad_accum = jnp.stack(accum_grads)[:, None]
    return (
        layer_out,
        grad_stream,
        grad_accum,
        summed[0],
        summed[1],
        summed[2],
        summed[3],
        summed[4],
        summed[5],
        summed[6],
        summed[7],
        summed[8],
        summed[9],
        summed[10],
        summed[11],
        summed[12],
        summed[13],
    )


def dot_t(a, b):
    return lax.dot_general(a, b, (((1,), (1,)), ((), ())), preferred_element_type=f32)

def dot_n(a, b):
    return lax.dot_general(a, b, (((1,), (0,)), ((), ())), preferred_element_type=f32)

def dot_0(a, b):
    return lax.dot_general(a, b, (((0,), (0,)), ((), ())), preferred_element_type=f32)

def lanes(shape):
    return lax.broadcasted_iota(jnp.int32, shape, len(shape) - 1)

def query_marks(seg_row):
    wide = jnp.broadcast_to(seg_row, (128, seg_row.shape[1])).T
    return (wide == lanes(wide.shape)).astype(f32).astype(bf16)

def half_lanes(tile, half):
    wide = tile.astype(f32)
    if half:
        wide = pltpu.roll(wide, 64, 1)
    return jnp.where(lanes(wide.shape) < 64, wide, 0.0).astype(bf16)

def key_steps(bounds, low, high):
    chunks, keys = bounds.shape
    first = sum(jnp.where(bounds[t, keys - 1] < low, 1, 0) for t in range(chunks))
    last = sum(jnp.where(bounds[t, 0] <= high, 1, 0) for t in range(chunks))
    pairs = (last - first + 1) // 2
    start = jnp.minimum(first, chunks - 2 * pairs)
    return start, pairs // 2, lax.rem(pairs, 2)


def walk(step, fours, twos, carry):
    carry = lax.fori_loop(0, fours, lambda t, c: step(4, 4 * t, c), carry)
    return lax.fori_loop(0, twos, lambda t, c: step(2, 4 * fours, c), carry)


def attn_fwd_kernel(
    q_hbm, kv_hbm, seg_q_hbm, seg_k_hbm, o_hbm, of_hbm, lse_hbm, kv2_hbm, kvt_hbm,
    q_ref, kv_ref, seg_q_ref, seg_k_ref, bounds, o_ref, of_ref, lse_ref, kv2_ref, kvt_ref, vo_ref, in_sem, out_sem,
):
    loads = copies(
        [(seg_q_hbm, seg_q_ref), (seg_k_hbm, seg_k_ref), (seg_k_hbm, bounds), (kv_hbm, kv_ref), (q_hbm, q_ref)], in_sem
    )
    wait_all(loads)
    chunks, keys = seg_k_ref.shape
    log_scale = math.log2(math.e) * DH ** (-0.5)

    def prepare(t, c):
        rows = pl.ds(pl.multiple_of(t * keys, keys), keys)
        kv = kv_ref[rows, :]
        marks = jnp.where(seg_k_ref[pl.ds(t, 1), :] == rows_of((128, keys)), 0.0, FAR)
        kvt_ref[0:128, rows] = kv.T
        kvt_ref[128:256, rows] = marks.astype(bf16)
        kv2_ref[rows, 0:128] = kv
        kv2_ref[rows, 128:256] = marks.T.astype(bf16)
        vo_ref[rows, :] = jnp.where(lanes(kv.shape) < 64, 1.0, kv.astype(f32)).astype(bf16)
        return c

    lax.fori_loop(0, chunks, prepare, 0)
    stores = copies([(kv2_ref, kv2_hbm), (kvt_ref, kvt_hbm)], out_sem)

    def tile(j, c):
        q_tile = q_ref[j]
        rows = q_tile.shape[0]
        outs = []
        for half in range(2):
            i = half * (chunks // 2) + j
            left = half_lanes(q_tile, half)
            left = jnp.concatenate([left, query_marks(seg_q_ref[pl.ds(i, 1), :])], axis=1)
            low, high = bounds[i, 0], bounds[i, keys - 1]
            start, fours, twos = key_steps(bounds, low, high)

            def step(width, t, carry):
                top, acc = carry
                at = pl.ds(pl.multiple_of((start + t) * keys, keys), width * keys)
                s = dot_n(left, kvt_ref[:, at])
                new = jnp.maximum(top, jnp.max(s, axis=1, keepdims=True))
                p = jnp.exp2((s - new) * log_scale)
                acc = acc * jnp.exp2((top - new) * log_scale) + dot_n(p.astype(bf16), vo_ref[at, :])
                return new, acc

            carry = (jnp.full((rows, 1), FAR, f32), jnp.zeros((rows, 128), f32))
            top, acc = walk(step, fours, twos, carry)
            total = pltpu.roll(acc, 64, 1)
            outs.append(acc / total)
            lse = jnp.broadcast_to(top * log_scale, acc.shape) + jnp.log2(acc)
            lse_ref[pl.ds(i, 1), :] = lse.T[0:1, :]
        o = jnp.where(lanes(outs[0].shape) < 64, pltpu.roll(outs[0], 64, 1), outs[1])
        of_ref[j] = o
        o_ref[j] = o.astype(bf16)
        return c

    lax.fori_loop(0, chunks // 2, tile, 0)
    stores += copies([(o_ref, o_hbm), (of_ref, of_hbm), (lse_ref, lse_hbm)], out_sem.at[pl.ds(2, 3)])
    wait_all(stores)


def attn_fwd(q, kv, seg_q, seg_k):
    chunks, keys = seg_k.shape
    dma = pltpu.SemaphoreType.DMA
    shapes = (
        (q.shape, bf16), (q.shape, f32), (seg_q.shape, f32), ((chunks * keys, 256), bf16), ((256, chunks * keys), bf16)
    )
    return pl.pallas_call(
        attn_fwd_kernel,
        out_shape=[jax.ShapeDtypeStruct(shape, kind) for shape, kind in shapes],
        in_specs=any_specs(4),
        out_specs=any_specs(5),
        scratch_shapes=[
            *[pltpu.VMEM(a.shape, a.dtype) for a in (q, kv, seg_q, seg_k)],
            pltpu.SMEM(seg_k.shape, jnp.int32),
            *[pltpu.VMEM(shape, kind) for shape, kind in shapes],
            pltpu.VMEM((chunks * keys, 128), bf16),
            dma((5,)),
            dma((5,)),
        ],
        compiler_params=pltpu.CompilerParams(vmem_limit_bytes=VMEM_BYTES),
        name="attn_fwd",
    )(q, kv, seg_q, seg_k)


def attn_bwd_kernel(
    q_hbm, do_hbm, of_hbm, lse_hbm, kv2_hbm, kvt_hbm, seg_q_hbm, seg_k_hbm, pass1, pass2, dq_hbm, dkv_hbm, out1, out2,
    q_ref, do_ref, of_ref, lse_ref, kv2_ref, kvt_ref, seg_q_ref, bounds, dq_ref, dkv_ref, hold1, hold2, in_sem, out_sem,
):
    loads = copies(
        [
            (q_hbm, q_ref), (do_hbm, do_ref), (of_hbm, of_ref), (lse_hbm, lse_ref), (kv2_hbm, kv2_ref),
            (seg_q_hbm, seg_q_ref), (seg_k_hbm, bounds),
            (pass1, hold1), (pass2, hold2), (kvt_hbm, kvt_ref),
        ],
        in_sem,
    )
    dkv_ref[...] = jnp.zeros_like(dkv_ref)
    wait_all(loads)
    stores = copies([(hold1, out1), (hold2, out2)], out_sem)
    chunks, keys = bounds.shape
    log_scale = math.log2(math.e) * DH ** (-0.5)

    def tile(j, c):
        q_tile, do_tile = q_ref[j], do_ref[j]
        rows = q_tile.shape[0]
        prod = do_tile.astype(f32) * of_ref[j]
        prod = prod.T
        dqs = []
        for half in range(2):
            i = half * (chunks // 2) + j
            left = half_lanes(q_tile, half)
            grad = do_tile.astype(f32)
            if not half:
                grad = pltpu.roll(grad, 64, 1)
            grad = jnp.where(lanes(grad.shape) < 64, 0.0, grad).astype(bf16)
            delta = jnp.sum(prod[64 * half:64 * half + 64], axis=0, keepdims=True)
            lse = lse_ref[pl.ds(i, 1), :]
            both = jnp.concatenate([left, grad], axis=0)
            marks = query_marks(seg_q_ref[pl.ds(i, 1), :])
            right = jnp.concatenate([both, jnp.concatenate([marks, jnp.zeros_like(marks)], axis=0)], axis=1).T
            low, high = bounds[i, 0], bounds[i, keys - 1]
            start, fours, twos = key_steps(bounds, low, high)

            def step(width, t, dq):
                at = pl.ds(pl.multiple_of((start + t) * keys, keys), width * keys)
                sdp = dot_n(kv2_ref[at, :], right)
                p = jnp.exp2(sdp[:, :rows] * log_scale - lse)
                ds = (p * (sdp[:, rows:] - delta)).astype(bf16)
                dkv_ref[at, :] += dot_n(jnp.concatenate([ds, p.astype(bf16)], axis=1), both)
                return dq + dot_n(kvt_ref[0:128, at], ds)

            dqs.append(walk(step, fours, twos, jnp.zeros((128, rows), f32)).T)
        dq = jnp.where(lanes(dqs[0].shape) < 64, dqs[0], pltpu.roll(dqs[1], 64, 1))
        dq_ref[j] = (dq * DH ** (-0.5)).astype(bf16)
        return c

    lax.fori_loop(0, chunks // 2, tile, 0)
    dkv = dkv_ref[...]
    dkv_ref[...] = jnp.where(lanes(dkv.shape) < 64, dkv * DH ** (-0.5), dkv)
    stores += copies([(dq_ref, dq_hbm), (dkv_ref, dkv_hbm)], out_sem.at[pl.ds(2, 2)])
    wait_all(stores)


def attn_bwd(q, do, of, lse, kv2, kvt, seg_q, seg_k, pass1, pass2):
    dma = pltpu.SemaphoreType.DMA
    shapes = ((q.shape, bf16), ((kv2.shape[0], 128), f32))
    return pl.pallas_call(
        attn_bwd_kernel,
        out_shape=[jax.ShapeDtypeStruct(shape, kind) for shape, kind in shapes]
        + [jax.ShapeDtypeStruct(a.shape, a.dtype) for a in (pass1, pass2)],
        in_specs=any_specs(10),
        out_specs=any_specs(4),
        scratch_shapes=[
            *[pltpu.VMEM(a.shape, a.dtype) for a in (q, do, of, lse, kv2, kvt, seg_q)],
            pltpu.SMEM(seg_k.shape, jnp.int32),
            *[pltpu.VMEM(shape, kind) for shape, kind in shapes],
            *[pltpu.VMEM(a.shape, a.dtype) for a in (pass1, pass2)],
            dma((10,)),
            dma((4,)),
        ],
        compiler_params=pltpu.CompilerParams(vmem_limit_bytes=VMEM_BYTES),
        name="attn_bwd",
    )(q, do, of, lse, kv2, kvt, seg_q, seg_k, pass1, pass2)


class Spot:
    def __init__(self, nb):
        self.nb, self.nz = nb, nb // 2
        self.h, b = lax.axis_index("head"), lax.axis_index("blk")
        self.z, self.c = b // 2, lax.rem(b, 2)
        self.near = (self.h + 1 - 2 * lax.rem(self.h, 2), lax.rem(self.h + 2, 4))
        self.diag = 3 - self.h
        self.me = self.h * nb + b

    def index(self, h, z, c):
        return h * self.nb + z * 2 + c

    def ahead(self, k):
        return lax.rem(self.z + k, self.nz)


def remote(src, dst, send, recv, h, b):
    return pltpu.make_async_remote_copy(
        src_ref=src,
        dst_ref=dst,
        send_sem=send,
        recv_sem=recv,
        device_id={"head": h, "blk": b},
        device_id_type=MESH,
    )


def each(count, body, start=0):
    def run(i, c):
        body(i)
        return c

    lax.fori_loop(start, count, run, 0)


def greet_all(n, nb, me):
    barrier = pltpu.get_barrier_semaphore()

    def signal(i):
        t = lax.rem(me + i, n)
        pl.semaphore_signal(
            barrier, inc=1, device_id={"head": t // nb, "blk": lax.rem(t, nb)}, device_id_type=MESH
        )

    each(n, signal, 1)
    pl.semaphore_wait(barrier, n - 1)


def halves(shape):
    rows, width = shape
    if width > 128:
        return [(slice(None), slice(w * width // 2, (w + 1) * width // 2)) for w in range(2)]
    return [(slice(w * rows // 2, (w + 1) * rows // 2), slice(None)) for w in range(2)]


class Gather:
    def __init__(self, spot, shard, full, send, recv, local):
        self.s, self.shard, self.full, self.local = spot, shard, full, local
        self.send, self.recv = send, recv
        self.cut = halves(shard.shape)

    def copy(self, src, dst, k, h, z, c, recv_k=None):
        recv_k = k if recv_k is None else recv_k
        return remote(src, dst, self.send.at[k], self.recv.at[recv_k], h, z * 2 + c)

    def to_z(self, z):
        s = self.s
        return self.copy(self.shard, self.full.at[s.me], z, s.h, z, s.c, s.z)

    def from_z(self, z):
        s = self.s
        slot = self.full.at[s.index(s.h, z, s.c)]
        return self.copy(slot, slot, z, s.h, z, s.c)

    def near(self, w, z, own=False):
        s = self.s
        slot = self.full.at[s.index(s.h, z, s.c)]
        return self.copy(self.shard if own else slot, slot, (1 + w) * s.nz + z, s.near[w], s.z, s.c)

    def from_near(self, w, z):
        s = self.s
        slot = self.full.at[s.index(s.near[w], z, s.c)]
        return self.copy(slot, slot, (1 + w) * s.nz + z, s.near[w], s.z, s.c)

    def lanes(self, slot, w):
        return slot.at[self.cut[w]]

    def onward(self, w, z):
        s = self.s
        slot = self.lanes(self.full.at[s.index(s.near[w], z, s.c)], w)
        return self.copy(slot, slot, (3 + w) * s.nz + z, s.near[1 - w], s.z, s.c)

    def from_onward(self, w, z):
        s = self.s
        slot = self.lanes(self.full.at[s.index(s.diag, z, s.c)], w)
        return self.copy(slot, slot, (3 + w) * s.nz + z, s.near[1 - w], s.z, s.c)

    def twin(self, h, z, own=False):
        s = self.s
        slot = self.full.at[s.index(h, z, s.c)]
        return self.copy(self.shard if own else slot, slot, 5 * s.nz + h * s.nz + z, s.h, s.z, 1 - s.c)

    def from_twin(self, h, z):
        s = self.s
        slot = self.full.at[s.index(h, z, 1 - s.c)]
        return self.copy(slot, slot, 5 * s.nz + h * s.nz + z, s.h, s.z, 1 - s.c)

    def begin(self):
        s = self.s
        self.own = pltpu.make_async_copy(self.shard, self.full.at[s.me], self.local)
        self.own.start()
        each(s.nz, lambda k: self.to_z(s.ahead(k)).start(), 1)
        self.near(0, s.z, True).start()
        self.near(1, s.z, True).start()
        self.twin(s.h, s.z, True).start()

    def spread(self):
        s = self.s

        def go(k):
            z = s.ahead(k)
            self.from_z(z).wait_recv()
            self.near(0, z).start()
            self.near(1, z).start()
            self.twin(s.h, z).start()

        each(s.nz, go, 1)

    def cross(self):
        s = self.s

        def go(k):
            z = s.ahead(k)
            for w in range(2):
                self.from_near(w, z).wait_recv()
                self.onward(w, z).start()
                self.twin(s.near[w], z).start()

        each(s.nz, go)

    def last(self):
        s = self.s

        def go(k):
            z = s.ahead(k)
            for w in range(2):
                self.from_onward(w, z).wait_recv()
            self.twin(s.diag, z).start()

        each(s.nz, go)

    def arrive(self):
        s = self.s
        each(4, lambda h: each(s.nz, lambda z: self.from_twin(h, z).wait_recv()))
        self.own.wait()

    def sent(self):
        s = self.s
        each(s.nz, lambda k: self.to_z(s.ahead(k)).wait_send(), 1)

        def go(z):
            for w in range(2):
                self.near(w, z).wait_send()
                self.onward(w, z).wait_send()
            each(4, lambda h: self.twin(h, z).wait_send())

        each(s.nz, go)


class Scatter:
    def __init__(self, spot, part, twin, diag, near, line, send, recv):
        self.s, self.part, self.t, self.d, self.n, self.l = spot, part, twin, diag, near, line
        self.send, self.recv = send, recv
        self.cut = halves(part.shape[1:])
        self.axis = 1 if self.cut[0][0] == slice(None) else 0

    def copy(self, src, dst, k, h, z, c, recv_k=None):
        recv_k = k if recv_k is None else recv_k
        return remote(src, dst, self.send.at[k], self.recv.at[recv_k], h, z * 2 + c)

    def mine(self, h, z):
        return self.s.index(h, z, self.s.c)

    def to_twin(self, h, z):
        s = self.s
        src = self.part.at[s.index(h, z, 1 - s.c)]
        return self.copy(src, self.t.at[h, z], h * s.nz + z, s.h, s.z, 1 - s.c)

    def to_diag(self, w, z):
        s = self.s
        src = self.part.at[self.mine(s.diag, z)].at[self.cut[w]]
        return self.copy(src, self.d.at[w, z], (4 + w) * s.nz + z, s.near[w], s.z, s.c)

    def to_near(self, w, z):
        s = self.s
        src = self.part.at[self.mine(s.near[w], z)]
        return self.copy(src, self.n.at[w, z], (6 + w) * s.nz + z, s.near[w], s.z, s.c)

    def to_line(self, z):
        s = self.s
        src = self.part.at[self.mine(s.h, z)]
        return self.copy(src, self.l.at[s.z], 8 * s.nz + z, s.h, z, s.c, 8 * s.nz + s.z)

    def from_line(self, z):
        s = self.s
        src = self.part.at[self.mine(s.h, z)]
        return self.copy(src, self.l.at[z], 8 * s.nz + z, s.h, z, s.c)

    def begin(self):
        each(4, lambda h: each(self.s.nz, lambda z: self.to_twin(h, z).start()))

    def pair(self, h, z):
        self.to_twin(h, z).wait_recv()
        return self.part[self.mine(h, z)].astype(f32) + self.t[h, z].astype(f32)

    def keep(self, h, z, value):
        self.part[self.mine(h, z)] = value.astype(self.part.dtype)

    def first(self):
        s = self.s

        def go(k):
            z = s.ahead(k)
            self.keep(s.diag, z, self.pair(s.diag, z))
            for w in range(2):
                self.to_diag(w, z).start()

        each(s.nz + 1, go, 1)

    def second(self):
        s = self.s

        def go(k):
            z = s.ahead(k)
            for w in range(2):
                value = self.pair(s.near[w], z)
                self.to_diag(1 - w, z).wait_recv()
                other = self.d[1 - w, z].astype(f32)
                pieces = [value[cut] for cut in self.cut]
                pieces[1 - w] = pieces[1 - w] + other
                value = jnp.concatenate(pieces, axis=self.axis)
                self.keep(s.near[w], z, value)
                self.to_near(w, z).start()

        each(s.nz + 1, go, 1)

    def joined(self, z):
        value = self.pair(self.s.h, z)
        for w in range(2):
            self.to_near(w, z).wait_recv()
            value = value + self.n[w, z].astype(f32)
        return value

    def third(self):
        s = self.s

        def go(k):
            z = s.ahead(k)
            self.keep(s.h, z, self.joined(z))
            self.to_line(z).start()

        each(s.nz, go, 1)

    def total(self):
        s = self.s
        value = self.joined(s.z)

        def go(k, value):
            z = s.ahead(k)
            self.from_line(z).wait_recv()
            return value + self.l[z].astype(f32)

        return lax.fori_loop(1, s.nz, go, value)

    def sent(self):
        s = self.s

        def go(z):
            each(4, lambda h: self.to_twin(h, z).wait_send())
            for w in range(2):
                self.to_diag(w, z).wait_send()
                self.to_near(w, z).wait_send()

        each(s.nz, go)
        each(s.nz, lambda k: self.to_line(s.ahead(k)).wait_send(), 1)


class Exchange:
    def __init__(self, spot, src, dst, send, recv, local):
        self.s, self.src, self.dst, self.send, self.recv, self.local = spot, src, dst, send, recv, local
        self.g = spot.me // 2

    def copy(self, i, back=False):
        s = self.s
        to = lax.rem(self.g + i, 16)
        t = to * 2 + s.c
        src = self.src(to)
        dst = self.dst(lax.rem(self.g + 16 - i, 16)) if back else self.dst(self.g)
        return remote(src, dst, self.send.at[i], self.recv.at[i], t // s.nb, lax.rem(t, s.nb))

    def own(self):
        return pltpu.make_async_copy(self.src(self.g), self.dst(self.g), self.local)

    def begin(self):
        self.own().start()
        each(16, lambda i: self.copy(i).start(), 1)

    def arrive(self, i):
        self.copy(i, True).wait_recv()

    def end(self):
        each(16, self.arrive, 1)
        self.sent()

    def sent(self):
        self.own().wait()
        each(16, lambda i: self.copy(i).wait_send(), 1)


def weave(left, right):
    kind = left.dtype
    left, right = left.astype(f32), right.astype(f32)
    low = lanes(left.shape) < 64
    first = jnp.where(low, left, pltpu.roll(right, 64, 1)).astype(kind)
    second = jnp.where(low, pltpu.roll(left, 64, 1), right).astype(kind)
    return first, second


def any_specs(count):
    return [pl.BlockSpec(memory_space=pl.ANY)] * count


def copies(pairs, sems):
    jobs = [pltpu.make_async_copy(src, dst, sems.at[k]) for k, (src, dst) in enumerate(pairs)]
    for job in jobs:
        job.start()
    return jobs


def wait_all(jobs):
    for job in jobs:
        job.wait()


def rows_of(shape):
    return lax.broadcasted_iota(jnp.int32, shape, 0)


def spread_row(block, width, each_lane):
    count = block.shape[0]
    pick = (rows_of((128, width)) == lax.rem(lanes((128, width)), each_lane)).astype(f32).astype(bf16)
    wide = dot_n(block.astype(bf16), pick)
    return column_sum(jnp.where(rows_of((count, width)) == lanes((count, width)) // each_lane, wide, 0.0))


def gather_row(row, count, each_lane):
    width = row.shape[1]
    wide = jnp.where(rows_of((count, width)) == lanes((count, width)) // each_lane, row, 0.0)
    pick = (lanes((width, 128)) == lax.rem(rows_of((width, 128)), each_lane)).astype(f32)
    return lax.dot_general(
        wide, pick, (((1,), (0,)), ((), ())), precision=lax.Precision.HIGHEST, preferred_element_type=f32
    )


def project_kernel(n, nb, *refs):
    x_hbm, wq_hbm, wk_hbm, wv_hbm, wo_hbm, wu_hbm, wd_hbm, seg_hbm = refs[:8]
    smalls = refs[8:16]
    q_out, kv_out, wa_out, wb_out, wd_out, par_out, bup_out, segk_out, segq_out = refs[16:25]
    (
        x, wq, wk, wv, wo, wu, wd, seg, *small, bup_small, vec, vecs, sa, sb, wa, kv_send, q_send, par, bup, segk, segq,
        in_sem, out_sem, ag_send, ag_recv, ag_local, ex_send, ex_recv, ex_local, tw_send, tw_recv,
    ) = refs[25:]
    s = Spot(nb)
    loads = copies(
        [(wq_hbm, wq), (wk_hbm, wk), (wv_hbm, wv), (seg_hbm, seg), (smalls[0], bup_small)]
        + [(smalls[k], small[k - 1]) for k in range(1, 8)]
        + [(wo_hbm, wo), (wu_hbm, wu), (wd_hbm, wd), (x_hbm, x)],
        in_sem,
    )
    greet_all(n, nb, s.me)
    wait_all(loads[:12])
    for t in range(4):
        tile = slice(128 * t, 128 * t + 128)
        first, second = weave(wk[:, tile], wv[:, tile])
        sa[:, 256 * t:256 * t + 128] = first
        sa[:, 256 * t + 128:256 * t + 256] = second
    sa[:, 1024:1536] = wq[...]
    vec[...] = jnp.zeros_like(vec)
    vec[0:1, 0:64] = bup_small[...].astype(f32).reshape(1, 64)
    for k in range(7):
        vec[k + 1:k + 2, 0:16] = small[k][...].astype(f32).reshape(1, 16)
    vec[8:10, :] = seg[...].astype(f32)
    jobs = [
        Gather(s, shard, full, ag_send.at[k], ag_recv.at[k], ag_local.at[k])
        for k, (shard, full) in enumerate(((sa, wa), (vec, vecs), (sb, wb_out), (wd, wd_out)))
    ]
    for job in jobs[:2]:
        job.begin()
    wait_all(loads[12:])
    sb[:, 0:512] = wo[...]
    sb[:, 512:2560] = wu[...]
    for job in jobs[:2]:
        job.spread()
    for job in jobs[:2]:
        job.cross()
    for job in jobs[:2]:
        job.last()
    for job in jobs[2:]:
        job.begin()
    for job in jobs[:2]:
        job.arrive()
    outs = copies([(wa, wa_out)], out_sem)
    qkv = dot_n(x[...], wa[...].reshape(512, 1536)).astype(bf16)
    for m in range(2):
        rows = slice(128 * m, 128 * m + 128)
        for h in range(8):
            kv_send[8 * m + h] = qkv[rows, 128 * h:128 * h + 128].reshape(8, 16, 128)
        for t in range(4):
            tile = qkv[rows, 1024 + 128 * t:1152 + 128 * t]
            first, second = weave(tile[0:64], tile[64:128])
            q_send[8 * m + 2 * t] = first.reshape(4, 16, 128)
            q_send[8 * m + 2 * t + 1] = second.reshape(4, 16, 128)
    kv_ex = Exchange(
        s, lambda p: kv_send.at[p], lambda g: kv_out.at[:, g, s.c], ex_send.at[0], ex_recv.at[0], ex_local.at[0]
    )
    q_ex = Exchange(s, lambda p: q_send.at[p], lambda g: q_out.at[:, g], ex_send.at[1], ex_recv.at[1], ex_local.at[1])
    kv_ex.begin()
    q_ex.begin()
    for job in jobs[2:]:
        job.spread()
    bup[...] = spread_row(vecs[:, 0, :], 2048, 64)
    for k in range(7):
        par[k:k + 1, :] = spread_row(vecs[:, k + 1, :], 512, 16)
    par[7:8, :] = jnp.zeros((1, 512), f32)
    ids = jnp.where(kv_ex.g < 8, vecs[:, 8, :], vecs[:, 9, :]).astype(bf16)
    for i in range(8):
        pick = (rows_of((128, 512)) == 16 * i + lax.rem(lanes((128, 512)), 16)).astype(f32).astype(bf16)
        wide = dot_n(ids, pick)
        source = rows_of((n, 512))
        row = jnp.where(source == lanes((n, 512)) // 16, wide, 0.0)
        segk[i:i + 1, :] = column_sum(row).astype(jnp.int32)
        source = rows_of((n, 256))
        own = (source // 2 == lanes((n, 256)) // 16) & (lax.rem(source, 2) == s.c)
        segq[i:i + 1, :] = column_sum(jnp.where(own, wide[:, 0:256], 0.0)).astype(jnp.int32)
    outs += copies([(par, par_out), (bup, bup_out), (segk, segk_out), (segq, segq_out)], out_sem.at[pl.ds(1, 4)])
    for job in jobs[2:]:
        job.cross()

    def twin(g, c):
        slot = kv_out.at[:, g, c]
        return remote(slot, slot, tw_send.at[g], tw_recv.at[g], s.h, s.z * 2 + 1 - s.c)

    kv_ex.own().wait()
    twin(kv_ex.g, s.c).start()

    def forward(i):
        kv_ex.arrive(i)
        twin(lax.rem(kv_ex.g + 16 - i, 16), s.c).start()

    each(16, forward, 1)
    for job in jobs[2:]:
        job.last()
    for job in jobs[2:]:
        job.arrive()
    each(16, lambda g: twin(g, 1 - s.c).wait_recv())
    each(16, lambda g: twin(g, s.c).wait_send())
    each(16, lambda i: kv_ex.copy(i).wait_send(), 1)
    q_ex.end()
    for job in jobs:
        job.sent()
    wait_all(outs)


def project(n, nb, x, wq, wk, wv, wo, wu, wd, seg, smalls):
    dma = pltpu.SemaphoreType.DMA
    nz = nb // 2
    return pl.pallas_call(
        functools.partial(project_kernel, n, nb),
        out_shape=(
            jax.ShapeDtypeStruct((4, 16, 16, 128), bf16),
            jax.ShapeDtypeStruct((8, 16, 2, 16, 128), bf16),
            jax.ShapeDtypeStruct((n, 16, 1536), bf16),
            jax.ShapeDtypeStruct((n, 16, 2560), bf16),
            jax.ShapeDtypeStruct((n, 64, 512), bf16),
            jax.ShapeDtypeStruct((8, 512), f32),
            jax.ShapeDtypeStruct((1, 2048), f32),
            jax.ShapeDtypeStruct((8, 512), jnp.int32),
            jax.ShapeDtypeStruct((8, 256), jnp.int32),
        ),
        in_specs=any_specs(16),
        out_specs=any_specs(9),
        scratch_shapes=[
            pltpu.VMEM(x.shape, bf16),
            pltpu.VMEM((16, 512), bf16),
            pltpu.VMEM((16, 512), bf16),
            pltpu.VMEM((16, 512), bf16),
            pltpu.VMEM((16, 512), bf16),
            pltpu.VMEM((16, 2048), bf16),
            pltpu.VMEM((64, 512), bf16),
            pltpu.VMEM((2, 128), jnp.int32),
            *[pltpu.VMEM((16,), bf16)] * 7,
            pltpu.VMEM((64,), bf16),
            pltpu.VMEM((16, 128), f32),
            pltpu.VMEM((n, 16, 128), f32),
            pltpu.VMEM((16, 1536), bf16),
            pltpu.VMEM((16, 2560), bf16),
            pltpu.VMEM((n, 16, 1536), bf16),
            pltpu.VMEM((16, 8, 16, 128), bf16),
            pltpu.VMEM((16, 4, 16, 128), bf16),
            pltpu.VMEM((8, 512), f32),
            pltpu.VMEM((1, 2048), f32),
            pltpu.VMEM((8, 512), jnp.int32),
            pltpu.VMEM((8, 256), jnp.int32),
            dma((16,)),
            dma((5,)),
            dma((4, 9 * nz)),
            dma((4, 9 * nz)),
            dma((4,)),
            dma((2, 16)),
            dma((2, 16)),
            dma((2,)),
            dma((16,)),
            dma((16,)),
        ],
        compiler_params=pltpu.CompilerParams(
            collective_id=1, has_side_effects=True, vmem_limit_bytes=VMEM_BYTES
        ),
        name="project",
    )(x, wq, wk, wv, wo, wu, wd, seg, *smalls)


def row_norm(v):
    mean = jnp.mean(v, axis=-1, keepdims=True)
    mid = v - mean
    inv = lax.rsqrt(jnp.mean(mid * mid, axis=-1, keepdims=True) + EPSILON)
    return mid * inv, inv


def row_norm_back(grad, normed, inv, gain):
    part = grad * gain
    return inv * (
        part
        - jnp.mean(part, axis=-1, keepdims=True)
        - normed * jnp.mean(part * normed, axis=-1, keepdims=True)
    )


def column_sum(v):
    return jnp.sum(v, axis=0, keepdims=True)


def middle_kernel(n, nb, *refs):
    o_hbm, x_hbm, y_hbm, g_hbm, wb_hbm, wd_hbm, par_hbm, bup_hbm = refs[:8]
    outs_hbm = refs[9:20]
    do_out = refs[8]
    (
        o_in, x, y, g_in, wb, wd, par, bup, o_recv, do_send, slope,
        out, dacc_ref, dz1_ref, x1_ref, dur_ref, hid_ref, dfr_ref, omix, dar_ref, gvec, bias_up,
        in_sem, out_sem, ex_send, ex_recv, ex_local,
    ) = refs[20:]
    s = Spot(nb)
    loads = copies(
        [(o_hbm, o_in), (x_hbm, x), (y_hbm, y), (g_hbm, g_in), (par_hbm, par), (bup_hbm, bup), (wb_hbm, wb), (wd_hbm, wd)],
        in_sem,
    )
    greet_all(n, nb, s.me)
    loads[0].wait()
    o_ex = Exchange(
        s, lambda p: o_in.at[:, p], lambda g: o_recv.at[g], ex_send.at[0], ex_recv.at[0], ex_local.at[0]
    )
    o_ex.begin()
    wait_all(loads[1:])
    o_ex.end()
    for m in range(2):
        for t in range(4):
            first, second = weave(
                o_recv[8 * m + 2 * t].reshape(64, 128), o_recv[8 * m + 2 * t + 1].reshape(64, 128)
            )
            omix[128 * m:128 * m + 64, 128 * t:128 * t + 128] = first
            omix[128 * m + 64:128 * m + 128, 128 * t:128 * t + 128] = second
    gain1, bias1 = par[1:2], par[2:3]
    gain2, bias2 = par[3:4], par[4:5]
    gain3, bias3 = par[5:6], par[6:7]
    w_out = wb[:, :, 0:512].reshape(512, 512)
    a = dot_n(omix[...], w_out)
    n1, r1 = row_norm(x[...].astype(f32) + a)
    x1 = n1 * gain1 + bias1
    x1r = x1.astype(bf16)
    x1_ref[...] = x1r
    feed = jnp.zeros_like(x1)
    for t in range(4):
        cols = slice(512 * t, 512 * t + 512)
        u = dot_n(x1r, wb[:, :, 512 + 512 * t:1024 + 512 * t].reshape(512, 512)) + bup[:, cols]
        phi = 0.5 * (1.0 + lax.erf(u * (0.5**0.5)))
        hid = (u * phi).astype(bf16)
        slope[:, cols] = phi + u * jnp.exp(-0.5 * u * u) * ((2.0 * math.pi) ** -0.5)
        hid_ref[:, cols] = hid
        feed = feed + dot_n(hid, wd[8 * t:8 * t + 8].reshape(512, 512))
    feed = feed + par[0:1]
    n2, r2 = row_norm(x1 + feed)
    n3, r3 = row_norm(y[...].astype(f32) + a + feed)
    out[...] = (n2 * gain2 + bias2 + (n3 * gain3 + bias3)).astype(bf16)
    g = g_in[...].astype(f32)
    dacc = row_norm_back(g, n3, r3, gain3)
    dacc_ref[...] = dacc
    dz2 = row_norm_back(g, n2, r2, gain2)
    df = dz2 + dacc
    dfr = df.astype(bf16)
    dfr_ref[...] = dfr
    dx1 = dz2
    for t in range(4):
        cols = slice(512 * t, 512 * t + 512)
        du = dot_t(dfr, wd[8 * t:8 * t + 8].reshape(512, 512)) * slope[:, cols]
        bias_up[:, cols] = column_sum(du)
        dur = du.astype(bf16)
        dur_ref[:, cols] = dur
        dx1 = dx1 + dot_t(dur, wb[:, :, 512 + 512 * t:1024 + 512 * t].reshape(512, 512))
    dz1 = row_norm_back(dx1, n1, r1, gain1)
    dz1_ref[...] = dz1
    dar = (dz1 + dacc).astype(bf16)
    dar_ref[...] = dar
    do = dot_t(dar, w_out).astype(bf16)
    for m in range(2):
        for t in range(4):
            tile = do[128 * m:128 * m + 128, 128 * t:128 * t + 128]
            first, second = weave(tile[0:64], tile[64:128])
            do_send[8 * m + 2 * t] = first.reshape(4, 16, 128)
            do_send[8 * m + 2 * t + 1] = second.reshape(4, 16, 128)
    do_ex = Exchange(
        s, lambda p: do_send.at[p], lambda g: do_out.at[:, g], ex_send.at[1], ex_recv.at[1], ex_local.at[1]
    )
    do_ex.begin()
    stores = copies(
        zip((out, dacc_ref, dz1_ref, x1_ref, dur_ref, hid_ref, dfr_ref, omix, dar_ref), outs_hbm[:9]), out_sem
    )
    sum_g = column_sum(g)
    sums = (
        column_sum(df), column_sum(dx1 * n1), column_sum(dx1), column_sum(g * n2), sum_g, column_sum(g * n3), sum_g
    )
    gvec[...] = jnp.zeros_like(gvec)
    gvec[:, 0, :] = gather_row(bias_up[...], n, 64)
    for k in range(7):
        gvec[:, k + 1, :] = gather_row(sums[k], n, 16)
    stores += copies([(gvec, outs_hbm[9])], out_sem.at[pl.ds(9, 1)])
    do_ex.end()
    wait_all(stores)


def middle(n, nb, o, x, y, g, wb, wd, par, bup):
    dma = pltpu.SemaphoreType.DMA
    rows = x.shape[0]
    saved = [
        ((rows, 512), bf16), ((rows, 512), f32), ((rows, 512), f32), ((rows, 512), bf16), ((rows, 2048), bf16),
        ((rows, 2048), bf16), ((rows, 512), bf16), ((rows, 512), bf16), ((rows, 512), bf16), ((n, 16, 128), f32),
    ]
    return pl.pallas_call(
        functools.partial(middle_kernel, n, nb),
        out_shape=[jax.ShapeDtypeStruct((4, 16, 16, 128), bf16)]
        + [jax.ShapeDtypeStruct(shape, kind) for shape, kind in saved]
        + [jax.ShapeDtypeStruct((8, 128), f32)],
        in_specs=any_specs(8),
        out_specs=any_specs(12),
        scratch_shapes=[
            pltpu.VMEM(o.shape, bf16),
            pltpu.VMEM(x.shape, bf16),
            pltpu.VMEM(x.shape, bf16),
            pltpu.VMEM(x.shape, bf16),
            pltpu.VMEM(wb.shape, bf16),
            pltpu.VMEM(wd.shape, bf16),
            pltpu.VMEM(par.shape, f32),
            pltpu.VMEM(bup.shape, f32),
            pltpu.VMEM((16, 4, 16, 128), bf16),
            pltpu.VMEM((16, 4, 16, 128), bf16),
            pltpu.VMEM((rows, 2048), f32),
            *[pltpu.VMEM(shape, kind) for shape, kind in saved],
            pltpu.VMEM((1, 2048), f32),
            dma((8,)),
            dma((10,)),
            dma((2, 16)),
            dma((2, 16)),
            dma((2,)),
        ],
        compiler_params=pltpu.CompilerParams(
            collective_id=2, has_side_effects=True, vmem_limit_bytes=VMEM_BYTES
        ),
        name="middle",
    )(o, x, y, g, wb, wd, par, bup)[:11]


def finish_kernel(n, nb, *refs):
    ins = refs[:12]
    outs = refs[12:20]
    (
        dq, dkv, x, dz1, x1, dur, hid, dfr, omix, dar, gvec, wa,
        pa, ta, da, na, la, pb, tb, db, nb_, lb, pd, td, dd, nd, ld, tv, dv, nv, lv,
        twin_buf, dkv_send, dkv_recv, dq_recv, dqkv, gx, gq, gk, gv, go, gu, gd, gs,
        in_sem, out_sem, rs_send, rs_recv, ex_send, ex_recv, ex_local, tw_send, tw_recv,
    ) = refs[20:]
    s = Spot(nb)
    order = (1, 10, 8, 9, 4, 5, 6, 7, 0, 2, 3, 11)
    local = (dq, dkv, x, dz1, x1, dur, hid, dfr, omix, dar, gvec, wa)
    loads = copies([(ins[k], local[k]) for k in order], in_sem)
    greet_all(n, nb, s.me)
    swap = remote(ins[1].at[:, :, 1 - s.c], twin_buf, tw_send, tw_recv, s.h, s.z * 2 + 1 - s.c)
    swap.start()
    jobs = [
        Scatter(s, *bufs, rs_send.at[k], rs_recv.at[k])
        for k, bufs in enumerate(
            ((pb, tb, db, nb_, lb), (pd, td, dd, nd, ld), (gvec, tv, dv, nv, lv), (pa, ta, da, na, la))
        )
    ]
    wait_all(loads[:6])
    jobs[2].begin()
    pb[:, :, 0:512] = dot_0(omix[...], dar[...]).astype(bf16).reshape(n, 16, 512)
    for t in range(4):
        cols = slice(512 * t, 512 * t + 512)
        pb[:, :, 512 + 512 * t:1024 + 512 * t] = dot_0(x1[...], dur[:, cols]).astype(bf16).reshape(n, 16, 512)
    jobs[0].begin()
    wait_all(loads[6:])
    for t in range(4):
        cols = slice(512 * t, 512 * t + 512)
        pd[8 * t:8 * t + 8] = dot_0(hid[:, cols], dfr[...]).astype(bf16).reshape(8, 64, 512)
    jobs[1].begin()
    swap.wait()

    def add(g):
        dkv_send[g] = (dkv[:, g, s.c] + twin_buf[:, g]).astype(bf16)

    each(16, add)
    kv_ex = Exchange(
        s, lambda p: dkv_send.at[p], lambda g: dkv_recv.at[g], ex_send.at[0], ex_recv.at[0], ex_local.at[0]
    )
    q_ex = Exchange(s, lambda p: dq.at[:, p], lambda g: dq_recv.at[g], ex_send.at[1], ex_recv.at[1], ex_local.at[1])
    kv_ex.begin()
    q_ex.begin()
    for job in jobs[:3]:
        job.first()
    for job in jobs[:3]:
        job.second()
    for job in jobs[:3]:
        job.third()
    kv_ex.end()
    q_ex.end()
    for m in range(2):
        rows = slice(128 * m, 128 * m + 128)
        for h in range(8):
            dqkv[rows, 128 * h:128 * h + 128] = dkv_recv[8 * m + h].reshape(128, 128)
        for t in range(4):
            first, second = weave(
                dq_recv[8 * m + 2 * t].reshape(64, 128), dq_recv[8 * m + 2 * t + 1].reshape(64, 128)
            )
            dqkv[128 * m:128 * m + 64, 1024 + 128 * t:1152 + 128 * t] = first
            dqkv[128 * m + 64:128 * m + 128, 1024 + 128 * t:1152 + 128 * t] = second
    for t in range(3):
        cols = slice(512 * t, 512 * t + 512)
        pa[:, :, cols] = dot_0(x[...], dqkv[:, cols]).astype(bf16).reshape(n, 16, 512)
    jobs[3].begin()
    gx[...] = dz1[...] + dot_t(dqkv[...], wa[...].reshape(512, 1536))
    stores = copies([(gx, outs[0])], out_sem)
    total = jobs[0].total()
    go[...] = total[:, 0:512]
    gu[...] = total[:, 512:2560]
    gd[...] = jobs[1].total()
    gs[...] = jobs[2].total()
    stores += copies(zip((go, gu, gd, gs), outs[4:8]), out_sem.at[pl.ds(1, 4)])
    jobs[3].first()
    jobs[3].second()
    jobs[3].third()
    total = jobs[3].total()
    gq[...] = total[:, 1024:1536]
    for t in range(4):
        first, second = weave(total[:, 256 * t:256 * t + 128], total[:, 256 * t + 128:256 * t + 256])
        gk[:, 128 * t:128 * t + 128] = first
        gv[:, 128 * t:128 * t + 128] = second
    stores += copies(zip((gq, gk, gv), outs[1:4]), out_sem.at[pl.ds(5, 3)])
    for job in jobs:
        job.sent()
    wait_all(stores)


def finish(n, nb, dq, dkv, x, dz1, x1, dur, hid, dfr, omix, dar, gvec, wa):
    dma = pltpu.SemaphoreType.DMA
    nz = nb // 2
    rows = x.shape[0]

    def buffers(depth, width, kind):
        return [
            pltpu.VMEM((n, depth, width), kind),
            pltpu.VMEM((4, nz, depth, width), kind),
            pltpu.VMEM((2, nz, depth, width // 2), kind),
            pltpu.VMEM((2, nz, depth, width), kind),
            pltpu.VMEM((nz, depth, width), kind),
        ]

    args = (dq, dkv, x, dz1, x1, dur, hid, dfr, omix, dar, gvec, wa)
    shapes = ((rows, 512), (16, 512), (16, 512), (16, 512), (16, 512), (16, 2048), (64, 512), (16, 128))
    return pl.pallas_call(
        functools.partial(finish_kernel, n, nb),
        out_shape=[jax.ShapeDtypeStruct(shape, f32) for shape in shapes],
        in_specs=any_specs(12),
        out_specs=any_specs(8),
        scratch_shapes=[
            *[pltpu.VMEM(arg.shape, arg.dtype) for arg in args],
            *buffers(16, 1536, bf16),
            *buffers(16, 2560, bf16),
            *buffers(64, 512, bf16),
            *buffers(16, 128, f32)[1:2],
            pltpu.VMEM((2, nz, 8, 128), f32),
            *buffers(16, 128, f32)[3:],
            pltpu.VMEM((8, 16, 16, 128), f32),
            pltpu.VMEM((16, 8, 16, 128), bf16),
            pltpu.VMEM((16, 8, 16, 128), bf16),
            pltpu.VMEM((16, 4, 16, 128), bf16),
            pltpu.VMEM((rows, 1536), bf16),
            *[pltpu.VMEM(shape, f32) for shape in shapes],
            dma((12,)),
            dma((8,)),
            dma((4, 9 * nz)),
            dma((4, 9 * nz)),
            dma((2, 16)),
            dma((2, 16)),
            dma((2,)),
            dma,
            dma,
        ],
        compiler_params=pltpu.CompilerParams(
            collective_id=3, has_side_effects=True, vmem_limit_bytes=VMEM_BYTES
        ),
        name="finish",
    )(*args)


def deliver_kernel(count, *refs):
    ins, outs = refs[:count], refs[count:2 * count + 7]
    stage, lines, (in_sem, sems) = refs[2 * count + 7:3 * count + 7], refs[3 * count + 7:3 * count + 15], refs[-2:]
    loads = copies(zip(ins, stage), in_sem)
    jobs = []
    for k in range(count - 1):
        loads[k].wait()
        jobs += copies([(stage[k], outs[k])], sems.at[pl.ds(k, 1)])
    loads[-1].wait()
    vec = stage[-1]
    lines[0][...] = vec[0:1, 0:64].reshape(64)
    for k in range(1, 8):
        lines[k][...] = vec[k:k + 1, 0:16].reshape(16)
    jobs += copies(zip(lines, outs[count - 1:]), sems.at[pl.ds(count - 1, 8)])
    wait_all(jobs)


def deliver(arrays, vec):
    count = len(arrays) + 1
    lines = [(64,)] + [(16,)] * 7
    return pl.pallas_call(
        functools.partial(deliver_kernel, count),
        out_shape=[jax.ShapeDtypeStruct(a.shape, a.dtype) for a in arrays]
        + [jax.ShapeDtypeStruct(shape, f32) for shape in lines],
        in_specs=any_specs(count),
        out_specs=any_specs(count + 7),
        scratch_shapes=[
            *[pltpu.VMEM(a.shape, a.dtype) for a in (*arrays, vec)],
            *[pltpu.VMEM(shape, f32) for shape in lines],
            pltpu.SemaphoreType.DMA((count,)),
            pltpu.SemaphoreType.DMA((count + 7,)),
        ],
        compiler_params=pltpu.CompilerParams(vmem_limit_bytes=VMEM_BYTES),
        name="deliver",
    )(*arrays, vec)


def by_pairs(
    stream, accumulator, upstream, segment_ids, w_query, w_key, w_value, w_out, w_up, b_up, w_down, b_down,
    gain_attn, bias_attn, gain_ffn, bias_ffn, gain_final, bias_final,
):
    nb = lax.axis_size("blk")
    n = 4 * nb
    x = stream.reshape(256, 512)
    y = accumulator.reshape(256, 512)
    g = upstream.reshape(256, 512)
    smalls = (b_up, b_down, gain_attn, bias_attn, gain_ffn, bias_ffn, gain_final, bias_final)
    q, kv, wa, wb, wd, par, bup, seg_k, seg_q = project(
        n, nb, x, w_query, w_key, w_value, w_out, w_up, w_down, segment_ids.reshape(2, 128), smalls
    )
    o, of, lse, kv2, kvt = attn_fwd(q.reshape(4, 256, 128), kv.reshape(4096, 128), seg_q, seg_k)
    do, out, dacc, dz1, x1, dur, hid, dfr, omix, dar, gvec = middle(
        n, nb, o.reshape(4, 16, 16, 128), x, y, g, wb, wd, par, bup
    )
    dq, dkv, out, dacc = attn_bwd(
        q.reshape(4, 256, 128), do.reshape(4, 256, 128), of, lse, kv2, kvt, seg_q, seg_k, out, dacc
    )
    gx, gq, gk, gv, go, gu, gd, gs = finish(
        n, nb, dq.reshape(4, 16, 16, 128), dkv.reshape(8, 16, 2, 16, 128), x, dz1, x1, dur, hid, dfr, omix, dar, gvec, wa
    )
    gx, gq, gk, gv, go, gu, gd, gbu, *small_grads = deliver((gx, gq, gk, gv, go, gu, gd), gs)
    return (
        out.reshape(stream.shape), gx.reshape(stream.shape), dacc.reshape(stream.shape),
        gq, gk, gv, go, gu, gbu, gd, *small_grads,
    )


def pairs_fit(mesh, shape):
    return mesh.shape["head"] == 4 and mesh.shape["blk"] == 8 and shape == (2, 32, 128, 512)


def solution(mesh):
    def step(*args):
        return run(by_pairs if pairs_fit(mesh, args[0].shape) else local, mesh)(*args)

    return step


def run(body, mesh):
    return jax.shard_map(
        body,
        mesh=mesh,
        in_specs=(
            P(None, ("head", "blk"), None, None),
            P(None, ("head", "blk"), None, None),
            P(None, ("head", "blk"), None, None),
            P(None, ("head", "blk"), None),
            P(("head", "blk"), None),
            P(("head", "blk"), None),
            P(("head", "blk"), None),
            P(("head", "blk"), None),
            P(("head", "blk"), None),
            P(("head", "blk")),
            P(("head", "blk"), None),
            P(("head", "blk")),
            P(("head", "blk")),
            P(("head", "blk")),
            P(("head", "blk")),
            P(("head", "blk")),
            P(("head", "blk")),
            P(("head", "blk")),
        ),
        out_specs=(
            P(None, ("head", "blk"), None, None),
            P(None, ("head", "blk"), None, None),
            P(None, ("head", "blk"), None, None),
            P(("head", "blk"), None),
            P(("head", "blk"), None),
            P(("head", "blk"), None),
            P(("head", "blk"), None),
            P(("head", "blk"), None),
            P(("head", "blk")),
            P(("head", "blk"), None),
            P(("head", "blk")),
            P(("head", "blk")),
            P(("head", "blk")),
            P(("head", "blk")),
            P(("head", "blk")),
            P(("head", "blk")),
            P(("head", "blk")),
        ),
        check_vma=False,
    )
```

```python
import functools
import math

import jax
import jax.numpy as jnp
from jax import lax
from jax.experimental import pallas as pl
from jax.experimental.pallas import tpu as pltpu
from jax.sharding import PartitionSpec as P

DH = 64
f32, bf16 = jnp.float32, jnp.bfloat16
MESH = pl.DeviceIdType.MESH
FAR = -1e30
VMEM_BYTES = 60 << 20


EPSILON = 1e-05


def norm_forward(inputs, norm_gain, norm_bias):
    average = jnp.mean(inputs, axis=-1, keepdims=True)
    centered = inputs - average
    inv_std = lax.rsqrt(jnp.mean(centered * centered, axis=-1, keepdims=True) + EPSILON)
    normed = centered * inv_std
    return (normed * norm_gain + norm_bias, normed, inv_std)


def norm_backward(gradient, normed, inv_std, norm_gain):
    scaled = gradient * norm_gain
    projected = (
        scaled
        - jnp.mean(scaled, axis=-1, keepdims=True)
        - normed * jnp.mean(scaled * normed, axis=-1, keepdims=True)
    )
    return (inv_std * projected, jnp.sum(gradient * normed, axis=0), jnp.sum(gradient, axis=0))


def smooth_gate(pre_act):
    return jax.nn.gelu(pre_act, approximate=False)


def split_rows(length):
    block_len = math.gcd(length, 512)
    return (length // block_len, block_len)


def block_scores(queries, query_seg, key_rows, key_seg, scaling):
    scores = (
        jnp.einsum("sgd,kgd->sgk", queries, key_rows, preferred_element_type=jnp.float32) * scaling
    )
    allowed = query_seg[:, None, None] == key_seg[None, None, :]
    return (scores, allowed)


def block_grads(
    queries, query_seg, grad_rows, log_total, row_delta, key_rows, value_rows, key_seg, scaling
):
    scores, allowed = block_scores(queries, query_seg, key_rows, key_seg, scaling)
    attn_prob = jnp.where(allowed, jnp.exp(scores - log_total[:, :, None]), 0.0)
    prob_grad = jnp.einsum(
        "sgd,kgd->sgk", grad_rows, value_rows, preferred_element_type=jnp.float32
    )
    score_grad = (attn_prob * (prob_grad - row_delta[:, :, None]) * scaling).astype(jnp.bfloat16)
    return (attn_prob.astype(jnp.bfloat16), score_grad)


def key_blocks(key_rows, value_rows, key_seg, groups):
    block_num, block_len = split_rows(key_rows.shape[0])
    return (
        key_rows.reshape(block_num, block_len, groups, -1),
        value_rows.reshape(block_num, block_len, groups, -1),
        key_seg.reshape(block_num, block_len),
    )


def attend_fold(queries, query_seg, scaling, carried, portion):
    key_rows, value_rows, key_seg = portion

    def step(running, blocks):
        key_part, value_part, seg_part = blocks
        old_max, old_total, weighted = running
        scores, allowed = block_scores(queries, query_seg, key_part, seg_part, scaling)
        row_max = jnp.maximum(old_max, jnp.max(jnp.where(allowed, scores, -1e30), axis=2))
        exp_scores = jnp.where(allowed, jnp.exp(scores - row_max[:, :, None]), 0.0)
        rescale = jnp.exp(old_max - row_max)
        new_total = old_total * rescale + jnp.sum(exp_scores, axis=2)
        weighted = weighted * rescale[:, :, None] + jnp.einsum(
            "sgk,kgd->sgd",
            exp_scores.astype(jnp.bfloat16),
            value_part,
            preferred_element_type=jnp.float32,
        )
        return ((row_max, new_total, weighted), None)

    running, unused = lax.scan(
        step, carried, key_blocks(key_rows, value_rows, key_seg, queries.shape[1])
    )
    return running


def local(
    stream,
    accumulator,
    upstream,
    segment_ids,
    w_query,
    w_key,
    w_value,
    w_out,
    w_up,
    b_up,
    w_down,
    b_down,
    gain_attn,
    bias_attn,
    gain_ffn,
    bias_ffn,
    gain_final,
    bias_final,
):
    heads_axis = lax.axis_size("head")
    micro = stream.shape[0]
    tokens = stream.shape[2]
    width = stream.shape[3]
    group_width = width // heads_axis
    groups = group_width // DH
    scaling = DH ** (-0.5)
    f32 = jnp.float32
    bf16 = jnp.bfloat16
    out_list = []
    stream_grads = []
    accum_grads = []
    grad_totals = None
    for micro_step in range(micro):
        (
            q_weight,
            k_weight,
            v_weight,
            o_weight,
            up_weight,
            up_bias,
            down_weight,
            down_bias,
            gain_one,
            shift_one,
            gain_two,
            shift_two,
            gain_three,
            shift_three,
        ) = (
            lax.all_gather(w_query, ("head", "blk"), axis=0, tiled=True),
            lax.all_gather(w_key, ("head", "blk"), axis=0, tiled=True),
            lax.all_gather(w_value, ("head", "blk"), axis=0, tiled=True),
            lax.all_gather(w_out, ("head", "blk"), axis=0, tiled=True),
            lax.all_gather(w_up, ("head", "blk"), axis=0, tiled=True),
            lax.all_gather(b_up, ("head", "blk"), axis=0, tiled=True),
            lax.all_gather(w_down, ("head", "blk"), axis=0, tiled=True),
            lax.all_gather(b_down, ("head", "blk"), axis=0, tiled=True),
            lax.all_gather(gain_attn, ("head", "blk"), axis=0, tiled=True),
            lax.all_gather(bias_attn, ("head", "blk"), axis=0, tiled=True),
            lax.all_gather(gain_ffn, ("head", "blk"), axis=0, tiled=True),
            lax.all_gather(bias_ffn, ("head", "blk"), axis=0, tiled=True),
            lax.all_gather(gain_final, ("head", "blk"), axis=0, tiled=True),
            lax.all_gather(bias_final, ("head", "blk"), axis=0, tiled=True),
        )
        inputs = stream[micro_step, 0]
        input_wide = inputs.astype(f32)
        carried = accumulator[micro_step, 0].astype(f32)
        segs = segment_ids[micro_step, 0]
        projections = jnp.stack(
            [
                jnp.dot(inputs, q_weight, preferred_element_type=f32),
                jnp.dot(inputs, k_weight, preferred_element_type=f32),
                jnp.dot(inputs, v_weight, preferred_element_type=f32),
            ]
        ).astype(bf16)
        projections = projections.reshape(3, tokens, heads_axis, group_width)
        seg_wide = jnp.broadcast_to(segs[None, :, None, None], (1, tokens, heads_axis, 1))
        regrouped, seg_group = (
            lax.all_to_all(projections, "head", split_axis=2, concat_axis=1, tiled=True),
            lax.all_to_all(seg_wide, "head", split_axis=2, concat_axis=1, tiled=True),
        )
        rows = regrouped.shape[1]
        query_loc = regrouped[0, :, 0]
        key_loc = regrouped[1, :, 0]
        value_loc = regrouped[2, :, 0]
        seg_loc = seg_group[0, :, 0, 0]
        queries3 = query_loc.reshape(rows, groups, DH)
        start_state = (
            jnp.full((rows, groups), -1e30, f32),
            jnp.zeros((rows, groups), f32),
            jnp.zeros((rows, groups, DH), f32),
        )
        row_max, row_total, weighted = attend_fold(
            queries3,
            seg_loc,
            scaling,
            start_state,
            (
                lax.all_gather(key_loc, "blk", axis=0, tiled=True),
                lax.all_gather(value_loc, "blk", axis=0, tiled=True),
                lax.all_gather(seg_loc, "blk", axis=0, tiled=True),
            ),
        )
        attn_out = weighted / row_total[:, :, None]
        log_total = row_max + jnp.log(row_total)
        attn_send = attn_out.astype(bf16).reshape(rows, 1, group_width)
        mixed = lax.all_to_all(attn_send, "head", split_axis=0, concat_axis=1, tiled=True).reshape(
            tokens, width
        )
        branch = jnp.dot(mixed, o_weight, preferred_element_type=f32)
        first, normed_one, inv_one = norm_forward(
            input_wide + branch, gain_one.astype(f32), shift_one.astype(f32)
        )
        first_low = first.astype(bf16)
        hidden_pre = jnp.dot(first_low, up_weight, preferred_element_type=f32) + up_bias.astype(f32)
        hidden_act, gate_pull = jax.vjp(smooth_gate, hidden_pre)
        hidden = hidden_act.astype(bf16)
        feed = jnp.dot(hidden, down_weight, preferred_element_type=f32) + down_bias.astype(f32)
        second, normed_two, inv_two = norm_forward(
            first + feed, gain_two.astype(f32), shift_two.astype(f32)
        )
        final, normed_three, inv_three = norm_forward(
            carried + branch + feed, gain_three.astype(f32), shift_three.astype(f32)
        )
        out_list.append((second + final).astype(bf16))
        cotangent = upstream[micro_step, 0].astype(f32)
        accum_grad, gain3_grad, shift3_grad = norm_backward(
            cotangent, normed_three, inv_three, gain_three.astype(f32)
        )
        second_grad, gain2_grad, shift2_grad = norm_backward(
            cotangent, normed_two, inv_two, gain_two.astype(f32)
        )
        feed_grad = second_grad + accum_grad
        feed_low = feed_grad.astype(bf16)
        down_grad = jnp.dot(hidden.T, feed_low, preferred_element_type=f32)
        (hidden_grad,) = gate_pull(jnp.dot(feed_low, down_weight.T, preferred_element_type=f32))
        hidden_low = hidden_grad.astype(bf16)
        up_grad = jnp.dot(first_low.T, hidden_low, preferred_element_type=f32)
        first_grad = second_grad + jnp.dot(hidden_low, up_weight.T, preferred_element_type=f32)
        resid_grad, gain1_grad, shift1_grad = norm_backward(
            first_grad, normed_one, inv_one, gain_one.astype(f32)
        )
        branch_low = (resid_grad + accum_grad).astype(bf16)
        out_wgrad = jnp.dot(mixed.T, branch_low, preferred_element_type=f32)
        mixed_grad = jnp.dot(branch_low, o_weight.T, preferred_element_type=f32).astype(bf16)
        mixed_grad = mixed_grad.reshape(tokens, heads_axis, group_width)
        grad_group = lax.all_to_all(mixed_grad, "head", split_axis=1, concat_axis=0, tiled=True)
        grad_loc = grad_group[:, 0]
        grad3 = grad_loc.reshape(rows, groups, DH)
        row_delta = jnp.sum(grad3.astype(f32) * attn_out, axis=2)
        whole_keys, whole_values, whole_seg = (
            lax.all_gather(key_loc, "blk", axis=0, tiled=True),
            lax.all_gather(value_loc, "blk", axis=0, tiled=True),
            lax.all_gather(seg_loc, "blk", axis=0, tiled=True),
        )

        def backward_step(running, blocks):
            key_part, value_part, seg_part = blocks
            attn_prob, score_grad = block_grads(
                queries3,
                seg_loc,
                grad3,
                log_total,
                row_delta,
                key_part,
                value_part,
                seg_part,
                scaling,
            )
            running = running + jnp.einsum(
                "sgk,kgd->sgd", score_grad, key_part, preferred_element_type=f32
            )
            key_term = jnp.einsum("sgk,sgd->kgd", score_grad, queries3, preferred_element_type=f32)
            value_term = jnp.einsum("sgk,sgd->kgd", attn_prob, grad3, preferred_element_type=f32)
            return (running, (key_term, value_term))

        query_grad, (key_terms, value_terms) = lax.scan(
            backward_step,
            jnp.zeros((rows, groups, DH), f32),
            key_blocks(whole_keys, whole_values, whole_seg, groups),
        )
        key_grad, value_grad = (
            lax.psum_scatter(
                key_terms.reshape(-1, group_width), "blk", scatter_dimension=0, tiled=True
            ),
            lax.psum_scatter(
                value_terms.reshape(-1, group_width), "blk", scatter_dimension=0, tiled=True
            ),
        )
        grad_stack = jnp.stack(
            [query_grad.reshape(rows, group_width), key_grad, value_grad]
        ).astype(bf16)
        grad_stack = grad_stack.reshape(3, rows, 1, group_width)
        returned = lax.all_to_all(
            grad_stack, "head", split_axis=1, concat_axis=2, tiled=True
        ).reshape(3, tokens, width)
        query_wgrad = jnp.dot(inputs.T, returned[0], preferred_element_type=f32)
        key_wgrad = jnp.dot(inputs.T, returned[1], preferred_element_type=f32)
        value_wgrad = jnp.dot(inputs.T, returned[2], preferred_element_type=f32)
        input_grad = (
            resid_grad
            + jnp.dot(returned[0], q_weight.T, preferred_element_type=f32)
            + jnp.dot(returned[1], k_weight.T, preferred_element_type=f32)
            + jnp.dot(returned[2], v_weight.T, preferred_element_type=f32)
        )
        stream_grads.append(input_grad)
        accum_grads.append(accum_grad)
        step_grads = (
            query_wgrad,
            key_wgrad,
            value_wgrad,
            out_wgrad,
            up_grad,
            jnp.sum(hidden_grad, axis=0),
            down_grad,
            jnp.sum(feed_grad, axis=0),
            gain1_grad,
            shift1_grad,
            gain2_grad,
            shift2_grad,
            gain3_grad,
            shift3_grad,
        )
        if grad_totals is None:
            grad_totals = step_grads
        else:
            grad_totals = tuple((older + newer for older, newer in zip(grad_totals, step_grads)))
    summed = lax.psum_scatter(grad_totals, ("head", "blk"), scatter_dimension=0, tiled=True)
    layer_out = jnp.stack(out_list)[:, None]
    grad_stream = jnp.stack(stream_grads)[:, None]
    grad_accum = jnp.stack(accum_grads)[:, None]
    return (
        layer_out,
        grad_stream,
        grad_accum,
        summed[0],
        summed[1],
        summed[2],
        summed[3],
        summed[4],
        summed[5],
        summed[6],
        summed[7],
        summed[8],
        summed[9],
        summed[10],
        summed[11],
        summed[12],
        summed[13],
    )


def dot_t(a, b):
    return lax.dot_general(a, b, (((1,), (1,)), ((), ())), preferred_element_type=f32)

def dot_n(a, b):
    return lax.dot_general(a, b, (((1,), (0,)), ((), ())), preferred_element_type=f32)

def dot_0(a, b):
    return lax.dot_general(a, b, (((0,), (0,)), ((), ())), preferred_element_type=f32)

def lanes(shape):
    return lax.broadcasted_iota(jnp.int32, shape, len(shape) - 1)

def query_marks(seg_row):
    wide = jnp.broadcast_to(seg_row, (128, seg_row.shape[1])).T
    return (wide == lanes(wide.shape)).astype(f32).astype(bf16)

def half_lanes(tile, half):
    wide = tile.astype(f32)
    if half:
        wide = pltpu.roll(wide, 64, 1)
    return jnp.where(lanes(wide.shape) < 64, wide, 0.0).astype(bf16)

def key_steps(bounds, low, high):
    chunks, keys = bounds.shape
    first = sum(jnp.where(bounds[t, keys - 1] < low, 1, 0) for t in range(chunks))
    last = sum(jnp.where(bounds[t, 0] <= high, 1, 0) for t in range(chunks))
    pairs = (last - first + 1) // 2
    start = jnp.minimum(first, chunks - 2 * pairs)
    return start, pairs // 2, lax.rem(pairs, 2)


def walk(step, fours, twos, carry):
    carry = lax.fori_loop(0, fours, lambda t, c: step(4, 4 * t, c), carry)
    return lax.fori_loop(0, twos, lambda t, c: step(2, 4 * fours, c), carry)


def attn_fwd_kernel(
    q_hbm, kv_hbm, seg_q_hbm, seg_k_hbm, o_hbm, of_hbm, lse_hbm, kv2_hbm, kvt_hbm,
    q_ref, kv_ref, seg_q_ref, seg_k_ref, bounds, o_ref, of_ref, lse_ref, kv2_ref, kvt_ref, vo_ref, in_sem, out_sem,
):
    loads = copies(
        [(seg_q_hbm, seg_q_ref), (seg_k_hbm, seg_k_ref), (seg_k_hbm, bounds), (kv_hbm, kv_ref), (q_hbm, q_ref)], in_sem
    )
    wait_all(loads)
    chunks, keys = seg_k_ref.shape
    log_scale = math.log2(math.e) * DH ** (-0.5)

    def prepare(t, c):
        rows = pl.ds(pl.multiple_of(t * keys, keys), keys)
        kv = kv_ref[rows, :]
        marks = jnp.where(seg_k_ref[pl.ds(t, 1), :] == rows_of((128, keys)), 0.0, FAR)
        kvt_ref[0:128, rows] = kv.T
        kvt_ref[128:256, rows] = marks.astype(bf16)
        kv2_ref[rows, 0:128] = kv
        kv2_ref[rows, 128:256] = marks.T.astype(bf16)
        vo_ref[rows, :] = jnp.where(lanes(kv.shape) < 64, 1.0, kv.astype(f32)).astype(bf16)
        return c

    lax.fori_loop(0, chunks, prepare, 0)
    stores = copies([(kv2_ref, kv2_hbm), (kvt_ref, kvt_hbm)], out_sem)

    def tile(j, c):
        q_tile = q_ref[j]
        rows = q_tile.shape[0]
        outs = []
        for half in range(2):
            i = half * (chunks // 2) + j
            left = half_lanes(q_tile, half)
            left = jnp.concatenate([left, query_marks(seg_q_ref[pl.ds(i, 1), :])], axis=1)
            low, high = bounds[i, 0], bounds[i, keys - 1]
            start, fours, twos = key_steps(bounds, low, high)

            def step(width, t, carry):
                top, acc = carry
                at = pl.ds(pl.multiple_of((start + t) * keys, keys), width * keys)
                s = dot_n(left, kvt_ref[:, at])
                new = jnp.maximum(top, jnp.max(s, axis=1, keepdims=True))
                p = jnp.exp2((s - new) * log_scale)
                acc = acc * jnp.exp2((top - new) * log_scale) + dot_n(p.astype(bf16), vo_ref[at, :])
                return new, acc

            carry = (jnp.full((rows, 1), FAR, f32), jnp.zeros((rows, 128), f32))
            top, acc = walk(step, fours, twos, carry)
            total = pltpu.roll(acc, 64, 1)
            outs.append(acc / total)
            lse = jnp.broadcast_to(top * log_scale, acc.shape) + jnp.log2(acc)
            lse_ref[pl.ds(i, 1), :] = lse.T[0:1, :]
        o = jnp.where(lanes(outs[0].shape) < 64, pltpu.roll(outs[0], 64, 1), outs[1])
        of_ref[j] = o
        o_ref[j] = o.astype(bf16)
        return c

    lax.fori_loop(0, chunks // 2, tile, 0)
    stores += copies([(o_ref, o_hbm), (of_ref, of_hbm), (lse_ref, lse_hbm)], out_sem.at[pl.ds(2, 3)])
    wait_all(stores)


def attn_fwd(q, kv, seg_q, seg_k):
    chunks, keys = seg_k.shape
    dma = pltpu.SemaphoreType.DMA
    shapes = (
        (q.shape, bf16), (q.shape, f32), (seg_q.shape, f32), ((chunks * keys, 256), bf16), ((256, chunks * keys), bf16)
    )
    return pl.pallas_call(
        attn_fwd_kernel,
        out_shape=[jax.ShapeDtypeStruct(shape, kind) for shape, kind in shapes],
        in_specs=any_specs(4),
        out_specs=any_specs(5),
        scratch_shapes=[
            *[pltpu.VMEM(a.shape, a.dtype) for a in (q, kv, seg_q, seg_k)],
            pltpu.SMEM(seg_k.shape, jnp.int32),
            *[pltpu.VMEM(shape, kind) for shape, kind in shapes],
            pltpu.VMEM((chunks * keys, 128), bf16),
            dma((5,)),
            dma((5,)),
        ],
        compiler_params=pltpu.CompilerParams(vmem_limit_bytes=VMEM_BYTES),
        cost_estimate=pl.CostEstimate(flops=10**10, bytes_accessed=10**7, transcendentals=10**7),
        name="attn_fwd",
    )(q, kv, seg_q, seg_k)


def attn_bwd_kernel(
    q_hbm, do_hbm, of_hbm, lse_hbm, kv2_hbm, kvt_hbm, seg_q_hbm, seg_k_hbm, pass1, pass2, dq_hbm, dkv_hbm, out1, out2,
    q_ref, do_ref, of_ref, lse_ref, kv2_ref, kvt_ref, seg_q_ref, bounds, dq_ref, dkv_low, dkv_ref, hold1, hold2, in_sem, out_sem,
):
    loads = copies(
        [
            (q_hbm, q_ref), (do_hbm, do_ref), (of_hbm, of_ref), (lse_hbm, lse_ref), (kv2_hbm, kv2_ref),
            (seg_q_hbm, seg_q_ref), (seg_k_hbm, bounds),
            (pass1, hold1), (pass2, hold2), (kvt_hbm, kvt_ref),
        ],
        in_sem,
    )
    dkv_ref[...] = jnp.zeros_like(dkv_ref)
    wait_all(loads)
    stores = copies([(hold1, out1), (hold2, out2)], out_sem)
    chunks, keys = bounds.shape
    log_scale = math.log2(math.e) * DH ** (-0.5)

    def tile(j, c):
        q_tile, do_tile = q_ref[j], do_ref[j]
        rows = q_tile.shape[0]
        prod = do_tile.astype(f32) * of_ref[j]
        prod = prod.T
        dqs = []
        for half in range(2):
            i = half * (chunks // 2) + j
            left = half_lanes(q_tile, half)
            grad = do_tile.astype(f32)
            if not half:
                grad = pltpu.roll(grad, 64, 1)
            grad = jnp.where(lanes(grad.shape) < 64, 0.0, grad).astype(bf16)
            delta = jnp.sum(prod[64 * half:64 * half + 64], axis=0, keepdims=True)
            lse = lse_ref[pl.ds(i, 1), :]
            both = jnp.concatenate([left, grad], axis=0)
            marks = query_marks(seg_q_ref[pl.ds(i, 1), :])
            right = jnp.concatenate([both, jnp.concatenate([marks, jnp.zeros_like(marks)], axis=0)], axis=1).T
            low, high = bounds[i, 0], bounds[i, keys - 1]
            start, fours, twos = key_steps(bounds, low, high)

            def step(width, t, dq):
                at = pl.ds(pl.multiple_of((start + t) * keys, keys), width * keys)
                sdp = dot_n(kv2_ref[at, :], right)
                p = jnp.exp2(sdp[:, :rows] * log_scale - lse)
                ds = (p * (sdp[:, rows:] - delta)).astype(bf16)
                dkv_ref[at, :] += dot_n(jnp.concatenate([ds, p.astype(bf16)], axis=1), both)
                return dq + dot_n(kvt_ref[0:128, at], ds)

            dqs.append(walk(step, fours, twos, jnp.zeros((128, rows), f32)).T)
        dq = jnp.where(lanes(dqs[0].shape) < 64, dqs[0], pltpu.roll(dqs[1], 64, 1))
        dq_ref[j] = (dq * DH ** (-0.5)).astype(bf16)
        return c

    lax.fori_loop(0, chunks // 2, tile, 0)
    dkv = dkv_ref[...]
    dkv_low[...] = jnp.where(lanes(dkv.shape) < 64, dkv * DH ** (-0.5), dkv).astype(bf16)
    stores += copies([(dq_ref, dq_hbm), (dkv_low, dkv_hbm)], out_sem.at[pl.ds(2, 2)])
    wait_all(stores)


def attn_bwd(q, do, of, lse, kv2, kvt, seg_q, seg_k, pass1, pass2):
    dma = pltpu.SemaphoreType.DMA
    shapes = ((q.shape, bf16), ((kv2.shape[0], 128), bf16))
    return pl.pallas_call(
        attn_bwd_kernel,
        out_shape=[jax.ShapeDtypeStruct(shape, kind) for shape, kind in shapes]
        + [jax.ShapeDtypeStruct(a.shape, a.dtype) for a in (pass1, pass2)],
        in_specs=any_specs(10),
        out_specs=any_specs(4),
        scratch_shapes=[
            *[pltpu.VMEM(a.shape, a.dtype) for a in (q, do, of, lse, kv2, kvt, seg_q)],
            pltpu.SMEM(seg_k.shape, jnp.int32),
            *[pltpu.VMEM(shape, kind) for shape, kind in shapes],
            pltpu.VMEM((kv2.shape[0], 128), f32),
            *[pltpu.VMEM(a.shape, a.dtype) for a in (pass1, pass2)],
            dma((10,)),
            dma((4,)),
        ],
        compiler_params=pltpu.CompilerParams(vmem_limit_bytes=VMEM_BYTES),
        name="attn_bwd",
    )(q, do, of, lse, kv2, kvt, seg_q, seg_k, pass1, pass2)


class Spot:
    def __init__(self, nb):
        self.nb, self.nz = nb, nb // 2
        self.h, b = lax.axis_index("head"), lax.axis_index("blk")
        self.z, self.c = b // 2, lax.rem(b, 2)
        self.near = (self.h + 1 - 2 * lax.rem(self.h, 2), lax.rem(self.h + 2, 4))
        self.diag = 3 - self.h
        self.me = self.h * nb + b

    def index(self, h, z, c):
        return h * self.nb + z * 2 + c

    def ahead(self, k):
        return lax.rem(self.z + k, self.nz)


def remote(src, dst, send, recv, h, b):
    return pltpu.make_async_remote_copy(
        src_ref=src,
        dst_ref=dst,
        send_sem=send,
        recv_sem=recv,
        device_id={"head": h, "blk": b},
        device_id_type=MESH,
    )


def each(count, body, start=0):
    def run(i, c):
        body(i)
        return c

    lax.fori_loop(start, count, run, 0)


def greet_all(n, nb, me):
    barrier = pltpu.get_barrier_semaphore()

    def signal(i):
        t = lax.rem(me + i, n)
        pl.semaphore_signal(
            barrier, inc=1, device_id={"head": t // nb, "blk": lax.rem(t, nb)}, device_id_type=MESH
        )

    each(n, signal, 1)
    pl.semaphore_wait(barrier, n - 1)


def halves(shape):
    rows, width = shape
    if width > 128:
        return [(slice(None), slice(w * width // 2, (w + 1) * width // 2)) for w in range(2)]
    return [(slice(w * rows // 2, (w + 1) * rows // 2), slice(None)) for w in range(2)]


class Gather:
    def __init__(self, spot, shard, full, send, recv, local):
        self.s, self.full, self.local = spot, full, local
        self.shard = shard if callable(shard) else lambda z: shard
        self.send, self.recv = send, recv
        self.cut = halves(full.shape[1:])

    def copy(self, src, dst, k, h, z, c, recv_k=None):
        recv_k = k if recv_k is None else recv_k
        return remote(src, dst, self.send.at[k], self.recv.at[recv_k], h, z * 2 + c)

    def to_z(self, z):
        s = self.s
        return self.copy(self.shard(z), self.full.at[s.me], z, s.h, z, s.c, s.z)

    def from_z(self, z):
        s = self.s
        slot = self.full.at[s.index(s.h, z, s.c)]
        return self.copy(slot, slot, z, s.h, z, s.c)

    def near(self, w, z, own=False):
        s = self.s
        slot = self.full.at[s.index(s.h, z, s.c)]
        return self.copy(self.shard(s.z) if own else slot, slot, (1 + w) * s.nz + z, s.near[w], s.z, s.c)

    def from_near(self, w, z):
        s = self.s
        slot = self.full.at[s.index(s.near[w], z, s.c)]
        return self.copy(slot, slot, (1 + w) * s.nz + z, s.near[w], s.z, s.c)

    def lanes(self, slot, w):
        return slot.at[self.cut[w]]

    def onward(self, w, z):
        s = self.s
        slot = self.lanes(self.full.at[s.index(s.near[w], z, s.c)], w)
        return self.copy(slot, slot, (3 + w) * s.nz + z, s.near[1 - w], s.z, s.c)

    def from_onward(self, w, z):
        s = self.s
        slot = self.lanes(self.full.at[s.index(s.diag, z, s.c)], w)
        return self.copy(slot, slot, (3 + w) * s.nz + z, s.near[1 - w], s.z, s.c)

    def twin(self, h, z, own=False):
        s = self.s
        slot = self.full.at[s.index(h, z, s.c)]
        return self.copy(self.shard(s.z) if own else slot, slot, 5 * s.nz + h * s.nz + z, s.h, s.z, 1 - s.c)

    def from_twin(self, h, z):
        s = self.s
        slot = self.full.at[s.index(h, z, 1 - s.c)]
        return self.copy(slot, slot, 5 * s.nz + h * s.nz + z, s.h, s.z, 1 - s.c)

    def begin(self):
        s = self.s
        each(s.nz, lambda k: self.to_z(s.ahead(k)).start(), 1)

    def begin_near(self):
        s = self.s
        self.own = pltpu.make_async_copy(self.shard(s.z), self.full.at[s.me], self.local)
        self.own.start()
        self.near(0, s.z, True).start()
        self.near(1, s.z, True).start()
        self.twin(s.h, s.z, True).start()

    def spread(self):
        s = self.s

        def go(k):
            z = s.ahead(k)
            self.from_z(z).wait_recv()
            self.near(0, z).start()
            self.near(1, z).start()
            self.twin(s.h, z).start()

        each(s.nz, go, 1)

    def cross(self):
        s = self.s

        def go(k):
            z = s.ahead(k)
            for w in range(2):
                self.from_near(w, z).wait_recv()
                self.onward(w, z).start()
                self.twin(s.near[w], z).start()

        each(s.nz, go)

    def last(self):
        s = self.s

        def go(k):
            z = s.ahead(k)
            for w in range(2):
                self.from_onward(w, z).wait_recv()
            self.twin(s.diag, z).start()

        each(s.nz, go)

    def arrive(self):
        s = self.s
        each(4, lambda h: each(s.nz, lambda z: self.from_twin(h, z).wait_recv()))
        self.own.wait()

    def sent(self):
        s = self.s
        each(s.nz, lambda k: self.to_z(s.ahead(k)).wait_send(), 1)

        def go(z):
            for w in range(2):
                self.near(w, z).wait_send()
                self.onward(w, z).wait_send()
            each(4, lambda h: self.twin(h, z).wait_send())

        each(s.nz, go)


class Scatter:
    def __init__(self, spot, part, twin, diag, near, line, send, recv):
        self.s, self.part, self.t, self.d, self.n, self.l = spot, part, twin, diag, near, line
        self.send, self.recv = send, recv
        self.cut = halves(part.shape[1:])
        self.axis = 1 if self.cut[0][0] == slice(None) else 0

    def copy(self, src, dst, k, h, z, c, recv_k=None):
        recv_k = k if recv_k is None else recv_k
        return remote(src, dst, self.send.at[k], self.recv.at[recv_k], h, z * 2 + c)

    def mine(self, h, z):
        return self.s.index(h, z, self.s.c)

    def to_twin(self, h, z):
        s = self.s
        src = self.part.at[s.index(h, z, 1 - s.c)]
        return self.copy(src, self.t.at[h, z], h * s.nz + z, s.h, s.z, 1 - s.c)

    def to_diag(self, w, z):
        s = self.s
        src = self.part.at[self.mine(s.diag, z)].at[self.cut[w]]
        return self.copy(src, self.d.at[w, z], (4 + w) * s.nz + z, s.near[w], s.z, s.c)

    def to_near(self, w, z):
        s = self.s
        src = self.part.at[self.mine(s.near[w], z)]
        return self.copy(src, self.n.at[w, z], (6 + w) * s.nz + z, s.near[w], s.z, s.c)

    def to_line(self, z):
        s = self.s
        src = self.part.at[self.mine(s.h, z)]
        return self.copy(src, self.l.at[s.z], 8 * s.nz + z, s.h, z, s.c, 8 * s.nz + s.z)

    def from_line(self, z):
        s = self.s
        src = self.part.at[self.mine(s.h, z)]
        return self.copy(src, self.l.at[z], 8 * s.nz + z, s.h, z, s.c)

    def begin(self):
        each(4, lambda h: each(self.s.nz, lambda z: self.to_twin(h, z).start()))

    def pair(self, h, z):
        self.to_twin(h, z).wait_recv()
        return self.part[self.mine(h, z)].astype(f32) + self.t[h, z].astype(f32)

    def keep(self, h, z, value):
        self.part[self.mine(h, z)] = value.astype(self.part.dtype)

    def first(self):
        s = self.s

        def go(k):
            z = s.ahead(k)
            self.keep(s.diag, z, self.pair(s.diag, z))
            for w in range(2):
                self.to_diag(w, z).start()

        each(s.nz + 1, go, 1)

    def second(self):
        s = self.s

        def go(k):
            z = s.ahead(k)
            for w in range(2):
                value = self.pair(s.near[w], z)
                self.to_diag(1 - w, z).wait_recv()
                other = self.d[1 - w, z].astype(f32)
                pieces = [value[cut] for cut in self.cut]
                pieces[1 - w] = pieces[1 - w] + other
                value = jnp.concatenate(pieces, axis=self.axis)
                self.keep(s.near[w], z, value)
                self.to_near(w, z).start()

        each(s.nz + 1, go, 1)

    def joined(self, z):
        value = self.pair(self.s.h, z)
        for w in range(2):
            self.to_near(w, z).wait_recv()
            value = value + self.n[w, z].astype(f32)
        return value

    def third(self):
        s = self.s

        def go(k):
            z = s.ahead(k)
            self.keep(s.h, z, self.joined(z))
            self.to_line(z).start()

        each(s.nz, go, 1)

    def columns(self):
        s = self.s
        self.l[s.z] = self.joined(s.z).astype(self.l.dtype)
        each(s.nz, lambda k: self.from_line(s.ahead(k)).wait_recv(), 1)
        return [self.l[w].astype(f32) + self.l[w + 2].astype(f32) for w in range(2)]

    def total(self):
        s = self.s
        value = self.joined(s.z)

        def go(k, value):
            z = s.ahead(k)
            self.from_line(z).wait_recv()
            return value + self.l[z].astype(f32)

        return lax.fori_loop(1, s.nz, go, value)

    def sent(self):
        s = self.s

        def go(z):
            each(4, lambda h: self.to_twin(h, z).wait_send())
            for w in range(2):
                self.to_diag(w, z).wait_send()
                self.to_near(w, z).wait_send()

        each(s.nz, go)
        each(s.nz, lambda k: self.to_line(s.ahead(k)).wait_send(), 1)


class Exchange:
    def __init__(self, spot, src, dst, send, recv, local):
        self.s, self.src, self.dst, self.send, self.recv, self.local = spot, src, dst, send, recv, local
        self.g = spot.me // 2

    def copy(self, i, back=False):
        s = self.s
        to = lax.rem(self.g + i, 16)
        t = to * 2 + s.c
        src = self.src(to)
        dst = self.dst(lax.rem(self.g + 16 - i, 16)) if back else self.dst(self.g)
        return remote(src, dst, self.send.at[i], self.recv.at[i], t // s.nb, lax.rem(t, s.nb))

    def own(self):
        return pltpu.make_async_copy(self.src(self.g), self.dst(self.g), self.local)

    def begin(self):
        self.own().start()
        each(16, lambda i: self.copy(i).start(), 1)

    def arrive(self, i):
        self.copy(i, True).wait_recv()

    def end(self):
        each(16, self.arrive, 1)
        self.sent()

    def sent(self):
        self.own().wait()
        each(16, lambda i: self.copy(i).wait_send(), 1)


class Plane:
    def __init__(self, spot, send, recv):
        self.s, self.send, self.recv = spot, send, recv

    def to(self, k):
        return lax.rem(self.s.h + k, 4)

    def frm(self, k):
        return lax.rem(self.s.h + 4 - k, 4)

    def copy(self, src, dst, j, at_send, at_recv):
        s = self.s
        return remote(src, dst, self.send.at[at_send], self.recv.at[at_recv], j, s.z * 2 + s.c)


def pair_of(g):
    return lax.rem(g, 4) * 4 + g // 4


def weave(left, right):
    kind = left.dtype
    left, right = left.astype(f32), right.astype(f32)
    low = lanes(left.shape) < 64
    first = jnp.where(low, left, pltpu.roll(right, 64, 1)).astype(kind)
    second = jnp.where(low, pltpu.roll(left, 64, 1), right).astype(kind)
    return first, second


def any_specs(count):
    return [pl.BlockSpec(memory_space=pl.ANY)] * count


def copies(pairs, sems):
    jobs = [pltpu.make_async_copy(src, dst, sems.at[k]) for k, (src, dst) in enumerate(pairs)]
    for job in jobs:
        job.start()
    return jobs


def wait_all(jobs):
    for job in jobs:
        job.wait()


def rows_of(shape):
    return lax.broadcasted_iota(jnp.int32, shape, 0)


def spread_row(block, width, each_lane):
    count = block.shape[0]
    pick = (rows_of((128, width)) == lax.rem(lanes((128, width)), each_lane)).astype(f32).astype(bf16)
    wide = dot_n(block.astype(bf16), pick)
    return column_sum(jnp.where(rows_of((count, width)) == lanes((count, width)) // each_lane, wide, 0.0))


def gather_row(row, count, each_lane):
    width = row.shape[1]
    wide = jnp.where(rows_of((count, width)) == lanes((count, width)) // each_lane, row, 0.0)
    pick = (lanes((width, 128)) == lax.rem(rows_of((width, 128)), each_lane)).astype(f32)
    return lax.dot_general(
        wide, pick, (((1,), (0,)), ((), ())), precision=lax.Precision.HIGHEST, preferred_element_type=f32
    )


class Line:
    def __init__(self, spot, shard, full, send, recv, local):
        self.s, self.shard, self.full, self.send, self.recv = spot, shard, full, send, recv
        self.own = pltpu.make_async_copy(shard, full.at[spot.z], local)

    def copy(self, way, t):
        s = self.s
        k = 2 * t + (way + 1) // 2
        src = self.full.at[s.z - way * t] if t else self.shard
        dst = self.full.at[s.z - way * t]
        return remote(src, dst, self.send.at[k], self.recv.at[k], s.h, (s.z + way) * 2 + s.c)

    def inside(self, z):
        return (z >= 0) & (z < self.s.nz)

    def sends(self, t, act):
        for way in (1, -1):
            z = self.s.z

            @pl.when(self.inside(z + way) & self.inside(z - way * t))
            def _():
                act(self.copy(way, t))

    def arrive(self, t):
        for way in (1, -1):
            s = self.s

            @pl.when(self.inside(s.z - way * (t + 1)))
            def _():
                slot = self.full.at[s.z - way * (t + 1)]
                k = 2 * t + (way + 1) // 2
                remote(slot, slot, self.send.at[k], self.recv.at[k], s.h, (s.z - way) * 2 + s.c).wait_recv()

    def begin(self):
        self.own.start()
        self.sends(0, lambda copy: copy.start())

    def onward(self, t):
        self.arrive(t)
        if t + 1 < self.s.nz - 1:
            self.sends(t + 1, lambda copy: copy.start())

    def sent(self):
        self.own.wait()
        for t in range(self.s.nz - 1):
            self.sends(t, lambda copy: copy.wait_send())


def project_kernel(n, nb, *refs):
    x_hbm, wq_hbm, wk_hbm, wv_hbm, wo_hbm, wu_hbm, wd_hbm, seg_hbm = refs[:8]
    smalls = refs[8:16]
    q_out, kv_out, x_out, wa_out, fz_out, par_out, bup_out, segk_out, segq_out = refs[16:25]
    (
        x, wq, wk, wv, wo, wu, wd, seg, *small, bup_small, vec, sa, sb, wa, x_all, kv_send, q_send,
        par, bup, segk, segq,
        in_sem, out_sem, w_send, w_recv, w_local, f_send, f_recv, f_local,
        x_send, x_recv, x_local, ex_send, ex_recv, ex_local, tw_send, tw_recv,
    ) = refs[25:]
    s = Spot(nb)
    loads = copies(
        [(wq_hbm, wq), (wk_hbm, wk), (wv_hbm, wv), (seg_hbm, seg), (smalls[0], bup_small)]
        + [(smalls[k], small[k - 1]) for k in range(1, 8)]
        + [(x_hbm, x), (wo_hbm, wo), (wu_hbm, wu), (wd_hbm, wd)],
        in_sem,
    )
    greet_all(n, nb, s.me)

    def pass_x(z, slot):
        return remote(x.at[z // 2], x_all.at[slot], x_send.at[z], x_recv.at[slot], s.h, z * 2 + s.c)

    wait_all(loads[:13])
    vec[...] = jnp.zeros_like(vec)
    vec[0:1, 0:64] = bup_small[...].astype(f32).reshape(1, 64)
    for k in range(7):
        vec[k + 1:k + 2, 0:16] = small[k][...].astype(f32).reshape(1, 16)
    vec[8:10, :] = seg[...].astype(f32)
    for t in range(4):
        tile, at = slice(128 * t, 128 * t + 128), 256 * (t % 2)
        first, second = weave(wk[:, tile], wv[:, tile])
        sa[t // 2, :, at:at + 128] = first
        sa[t // 2, :, at + 128:at + 256] = second
    for w in range(2):
        sa[w, :, 512:768] = wq[:, 256 * w:256 * w + 256]
        sa[w, :, 768:896] = vec[...].astype(bf16)

    def w_line(z, slot):
        return remote(
            sa.at[lax.rem(z, 2)], wa.at[s.h, slot, s.c], w_send.at[z], w_recv.at[slot], s.h, z * 2 + s.c
        )

    def w_plane(j, h):
        slot = wa.at[h, :, s.c]
        return remote(slot, slot, w_send.at[4 + j], w_recv.at[4 + h], j, s.z * 2 + s.c)

    def w_twin(h, c):
        slot = wa.at[h, :, c]
        return remote(slot, slot, w_send.at[8 + h], w_recv.at[8 + h], s.h, s.z * 2 + 1 - s.c)

    each(s.nz, lambda k: w_line(s.ahead(k), s.z).start(), 1)
    own_w = pltpu.make_async_copy(sa.at[lax.rem(s.z, 2)], wa.at[s.h, s.z, s.c], w_local)
    own_w.start()
    each(s.nz, lambda k: pass_x(s.ahead(k), s.z).start(), 1)
    own_x = pltpu.make_async_copy(x.at[s.z // 2], x_all.at[s.z], x_local)
    own_x.start()
    wait_all(loads[13:])
    sb[:, 0:512] = wo[...]
    sb[:, 512:2560] = wu[...]
    for t in range(4):
        sb[:, 2560 + 512 * t:3072 + 512 * t] = wd[16 * t:16 * t + 16, :]
    line = Line(s, sb, fz_out, f_send, f_recv, f_local)
    line.begin()
    own_w.wait()
    each(s.nz, lambda k: w_line(s.ahead(k), s.ahead(k)).wait_recv(), 1)
    each(4, lambda i: w_plane(lax.rem(s.h + i, 4), s.h).start(), 1)
    w_twin(s.h, s.c).start()

    def w_arrive(i):
        h = lax.rem(s.h + 4 - i, 4)
        w_plane(h, h).wait_recv()
        w_twin(h, s.c).start()

    each(4, w_arrive, 1)
    each(4, lambda h: w_twin(h, 1 - s.c).wait_recv())
    outs = copies([(wa, wa_out)], out_sem)
    own_x.wait()
    plane = [Plane(s, ex_send.at[k], ex_recv.at[k]) for k in range(2)]
    kinds = ((kv_send, lambda g: kv_out.at[:, g, s.c]), (q_send, lambda g: q_out.at[:, g]))

    def block(w, j, z):
        src, dst = kinds[w]
        return plane[w].copy(src.at[j, z], dst(s.h * 4 + z), j, j * 4 + z, s.h * 4 + z)

    def from_block(w, j, z):
        src, dst = kinds[w]
        slot = dst(j * 4 + z)
        return plane[w].copy(slot, slot, j, j * 4 + z, j * 4 + z)

    def own_block(w, z):
        src, dst = kinds[w]
        return pltpu.make_async_copy(src.at[s.h, z], dst(s.h * 4 + z), ex_local.at[w, z])

    def twin(src, j, z, c):
        slot = kv_out.at[:, j * 4 + z, c]
        k = j * 4 + z
        return remote(slot if src is None else src, slot, tw_send.at[k], tw_recv.at[k], s.h, s.z * 2 + 1 - s.c)

    def project_rows(k):
        z = s.ahead(k)
        qkv = dot_n(x_all[z], wa[:, :, :, :, 0:768].reshape(512, 768)).astype(bf16)
        for j in range(4):
            kv_send[j, z] = qkv[:, 128 * j:128 * j + 128].reshape(8, 16, 128)
        for t in range(2):
            tile = qkv[:, 512 + 128 * t:640 + 128 * t]
            first, second = weave(tile[0:64], tile[64:128])
            q_send[2 * t, z] = first.reshape(4, 16, 128)
            q_send[2 * t + 1, z] = second.reshape(4, 16, 128)
        for w in range(2):
            each(4, lambda i: block(w, plane[w].to(i), z).start(), 1)
            own_block(w, z).start()
        twin(kv_send.at[s.h, z], s.h, z, s.c).start()

    project_rows(0)

    def project_next(k):
        z = s.ahead(k)
        pass_x(z, z).wait_recv()
        project_rows(k)

    each(s.nz, project_next, 1)
    line.onward(0)
    line.onward(1)
    vecs = wa[:, :, :, :, 768:896].reshape(n, 16, 128).astype(f32)
    outs += copies([(x_all, x_out)], out_sem.at[pl.ds(5, 1)])
    bup[...] = spread_row(vecs[:, 0, :], 2048, 64)
    for k in range(7):
        par[k:k + 1, :] = spread_row(vecs[:, k + 1, :], 512, 16)
    par[7:8, :] = jnp.zeros((1, 512), f32)
    ids = jnp.where(s.z < 2, vecs[:, 8, :], vecs[:, 9, :]).astype(bf16)
    for i in range(8):
        pick = (rows_of((128, 512)) == 16 * i + lax.rem(lanes((128, 512)), 16)).astype(f32).astype(bf16)
        wide = dot_n(ids, pick)
        source = rows_of((n, 512))
        row = jnp.where(source == lanes((n, 512)) // 16, wide, 0.0)
        segk[i:i + 1, :] = column_sum(row).astype(jnp.int32)
        source = rows_of((n, 256))
        own = (source // 2 == lanes((n, 256)) // 16) & (lax.rem(source, 2) == s.c)
        segq[i:i + 1, :] = column_sum(jnp.where(own, wide[:, 0:256], 0.0)).astype(jnp.int32)
    outs += copies([(par, par_out), (bup, bup_out), (segk, segk_out), (segq, segq_out)], out_sem.at[pl.ds(1, 4)])
    def forward(i):
        j = plane[0].frm(i)

        def go(k):
            z = s.ahead(k)
            from_block(0, j, z).wait_recv()
            twin(None, j, z, s.c).start()

        each(s.nz, go)

    each(4, forward, 1)
    line.onward(2)
    each(4, lambda i: each(s.nz, lambda z: from_block(1, plane[1].frm(i), z).wait_recv()), 1)
    each(4, lambda j: each(s.nz, lambda z: twin(None, j, z, 1 - s.c).wait_recv()))
    each(4, lambda j: each(s.nz, lambda z: twin(None, j, z, s.c).wait_send()))
    for w in range(2):
        each(s.nz, lambda z: own_block(w, z).wait())
        each(4, lambda i: each(s.nz, lambda z: block(w, plane[w].to(i), z).wait_send()), 1)
    each(s.nz, lambda k: pass_x(s.ahead(k), s.z).wait_send(), 1)
    each(s.nz, lambda k: w_line(s.ahead(k), s.z).wait_send(), 1)
    each(4, lambda i: w_plane(lax.rem(s.h + i, 4), s.h).wait_send(), 1)
    each(4, lambda h: w_twin(h, s.c).wait_send())
    line.sent()
    wait_all(outs)


def project(n, nb, x, wq, wk, wv, wo, wu, wd, seg, smalls):
    dma = pltpu.SemaphoreType.DMA
    nz = nb // 2
    return pl.pallas_call(
        functools.partial(project_kernel, n, nb),
        out_shape=(
            jax.ShapeDtypeStruct((4, 16, 16, 128), bf16),
            jax.ShapeDtypeStruct((8, 16, 2, 16, 128), bf16),
            jax.ShapeDtypeStruct((nz, 128, 512), bf16),
            jax.ShapeDtypeStruct((4, nz, 2, 16, 896), bf16),
            jax.ShapeDtypeStruct((nz, 16, 4608), bf16),
            jax.ShapeDtypeStruct((8, 512), f32),
            jax.ShapeDtypeStruct((1, 2048), f32),
            jax.ShapeDtypeStruct((8, 512), jnp.int32),
            jax.ShapeDtypeStruct((8, 256), jnp.int32),
        ),
        in_specs=any_specs(16),
        out_specs=any_specs(9),
        scratch_shapes=[
            pltpu.VMEM(x.shape, bf16),
            pltpu.VMEM((16, 512), bf16),
            pltpu.VMEM((16, 512), bf16),
            pltpu.VMEM((16, 512), bf16),
            pltpu.VMEM((16, 512), bf16),
            pltpu.VMEM((16, 2048), bf16),
            pltpu.VMEM((64, 512), bf16),
            pltpu.VMEM((2, 128), jnp.int32),
            *[pltpu.VMEM((16,), bf16)] * 7,
            pltpu.VMEM((64,), bf16),
            pltpu.VMEM((16, 128), f32),
            pltpu.VMEM((2, 16, 896), bf16),
            pltpu.VMEM((16, 4608), bf16),
            pltpu.VMEM((4, nz, 2, 16, 896), bf16),
            pltpu.VMEM((nz, 128, 512), bf16),
            pltpu.VMEM((4, nz, 8, 16, 128), bf16),
            pltpu.VMEM((4, nz, 4, 16, 128), bf16),
            pltpu.VMEM((8, 512), f32),
            pltpu.VMEM((1, 2048), f32),
            pltpu.VMEM((8, 512), jnp.int32),
            pltpu.VMEM((8, 256), jnp.int32),
            dma((16,)),
            dma((6,)),
            dma((12,)),
            dma((12,)),
            dma,
            dma((2 * nz,)),
            dma((2 * nz,)),
            dma,
            dma((nz,)),
            dma((nz,)),
            dma,
            dma((2, 4 * nz)),
            dma((2, 4 * nz)),
            dma((2, nz)),
            dma((4 * nz,)),
            dma((4 * nz,)),
        ],
        compiler_params=pltpu.CompilerParams(
            collective_id=1, has_side_effects=True, vmem_limit_bytes=VMEM_BYTES
        ),
        name="project",
    )(x, wq, wk, wv, wo, wu, wd, seg, *smalls)


def row_norm(v):
    mean = jnp.mean(v, axis=-1, keepdims=True)
    mid = v - mean
    inv = lax.rsqrt(jnp.mean(mid * mid, axis=-1, keepdims=True) + EPSILON)
    return mid * inv, inv


def row_norm_back(grad, normed, inv, gain):
    part = grad * gain
    return inv * (
        part
        - jnp.mean(part, axis=-1, keepdims=True)
        - normed * jnp.mean(part * normed, axis=-1, keepdims=True)
    )


def column_sum(v):
    return jnp.sum(v, axis=0, keepdims=True)


def middle_kernel(n, nb, *refs):
    o_hbm, x_hbm, y_hbm, g_hbm, fz_hbm, fx_hbm, fy_hbm, par_hbm, bup_hbm = refs[:9]
    outs_hbm = refs[10:20]
    do_out = refs[9]
    (
        o_in, x, y, g_in, wb, wd, par, bup, o_recv, do_send, slope,
        out, dacc_ref, dz1_ref, x1_ref, dur_ref, hid_ref, dfr_ref, omix, dar_ref, gvec, bias_up,
        in_sem, out_sem, ex_send, ex_recv, ex_local, f_send, f_recv,
    ) = refs[20:]
    s = Spot(nb)
    loads = copies(
        [
            (o_hbm, o_in), (x_hbm, x), (y_hbm, y), (g_hbm, g_in), (par_hbm, par), (bup_hbm, bup),
            (fz_hbm, wb.at[s.h, :, s.c]), (fx_hbm, wb.at[s.near[0], :, s.c]), (fy_hbm, wb.at[s.near[1], :, s.c]),
        ],
        in_sem,
    )
    greet_all(n, nb, s.me)
    loads[0].wait()
    o_ex = Exchange(
        s, lambda g: o_in.at[:, g], lambda g: o_recv.at[pair_of(g)], ex_send.at[0], ex_recv.at[0], ex_local.at[0]
    )
    o_ex.begin()
    cut = [pl.ds(0, 2304), pl.ds(2304, 2304)]
    heads = (s.h, s.near[0], s.near[1], s.diag)

    def onward(w, h, to):
        src = (fx_hbm, fy_hbm)[w].at[:, :, cut[w]]
        return remote(src, wb.at[h, :, s.c, :, cut[w]], f_send.at[4 + w], f_recv.at[4 + w], to, s.z * 2 + s.c)

    def twin(k, c):
        slot = wb.at[heads[k], :, c]
        src = (fz_hbm, fx_hbm, fy_hbm, slot)[k]
        return remote(src, slot, f_send.at[k], f_recv.at[k], s.h, s.z * 2 + 1 - s.c)

    for w in range(2):
        onward(w, s.near[w], s.near[1 - w]).start()
    for k in range(3):
        twin(k, s.c).start()
    for w in range(2):
        onward(w, s.diag, s.near[1 - w]).wait_recv()
    twin(3, s.c).start()
    o_ex.end()
    wait_all(loads[1:])
    for m in range(2):
        for t in range(4):
            first, second = weave(
                o_recv[8 * m + 2 * t].reshape(64, 128), o_recv[8 * m + 2 * t + 1].reshape(64, 128)
            )
            omix[128 * m:128 * m + 64, 128 * t:128 * t + 128] = first
            omix[128 * m + 64:128 * m + 128, 128 * t:128 * t + 128] = second
    gain1, bias1 = par[1:2], par[2:3]
    gain2, bias2 = par[3:4], par[4:5]
    gain3, bias3 = par[5:6], par[6:7]
    for k in range(4):
        twin(k, 1 - s.c).wait_recv()
    for t in range(4):
        for r in range(4):
            wd[t, :, :, r] = wb[t, :, :, :, 2560 + 512 * r:3072 + 512 * r]
    w_out = wb[:, :, :, :, 0:512].reshape(512, 512)
    a = dot_n(omix[...], w_out)
    n1, r1 = row_norm(x[...].astype(f32) + a)
    x1 = n1 * gain1 + bias1
    x1r = x1.astype(bf16)
    x1_ref[...] = x1r
    feed = jnp.zeros_like(x1)
    for t in range(4):
        cols = slice(512 * t, 512 * t + 512)
        u = dot_n(x1r, wb[:, :, :, :, 512 + 512 * t:1024 + 512 * t].reshape(512, 512)) + bup[:, cols]
        phi = 0.5 * (1.0 + lax.erf(u * (0.5**0.5)))
        hid = (u * phi).astype(bf16)
        slope[:, cols] = phi + u * jnp.exp(-0.5 * u * u) * ((2.0 * math.pi) ** -0.5)
        hid_ref[:, cols] = hid
        feed = feed + dot_n(hid, wd[t].reshape(512, 512))
    feed = feed + par[0:1]
    n2, r2 = row_norm(x1 + feed)
    n3, r3 = row_norm(y[...].astype(f32) + a + feed)
    out[...] = (n2 * gain2 + bias2 + (n3 * gain3 + bias3)).astype(bf16)
    g = g_in[...].astype(f32)
    dacc = row_norm_back(g, n3, r3, gain3)
    dacc_ref[...] = dacc
    dz2 = row_norm_back(g, n2, r2, gain2)
    df = dz2 + dacc
    dfr = df.astype(bf16)
    dfr_ref[...] = dfr
    dx1 = dz2
    for t in range(4):
        cols = slice(512 * t, 512 * t + 512)
        du = dot_t(dfr, wd[t].reshape(512, 512)) * slope[:, cols]
        bias_up[:, cols] = column_sum(du)
        dur = du.astype(bf16)
        dur_ref[:, cols] = dur
        dx1 = dx1 + dot_t(dur, wb[:, :, :, :, 512 + 512 * t:1024 + 512 * t].reshape(512, 512))
    dz1 = row_norm_back(dx1, n1, r1, gain1)
    dz1_ref[...] = dz1
    dar = (dz1 + dacc).astype(bf16)
    dar_ref[...] = dar
    do = dot_t(dar, w_out).astype(bf16)
    for m in range(2):
        for t in range(4):
            tile = do[128 * m:128 * m + 128, 128 * t:128 * t + 128]
            first, second = weave(tile[0:64], tile[64:128])
            do_send[8 * m + 2 * t] = first.reshape(4, 16, 128)
            do_send[8 * m + 2 * t + 1] = second.reshape(4, 16, 128)
    do_ex = Exchange(
        s, lambda g: do_send.at[pair_of(g)], lambda g: do_out.at[:, g], ex_send.at[1], ex_recv.at[1], ex_local.at[1]
    )
    do_ex.begin()
    stores = copies(
        zip((out, dacc_ref, dz1_ref, x1_ref, dur_ref, hid_ref, dfr_ref, omix, dar_ref), outs_hbm[:9]), out_sem
    )
    sum_g = column_sum(g)
    sums = (
        column_sum(df), column_sum(dx1 * n1), column_sum(dx1), column_sum(g * n2), sum_g, column_sum(g * n3), sum_g
    )
    gvec[...] = jnp.zeros_like(gvec)
    gvec[:, 0, :] = gather_row(bias_up[...], n, 64)
    for k in range(7):
        gvec[:, k + 1, :] = gather_row(sums[k], n, 16)
    stores += copies([(gvec, outs_hbm[9])], out_sem.at[pl.ds(9, 1)])
    do_ex.end()
    for w in range(2):
        onward(w, s.near[w], s.near[1 - w]).wait_send()
    for k in range(4):
        twin(k, s.c).wait_send()
    wait_all(stores)


def middle(n, nb, o, x, y, g, fz, fx, fy, par, bup):
    dma = pltpu.SemaphoreType.DMA
    rows = x.shape[0]
    saved = [
        ((rows, 512), bf16), ((rows, 512), f32), ((rows, 512), f32), ((rows, 512), bf16), ((rows, 2048), bf16),
        ((rows, 2048), bf16), ((rows, 512), bf16), ((rows, 512), bf16), ((rows, 512), bf16), ((n, 16, 128), f32),
    ]
    return pl.pallas_call(
        functools.partial(middle_kernel, n, nb),
        out_shape=[jax.ShapeDtypeStruct((4, 16, 16, 128), bf16)]
        + [jax.ShapeDtypeStruct(shape, kind) for shape, kind in saved],
        in_specs=any_specs(9),
        out_specs=any_specs(11),
        scratch_shapes=[
            pltpu.VMEM(o.shape, bf16),
            pltpu.VMEM(x.shape, bf16),
            pltpu.VMEM(x.shape, bf16),
            pltpu.VMEM(x.shape, bf16),
            pltpu.VMEM((4, nb // 2, 2, 16, 4608), bf16),
            pltpu.VMEM((4, 4, 2, 4, 16, 512), bf16),
            pltpu.VMEM(par.shape, f32),
            pltpu.VMEM(bup.shape, f32),
            pltpu.VMEM((16, 4, 16, 128), bf16),
            pltpu.VMEM((16, 4, 16, 128), bf16),
            pltpu.VMEM((rows, 2048), f32),
            *[pltpu.VMEM(shape, kind) for shape, kind in saved],
            pltpu.VMEM((1, 2048), f32),
            dma((9,)),
            dma((10,)),
            dma((2, 16)),
            dma((2, 16)),
            dma((2,)),
            dma((6,)),
            dma((6,)),
        ],
        compiler_params=pltpu.CompilerParams(
            collective_id=2, has_side_effects=True, vmem_limit_bytes=VMEM_BYTES
        ),
        name="middle",
    )(o, x, y, g, fz, fx, fy, par, bup)


def finish_kernel(n, nb, *refs):
    ins = refs[:12]
    outs = refs[12:20]
    (
        dq, dkv, xm, dz1, x1, dur, hid, dfr, omix, dar, gvec, wa,
        pa, ta, da, na, la, pb, tb, db, nb_, lb, pd, td, dd, nd, ld, tv, dv, nv, lv,
        twin_buf, dkv_send, dkv_recv, dq_recv, dqkv, dx_send, dx_recv, gx, gq, gk, gv, go, gu, gd, gs,
        in_sem, out_sem, rs_send, rs_recv, ex_send, ex_recv, dx_ssem, dx_rsem, tw_send, tw_recv,
    ) = refs[20:]
    s = Spot(nb)
    order = (1, 0, 10, 8, 9, 4, 5, 6, 7, 2, 11, 3)
    local = (dq, dkv, xm, dz1, x1, dur, hid, dfr, omix, dar, gvec, wa)
    loads = copies([(ins[k], local[k]) for k in order], in_sem)
    greet_all(n, nb, s.me)
    swap = remote(ins[1].at[:, :, 1 - s.c], twin_buf, tw_send, tw_recv, s.h, s.z * 2 + 1 - s.c)
    swap.start()
    jobs = [
        Scatter(s, *bufs, rs_send.at[k], rs_recv.at[k])
        for k, bufs in enumerate(
            ((pb, tb, db, nb_, lb), (pd, td, dd, nd, ld), (gvec, tv, dv, nv, lv), (pa, ta, da, na, la))
        )
    ]
    swap.wait()
    wait_all(loads[:2])

    def add(g):
        dkv_send[g] = (dkv[:, g, s.c].astype(f32) + twin_buf[:, g].astype(f32)).astype(bf16)

    each(4 * s.nz, add)
    plane = [Plane(s, ex_send.at[k], ex_recv.at[k]) for k in range(2)]

    def block(w, j, slot):
        group = pl.ds(j * s.nz, s.nz)
        src, dst = ((dkv_send.at[group], dkv_recv.at[slot]), (dq.at[:, group], dq_recv.at[slot]))[w]
        return plane[w].copy(src, dst, j, j, slot)

    for w in range(2):
        each(4, lambda i: block(w, plane[w].to(i), s.h).start(), 1)
    wait_all(loads[2:8])
    jobs[2].begin()
    pb[:, :, 0:512] = dot_0(omix[...], dar[...]).astype(bf16).reshape(n, 16, 512)
    for t in range(4):
        cols = slice(512 * t, 512 * t + 512)
        pb[:, :, 512 + 512 * t:1024 + 512 * t] = dot_0(x1[...], dur[:, cols]).astype(bf16).reshape(n, 16, 512)
    jobs[0].begin()
    wait_all(loads[8:])
    for t in range(4):
        cols = slice(512 * t, 512 * t + 512)
        pd[8 * t:8 * t + 8] = dot_0(hid[:, cols], dfr[...]).astype(bf16).reshape(8, 64, 512)
    jobs[1].begin()

    def own(z):
        dkv_recv[s.h, z] = dkv_send[s.h * s.nz + z]
        dq_recv[s.h, :, z] = dq[:, s.h * s.nz + z]

    each(s.nz, own)
    for job in jobs[:2]:
        job.first()
    for w in range(2):
        each(4, lambda i: block(w, plane[w].frm(i), plane[w].frm(i)).wait_recv(), 1)
    for z in range(4):
        rows = slice(128 * z, 128 * z + 128)
        for j in range(4):
            dqkv[rows, 128 * j:128 * j + 128] = dkv_recv[j, z].reshape(128, 128)
        for t in range(2):
            first, second = weave(
                dq_recv[2 * t, :, z].reshape(64, 128), dq_recv[2 * t + 1, :, z].reshape(64, 128)
            )
            dqkv[128 * z:128 * z + 64, 512 + 128 * t:640 + 128 * t] = first
            dqkv[128 * z + 64:128 * z + 128, 512 + 128 * t:640 + 128 * t] = second
    weight = wa[:, :, :, :, 0:768].reshape(512, 768)
    for z in range(4):
        dx_send[z] = dot_t(dqkv[128 * z:128 * z + 128, :], weight).astype(bf16)

    def back(z, slot):
        return remote(dx_send.at[z], dx_recv.at[slot], dx_ssem.at[z], dx_rsem.at[slot], s.h, z * 2 + s.c)

    each(s.nz, lambda k: back(s.ahead(k), s.z).start(), 1)
    dx_recv[s.z] = dx_send[s.z]
    tokens = xm[...].reshape(512, 512)
    pa[...] = dot_0(tokens, dqkv[...]).astype(bf16).reshape(n, 16, 768)
    jobs[3].begin()
    jobs[2].first()
    for job in jobs[:3]:
        job.second()
    jobs[3].first()
    for job in jobs[:3]:
        job.third()
    jobs[3].second()
    jobs[3].third()
    each(s.nz, lambda k: back(s.ahead(k), s.ahead(k)).wait_recv(), 1)
    for m in range(2):
        rows = slice(128 * m, 128 * m + 128)
        gx[rows, :] = dz1[rows, :] + (dx_recv[2 * m].astype(f32) + dx_recv[2 * m + 1].astype(f32))
    stores = copies([(gx, outs[0])], out_sem)
    total = jobs[0].total()
    go[...] = total[:, 0:512]
    gu[...] = total[:, 512:2560]
    gd[...] = jobs[1].total()
    gs[...] = jobs[2].total()
    stores += copies(zip((go, gu, gd, gs), outs[4:8]), out_sem.at[pl.ds(1, 4)])
    for w, part in enumerate(jobs[3].columns()):
        gq[:, 256 * w:256 * w + 256] = part[:, 512:768]
        for t in range(2):
            first, second = weave(part[:, 256 * t:256 * t + 128], part[:, 256 * t + 128:256 * t + 256])
            at = 256 * w + 128 * t
            gk[:, at:at + 128] = first
            gv[:, at:at + 128] = second
    stores += copies(zip((gq, gk, gv), outs[1:4]), out_sem.at[pl.ds(5, 3)])
    for w in range(2):
        each(4, lambda i: block(w, plane[w].to(i), s.h).wait_send(), 1)
    each(s.nz, lambda k: back(s.ahead(k), s.z).wait_send(), 1)
    for job in jobs:
        job.sent()
    wait_all(stores)


def finish(n, nb, dq, dkv, xm, dz1, x1, dur, hid, dfr, omix, dar, gvec, wa):
    dma = pltpu.SemaphoreType.DMA
    nz = nb // 2
    rows = dz1.shape[0]

    def buffers(depth, width, kind):
        return [
            pltpu.VMEM((n, depth, width), kind),
            pltpu.VMEM((4, nz, depth, width), kind),
            pltpu.VMEM((2, nz, depth, width // 2), kind),
            pltpu.VMEM((2, nz, depth, width), kind),
            pltpu.VMEM((nz, depth, width), kind),
        ]

    args = (dq, dkv, xm, dz1, x1, dur, hid, dfr, omix, dar, gvec, wa)
    shapes = ((rows, 512), (16, 512), (16, 512), (16, 512), (16, 512), (16, 2048), (64, 512), (16, 128))
    return pl.pallas_call(
        functools.partial(finish_kernel, n, nb),
        out_shape=[jax.ShapeDtypeStruct(shape, f32) for shape in shapes],
        in_specs=any_specs(12),
        out_specs=any_specs(8),
        scratch_shapes=[
            *[pltpu.VMEM(arg.shape, arg.dtype) for arg in args],
            *buffers(16, 768, bf16),
            *buffers(16, 2560, bf16),
            *buffers(64, 512, bf16),
            *buffers(16, 128, f32)[1:2],
            pltpu.VMEM((2, nz, 8, 128), f32),
            *buffers(16, 128, f32)[3:],
            pltpu.VMEM((8, 16, 16, 128), bf16),
            pltpu.VMEM((16, 8, 16, 128), bf16),
            pltpu.VMEM((4, nz, 8, 16, 128), bf16),
            pltpu.VMEM((4, 4, nz, 16, 128), bf16),
            pltpu.VMEM((512, 768), bf16),
            pltpu.VMEM((nz, 128, 512), bf16),
            pltpu.VMEM((nz, 128, 512), bf16),
            *[pltpu.VMEM(shape, f32) for shape in shapes],
            dma((12,)),
            dma((8,)),
            dma((4, 9 * nz)),
            dma((4, 9 * nz)),
            dma((2, 4)),
            dma((2, 4)),
            dma((nz,)),
            dma((nz,)),
            dma,
            dma,
        ],
        compiler_params=pltpu.CompilerParams(
            collective_id=3, has_side_effects=True, vmem_limit_bytes=VMEM_BYTES
        ),
        name="finish",
    )(*args)


def deliver_kernel(count, *refs):
    ins, outs = refs[:count], refs[count:2 * count + 7]
    stage, lines, (in_sem, sems) = refs[2 * count + 7:3 * count + 7], refs[3 * count + 7:3 * count + 15], refs[-2:]
    loads = copies(zip(ins, stage), in_sem)
    jobs = []
    for k in range(count - 1):
        loads[k].wait()
        jobs += copies([(stage[k], outs[k])], sems.at[pl.ds(k, 1)])
    loads[-1].wait()
    vec = stage[-1]
    lines[0][...] = vec[0:1, 0:64].reshape(64)
    for k in range(1, 8):
        lines[k][...] = vec[k:k + 1, 0:16].reshape(16)
    jobs += copies(zip(lines, outs[count - 1:]), sems.at[pl.ds(count - 1, 8)])
    wait_all(jobs)


def deliver(arrays, vec):
    count = len(arrays) + 1
    lines = [(64,)] + [(16,)] * 7
    return pl.pallas_call(
        functools.partial(deliver_kernel, count),
        out_shape=[jax.ShapeDtypeStruct(a.shape, a.dtype) for a in arrays]
        + [jax.ShapeDtypeStruct(shape, f32) for shape in lines],
        in_specs=any_specs(count),
        out_specs=any_specs(count + 7),
        scratch_shapes=[
            *[pltpu.VMEM(a.shape, a.dtype) for a in (*arrays, vec)],
            *[pltpu.VMEM(shape, f32) for shape in lines],
            pltpu.SemaphoreType.DMA((count,)),
            pltpu.SemaphoreType.DMA((count + 7,)),
        ],
        compiler_params=pltpu.CompilerParams(vmem_limit_bytes=VMEM_BYTES),
        name="deliver",
    )(*arrays, vec)


def by_pairs(
    stream, accumulator, upstream, segment_ids, w_query, w_key, w_value, w_out, w_up, b_up, w_down, b_down,
    gain_attn, bias_attn, gain_ffn, bias_ffn, gain_final, bias_final,
):
    nb = lax.axis_size("blk")
    n = 4 * nb
    x = stream.reshape(256, 512)
    y = accumulator.reshape(256, 512)
    g = upstream.reshape(256, 512)
    smalls = (b_up, b_down, gain_attn, bias_attn, gain_ffn, bias_ffn, gain_final, bias_final)
    q, kv, xm, wa, fz, par, bup, seg_k, seg_q = project(
        n, nb, stream.reshape(2, 128, 512), w_query, w_key, w_value, w_out, w_up, w_down, segment_ids.reshape(2, 128), smalls
    )
    fx, fy = (lax.ppermute(fz, "head", [(h, h ^ w) for h in range(4)]) for w in (1, 2))
    o, of, lse, kv2, kvt = attn_fwd(q.reshape(4, 256, 128), kv.reshape(4096, 128), seg_q, seg_k)
    do, out, dacc, dz1, x1, dur, hid, dfr, omix, dar, gvec = middle(
        n, nb, o.reshape(4, 16, 16, 128), x, y, g, fz, fx, fy, par, bup
    )
    dq, dkv, out, dacc = attn_bwd(
        q.reshape(4, 256, 128), do.reshape(4, 256, 128), of, lse, kv2, kvt, seg_q, seg_k, out, dacc
    )
    gx, gq, gk, gv, go, gu, gd, gs = finish(
        n, nb, dq.reshape(4, 16, 16, 128), dkv.reshape(8, 16, 2, 16, 128), xm, dz1, x1, dur, hid, dfr, omix, dar, gvec, wa
    )
    gx, gq, gk, gv, go, gu, gd, gbu, *small_grads = deliver((gx, gq, gk, gv, go, gu, gd), gs)
    return (
        out.reshape(stream.shape), gx.reshape(stream.shape), dacc.reshape(stream.shape),
        gq, gk, gv, go, gu, gbu, gd, *small_grads,
    )


def pairs_fit(mesh, shape):
    return mesh.shape["head"] == 4 and mesh.shape["blk"] == 8 and shape == (2, 32, 128, 512)


def solution(mesh):
    def step(*args):
        return run(by_pairs if pairs_fit(mesh, args[0].shape) else local, mesh)(*args)

    return step


def run(body, mesh):
    return jax.shard_map(
        body,
        mesh=mesh,
        in_specs=(
            P(None, ("head", "blk"), None, None),
            P(None, ("head", "blk"), None, None),
            P(None, ("head", "blk"), None, None),
            P(None, ("head", "blk"), None),
            P(("head", "blk"), None),
            P(("head", "blk"), None),
            P(("head", "blk"), None),
            P(("head", "blk"), None),
            P(("head", "blk"), None),
            P(("head", "blk")),
            P(("head", "blk"), None),
            P(("head", "blk")),
            P(("head", "blk")),
            P(("head", "blk")),
            P(("head", "blk")),
            P(("head", "blk")),
            P(("head", "blk")),
            P(("head", "blk")),
        ),
        out_specs=(
            P(None, ("head", "blk"), None, None),
            P(None, ("head", "blk"), None, None),
            P(None, ("head", "blk"), None, None),
            P(("head", "blk"), None),
            P(("head", "blk"), None),
            P(("head", "blk"), None),
            P(("head", "blk"), None),
            P(("head", "blk"), None),
            P(("head", "blk")),
            P(("head", "blk"), None),
            P(("head", "blk")),
            P(("head", "blk")),
            P(("head", "blk")),
            P(("head", "blk")),
            P(("head", "blk")),
            P(("head", "blk")),
            P(("head", "blk")),
        ),
        check_vma=False,
    )
```

```python
import functools
import math

import jax
import jax.numpy as jnp
from jax import lax
from jax.experimental import pallas as pl
from jax.experimental.pallas import tpu as pltpu
from jax.sharding import PartitionSpec as P

DH = 64
f32, bf16 = jnp.float32, jnp.bfloat16
MESH = pl.DeviceIdType.MESH
FAR = -1e30
VMEM_BYTES = 60 << 20


EPSILON = 1e-05


def norm_forward(inputs, norm_gain, norm_bias):
    average = jnp.mean(inputs, axis=-1, keepdims=True)
    centered = inputs - average
    inv_std = lax.rsqrt(jnp.mean(centered * centered, axis=-1, keepdims=True) + EPSILON)
    normed = centered * inv_std
    return (normed * norm_gain + norm_bias, normed, inv_std)


def norm_backward(gradient, normed, inv_std, norm_gain):
    scaled = gradient * norm_gain
    projected = (
        scaled
        - jnp.mean(scaled, axis=-1, keepdims=True)
        - normed * jnp.mean(scaled * normed, axis=-1, keepdims=True)
    )
    return (inv_std * projected, jnp.sum(gradient * normed, axis=0), jnp.sum(gradient, axis=0))


def smooth_gate(pre_act):
    return jax.nn.gelu(pre_act, approximate=False)


def split_rows(length):
    block_len = math.gcd(length, 512)
    return (length // block_len, block_len)


def block_scores(queries, query_seg, key_rows, key_seg, scaling):
    scores = (
        jnp.einsum("sgd,kgd->sgk", queries, key_rows, preferred_element_type=jnp.float32) * scaling
    )
    allowed = query_seg[:, None, None] == key_seg[None, None, :]
    return (scores, allowed)


def block_grads(
    queries, query_seg, grad_rows, log_total, row_delta, key_rows, value_rows, key_seg, scaling
):
    scores, allowed = block_scores(queries, query_seg, key_rows, key_seg, scaling)
    attn_prob = jnp.where(allowed, jnp.exp(scores - log_total[:, :, None]), 0.0)
    prob_grad = jnp.einsum(
        "sgd,kgd->sgk", grad_rows, value_rows, preferred_element_type=jnp.float32
    )
    score_grad = (attn_prob * (prob_grad - row_delta[:, :, None]) * scaling).astype(jnp.bfloat16)
    return (attn_prob.astype(jnp.bfloat16), score_grad)


def key_blocks(key_rows, value_rows, key_seg, groups):
    block_num, block_len = split_rows(key_rows.shape[0])
    return (
        key_rows.reshape(block_num, block_len, groups, -1),
        value_rows.reshape(block_num, block_len, groups, -1),
        key_seg.reshape(block_num, block_len),
    )


def attend_fold(queries, query_seg, scaling, carried, portion):
    key_rows, value_rows, key_seg = portion

    def step(running, blocks):
        key_part, value_part, seg_part = blocks
        old_max, old_total, weighted = running
        scores, allowed = block_scores(queries, query_seg, key_part, seg_part, scaling)
        row_max = jnp.maximum(old_max, jnp.max(jnp.where(allowed, scores, -1e30), axis=2))
        exp_scores = jnp.where(allowed, jnp.exp(scores - row_max[:, :, None]), 0.0)
        rescale = jnp.exp(old_max - row_max)
        new_total = old_total * rescale + jnp.sum(exp_scores, axis=2)
        weighted = weighted * rescale[:, :, None] + jnp.einsum(
            "sgk,kgd->sgd",
            exp_scores.astype(jnp.bfloat16),
            value_part,
            preferred_element_type=jnp.float32,
        )
        return ((row_max, new_total, weighted), None)

    running, unused = lax.scan(
        step, carried, key_blocks(key_rows, value_rows, key_seg, queries.shape[1])
    )
    return running


def local(
    stream,
    accumulator,
    upstream,
    segment_ids,
    w_query,
    w_key,
    w_value,
    w_out,
    w_up,
    b_up,
    w_down,
    b_down,
    gain_attn,
    bias_attn,
    gain_ffn,
    bias_ffn,
    gain_final,
    bias_final,
):
    heads_axis = lax.axis_size("head")
    micro = stream.shape[0]
    tokens = stream.shape[2]
    width = stream.shape[3]
    group_width = width // heads_axis
    groups = group_width // DH
    scaling = DH ** (-0.5)
    f32 = jnp.float32
    bf16 = jnp.bfloat16
    out_list = []
    stream_grads = []
    accum_grads = []
    grad_totals = None
    for micro_step in range(micro):
        (
            q_weight,
            k_weight,
            v_weight,
            o_weight,
            up_weight,
            up_bias,
            down_weight,
            down_bias,
            gain_one,
            shift_one,
            gain_two,
            shift_two,
            gain_three,
            shift_three,
        ) = (
            lax.all_gather(w_query, ("head", "blk"), axis=0, tiled=True),
            lax.all_gather(w_key, ("head", "blk"), axis=0, tiled=True),
            lax.all_gather(w_value, ("head", "blk"), axis=0, tiled=True),
            lax.all_gather(w_out, ("head", "blk"), axis=0, tiled=True),
            lax.all_gather(w_up, ("head", "blk"), axis=0, tiled=True),
            lax.all_gather(b_up, ("head", "blk"), axis=0, tiled=True),
            lax.all_gather(w_down, ("head", "blk"), axis=0, tiled=True),
            lax.all_gather(b_down, ("head", "blk"), axis=0, tiled=True),
            lax.all_gather(gain_attn, ("head", "blk"), axis=0, tiled=True),
            lax.all_gather(bias_attn, ("head", "blk"), axis=0, tiled=True),
            lax.all_gather(gain_ffn, ("head", "blk"), axis=0, tiled=True),
            lax.all_gather(bias_ffn, ("head", "blk"), axis=0, tiled=True),
            lax.all_gather(gain_final, ("head", "blk"), axis=0, tiled=True),
            lax.all_gather(bias_final, ("head", "blk"), axis=0, tiled=True),
        )
        inputs = stream[micro_step, 0]
        input_wide = inputs.astype(f32)
        carried = accumulator[micro_step, 0].astype(f32)
        segs = segment_ids[micro_step, 0]
        projections = jnp.stack(
            [
                jnp.dot(inputs, q_weight, preferred_element_type=f32),
                jnp.dot(inputs, k_weight, preferred_element_type=f32),
                jnp.dot(inputs, v_weight, preferred_element_type=f32),
            ]
        ).astype(bf16)
        projections = projections.reshape(3, tokens, heads_axis, group_width)
        seg_wide = jnp.broadcast_to(segs[None, :, None, None], (1, tokens, heads_axis, 1))
        regrouped, seg_group = (
            lax.all_to_all(projections, "head", split_axis=2, concat_axis=1, tiled=True),
            lax.all_to_all(seg_wide, "head", split_axis=2, concat_axis=1, tiled=True),
        )
        rows = regrouped.shape[1]
        query_loc = regrouped[0, :, 0]
        key_loc = regrouped[1, :, 0]
        value_loc = regrouped[2, :, 0]
        seg_loc = seg_group[0, :, 0, 0]
        queries3 = query_loc.reshape(rows, groups, DH)
        start_state = (
            jnp.full((rows, groups), -1e30, f32),
            jnp.zeros((rows, groups), f32),
            jnp.zeros((rows, groups, DH), f32),
        )
        row_max, row_total, weighted = attend_fold(
            queries3,
            seg_loc,
            scaling,
            start_state,
            (
                lax.all_gather(key_loc, "blk", axis=0, tiled=True),
                lax.all_gather(value_loc, "blk", axis=0, tiled=True),
                lax.all_gather(seg_loc, "blk", axis=0, tiled=True),
            ),
        )
        attn_out = weighted / row_total[:, :, None]
        log_total = row_max + jnp.log(row_total)
        attn_send = attn_out.astype(bf16).reshape(rows, 1, group_width)
        mixed = lax.all_to_all(attn_send, "head", split_axis=0, concat_axis=1, tiled=True).reshape(
            tokens, width
        )
        branch = jnp.dot(mixed, o_weight, preferred_element_type=f32)
        first, normed_one, inv_one = norm_forward(
            input_wide + branch, gain_one.astype(f32), shift_one.astype(f32)
        )
        first_low = first.astype(bf16)
        hidden_pre = jnp.dot(first_low, up_weight, preferred_element_type=f32) + up_bias.astype(f32)
        hidden_act, gate_pull = jax.vjp(smooth_gate, hidden_pre)
        hidden = hidden_act.astype(bf16)
        feed = jnp.dot(hidden, down_weight, preferred_element_type=f32) + down_bias.astype(f32)
        second, normed_two, inv_two = norm_forward(
            first + feed, gain_two.astype(f32), shift_two.astype(f32)
        )
        final, normed_three, inv_three = norm_forward(
            carried + branch + feed, gain_three.astype(f32), shift_three.astype(f32)
        )
        out_list.append((second + final).astype(bf16))
        cotangent = upstream[micro_step, 0].astype(f32)
        accum_grad, gain3_grad, shift3_grad = norm_backward(
            cotangent, normed_three, inv_three, gain_three.astype(f32)
        )
        second_grad, gain2_grad, shift2_grad = norm_backward(
            cotangent, normed_two, inv_two, gain_two.astype(f32)
        )
        feed_grad = second_grad + accum_grad
        feed_low = feed_grad.astype(bf16)
        down_grad = jnp.dot(hidden.T, feed_low, preferred_element_type=f32)
        (hidden_grad,) = gate_pull(jnp.dot(feed_low, down_weight.T, preferred_element_type=f32))
        hidden_low = hidden_grad.astype(bf16)
        up_grad = jnp.dot(first_low.T, hidden_low, preferred_element_type=f32)
        first_grad = second_grad + jnp.dot(hidden_low, up_weight.T, preferred_element_type=f32)
        resid_grad, gain1_grad, shift1_grad = norm_backward(
            first_grad, normed_one, inv_one, gain_one.astype(f32)
        )
        branch_low = (resid_grad + accum_grad).astype(bf16)
        out_wgrad = jnp.dot(mixed.T, branch_low, preferred_element_type=f32)
        mixed_grad = jnp.dot(branch_low, o_weight.T, preferred_element_type=f32).astype(bf16)
        mixed_grad = mixed_grad.reshape(tokens, heads_axis, group_width)
        grad_group = lax.all_to_all(mixed_grad, "head", split_axis=1, concat_axis=0, tiled=True)
        grad_loc = grad_group[:, 0]
        grad3 = grad_loc.reshape(rows, groups, DH)
        row_delta = jnp.sum(grad3.astype(f32) * attn_out, axis=2)
        whole_keys, whole_values, whole_seg = (
            lax.all_gather(key_loc, "blk", axis=0, tiled=True),
            lax.all_gather(value_loc, "blk", axis=0, tiled=True),
            lax.all_gather(seg_loc, "blk", axis=0, tiled=True),
        )

        def backward_step(running, blocks):
            key_part, value_part, seg_part = blocks
            attn_prob, score_grad = block_grads(
                queries3,
                seg_loc,
                grad3,
                log_total,
                row_delta,
                key_part,
                value_part,
                seg_part,
                scaling,
            )
            running = running + jnp.einsum(
                "sgk,kgd->sgd", score_grad, key_part, preferred_element_type=f32
            )
            key_term = jnp.einsum("sgk,sgd->kgd", score_grad, queries3, preferred_element_type=f32)
            value_term = jnp.einsum("sgk,sgd->kgd", attn_prob, grad3, preferred_element_type=f32)
            return (running, (key_term, value_term))

        query_grad, (key_terms, value_terms) = lax.scan(
            backward_step,
            jnp.zeros((rows, groups, DH), f32),
            key_blocks(whole_keys, whole_values, whole_seg, groups),
        )
        key_grad, value_grad = (
            lax.psum_scatter(
                key_terms.reshape(-1, group_width), "blk", scatter_dimension=0, tiled=True
            ),
            lax.psum_scatter(
                value_terms.reshape(-1, group_width), "blk", scatter_dimension=0, tiled=True
            ),
        )
        grad_stack = jnp.stack(
            [query_grad.reshape(rows, group_width), key_grad, value_grad]
        ).astype(bf16)
        grad_stack = grad_stack.reshape(3, rows, 1, group_width)
        returned = lax.all_to_all(
            grad_stack, "head", split_axis=1, concat_axis=2, tiled=True
        ).reshape(3, tokens, width)
        query_wgrad = jnp.dot(inputs.T, returned[0], preferred_element_type=f32)
        key_wgrad = jnp.dot(inputs.T, returned[1], preferred_element_type=f32)
        value_wgrad = jnp.dot(inputs.T, returned[2], preferred_element_type=f32)
        input_grad = (
            resid_grad
            + jnp.dot(returned[0], q_weight.T, preferred_element_type=f32)
            + jnp.dot(returned[1], k_weight.T, preferred_element_type=f32)
            + jnp.dot(returned[2], v_weight.T, preferred_element_type=f32)
        )
        stream_grads.append(input_grad)
        accum_grads.append(accum_grad)
        step_grads = (
            query_wgrad,
            key_wgrad,
            value_wgrad,
            out_wgrad,
            up_grad,
            jnp.sum(hidden_grad, axis=0),
            down_grad,
            jnp.sum(feed_grad, axis=0),
            gain1_grad,
            shift1_grad,
            gain2_grad,
            shift2_grad,
            gain3_grad,
            shift3_grad,
        )
        if grad_totals is None:
            grad_totals = step_grads
        else:
            grad_totals = tuple((older + newer for older, newer in zip(grad_totals, step_grads)))
    summed = lax.psum_scatter(grad_totals, ("head", "blk"), scatter_dimension=0, tiled=True)
    layer_out = jnp.stack(out_list)[:, None]
    grad_stream = jnp.stack(stream_grads)[:, None]
    grad_accum = jnp.stack(accum_grads)[:, None]
    return (
        layer_out,
        grad_stream,
        grad_accum,
        summed[0],
        summed[1],
        summed[2],
        summed[3],
        summed[4],
        summed[5],
        summed[6],
        summed[7],
        summed[8],
        summed[9],
        summed[10],
        summed[11],
        summed[12],
        summed[13],
    )


def dot_t(a, b):
    return lax.dot_general(a, b, (((1,), (1,)), ((), ())), preferred_element_type=f32)

def dot_n(a, b):
    return lax.dot_general(a, b, (((1,), (0,)), ((), ())), preferred_element_type=f32)

def dot_0(a, b):
    return lax.dot_general(a, b, (((0,), (0,)), ((), ())), preferred_element_type=f32)

def lanes(shape):
    return lax.broadcasted_iota(jnp.int32, shape, len(shape) - 1)

def query_marks(seg_row):
    wide = jnp.broadcast_to(seg_row, (128, seg_row.shape[1])).T
    return (wide == lanes(wide.shape)).astype(f32).astype(bf16)

def half_lanes(tile, half):
    wide = tile.astype(f32)
    if half:
        wide = pltpu.roll(wide, 64, 1)
    return jnp.where(lanes(wide.shape) < 64, wide, 0.0).astype(bf16)

def key_steps(bounds, low, high):
    chunks, keys = bounds.shape
    first = sum(jnp.where(bounds[t, keys - 1] < low, 1, 0) for t in range(chunks))
    last = sum(jnp.where(bounds[t, 0] <= high, 1, 0) for t in range(chunks))
    pairs = (last - first + 1) // 2
    start = jnp.minimum(first, chunks - 2 * pairs)
    return start, pairs // 2, lax.rem(pairs, 2)


def walk(step, fours, twos, carry):
    carry = lax.fori_loop(0, fours, lambda t, c: step(4, 4 * t, c), carry)
    return lax.fori_loop(0, twos, lambda t, c: step(2, 4 * fours, c), carry)


def attn_fwd_kernel(
    q_hbm, kv_hbm, seg_q_hbm, seg_k_hbm, o_hbm, of_hbm, lse_hbm, kv2_hbm, kvt_hbm,
    q_ref, kv_ref, seg_q_ref, seg_k_ref, bounds, o_ref, of_ref, lse_ref, kv2_ref, kvt_ref, vo_ref, in_sem, out_sem,
):
    loads = copies(
        [(seg_q_hbm, seg_q_ref), (seg_k_hbm, seg_k_ref), (seg_k_hbm, bounds), (kv_hbm, kv_ref), (q_hbm, q_ref)], in_sem
    )
    wait_all(loads)
    chunks, keys = seg_k_ref.shape
    log_scale = math.log2(math.e) * DH ** (-0.5)

    def prepare(t, c):
        rows = pl.ds(pl.multiple_of(t * keys, keys), keys)
        kv = kv_ref[rows, :]
        marks = jnp.where(seg_k_ref[pl.ds(t, 1), :] == rows_of((128, keys)), 0.0, FAR)
        kvt_ref[0:128, rows] = kv.T
        kvt_ref[128:256, rows] = marks.astype(bf16)
        kv2_ref[rows, 0:128] = kv
        kv2_ref[rows, 128:256] = marks.T.astype(bf16)
        vo_ref[rows, :] = jnp.where(lanes(kv.shape) < 64, 1.0, kv.astype(f32)).astype(bf16)
        return c

    lax.fori_loop(0, chunks, prepare, 0)
    stores = copies([(kv2_ref, kv2_hbm), (kvt_ref, kvt_hbm)], out_sem)

    def tile(j, c):
        q_tile = q_ref[j]
        rows = q_tile.shape[0]
        outs = []
        for half in range(2):
            i = half * (chunks // 2) + j
            left = half_lanes(q_tile, half)
            left = jnp.concatenate([left, query_marks(seg_q_ref[pl.ds(i, 1), :])], axis=1)
            low, high = bounds[i, 0], bounds[i, keys - 1]
            start, fours, twos = key_steps(bounds, low, high)

            def step(width, t, carry):
                top, acc = carry
                at = pl.ds(pl.multiple_of((start + t) * keys, keys), width * keys)
                s = dot_n(left, kvt_ref[:, at])
                new = jnp.maximum(top, jnp.max(s, axis=1, keepdims=True))
                p = jnp.exp2((s - new) * log_scale)
                acc = acc * jnp.exp2((top - new) * log_scale) + dot_n(p.astype(bf16), vo_ref[at, :])
                return new, acc

            carry = (jnp.full((rows, 1), FAR, f32), jnp.zeros((rows, 128), f32))
            top, acc = walk(step, fours, twos, carry)
            total = pltpu.roll(acc, 64, 1)
            outs.append(acc / total)
            lse = jnp.broadcast_to(top * log_scale, acc.shape) + jnp.log2(acc)
            lse_ref[pl.ds(i, 1), :] = lse.T[0:1, :]
        o = jnp.where(lanes(outs[0].shape) < 64, pltpu.roll(outs[0], 64, 1), outs[1])
        of_ref[j] = o
        o_ref[j] = o.astype(bf16)
        return c

    lax.fori_loop(0, chunks // 2, tile, 0)
    stores += copies([(o_ref, o_hbm), (of_ref, of_hbm), (lse_ref, lse_hbm)], out_sem.at[pl.ds(2, 3)])
    wait_all(stores)


def attn_fwd(q, kv, seg_q, seg_k):
    chunks, keys = seg_k.shape
    dma = pltpu.SemaphoreType.DMA
    shapes = (
        (q.shape, bf16), (q.shape, f32), (seg_q.shape, f32), ((chunks * keys, 256), bf16), ((256, chunks * keys), bf16)
    )
    return pl.pallas_call(
        attn_fwd_kernel,
        out_shape=[jax.ShapeDtypeStruct(shape, kind) for shape, kind in shapes],
        in_specs=any_specs(4),
        out_specs=any_specs(5),
        scratch_shapes=[
            *[pltpu.VMEM(a.shape, a.dtype) for a in (q, kv, seg_q, seg_k)],
            pltpu.SMEM(seg_k.shape, jnp.int32),
            *[pltpu.VMEM(shape, kind) for shape, kind in shapes],
            pltpu.VMEM((chunks * keys, 128), bf16),
            dma((5,)),
            dma((5,)),
        ],
        compiler_params=pltpu.CompilerParams(vmem_limit_bytes=VMEM_BYTES),
        cost_estimate=pl.CostEstimate(flops=10**10, bytes_accessed=10**7, transcendentals=10**7),
        name="attn_fwd",
    )(q, kv, seg_q, seg_k)


def attn_bwd_kernel(
    q_hbm, do_hbm, of_hbm, lse_hbm, kv2_hbm, kvt_hbm, seg_q_hbm, seg_k_hbm, pass1, pass2, dq_hbm, dkv_hbm, out1, out2,
    q_ref, do_ref, of_ref, lse_ref, kv2_ref, kvt_ref, seg_q_ref, bounds, dq_ref, dkv_low, dkv_ref, hold1, hold2, in_sem, out_sem,
):
    loads = copies(
        [
            (q_hbm, q_ref), (do_hbm, do_ref), (of_hbm, of_ref), (lse_hbm, lse_ref), (kv2_hbm, kv2_ref),
            (seg_q_hbm, seg_q_ref), (seg_k_hbm, bounds),
            (pass1, hold1), (pass2, hold2), (kvt_hbm, kvt_ref),
        ],
        in_sem,
    )
    dkv_ref[...] = jnp.zeros_like(dkv_ref)
    wait_all(loads)
    stores = copies([(hold1, out1), (hold2, out2)], out_sem)
    chunks, keys = bounds.shape
    log_scale = math.log2(math.e) * DH ** (-0.5)

    def tile(j, c):
        q_tile, do_tile = q_ref[j], do_ref[j]
        rows = q_tile.shape[0]
        prod = do_tile.astype(f32) * of_ref[j]
        prod = prod.T
        dqs = []
        for half in range(2):
            i = half * (chunks // 2) + j
            left = half_lanes(q_tile, half)
            grad = do_tile.astype(f32)
            if not half:
                grad = pltpu.roll(grad, 64, 1)
            grad = jnp.where(lanes(grad.shape) < 64, 0.0, grad).astype(bf16)
            delta = jnp.sum(prod[64 * half:64 * half + 64], axis=0, keepdims=True)
            lse = lse_ref[pl.ds(i, 1), :]
            both = jnp.concatenate([left, grad], axis=0)
            marks = query_marks(seg_q_ref[pl.ds(i, 1), :])
            right = jnp.concatenate([both, jnp.concatenate([marks, jnp.zeros_like(marks)], axis=0)], axis=1).T
            low, high = bounds[i, 0], bounds[i, keys - 1]
            start, fours, twos = key_steps(bounds, low, high)

            def step(width, t, dq):
                at = pl.ds(pl.multiple_of((start + t) * keys, keys), width * keys)
                sdp = dot_n(kv2_ref[at, :], right)
                p = jnp.exp2(sdp[:, :rows] * log_scale - lse)
                ds = (p * (sdp[:, rows:] - delta)).astype(bf16)
                dkv_ref[at, :] += dot_n(jnp.concatenate([ds, p.astype(bf16)], axis=1), both)
                return dq + dot_n(kvt_ref[0:128, at], ds)

            dqs.append(walk(step, fours, twos, jnp.zeros((128, rows), f32)).T)
        dq = jnp.where(lanes(dqs[0].shape) < 64, dqs[0], pltpu.roll(dqs[1], 64, 1))
        dq_ref[j] = (dq * DH ** (-0.5)).astype(bf16)
        return c

    lax.fori_loop(0, chunks // 2, tile, 0)
    dkv = dkv_ref[...]
    dkv_low[...] = jnp.where(lanes(dkv.shape) < 64, dkv * DH ** (-0.5), dkv).astype(bf16)
    stores += copies([(dq_ref, dq_hbm), (dkv_low, dkv_hbm)], out_sem.at[pl.ds(2, 2)])
    wait_all(stores)


def attn_bwd(q, do, of, lse, kv2, kvt, seg_q, seg_k, pass1, pass2):
    dma = pltpu.SemaphoreType.DMA
    shapes = ((q.shape, bf16), ((kv2.shape[0], 128), bf16))
    return pl.pallas_call(
        attn_bwd_kernel,
        out_shape=[jax.ShapeDtypeStruct(shape, kind) for shape, kind in shapes]
        + [jax.ShapeDtypeStruct(a.shape, a.dtype) for a in (pass1, pass2)],
        in_specs=any_specs(10),
        out_specs=any_specs(4),
        scratch_shapes=[
            *[pltpu.VMEM(a.shape, a.dtype) for a in (q, do, of, lse, kv2, kvt, seg_q)],
            pltpu.SMEM(seg_k.shape, jnp.int32),
            *[pltpu.VMEM(shape, kind) for shape, kind in shapes],
            pltpu.VMEM((kv2.shape[0], 128), f32),
            *[pltpu.VMEM(a.shape, a.dtype) for a in (pass1, pass2)],
            dma((10,)),
            dma((4,)),
        ],
        compiler_params=pltpu.CompilerParams(vmem_limit_bytes=VMEM_BYTES),
        name="attn_bwd",
    )(q, do, of, lse, kv2, kvt, seg_q, seg_k, pass1, pass2)


class Spot:
    def __init__(self, nb):
        self.nb, self.nz = nb, nb // 2
        self.h, b = lax.axis_index("head"), lax.axis_index("blk")
        self.z, self.c = b // 2, lax.rem(b, 2)
        self.near = (self.h + 1 - 2 * lax.rem(self.h, 2), lax.rem(self.h + 2, 4))
        self.diag = 3 - self.h
        self.me = self.h * nb + b

    def index(self, h, z, c):
        return h * self.nb + z * 2 + c

    def ahead(self, k):
        return lax.rem(self.z + k, self.nz)


def remote(src, dst, send, recv, h, b):
    return pltpu.make_async_remote_copy(
        src_ref=src,
        dst_ref=dst,
        send_sem=send,
        recv_sem=recv,
        device_id={"head": h, "blk": b},
        device_id_type=MESH,
    )


def each(count, body, start=0):
    def run(i, c):
        body(i)
        return c

    lax.fori_loop(start, count, run, 0)


def hail(h, b):
    pl.semaphore_signal(
        pltpu.get_barrier_semaphore(), inc=1, device_id={"head": h, "blk": b}, device_id_type=MESH
    )


def greet_near(s):
    for k in range(1, s.nz):
        hail(s.h, s.ahead(k) * 2 + s.c)
    for i in range(1, 4):
        hail(lax.rem(s.h + i, 4), s.z * 2 + s.c)
    hail(s.h, s.z * 2 + 1 - s.c)
    pl.semaphore_wait(pltpu.get_barrier_semaphore(), s.nz + 3)


def greet_core(s):
    def signal(i):
        t = lax.rem(s.me + 2 * i, 4 * s.nb)
        hail(t // s.nb, lax.rem(t, s.nb))

    each(2 * s.nb, signal, 1)
    hail(s.h, s.z * 2 + 1 - s.c)
    pl.semaphore_wait(pltpu.get_barrier_semaphore(), 2 * s.nb)


def halves(shape):
    rows, width = shape
    if width > 128:
        return [(slice(None), slice(w * width // 2, (w + 1) * width // 2)) for w in range(2)]
    return [(slice(w * rows // 2, (w + 1) * rows // 2), slice(None)) for w in range(2)]


class Gather:
    def __init__(self, spot, shard, full, send, recv, local):
        self.s, self.full, self.local = spot, full, local
        self.shard = shard if callable(shard) else lambda z: shard
        self.send, self.recv = send, recv
        self.cut = halves(full.shape[1:])

    def copy(self, src, dst, k, h, z, c, recv_k=None):
        recv_k = k if recv_k is None else recv_k
        return remote(src, dst, self.send.at[k], self.recv.at[recv_k], h, z * 2 + c)

    def to_z(self, z):
        s = self.s
        return self.copy(self.shard(z), self.full.at[s.me], z, s.h, z, s.c, s.z)

    def from_z(self, z):
        s = self.s
        slot = self.full.at[s.index(s.h, z, s.c)]
        return self.copy(slot, slot, z, s.h, z, s.c)

    def near(self, w, z, own=False):
        s = self.s
        slot = self.full.at[s.index(s.h, z, s.c)]
        return self.copy(self.shard(s.z) if own else slot, slot, (1 + w) * s.nz + z, s.near[w], s.z, s.c)

    def from_near(self, w, z):
        s = self.s
        slot = self.full.at[s.index(s.near[w], z, s.c)]
        return self.copy(slot, slot, (1 + w) * s.nz + z, s.near[w], s.z, s.c)

    def lanes(self, slot, w):
        return slot.at[self.cut[w]]

    def onward(self, w, z):
        s = self.s
        slot = self.lanes(self.full.at[s.index(s.near[w], z, s.c)], w)
        return self.copy(slot, slot, (3 + w) * s.nz + z, s.near[1 - w], s.z, s.c)

    def from_onward(self, w, z):
        s = self.s
        slot = self.lanes(self.full.at[s.index(s.diag, z, s.c)], w)
        return self.copy(slot, slot, (3 + w) * s.nz + z, s.near[1 - w], s.z, s.c)

    def twin(self, h, z, own=False):
        s = self.s
        slot = self.full.at[s.index(h, z, s.c)]
        return self.copy(self.shard(s.z) if own else slot, slot, 5 * s.nz + h * s.nz + z, s.h, s.z, 1 - s.c)

    def from_twin(self, h, z):
        s = self.s
        slot = self.full.at[s.index(h, z, 1 - s.c)]
        return self.copy(slot, slot, 5 * s.nz + h * s.nz + z, s.h, s.z, 1 - s.c)

    def begin(self):
        s = self.s
        each(s.nz, lambda k: self.to_z(s.ahead(k)).start(), 1)

    def begin_near(self):
        s = self.s
        self.own = pltpu.make_async_copy(self.shard(s.z), self.full.at[s.me], self.local)
        self.own.start()
        self.near(0, s.z, True).start()
        self.near(1, s.z, True).start()
        self.twin(s.h, s.z, True).start()

    def spread(self):
        s = self.s

        def go(k):
            z = s.ahead(k)
            self.from_z(z).wait_recv()
            self.near(0, z).start()
            self.near(1, z).start()
            self.twin(s.h, z).start()

        each(s.nz, go, 1)

    def cross(self):
        s = self.s

        def go(k):
            z = s.ahead(k)
            for w in range(2):
                self.from_near(w, z).wait_recv()
                self.onward(w, z).start()
                self.twin(s.near[w], z).start()

        each(s.nz, go)

    def last(self):
        s = self.s

        def go(k):
            z = s.ahead(k)
            for w in range(2):
                self.from_onward(w, z).wait_recv()
            self.twin(s.diag, z).start()

        each(s.nz, go)

    def arrive(self):
        s = self.s
        each(4, lambda h: each(s.nz, lambda z: self.from_twin(h, z).wait_recv()))
        self.own.wait()

    def sent(self):
        s = self.s
        each(s.nz, lambda k: self.to_z(s.ahead(k)).wait_send(), 1)

        def go(z):
            for w in range(2):
                self.near(w, z).wait_send()
                self.onward(w, z).wait_send()
            each(4, lambda h: self.twin(h, z).wait_send())

        each(s.nz, go)


class Scatter:
    def __init__(self, spot, part, twin, diag, near, line, send, recv):
        self.s, self.part, self.t, self.d, self.n, self.l = spot, part, twin, diag, near, line
        self.send, self.recv = send, recv
        self.cut = halves(part.shape[1:])
        self.axis = 1 if self.cut[0][0] == slice(None) else 0

    def copy(self, src, dst, k, h, z, c, recv_k=None):
        recv_k = k if recv_k is None else recv_k
        return remote(src, dst, self.send.at[k], self.recv.at[recv_k], h, z * 2 + c)

    def mine(self, h, z):
        return h * self.s.nz + z if self.t is None else self.s.index(h, z, self.s.c)

    def to_twin(self, h, z):
        s = self.s
        src = self.part.at[s.index(h, z, 1 - s.c)]
        return self.copy(src, self.t.at[h, z], h * s.nz + z, s.h, s.z, 1 - s.c)

    def to_diag(self, w, z):
        s = self.s
        src = self.part.at[self.mine(s.diag, z)].at[self.cut[w]]
        return self.copy(src, self.d.at[w, z], (4 + w) * s.nz + z, s.near[w], s.z, s.c)

    def to_near(self, w, z):
        s = self.s
        src = self.part.at[self.mine(s.near[w], z)]
        return self.copy(src, self.n.at[w, z], (6 + w) * s.nz + z, s.near[w], s.z, s.c)

    def to_line(self, z):
        s = self.s
        src = self.part.at[self.mine(s.h, z)]
        return self.copy(src, self.l.at[s.z], 8 * s.nz + z, s.h, z, s.c, 8 * s.nz + s.z)

    def from_line(self, z):
        s = self.s
        src = self.part.at[self.mine(s.h, z)]
        return self.copy(src, self.l.at[z], 8 * s.nz + z, s.h, z, s.c)

    def begin(self):
        each(4, lambda h: each(self.s.nz, lambda z: self.to_twin(h, z).start()))

    def pair(self, h, z):
        if self.t is None:
            return self.part[self.mine(h, z)].astype(f32)
        self.to_twin(h, z).wait_recv()
        return self.part[self.mine(h, z)].astype(f32) + self.t[h, z].astype(f32)

    def keep(self, h, z, value):
        self.part[self.mine(h, z)] = value.astype(self.part.dtype)

    def first(self):
        s = self.s

        def go(k):
            z = s.ahead(k)
            if self.t is not None:
                self.keep(s.diag, z, self.pair(s.diag, z))
            for w in range(2):
                self.to_diag(w, z).start()

        each(s.nz + 1, go, 1)

    def second(self):
        s = self.s

        def go(k):
            z = s.ahead(k)
            for w in range(2):
                value = self.pair(s.near[w], z)
                self.to_diag(1 - w, z).wait_recv()
                other = self.d[1 - w, z].astype(f32)
                pieces = [value[cut] for cut in self.cut]
                pieces[1 - w] = pieces[1 - w] + other
                value = jnp.concatenate(pieces, axis=self.axis)
                self.keep(s.near[w], z, value)
                self.to_near(w, z).start()

        each(s.nz + 1, go, 1)

    def joined(self, z):
        value = self.pair(self.s.h, z)
        for w in range(2):
            self.to_near(w, z).wait_recv()
            value = value + self.n[w, z].astype(f32)
        return value

    def third(self):
        s = self.s

        def go(k):
            z = s.ahead(k)
            self.keep(s.h, z, self.joined(z))
            self.to_line(z).start()

        each(s.nz, go, 1)

    def columns(self):
        s = self.s
        self.l[s.z] = self.joined(s.z).astype(self.l.dtype)
        each(s.nz, lambda k: self.from_line(s.ahead(k)).wait_recv(), 1)
        return [self.l[w].astype(f32) + self.l[w + 2].astype(f32) for w in range(2)]

    def total(self):
        s = self.s
        value = self.joined(s.z)

        def go(k, value):
            z = s.ahead(k)
            self.from_line(z).wait_recv()
            return value + self.l[z].astype(f32)

        return lax.fori_loop(1, s.nz, go, value)

    def sent(self):
        s = self.s

        def go(z):
            if self.t is not None:
                each(4, lambda h: self.to_twin(h, z).wait_send())
            for w in range(2):
                self.to_diag(w, z).wait_send()
                self.to_near(w, z).wait_send()

        each(s.nz, go)
        each(s.nz, lambda k: self.to_line(s.ahead(k)).wait_send(), 1)


class Exchange:
    def __init__(self, spot, src, dst, send, recv, local):
        self.s, self.src, self.dst, self.send, self.recv, self.local = spot, src, dst, send, recv, local
        self.g = spot.me // 2

    def copy(self, i, back=False):
        s = self.s
        to = lax.rem(self.g + i, 16)
        t = to * 2 + s.c
        src = self.src(to)
        dst = self.dst(lax.rem(self.g + 16 - i, 16)) if back else self.dst(self.g)
        return remote(src, dst, self.send.at[i], self.recv.at[i], t // s.nb, lax.rem(t, s.nb))

    def own(self):
        return pltpu.make_async_copy(self.src(self.g), self.dst(self.g), self.local)

    def begin(self):
        self.own().start()
        each(16, lambda i: self.copy(i).start(), 1)

    def arrive(self, i):
        self.copy(i, True).wait_recv()

    def end(self):
        each(16, self.arrive, 1)
        self.sent()

    def sent(self):
        self.own().wait()
        each(16, lambda i: self.copy(i).wait_send(), 1)


class Plane:
    def __init__(self, spot, send, recv):
        self.s, self.send, self.recv = spot, send, recv

    def to(self, k):
        return lax.rem(self.s.h + k, 4)

    def frm(self, k):
        return lax.rem(self.s.h + 4 - k, 4)

    def copy(self, src, dst, j, at_send, at_recv):
        s = self.s
        return remote(src, dst, self.send.at[at_send], self.recv.at[at_recv], j, s.z * 2 + s.c)


def pair_of(g):
    return lax.rem(g, 4) * 4 + g // 4


def weave(left, right):
    kind = left.dtype
    left, right = left.astype(f32), right.astype(f32)
    low = lanes(left.shape) < 64
    first = jnp.where(low, left, pltpu.roll(right, 64, 1)).astype(kind)
    second = jnp.where(low, pltpu.roll(left, 64, 1), right).astype(kind)
    return first, second


def any_specs(count):
    return [pl.BlockSpec(memory_space=pl.ANY)] * count


def copies(pairs, sems):
    jobs = [pltpu.make_async_copy(src, dst, sems.at[k]) for k, (src, dst) in enumerate(pairs)]
    for job in jobs:
        job.start()
    return jobs


def wait_all(jobs):
    for job in jobs:
        job.wait()


def rows_of(shape):
    return lax.broadcasted_iota(jnp.int32, shape, 0)


def spread_row(block, width, each_lane):
    count = block.shape[0]
    pick = (rows_of((128, width)) == lax.rem(lanes((128, width)), each_lane)).astype(f32).astype(bf16)
    wide = dot_n(block.astype(bf16), pick)
    return column_sum(jnp.where(rows_of((count, width)) == lanes((count, width)) // each_lane, wide, 0.0))


def gather_row(row, count, each_lane):
    width = row.shape[1]
    wide = jnp.where(rows_of((count, width)) == lanes((count, width)) // each_lane, row, 0.0)
    pick = (lanes((width, 128)) == lax.rem(rows_of((width, 128)), each_lane)).astype(f32)
    return lax.dot_general(
        wide, pick, (((1,), (0,)), ((), ())), precision=lax.Precision.HIGHEST, preferred_element_type=f32
    )


class Line:
    def __init__(self, spot, shard, full, send, recv, local):
        self.s, self.shard, self.full, self.send, self.recv = spot, shard, full, send, recv
        self.own = pltpu.make_async_copy(shard, full.at[spot.z], local)

    def copy(self, way, t):
        s = self.s
        k = 2 * t + (way + 1) // 2
        src = self.full.at[s.z - way * t] if t else self.shard
        dst = self.full.at[s.z - way * t]
        return remote(src, dst, self.send.at[k], self.recv.at[k], s.h, (s.z + way) * 2 + s.c)

    def inside(self, z):
        return (z >= 0) & (z < self.s.nz)

    def sends(self, t, act):
        for way in (1, -1):
            z = self.s.z

            @pl.when(self.inside(z + way) & self.inside(z - way * t))
            def _():
                act(self.copy(way, t))

    def arrive(self, t):
        for way in (1, -1):
            s = self.s

            @pl.when(self.inside(s.z - way * (t + 1)))
            def _():
                slot = self.full.at[s.z - way * (t + 1)]
                k = 2 * t + (way + 1) // 2
                remote(slot, slot, self.send.at[k], self.recv.at[k], s.h, (s.z - way) * 2 + s.c).wait_recv()

    def begin(self):
        self.own.start()
        self.sends(0, lambda copy: copy.start())

    def onward(self, t):
        self.arrive(t)
        if t + 1 < self.s.nz - 1:
            self.sends(t + 1, lambda copy: copy.start())

    def sent(self):
        self.own.wait()
        for t in range(self.s.nz - 1):
            self.sends(t, lambda copy: copy.wait_send())


def project_kernel(n, nb, *refs):
    x_hbm, wq_hbm, wk_hbm, wv_hbm, wo_hbm, wu_hbm, wd_hbm, seg_hbm = refs[:8]
    smalls = refs[8:16]
    q_out, kv_out, x_out, wa_out, fz_out, par_out, bup_out, segk_out, segq_out = refs[16:25]
    (
        x, wq, wk, wv, wo, wu, wd, seg, *small, bup_small, vec, sa, sb, wa, x_all, kv_send, q_send,
        par, bup, segk, segq,
        in_sem, out_sem, w_send, w_recv, w_local, f_send, f_recv, f_local,
        x_send, x_recv, x_local, ex_send, ex_recv, ex_local, tw_send, tw_recv,
    ) = refs[25:]
    s = Spot(nb)
    loads = copies(
        [(wq_hbm, wq), (wk_hbm, wk), (wv_hbm, wv), (seg_hbm, seg), (smalls[0], bup_small)]
        + [(smalls[k], small[k - 1]) for k in range(1, 8)]
        + [(x_hbm, x), (wo_hbm, wo), (wu_hbm, wu), (wd_hbm, wd)],
        in_sem,
    )
    greet_near(s)

    def pass_x(z, slot):
        return remote(x.at[z // 2], x_all.at[slot], x_send.at[z], x_recv.at[slot], s.h, z * 2 + s.c)

    wait_all(loads[:13])
    vec[...] = jnp.zeros_like(vec)
    vec[0:1, 0:64] = bup_small[...].astype(f32).reshape(1, 64)
    for k in range(7):
        vec[k + 1:k + 2, 0:16] = small[k][...].astype(f32).reshape(1, 16)
    vec[8:10, :] = seg[...].astype(f32)
    for t in range(4):
        tile, at = slice(128 * t, 128 * t + 128), 256 * (t % 2)
        first, second = weave(wk[:, tile], wv[:, tile])
        sa[t // 2, :, at:at + 128] = first
        sa[t // 2, :, at + 128:at + 256] = second
    for w in range(2):
        sa[w, :, 512:768] = wq[:, 256 * w:256 * w + 256]
        sa[w, :, 768:896] = vec[...].astype(bf16)

    def w_line(z, slot):
        return remote(
            sa.at[lax.rem(z, 2)], wa.at[s.h, slot, s.c], w_send.at[z], w_recv.at[slot], s.h, z * 2 + s.c
        )

    def w_plane(j, h):
        slot = wa.at[h, :, s.c]
        return remote(slot, slot, w_send.at[4 + j], w_recv.at[4 + h], j, s.z * 2 + s.c)

    def w_twin(h, c):
        slot = wa.at[h, :, c]
        return remote(slot, slot, w_send.at[8 + h], w_recv.at[8 + h], s.h, s.z * 2 + 1 - s.c)

    each(s.nz, lambda k: w_line(s.ahead(k), s.z).start(), 1)
    own_w = pltpu.make_async_copy(sa.at[lax.rem(s.z, 2)], wa.at[s.h, s.z, s.c], w_local)
    own_w.start()
    each(s.nz, lambda k: pass_x(s.ahead(k), s.z).start(), 1)
    own_x = pltpu.make_async_copy(x.at[s.z // 2], x_all.at[s.z], x_local)
    own_x.start()
    wait_all(loads[13:])
    sb[:, 0:512] = wo[...]
    sb[:, 512:2560] = wu[...]
    for t in range(4):
        sb[:, 2560 + 512 * t:3072 + 512 * t] = wd[16 * t:16 * t + 16, :]
    line = Line(s, sb, fz_out, f_send, f_recv, f_local)
    line.begin()
    own_w.wait()
    each(s.nz, lambda k: w_line(s.ahead(k), s.ahead(k)).wait_recv(), 1)
    each(4, lambda i: w_plane(lax.rem(s.h + i, 4), s.h).start(), 1)
    w_twin(s.h, s.c).start()

    def w_arrive(i):
        h = lax.rem(s.h + 4 - i, 4)
        w_plane(h, h).wait_recv()
        w_twin(h, s.c).start()

    each(4, w_arrive, 1)
    each(4, lambda h: w_twin(h, 1 - s.c).wait_recv())
    outs = copies([(wa, wa_out)], out_sem)
    own_x.wait()
    plane = [Plane(s, ex_send.at[k], ex_recv.at[k]) for k in range(2)]
    kinds = ((kv_send, lambda g: kv_out.at[:, g, s.c]), (q_send, lambda g: q_out.at[:, g]))

    def block(w, j, z):
        src, dst = kinds[w]
        return plane[w].copy(src.at[j, z], dst(s.h * 4 + z), j, j * 4 + z, s.h * 4 + z)

    def from_block(w, j, z):
        src, dst = kinds[w]
        slot = dst(j * 4 + z)
        return plane[w].copy(slot, slot, j, j * 4 + z, j * 4 + z)

    def own_block(w, z):
        src, dst = kinds[w]
        return pltpu.make_async_copy(src.at[s.h, z], dst(s.h * 4 + z), ex_local.at[w, z])

    def twin(src, j, z, c):
        slot = kv_out.at[:, j * 4 + z, c]
        k = j * 4 + z
        return remote(slot if src is None else src, slot, tw_send.at[k], tw_recv.at[k], s.h, s.z * 2 + 1 - s.c)

    def project_rows(k):
        z = s.ahead(k)
        qkv = dot_n(x_all[z], wa[:, :, :, :, 0:768].reshape(512, 768)).astype(bf16)
        for j in range(4):
            kv_send[j, z] = qkv[:, 128 * j:128 * j + 128].reshape(8, 16, 128)
        for t in range(2):
            tile = qkv[:, 512 + 128 * t:640 + 128 * t]
            first, second = weave(tile[0:64], tile[64:128])
            q_send[2 * t, z] = first.reshape(4, 16, 128)
            q_send[2 * t + 1, z] = second.reshape(4, 16, 128)
        for w in range(2):
            each(4, lambda i: block(w, plane[w].to(i), z).start(), 1)
            own_block(w, z).start()
        twin(kv_send.at[s.h, z], s.h, z, s.c).start()

    project_rows(0)

    def project_next(k):
        z = s.ahead(k)
        pass_x(z, z).wait_recv()
        project_rows(k)

    each(s.nz, project_next, 1)
    line.onward(0)
    line.onward(1)
    vecs = wa[:, :, :, :, 768:896].reshape(n, 16, 128).astype(f32)
    outs += copies([(x_all, x_out)], out_sem.at[pl.ds(5, 1)])
    bup[...] = spread_row(vecs[:, 0, :], 2048, 64)
    for k in range(7):
        par[k:k + 1, :] = spread_row(vecs[:, k + 1, :], 512, 16)
    par[7:8, :] = jnp.zeros((1, 512), f32)
    ids = jnp.where(s.z < 2, vecs[:, 8, :], vecs[:, 9, :]).astype(bf16)
    for i in range(8):
        pick = (rows_of((128, 512)) == 16 * i + lax.rem(lanes((128, 512)), 16)).astype(f32).astype(bf16)
        wide = dot_n(ids, pick)
        source = rows_of((n, 512))
        row = jnp.where(source == lanes((n, 512)) // 16, wide, 0.0)
        segk[i:i + 1, :] = column_sum(row).astype(jnp.int32)
        source = rows_of((n, 256))
        own = (source // 2 == lanes((n, 256)) // 16) & (lax.rem(source, 2) == s.c)
        segq[i:i + 1, :] = column_sum(jnp.where(own, wide[:, 0:256], 0.0)).astype(jnp.int32)
    outs += copies([(par, par_out), (bup, bup_out), (segk, segk_out), (segq, segq_out)], out_sem.at[pl.ds(1, 4)])
    def forward(i):
        j = plane[0].frm(i)

        def go(k):
            z = s.ahead(k)
            from_block(0, j, z).wait_recv()
            twin(None, j, z, s.c).start()

        each(s.nz, go)

    each(4, forward, 1)
    line.onward(2)
    each(4, lambda i: each(s.nz, lambda z: from_block(1, plane[1].frm(i), z).wait_recv()), 1)
    each(4, lambda j: each(s.nz, lambda z: twin(None, j, z, 1 - s.c).wait_recv()))
    each(4, lambda j: each(s.nz, lambda z: twin(None, j, z, s.c).wait_send()))
    for w in range(2):
        each(s.nz, lambda z: own_block(w, z).wait())
        each(4, lambda i: each(s.nz, lambda z: block(w, plane[w].to(i), z).wait_send()), 1)
    each(s.nz, lambda k: pass_x(s.ahead(k), s.z).wait_send(), 1)
    each(s.nz, lambda k: w_line(s.ahead(k), s.z).wait_send(), 1)
    each(4, lambda i: w_plane(lax.rem(s.h + i, 4), s.h).wait_send(), 1)
    each(4, lambda h: w_twin(h, s.c).wait_send())
    line.sent()
    wait_all(outs)


def project(n, nb, x, wq, wk, wv, wo, wu, wd, seg, smalls):
    dma = pltpu.SemaphoreType.DMA
    nz = nb // 2
    return pl.pallas_call(
        functools.partial(project_kernel, n, nb),
        out_shape=(
            jax.ShapeDtypeStruct((4, 16, 16, 128), bf16),
            jax.ShapeDtypeStruct((8, 16, 2, 16, 128), bf16),
            jax.ShapeDtypeStruct((nz, 128, 512), bf16),
            jax.ShapeDtypeStruct((4, nz, 2, 16, 896), bf16),
            jax.ShapeDtypeStruct((nz, 16, 4608), bf16),
            jax.ShapeDtypeStruct((8, 512), f32),
            jax.ShapeDtypeStruct((1, 2048), f32),
            jax.ShapeDtypeStruct((8, 512), jnp.int32),
            jax.ShapeDtypeStruct((8, 256), jnp.int32),
        ),
        in_specs=any_specs(16),
        out_specs=any_specs(9),
        scratch_shapes=[
            pltpu.VMEM(x.shape, bf16),
            pltpu.VMEM((16, 512), bf16),
            pltpu.VMEM((16, 512), bf16),
            pltpu.VMEM((16, 512), bf16),
            pltpu.VMEM((16, 512), bf16),
            pltpu.VMEM((16, 2048), bf16),
            pltpu.VMEM((64, 512), bf16),
            pltpu.VMEM((2, 128), jnp.int32),
            *[pltpu.VMEM((16,), bf16)] * 7,
            pltpu.VMEM((64,), bf16),
            pltpu.VMEM((16, 128), f32),
            pltpu.VMEM((2, 16, 896), bf16),
            pltpu.VMEM((16, 4608), bf16),
            pltpu.VMEM((4, nz, 2, 16, 896), bf16),
            pltpu.VMEM((nz, 128, 512), bf16),
            pltpu.VMEM((4, nz, 8, 16, 128), bf16),
            pltpu.VMEM((4, nz, 4, 16, 128), bf16),
            pltpu.VMEM((8, 512), f32),
            pltpu.VMEM((1, 2048), f32),
            pltpu.VMEM((8, 512), jnp.int32),
            pltpu.VMEM((8, 256), jnp.int32),
            dma((16,)),
            dma((6,)),
            dma((12,)),
            dma((12,)),
            dma,
            dma((2 * nz,)),
            dma((2 * nz,)),
            dma,
            dma((nz,)),
            dma((nz,)),
            dma,
            dma((2, 4 * nz)),
            dma((2, 4 * nz)),
            dma((2, nz)),
            dma((4 * nz,)),
            dma((4 * nz,)),
        ],
        compiler_params=pltpu.CompilerParams(
            collective_id=1, has_side_effects=True, vmem_limit_bytes=VMEM_BYTES
        ),
        name="project",
    )(x, wq, wk, wv, wo, wu, wd, seg, *smalls)


def row_norm(v):
    mean = jnp.mean(v, axis=-1, keepdims=True)
    mid = v - mean
    inv = lax.rsqrt(jnp.mean(mid * mid, axis=-1, keepdims=True) + EPSILON)
    return mid * inv, inv


def row_norm_back(grad, normed, inv, gain):
    part = grad * gain
    return inv * (
        part
        - jnp.mean(part, axis=-1, keepdims=True)
        - normed * jnp.mean(part * normed, axis=-1, keepdims=True)
    )


def normal(u):
    bell = jnp.exp(-0.5 * u * u)
    t = 1.0 / (1.0 + (0.3275911 * 0.5**0.5) * jnp.abs(u))
    poly = 0.5 * 1.061405429
    for factor in (-1.453152027, 1.421413741, -0.284496736, 0.254829592):
        poly = poly * t + 0.5 * factor
    tail = poly * t * bell
    return jnp.where(u < 0, tail, 1.0 - tail), bell * ((2.0 * math.pi) ** -0.5)


def column_sum(v):
    return jnp.sum(v, axis=0, keepdims=True)


def middle_kernel(n, nb, *refs):
    o_hbm, x_hbm, y_hbm, g_hbm, fz_hbm, fx_hbm, fy_hbm, par_hbm, bup_hbm = refs[:9]
    outs_hbm = refs[10:16]
    do_out = refs[9]
    (
        o_in, x, y, g_in, wb, wd, par, bup, o_recv, do_send, slope,
        out, dacc_ref, dz1_ref, gvec, sum_b, sum_d, bias_up, omix, hid_ref, dur_ref, po, pu, pd, to, tu, td,
        in_sem, out_sem, ex_send, ex_recv, ex_local, f_send, f_recv, p_send, p_recv,
    ) = refs[16:]
    s = Spot(nb)
    loads = copies(
        [
            (o_hbm, o_in), (x_hbm, x), (y_hbm, y), (g_hbm, g_in), (par_hbm, par), (bup_hbm, bup),
            (fz_hbm, wb.at[s.h, :, s.c]), (fx_hbm, wb.at[s.near[0], :, s.c]), (fy_hbm, wb.at[s.near[1], :, s.c]),
        ],
        in_sem,
    )
    greet_core(s)
    loads[0].wait()
    o_ex = Exchange(
        s, lambda g: o_in.at[:, g], lambda g: o_recv.at[pair_of(g)], ex_send.at[0], ex_recv.at[0], ex_local.at[0]
    )
    o_ex.begin()
    cut = [pl.ds(0, 2304), pl.ds(2304, 2304)]
    heads = (s.h, s.near[0], s.near[1], s.diag)

    def onward(w, h, to):
        src = (fx_hbm, fy_hbm)[w].at[:, :, cut[w]]
        return remote(src, wb.at[h, :, s.c, :, cut[w]], f_send.at[4 + w], f_recv.at[4 + w], to, s.z * 2 + s.c)

    def twin(k, c):
        slot = wb.at[heads[k], :, c]
        src = (fz_hbm, fx_hbm, fy_hbm, slot)[k]
        return remote(src, slot, f_send.at[k], f_recv.at[k], s.h, s.z * 2 + 1 - s.c)

    for w in range(2):
        onward(w, s.near[w], s.near[1 - w]).start()
    for k in range(3):
        twin(k, s.c).start()
    for w in range(2):
        onward(w, s.diag, s.near[1 - w]).wait_recv()
    twin(3, s.c).start()
    o_ex.end()
    wait_all(loads[1:])
    for m in range(2):
        for t in range(4):
            first, second = weave(
                o_recv[8 * m + 2 * t].reshape(64, 128), o_recv[8 * m + 2 * t + 1].reshape(64, 128)
            )
            omix[128 * m:128 * m + 64, 128 * t:128 * t + 128] = first
            omix[128 * m + 64:128 * m + 128, 128 * t:128 * t + 128] = second
    gain1, bias1 = par[1:2], par[2:3]
    gain2, bias2 = par[3:4], par[4:5]
    gain3, bias3 = par[5:6], par[6:7]
    for k in range(4):
        twin(k, 1 - s.c).wait_recv()
    for t in range(4):
        for r in range(4):
            wd[t, :, :, r] = wb[t, :, :, :, 2560 + 512 * r:3072 + 512 * r]
    w_out = wb[:, :, :, :, 0:512].reshape(512, 512)
    a = dot_n(omix[...], w_out)
    n1, r1 = row_norm(x[...].astype(f32) + a)
    x1 = n1 * gain1 + bias1
    x1r = x1.astype(bf16)
    feed = jnp.zeros_like(x1)
    for t in range(4):
        cols = slice(512 * t, 512 * t + 512)
        u = dot_n(x1r, wb[:, :, :, :, 512 + 512 * t:1024 + 512 * t].reshape(512, 512)) + bup[:, cols]
        phi, density = normal(u)
        hid = (u * phi).astype(bf16)
        slope[:, cols] = phi + u * density
        hid_ref[:, cols] = hid
        feed = feed + dot_n(hid, wd[t].reshape(512, 512))
    feed = feed + par[0:1]
    n2, r2 = row_norm(x1 + feed)
    n3, r3 = row_norm(y[...].astype(f32) + a + feed)
    out[...] = (n2 * gain2 + bias2 + (n3 * gain3 + bias3)).astype(bf16)
    g = g_in[...].astype(f32)
    dacc = row_norm_back(g, n3, r3, gain3)
    dacc_ref[...] = dacc
    dz2 = row_norm_back(g, n2, r2, gain2)
    df = dz2 + dacc
    dfr = df.astype(bf16)
    swaps = [
        remote(part.at[:, :, 1 - s.c], there, p_send.at[k], p_recv.at[k], s.h, s.z * 2 + 1 - s.c)
        for k, (part, there) in enumerate(((pd, td), (pu, tu), (po, to)))
    ]
    for t in range(4):
        pd[t] = dot_0(hid_ref[:, 512 * t:512 * t + 512], dfr).astype(bf16).reshape(nb // 2, 2, 64, 512)
    swaps[0].start()
    dx1 = dz2
    for t in range(4):
        cols = slice(512 * t, 512 * t + 512)
        du = dot_t(dfr, wd[t].reshape(512, 512)) * slope[:, cols]
        bias_up[:, cols] = column_sum(du)
        dur = du.astype(bf16)
        dur_ref[:, cols] = dur
        dx1 = dx1 + dot_t(dur, wb[:, :, :, :, 512 + 512 * t:1024 + 512 * t].reshape(512, 512))
    dz1 = row_norm_back(dx1, n1, r1, gain1)
    dz1_ref[...] = dz1
    dar = (dz1 + dacc).astype(bf16)
    do = dot_t(dar, w_out).astype(bf16)
    for m in range(2):
        for t in range(4):
            tile = do[128 * m:128 * m + 128, 128 * t:128 * t + 128]
            first, second = weave(tile[0:64], tile[64:128])
            do_send[8 * m + 2 * t] = first.reshape(4, 16, 128)
            do_send[8 * m + 2 * t + 1] = second.reshape(4, 16, 128)
    do_ex = Exchange(
        s, lambda g: do_send.at[pair_of(g)], lambda g: do_out.at[:, g], ex_send.at[1], ex_recv.at[1], ex_local.at[1]
    )
    do_ex.begin()
    stores = copies(zip((out, dacc_ref, dz1_ref), outs_hbm[:3]), out_sem)
    for t in range(4):
        cols = slice(512 * t, 512 * t + 512)
        pu[:, :, :, :, cols] = dot_0(x1r, dur_ref[:, cols]).astype(bf16).reshape(4, nb // 2, 2, 16, 512)
    swaps[1].start()
    po[...] = dot_0(omix[...], dar).astype(bf16).reshape(po.shape)
    swaps[2].start()
    sum_g = column_sum(g)
    sums = (
        column_sum(df), column_sum(dx1 * n1), column_sum(dx1), column_sum(g * n2), sum_g, column_sum(g * n3), sum_g
    )
    gvec[...] = jnp.zeros_like(gvec)
    gvec[:, 0, :] = gather_row(bias_up[...], n, 64)
    for k in range(7):
        gvec[:, k + 1, :] = gather_row(sums[k], n, 16)
    stores += copies([(gvec, outs_hbm[3])], out_sem.at[pl.ds(3, 1)])
    for swap in swaps:
        swap.wait()

    def join(part, there):
        value = part[:, :, s.c].astype(f32) + there[...].astype(f32)
        return value.astype(bf16).reshape(-1, *value.shape[2:])

    sum_d[...] = join(pd, td)
    sum_b[:, :, 512:2560] = join(pu, tu)
    sum_b[:, :, 0:512] = join(po, to)
    stores += copies(zip((sum_b, sum_d), outs_hbm[4:6]), out_sem.at[pl.ds(4, 2)])
    do_ex.end()
    for w in range(2):
        onward(w, s.near[w], s.near[1 - w]).wait_send()
    for k in range(4):
        twin(k, s.c).wait_send()
    wait_all(stores)


def middle(n, nb, o, x, y, g, fz, fx, fy, par, bup):
    dma = pltpu.SemaphoreType.DMA
    rows = x.shape[0]
    nz = nb // 2
    saved = [
        ((rows, 512), bf16), ((rows, 512), f32), ((rows, 512), f32), ((n, 16, 128), f32),
        ((4 * nz, 16, 2560), bf16), ((4 * nz, 64, 512), bf16),
    ]
    return pl.pallas_call(
        functools.partial(middle_kernel, n, nb),
        out_shape=[jax.ShapeDtypeStruct((4, 16, 16, 128), bf16)]
        + [jax.ShapeDtypeStruct(shape, kind) for shape, kind in saved],
        in_specs=any_specs(9),
        out_specs=any_specs(7),
        scratch_shapes=[
            pltpu.VMEM(o.shape, bf16),
            pltpu.VMEM(x.shape, bf16),
            pltpu.VMEM(x.shape, bf16),
            pltpu.VMEM(x.shape, bf16),
            pltpu.VMEM((4, nb // 2, 2, 16, 4608), bf16),
            pltpu.VMEM((4, 4, 2, 4, 16, 512), bf16),
            pltpu.VMEM(par.shape, f32),
            pltpu.VMEM(bup.shape, f32),
            pltpu.VMEM((16, 4, 16, 128), bf16),
            pltpu.VMEM((16, 4, 16, 128), bf16),
            pltpu.VMEM((rows, 2048), f32),
            *[pltpu.VMEM(shape, kind) for shape, kind in saved],
            pltpu.VMEM((1, 2048), f32),
            pltpu.VMEM((rows, 512), bf16),
            pltpu.VMEM((rows, 2048), bf16),
            pltpu.VMEM((rows, 2048), bf16),
            *[pltpu.VMEM((4, nz, 2, *tail), bf16) for tail in ((16, 512), (16, 2048), (64, 512))],
            *[pltpu.VMEM((4, nz, *tail), bf16) for tail in ((16, 512), (16, 2048), (64, 512))],
            dma((9,)),
            dma((6,)),
            dma((2, 16)),
            dma((2, 16)),
            dma((2,)),
            dma((6,)),
            dma((6,)),
            dma((3,)),
            dma((3,)),
        ],
        compiler_params=pltpu.CompilerParams(
            collective_id=2, has_side_effects=True, vmem_limit_bytes=VMEM_BYTES
        ),
        name="middle",
    )(o, x, y, g, fz, fx, fy, par, bup)


def finish_kernel(n, nb, *refs):
    ins = refs[:8]
    outs = refs[8:16]
    (
        dq, dkv, xm, dz1, pb, pd, gvec, wa,
        pa, ta, da, na, la, db, nb_, lb, dd, nd, ld, tv, dv, nv, lv,
        twin_buf, dkv_send, dkv_recv, dq_recv, dqkv, dx_send, dx_recv, gx, gq, gk, gv, go, gu, gd, gs,
        in_sem, out_sem, rs_send, rs_recv, ex_send, ex_recv, dx_ssem, dx_rsem, tw_send, tw_recv,
    ) = refs[16:]
    s = Spot(nb)
    order = (1, 0, 4, 5, 6, 7, 2, 3)
    local = (dq, dkv, xm, dz1, pb, pd, gvec, wa)
    loads = copies([(ins[k], local[k]) for k in order], in_sem)
    greet_near(s)
    swap = remote(ins[1].at[:, :, 1 - s.c], twin_buf, tw_send, tw_recv, s.h, s.z * 2 + 1 - s.c)
    swap.start()
    jobs = [
        Scatter(s, *bufs, rs_send.at[k], rs_recv.at[k])
        for k, bufs in enumerate(
            ((pb, None, db, nb_, lb), (pd, None, dd, nd, ld), (gvec, tv, dv, nv, lv), (pa, ta, da, na, la))
        )
    ]
    wait_all(loads[:5])
    jobs[2].begin()
    swap.wait()

    def add(g):
        dkv_send[g] = (dkv[:, g, s.c].astype(f32) + twin_buf[:, g].astype(f32)).astype(bf16)

    each(4 * s.nz, add)
    plane = [Plane(s, ex_send.at[k], ex_recv.at[k]) for k in range(2)]

    def block(w, j, z, slot):
        g = j * s.nz + z
        src, dst = ((dkv_send.at[g], dkv_recv.at[slot, z]), (dq.at[:, g], dq_recv.at[slot, z]))[w]
        return plane[w].copy(src, dst, j, g, slot * s.nz + z)

    def pass_on(k):
        z = s.ahead(k)
        for w in range(2):
            each(4, lambda i: block(w, plane[w].to(i), z, s.h).start(), 1)
        dkv_recv[s.h, z] = dkv_send[s.h * s.nz + z]
        dq_recv[s.h, z] = dq[:, s.h * s.nz + z]

    each(s.nz + 1, pass_on, 1)
    for job in jobs[:2]:
        job.first()
    wait_all(loads[5:])

    def back(z, slot):
        return remote(dx_send.at[z], dx_recv.at[slot], dx_ssem.at[z], dx_rsem.at[slot], s.h, z * 2 + s.c)

    def take(k):
        z = s.ahead(k)
        for w in range(2):
            each(4, lambda i: block(w, plane[w].frm(i), z, plane[w].frm(i)).wait_recv(), 1)
        for j in range(4):
            dqkv[z, :, 128 * j:128 * j + 128] = dkv_recv[j, z].reshape(128, 128)
        for t in range(2):
            first, second = weave(dq_recv[2 * t, z].reshape(64, 128), dq_recv[2 * t + 1, z].reshape(64, 128))
            dqkv[z, 0:64, 512 + 128 * t:640 + 128 * t] = first
            dqkv[z, 64:128, 512 + 128 * t:640 + 128 * t] = second
        dx_send[z] = dot_t(dqkv[z], wa[:, :, :, :, 0:768].reshape(512, 768)).astype(bf16)

    def take_and_send(k):
        take(k)
        back(s.ahead(k), s.z).start()

    each(s.nz, take_and_send, 1)
    take(s.nz)
    dx_recv[s.z] = dx_send[s.z]
    tokens = xm[...].reshape(512, 512)
    pa[...] = dot_0(tokens, dqkv[...].reshape(512, 768)).astype(bf16).reshape(n, 16, 768)
    jobs[3].begin()
    jobs[2].first()
    for job in jobs[:3]:
        job.second()
    jobs[3].first()
    for job in jobs[:3]:
        job.third()
    jobs[3].second()
    jobs[3].third()
    each(s.nz, lambda k: back(s.ahead(k), s.ahead(k)).wait_recv(), 1)
    for m in range(2):
        rows = slice(128 * m, 128 * m + 128)
        gx[rows, :] = dz1[rows, :] + (dx_recv[2 * m].astype(f32) + dx_recv[2 * m + 1].astype(f32))
    stores = copies([(gx, outs[0])], out_sem)
    total = jobs[0].total()
    go[...] = total[:, 0:512]
    gu[...] = total[:, 512:2560]
    gd[...] = jobs[1].total()
    gs[...] = jobs[2].total()
    stores += copies(zip((go, gu, gd, gs), outs[4:8]), out_sem.at[pl.ds(1, 4)])
    for w, part in enumerate(jobs[3].columns()):
        gq[:, 256 * w:256 * w + 256] = part[:, 512:768]
        for t in range(2):
            first, second = weave(part[:, 256 * t:256 * t + 128], part[:, 256 * t + 128:256 * t + 256])
            at = 256 * w + 128 * t
            gk[:, at:at + 128] = first
            gv[:, at:at + 128] = second
    stores += copies(zip((gq, gk, gv), outs[1:4]), out_sem.at[pl.ds(5, 3)])
    for w in range(2):
        each(4, lambda i: each(s.nz, lambda z: block(w, plane[w].to(i), z, s.h).wait_send()), 1)
    each(s.nz, lambda k: back(s.ahead(k), s.z).wait_send(), 1)
    for job in jobs:
        job.sent()
    wait_all(stores)


def finish(n, nb, dq, dkv, xm, dz1, pb, pd, gvec, wa):
    dma = pltpu.SemaphoreType.DMA
    nz = nb // 2
    rows = dz1.shape[0]

    def buffers(depth, width, kind):
        return [
            pltpu.VMEM((n, depth, width), kind),
            pltpu.VMEM((4, nz, depth, width), kind),
            pltpu.VMEM((2, nz, depth, width // 2), kind),
            pltpu.VMEM((2, nz, depth, width), kind),
            pltpu.VMEM((nz, depth, width), kind),
        ]

    args = (dq, dkv, xm, dz1, pb, pd, gvec, wa)
    shapes = ((rows, 512), (16, 512), (16, 512), (16, 512), (16, 512), (16, 2048), (64, 512), (16, 128))
    return pl.pallas_call(
        functools.partial(finish_kernel, n, nb),
        out_shape=[jax.ShapeDtypeStruct(shape, f32) for shape in shapes],
        in_specs=any_specs(8),
        out_specs=any_specs(8),
        scratch_shapes=[
            *[pltpu.VMEM(arg.shape, arg.dtype) for arg in args],
            *buffers(16, 768, bf16),
            *buffers(16, 2560, bf16)[2:],
            *buffers(64, 512, bf16)[2:],
            *buffers(16, 128, f32)[1:2],
            pltpu.VMEM((2, nz, 8, 128), f32),
            *buffers(16, 128, f32)[3:],
            pltpu.VMEM((8, 16, 16, 128), bf16),
            pltpu.VMEM((16, 8, 16, 128), bf16),
            pltpu.VMEM((4, nz, 8, 16, 128), bf16),
            pltpu.VMEM((4, nz, 4, 16, 128), bf16),
            pltpu.VMEM((nz, 128, 768), bf16),
            pltpu.VMEM((nz, 128, 512), bf16),
            pltpu.VMEM((nz, 128, 512), bf16),
            *[pltpu.VMEM(shape, f32) for shape in shapes],
            dma((8,)),
            dma((8,)),
            dma((4, 9 * nz)),
            dma((4, 9 * nz)),
            dma((2, 4 * nz)),
            dma((2, 4 * nz)),
            dma((nz,)),
            dma((nz,)),
            dma,
            dma,
        ],
        compiler_params=pltpu.CompilerParams(
            collective_id=3, has_side_effects=True, vmem_limit_bytes=VMEM_BYTES
        ),
        name="finish",
    )(*args)


def deliver_kernel(count, *refs):
    ins, outs = refs[:count], refs[count:2 * count + 7]
    stage, lines, (in_sem, sems) = refs[2 * count + 7:3 * count + 7], refs[3 * count + 7:3 * count + 15], refs[-2:]
    loads = copies(zip(ins, stage), in_sem)
    jobs = []
    for k in range(count - 1):
        loads[k].wait()
        jobs += copies([(stage[k], outs[k])], sems.at[pl.ds(k, 1)])
    loads[-1].wait()
    vec = stage[-1]
    lines[0][...] = vec[0:1, 0:64].reshape(64)
    for k in range(1, 8):
        lines[k][...] = vec[k:k + 1, 0:16].reshape(16)
    jobs += copies(zip(lines, outs[count - 1:]), sems.at[pl.ds(count - 1, 8)])
    wait_all(jobs)


def deliver(arrays, vec):
    count = len(arrays) + 1
    lines = [(64,)] + [(16,)] * 7
    return pl.pallas_call(
        functools.partial(deliver_kernel, count),
        out_shape=[jax.ShapeDtypeStruct(a.shape, a.dtype) for a in arrays]
        + [jax.ShapeDtypeStruct(shape, f32) for shape in lines],
        in_specs=any_specs(count),
        out_specs=any_specs(count + 7),
        scratch_shapes=[
            *[pltpu.VMEM(a.shape, a.dtype) for a in (*arrays, vec)],
            *[pltpu.VMEM(shape, f32) for shape in lines],
            pltpu.SemaphoreType.DMA((count,)),
            pltpu.SemaphoreType.DMA((count + 7,)),
        ],
        compiler_params=pltpu.CompilerParams(vmem_limit_bytes=VMEM_BYTES),
        name="deliver",
    )(*arrays, vec)


def by_pairs(
    stream, accumulator, upstream, segment_ids, w_query, w_key, w_value, w_out, w_up, b_up, w_down, b_down,
    gain_attn, bias_attn, gain_ffn, bias_ffn, gain_final, bias_final,
):
    nb = lax.axis_size("blk")
    n = 4 * nb
    x = stream.reshape(256, 512)
    y = accumulator.reshape(256, 512)
    g = upstream.reshape(256, 512)
    smalls = (b_up, b_down, gain_attn, bias_attn, gain_ffn, bias_ffn, gain_final, bias_final)
    q, kv, xm, wa, fz, par, bup, seg_k, seg_q = project(
        n, nb, stream.reshape(2, 128, 512), w_query, w_key, w_value, w_out, w_up, w_down, segment_ids.reshape(2, 128), smalls
    )
    fx, fy = (lax.ppermute(fz, "head", [(h, h ^ w) for h in range(4)]) for w in (1, 2))
    o, of, lse, kv2, kvt = attn_fwd(q.reshape(4, 256, 128), kv.reshape(4096, 128), seg_q, seg_k)
    do, out, dacc, dz1, gvec, pb, pd = middle(
        n, nb, o.reshape(4, 16, 16, 128), x, y, g, fz, fx, fy, par, bup
    )
    dq, dkv, out, dacc = attn_bwd(
        q.reshape(4, 256, 128), do.reshape(4, 256, 128), of, lse, kv2, kvt, seg_q, seg_k, out, dacc
    )
    gx, gq, gk, gv, go, gu, gd, gs = finish(
        n, nb, dq.reshape(4, 16, 16, 128), dkv.reshape(8, 16, 2, 16, 128), xm, dz1, pb, pd, gvec, wa
    )
    gx, gq, gk, gv, go, gu, gd, gbu, *small_grads = deliver((gx, gq, gk, gv, go, gu, gd), gs)
    return (
        out.reshape(stream.shape), gx.reshape(stream.shape), dacc.reshape(stream.shape),
        gq, gk, gv, go, gu, gbu, gd, *small_grads,
    )


def pairs_fit(mesh, shape):
    return mesh.shape["head"] == 4 and mesh.shape["blk"] == 8 and shape == (2, 32, 128, 512)


def solution(mesh):
    def step(*args):
        return run(by_pairs if pairs_fit(mesh, args[0].shape) else local, mesh)(*args)

    return step


def run(body, mesh):
    return jax.shard_map(
        body,
        mesh=mesh,
        in_specs=(
            P(None, ("head", "blk"), None, None),
            P(None, ("head", "blk"), None, None),
            P(None, ("head", "blk"), None, None),
            P(None, ("head", "blk"), None),
            P(("head", "blk"), None),
            P(("head", "blk"), None),
            P(("head", "blk"), None),
            P(("head", "blk"), None),
            P(("head", "blk"), None),
            P(("head", "blk")),
            P(("head", "blk"), None),
            P(("head", "blk")),
            P(("head", "blk")),
            P(("head", "blk")),
            P(("head", "blk")),
            P(("head", "blk")),
            P(("head", "blk")),
            P(("head", "blk")),
        ),
        out_specs=(
            P(None, ("head", "blk"), None, None),
            P(None, ("head", "blk"), None, None),
            P(None, ("head", "blk"), None, None),
            P(("head", "blk"), None),
            P(("head", "blk"), None),
            P(("head", "blk"), None),
            P(("head", "blk"), None),
            P(("head", "blk"), None),
            P(("head", "blk")),
            P(("head", "blk"), None),
            P(("head", "blk")),
            P(("head", "blk")),
            P(("head", "blk")),
            P(("head", "blk")),
            P(("head", "blk")),
            P(("head", "blk")),
            P(("head", "blk")),
        ),
        check_vma=False,
    )
```

```python
import functools
import math

import jax
import jax.numpy as jnp
from jax import lax
from jax.experimental import pallas as pl
from jax.experimental.pallas import tpu as pltpu
from jax.sharding import PartitionSpec as P

DH = 64
f32, bf16 = jnp.float32, jnp.bfloat16
MESH = pl.DeviceIdType.MESH
FAR = -1e30
VMEM_BYTES = 60 << 20


EPSILON = 1e-05


def norm_forward(inputs, norm_gain, norm_bias):
    average = jnp.mean(inputs, axis=-1, keepdims=True)
    centered = inputs - average
    inv_std = lax.rsqrt(jnp.mean(centered * centered, axis=-1, keepdims=True) + EPSILON)
    normed = centered * inv_std
    return (normed * norm_gain + norm_bias, normed, inv_std)


def norm_backward(gradient, normed, inv_std, norm_gain):
    scaled = gradient * norm_gain
    projected = (
        scaled
        - jnp.mean(scaled, axis=-1, keepdims=True)
        - normed * jnp.mean(scaled * normed, axis=-1, keepdims=True)
    )
    return (inv_std * projected, jnp.sum(gradient * normed, axis=0), jnp.sum(gradient, axis=0))


def smooth_gate(pre_act):
    return jax.nn.gelu(pre_act, approximate=False)


def split_rows(length):
    block_len = math.gcd(length, 512)
    return (length // block_len, block_len)


def block_scores(queries, query_seg, key_rows, key_seg, scaling):
    scores = (
        jnp.einsum("sgd,kgd->sgk", queries, key_rows, preferred_element_type=jnp.float32) * scaling
    )
    allowed = query_seg[:, None, None] == key_seg[None, None, :]
    return (scores, allowed)


def block_grads(
    queries, query_seg, grad_rows, log_total, row_delta, key_rows, value_rows, key_seg, scaling
):
    scores, allowed = block_scores(queries, query_seg, key_rows, key_seg, scaling)
    attn_prob = jnp.where(allowed, jnp.exp(scores - log_total[:, :, None]), 0.0)
    prob_grad = jnp.einsum(
        "sgd,kgd->sgk", grad_rows, value_rows, preferred_element_type=jnp.float32
    )
    score_grad = (attn_prob * (prob_grad - row_delta[:, :, None]) * scaling).astype(jnp.bfloat16)
    return (attn_prob.astype(jnp.bfloat16), score_grad)


def key_blocks(key_rows, value_rows, key_seg, groups):
    block_num, block_len = split_rows(key_rows.shape[0])
    return (
        key_rows.reshape(block_num, block_len, groups, -1),
        value_rows.reshape(block_num, block_len, groups, -1),
        key_seg.reshape(block_num, block_len),
    )


def attend_fold(queries, query_seg, scaling, carried, portion):
    key_rows, value_rows, key_seg = portion

    def step(running, blocks):
        key_part, value_part, seg_part = blocks
        old_max, old_total, weighted = running
        scores, allowed = block_scores(queries, query_seg, key_part, seg_part, scaling)
        row_max = jnp.maximum(old_max, jnp.max(jnp.where(allowed, scores, -1e30), axis=2))
        exp_scores = jnp.where(allowed, jnp.exp(scores - row_max[:, :, None]), 0.0)
        rescale = jnp.exp(old_max - row_max)
        new_total = old_total * rescale + jnp.sum(exp_scores, axis=2)
        weighted = weighted * rescale[:, :, None] + jnp.einsum(
            "sgk,kgd->sgd",
            exp_scores.astype(jnp.bfloat16),
            value_part,
            preferred_element_type=jnp.float32,
        )
        return ((row_max, new_total, weighted), None)

    running, unused = lax.scan(
        step, carried, key_blocks(key_rows, value_rows, key_seg, queries.shape[1])
    )
    return running


def local(
    stream,
    accumulator,
    upstream,
    segment_ids,
    w_query,
    w_key,
    w_value,
    w_out,
    w_up,
    b_up,
    w_down,
    b_down,
    gain_attn,
    bias_attn,
    gain_ffn,
    bias_ffn,
    gain_final,
    bias_final,
):
    heads_axis = lax.axis_size("head")
    micro = stream.shape[0]
    tokens = stream.shape[2]
    width = stream.shape[3]
    group_width = width // heads_axis
    groups = group_width // DH
    scaling = DH ** (-0.5)
    f32 = jnp.float32
    bf16 = jnp.bfloat16
    out_list = []
    stream_grads = []
    accum_grads = []
    grad_totals = None
    for micro_step in range(micro):
        (
            q_weight,
            k_weight,
            v_weight,
            o_weight,
            up_weight,
            up_bias,
            down_weight,
            down_bias,
            gain_one,
            shift_one,
            gain_two,
            shift_two,
            gain_three,
            shift_three,
        ) = (
            lax.all_gather(w_query, ("head", "blk"), axis=0, tiled=True),
            lax.all_gather(w_key, ("head", "blk"), axis=0, tiled=True),
            lax.all_gather(w_value, ("head", "blk"), axis=0, tiled=True),
            lax.all_gather(w_out, ("head", "blk"), axis=0, tiled=True),
            lax.all_gather(w_up, ("head", "blk"), axis=0, tiled=True),
            lax.all_gather(b_up, ("head", "blk"), axis=0, tiled=True),
            lax.all_gather(w_down, ("head", "blk"), axis=0, tiled=True),
            lax.all_gather(b_down, ("head", "blk"), axis=0, tiled=True),
            lax.all_gather(gain_attn, ("head", "blk"), axis=0, tiled=True),
            lax.all_gather(bias_attn, ("head", "blk"), axis=0, tiled=True),
            lax.all_gather(gain_ffn, ("head", "blk"), axis=0, tiled=True),
            lax.all_gather(bias_ffn, ("head", "blk"), axis=0, tiled=True),
            lax.all_gather(gain_final, ("head", "blk"), axis=0, tiled=True),
            lax.all_gather(bias_final, ("head", "blk"), axis=0, tiled=True),
        )
        inputs = stream[micro_step, 0]
        input_wide = inputs.astype(f32)
        carried = accumulator[micro_step, 0].astype(f32)
        segs = segment_ids[micro_step, 0]
        projections = jnp.stack(
            [
                jnp.dot(inputs, q_weight, preferred_element_type=f32),
                jnp.dot(inputs, k_weight, preferred_element_type=f32),
                jnp.dot(inputs, v_weight, preferred_element_type=f32),
            ]
        ).astype(bf16)
        projections = projections.reshape(3, tokens, heads_axis, group_width)
        seg_wide = jnp.broadcast_to(segs[None, :, None, None], (1, tokens, heads_axis, 1))
        regrouped, seg_group = (
            lax.all_to_all(projections, "head", split_axis=2, concat_axis=1, tiled=True),
            lax.all_to_all(seg_wide, "head", split_axis=2, concat_axis=1, tiled=True),
        )
        rows = regrouped.shape[1]
        query_loc = regrouped[0, :, 0]
        key_loc = regrouped[1, :, 0]
        value_loc = regrouped[2, :, 0]
        seg_loc = seg_group[0, :, 0, 0]
        queries3 = query_loc.reshape(rows, groups, DH)
        start_state = (
            jnp.full((rows, groups), -1e30, f32),
            jnp.zeros((rows, groups), f32),
            jnp.zeros((rows, groups, DH), f32),
        )
        row_max, row_total, weighted = attend_fold(
            queries3,
            seg_loc,
            scaling,
            start_state,
            (
                lax.all_gather(key_loc, "blk", axis=0, tiled=True),
                lax.all_gather(value_loc, "blk", axis=0, tiled=True),
                lax.all_gather(seg_loc, "blk", axis=0, tiled=True),
            ),
        )
        attn_out = weighted / row_total[:, :, None]
        log_total = row_max + jnp.log(row_total)
        attn_send = attn_out.astype(bf16).reshape(rows, 1, group_width)
        mixed = lax.all_to_all(attn_send, "head", split_axis=0, concat_axis=1, tiled=True).reshape(
            tokens, width
        )
        branch = jnp.dot(mixed, o_weight, preferred_element_type=f32)
        first, normed_one, inv_one = norm_forward(
            input_wide + branch, gain_one.astype(f32), shift_one.astype(f32)
        )
        first_low = first.astype(bf16)
        hidden_pre = jnp.dot(first_low, up_weight, preferred_element_type=f32) + up_bias.astype(f32)
        hidden_act, gate_pull = jax.vjp(smooth_gate, hidden_pre)
        hidden = hidden_act.astype(bf16)
        feed = jnp.dot(hidden, down_weight, preferred_element_type=f32) + down_bias.astype(f32)
        second, normed_two, inv_two = norm_forward(
            first + feed, gain_two.astype(f32), shift_two.astype(f32)
        )
        final, normed_three, inv_three = norm_forward(
            carried + branch + feed, gain_three.astype(f32), shift_three.astype(f32)
        )
        out_list.append((second + final).astype(bf16))
        cotangent = upstream[micro_step, 0].astype(f32)
        accum_grad, gain3_grad, shift3_grad = norm_backward(
            cotangent, normed_three, inv_three, gain_three.astype(f32)
        )
        second_grad, gain2_grad, shift2_grad = norm_backward(
            cotangent, normed_two, inv_two, gain_two.astype(f32)
        )
        feed_grad = second_grad + accum_grad
        feed_low = feed_grad.astype(bf16)
        down_grad = jnp.dot(hidden.T, feed_low, preferred_element_type=f32)
        (hidden_grad,) = gate_pull(jnp.dot(feed_low, down_weight.T, preferred_element_type=f32))
        hidden_low = hidden_grad.astype(bf16)
        up_grad = jnp.dot(first_low.T, hidden_low, preferred_element_type=f32)
        first_grad = second_grad + jnp.dot(hidden_low, up_weight.T, preferred_element_type=f32)
        resid_grad, gain1_grad, shift1_grad = norm_backward(
            first_grad, normed_one, inv_one, gain_one.astype(f32)
        )
        branch_low = (resid_grad + accum_grad).astype(bf16)
        out_wgrad = jnp.dot(mixed.T, branch_low, preferred_element_type=f32)
        mixed_grad = jnp.dot(branch_low, o_weight.T, preferred_element_type=f32).astype(bf16)
        mixed_grad = mixed_grad.reshape(tokens, heads_axis, group_width)
        grad_group = lax.all_to_all(mixed_grad, "head", split_axis=1, concat_axis=0, tiled=True)
        grad_loc = grad_group[:, 0]
        grad3 = grad_loc.reshape(rows, groups, DH)
        row_delta = jnp.sum(grad3.astype(f32) * attn_out, axis=2)
        whole_keys, whole_values, whole_seg = (
            lax.all_gather(key_loc, "blk", axis=0, tiled=True),
            lax.all_gather(value_loc, "blk", axis=0, tiled=True),
            lax.all_gather(seg_loc, "blk", axis=0, tiled=True),
        )

        def backward_step(running, blocks):
            key_part, value_part, seg_part = blocks
            attn_prob, score_grad = block_grads(
                queries3,
                seg_loc,
                grad3,
                log_total,
                row_delta,
                key_part,
                value_part,
                seg_part,
                scaling,
            )
            running = running + jnp.einsum(
                "sgk,kgd->sgd", score_grad, key_part, preferred_element_type=f32
            )
            key_term = jnp.einsum("sgk,sgd->kgd", score_grad, queries3, preferred_element_type=f32)
            value_term = jnp.einsum("sgk,sgd->kgd", attn_prob, grad3, preferred_element_type=f32)
            return (running, (key_term, value_term))

        query_grad, (key_terms, value_terms) = lax.scan(
            backward_step,
            jnp.zeros((rows, groups, DH), f32),
            key_blocks(whole_keys, whole_values, whole_seg, groups),
        )
        key_grad, value_grad = (
            lax.psum_scatter(
                key_terms.reshape(-1, group_width), "blk", scatter_dimension=0, tiled=True
            ),
            lax.psum_scatter(
                value_terms.reshape(-1, group_width), "blk", scatter_dimension=0, tiled=True
            ),
        )
        grad_stack = jnp.stack(
            [query_grad.reshape(rows, group_width), key_grad, value_grad]
        ).astype(bf16)
        grad_stack = grad_stack.reshape(3, rows, 1, group_width)
        returned = lax.all_to_all(
            grad_stack, "head", split_axis=1, concat_axis=2, tiled=True
        ).reshape(3, tokens, width)
        query_wgrad = jnp.dot(inputs.T, returned[0], preferred_element_type=f32)
        key_wgrad = jnp.dot(inputs.T, returned[1], preferred_element_type=f32)
        value_wgrad = jnp.dot(inputs.T, returned[2], preferred_element_type=f32)
        input_grad = (
            resid_grad
            + jnp.dot(returned[0], q_weight.T, preferred_element_type=f32)
            + jnp.dot(returned[1], k_weight.T, preferred_element_type=f32)
            + jnp.dot(returned[2], v_weight.T, preferred_element_type=f32)
        )
        stream_grads.append(input_grad)
        accum_grads.append(accum_grad)
        step_grads = (
            query_wgrad,
            key_wgrad,
            value_wgrad,
            out_wgrad,
            up_grad,
            jnp.sum(hidden_grad, axis=0),
            down_grad,
            jnp.sum(feed_grad, axis=0),
            gain1_grad,
            shift1_grad,
            gain2_grad,
            shift2_grad,
            gain3_grad,
            shift3_grad,
        )
        if grad_totals is None:
            grad_totals = step_grads
        else:
            grad_totals = tuple((older + newer for older, newer in zip(grad_totals, step_grads)))
    summed = lax.psum_scatter(grad_totals, ("head", "blk"), scatter_dimension=0, tiled=True)
    layer_out = jnp.stack(out_list)[:, None]
    grad_stream = jnp.stack(stream_grads)[:, None]
    grad_accum = jnp.stack(accum_grads)[:, None]
    return (
        layer_out,
        grad_stream,
        grad_accum,
        summed[0],
        summed[1],
        summed[2],
        summed[3],
        summed[4],
        summed[5],
        summed[6],
        summed[7],
        summed[8],
        summed[9],
        summed[10],
        summed[11],
        summed[12],
        summed[13],
    )


def dot_t(a, b):
    return lax.dot_general(a, b, (((1,), (1,)), ((), ())), preferred_element_type=f32)

def dot_n(a, b):
    return lax.dot_general(a, b, (((1,), (0,)), ((), ())), preferred_element_type=f32)

def dot_0(a, b):
    return lax.dot_general(a, b, (((0,), (0,)), ((), ())), preferred_element_type=f32)

def lanes(shape):
    return lax.broadcasted_iota(jnp.int32, shape, len(shape) - 1)

def query_marks(seg_row):
    wide = jnp.broadcast_to(seg_row, (128, seg_row.shape[1])).T
    return (wide == lanes(wide.shape)).astype(f32).astype(bf16)

def half_lanes(tile, half):
    wide = tile.astype(f32)
    if half:
        wide = pltpu.roll(wide, 64, 1)
    return jnp.where(lanes(wide.shape) < 64, wide, 0.0).astype(bf16)

def key_steps(bounds, low, high):
    chunks, keys = bounds.shape
    first = sum(jnp.where(bounds[t, keys - 1] < low, 1, 0) for t in range(chunks))
    last = sum(jnp.where(bounds[t, 0] <= high, 1, 0) for t in range(chunks))
    pairs = (last - first + 1) // 2
    start = jnp.minimum(first, chunks - 2 * pairs)
    return start, pairs // 2, lax.rem(pairs, 2)


def walk(step, fours, twos, carry):
    carry = lax.fori_loop(0, fours, lambda t, c: step(4, 4 * t, c), carry)
    return lax.fori_loop(0, twos, lambda t, c: step(2, 4 * fours, c), carry)


def attn_fwd_kernel(
    q_hbm, kv_hbm, seg_q_hbm, seg_k_hbm, o_hbm, of_hbm, lse_hbm, kv2_hbm, kvt_hbm,
    q_ref, kv_ref, seg_q_ref, seg_k_ref, bounds, o_ref, of_ref, lse_ref, kv2_ref, kvt_ref, vo_ref, in_sem, out_sem,
):
    loads = copies(
        [(seg_q_hbm, seg_q_ref), (seg_k_hbm, seg_k_ref), (seg_k_hbm, bounds), (kv_hbm, kv_ref), (q_hbm, q_ref)], in_sem
    )
    wait_all(loads)
    chunks, keys = seg_k_ref.shape
    log_scale = math.log2(math.e) * DH ** (-0.5)

    def prepare(t, c):
        rows = pl.ds(pl.multiple_of(t * keys, keys), keys)
        kv = kv_ref[rows, :]
        marks = jnp.where(seg_k_ref[pl.ds(t, 1), :] == rows_of((128, keys)), 0.0, FAR)
        kvt_ref[0:128, rows] = kv.T
        kvt_ref[128:256, rows] = marks.astype(bf16)
        kv2_ref[rows, 0:128] = kv
        kv2_ref[rows, 128:256] = marks.T.astype(bf16)
        vo_ref[rows, :] = jnp.where(lanes(kv.shape) < 64, 1.0, kv.astype(f32)).astype(bf16)
        return c

    lax.fori_loop(0, chunks, prepare, 0)
    stores = copies([(kv2_ref, kv2_hbm), (kvt_ref, kvt_hbm)], out_sem)

    def tile(j, c):
        q_tile = q_ref[j]
        rows = q_tile.shape[0]
        outs = []
        for half in range(2):
            i = half * (chunks // 2) + j
            left = half_lanes(q_tile, half)
            left = jnp.concatenate([left, query_marks(seg_q_ref[pl.ds(i, 1), :])], axis=1)
            low, high = bounds[i, 0], bounds[i, keys - 1]
            start, fours, twos = key_steps(bounds, low, high)

            def step(width, t, carry):
                top, acc = carry
                at = pl.ds(pl.multiple_of((start + t) * keys, keys), width * keys)
                s = dot_n(left, kvt_ref[:, at])
                new = jnp.maximum(top, jnp.max(s, axis=1, keepdims=True))
                p = jnp.exp2((s - new) * log_scale)
                acc = acc * jnp.exp2((top - new) * log_scale) + dot_n(p.astype(bf16), vo_ref[at, :])
                return new, acc

            carry = (jnp.full((rows, 1), FAR, f32), jnp.zeros((rows, 128), f32))
            top, acc = walk(step, fours, twos, carry)
            total = pltpu.roll(acc, 64, 1)
            outs.append(acc / total)
            lse = jnp.broadcast_to(top * log_scale, acc.shape) + jnp.log2(acc)
            lse_ref[pl.ds(i, 1), :] = lse.T[0:1, :]
        o = jnp.where(lanes(outs[0].shape) < 64, pltpu.roll(outs[0], 64, 1), outs[1])
        of_ref[j] = o
        o_ref[j] = o.astype(bf16)
        return c

    lax.fori_loop(0, chunks // 2, tile, 0)
    stores += copies([(o_ref, o_hbm), (of_ref, of_hbm), (lse_ref, lse_hbm)], out_sem.at[pl.ds(2, 3)])
    wait_all(stores)


def attn_fwd(q, kv, seg_q, seg_k):
    chunks, keys = seg_k.shape
    dma = pltpu.SemaphoreType.DMA
    shapes = (
        (q.shape, bf16), (q.shape, f32), (seg_q.shape, f32), ((chunks * keys, 256), bf16), ((256, chunks * keys), bf16)
    )
    return pl.pallas_call(
        attn_fwd_kernel,
        out_shape=[jax.ShapeDtypeStruct(shape, kind) for shape, kind in shapes],
        in_specs=any_specs(4),
        out_specs=any_specs(5),
        scratch_shapes=[
            *[pltpu.VMEM(a.shape, a.dtype) for a in (q, kv, seg_q, seg_k)],
            pltpu.SMEM(seg_k.shape, jnp.int32),
            *[pltpu.VMEM(shape, kind) for shape, kind in shapes],
            pltpu.VMEM((chunks * keys, 128), bf16),
            dma((5,)),
            dma((5,)),
        ],
        compiler_params=pltpu.CompilerParams(vmem_limit_bytes=VMEM_BYTES),
        cost_estimate=pl.CostEstimate(flops=10**10, bytes_accessed=10**7, transcendentals=10**7),
        name="attn_fwd",
    )(q, kv, seg_q, seg_k)


def attn_bwd_kernel(
    q_hbm, do_hbm, of_hbm, lse_hbm, kv2_hbm, kvt_hbm, seg_q_hbm, seg_k_hbm, pass1, pass2, dq_hbm, dkv_hbm, out1, out2,
    q_ref, do_ref, of_ref, lse_ref, kv2_ref, kvt_ref, seg_q_ref, bounds, dq_ref, dkv_low, dkv_ref, hold1, hold2, in_sem, out_sem,
):
    loads = copies(
        [
            (q_hbm, q_ref), (do_hbm, do_ref), (of_hbm, of_ref), (lse_hbm, lse_ref), (kv2_hbm, kv2_ref),
            (seg_q_hbm, seg_q_ref), (seg_k_hbm, bounds),
            (pass1, hold1), (pass2, hold2), (kvt_hbm, kvt_ref),
        ],
        in_sem,
    )
    dkv_ref[...] = jnp.zeros_like(dkv_ref)
    wait_all(loads)
    stores = copies([(hold1, out1), (hold2, out2)], out_sem)
    chunks, keys = bounds.shape
    log_scale = math.log2(math.e) * DH ** (-0.5)

    def tile(j, c):
        q_tile, do_tile = q_ref[j], do_ref[j]
        rows = q_tile.shape[0]
        prod = do_tile.astype(f32) * of_ref[j]
        prod = prod.T
        dqs = []
        for half in range(2):
            i = half * (chunks // 2) + j
            left = half_lanes(q_tile, half)
            grad = do_tile.astype(f32)
            if not half:
                grad = pltpu.roll(grad, 64, 1)
            grad = jnp.where(lanes(grad.shape) < 64, 0.0, grad).astype(bf16)
            delta = jnp.sum(prod[64 * half:64 * half + 64], axis=0, keepdims=True)
            lse = lse_ref[pl.ds(i, 1), :]
            both = jnp.concatenate([left, grad], axis=0)
            marks = query_marks(seg_q_ref[pl.ds(i, 1), :])
            right = jnp.concatenate([both, jnp.concatenate([marks, jnp.zeros_like(marks)], axis=0)], axis=1).T
            low, high = bounds[i, 0], bounds[i, keys - 1]
            start, fours, twos = key_steps(bounds, low, high)

            def step(width, t, dq):
                at = pl.ds(pl.multiple_of((start + t) * keys, keys), width * keys)
                sdp = dot_n(kv2_ref[at, :], right)
                p = jnp.exp2(sdp[:, :rows] * log_scale - lse)
                ds = (p * (sdp[:, rows:] - delta)).astype(bf16)
                dkv_ref[at, :] += dot_n(jnp.concatenate([ds, p.astype(bf16)], axis=1), both)
                return dq + dot_n(kvt_ref[0:128, at], ds)

            dqs.append(walk(step, fours, twos, jnp.zeros((128, rows), f32)).T)
        dq = jnp.where(lanes(dqs[0].shape) < 64, dqs[0], pltpu.roll(dqs[1], 64, 1))
        dq_ref[j] = (dq * DH ** (-0.5)).astype(bf16)
        return c

    lax.fori_loop(0, chunks // 2, tile, 0)
    dkv = dkv_ref[...]
    dkv_low[...] = jnp.where(lanes(dkv.shape) < 64, dkv * DH ** (-0.5), dkv).astype(bf16)
    stores += copies([(dq_ref, dq_hbm), (dkv_low, dkv_hbm)], out_sem.at[pl.ds(2, 2)])
    wait_all(stores)


def attn_bwd(q, do, of, lse, kv2, kvt, seg_q, seg_k, pass1, pass2):
    dma = pltpu.SemaphoreType.DMA
    shapes = ((q.shape, bf16), ((kv2.shape[0], 128), bf16))
    return pl.pallas_call(
        attn_bwd_kernel,
        out_shape=[jax.ShapeDtypeStruct(shape, kind) for shape, kind in shapes]
        + [jax.ShapeDtypeStruct(a.shape, a.dtype) for a in (pass1, pass2)],
        in_specs=any_specs(10),
        out_specs=any_specs(4),
        scratch_shapes=[
            *[pltpu.VMEM(a.shape, a.dtype) for a in (q, do, of, lse, kv2, kvt, seg_q)],
            pltpu.SMEM(seg_k.shape, jnp.int32),
            *[pltpu.VMEM(shape, kind) for shape, kind in shapes],
            pltpu.VMEM((kv2.shape[0], 128), f32),
            *[pltpu.VMEM(a.shape, a.dtype) for a in (pass1, pass2)],
            dma((10,)),
            dma((4,)),
        ],
        compiler_params=pltpu.CompilerParams(vmem_limit_bytes=VMEM_BYTES),
        cost_estimate=pl.CostEstimate(flops=10**10, bytes_accessed=10**7, transcendentals=10**7),
        name="attn_bwd",
    )(q, do, of, lse, kv2, kvt, seg_q, seg_k, pass1, pass2)


class Spot:
    def __init__(self, nb):
        self.nb, self.nz = nb, nb // 2
        self.h, b = lax.axis_index("head"), lax.axis_index("blk")
        self.z, self.c = b // 2, lax.rem(b, 2)
        self.near = (self.h + 1 - 2 * lax.rem(self.h, 2), lax.rem(self.h + 2, 4))
        self.diag = 3 - self.h
        self.me = self.h * nb + b

    def index(self, h, z, c):
        return h * self.nb + z * 2 + c

    def ahead(self, k):
        return lax.rem(self.z + k, self.nz)


def remote(src, dst, send, recv, h, b):
    return pltpu.make_async_remote_copy(
        src_ref=src,
        dst_ref=dst,
        send_sem=send,
        recv_sem=recv,
        device_id={"head": h, "blk": b},
        device_id_type=MESH,
    )


def each(count, body, start=0):
    def run(i, c):
        body(i)
        return c

    lax.fori_loop(start, count, run, 0)


def hail(h, b):
    pl.semaphore_signal(
        pltpu.get_barrier_semaphore(), inc=1, device_id={"head": h, "blk": b}, device_id_type=MESH
    )


def greet_near(s):
    for k in range(1, s.nz):
        hail(s.h, s.ahead(k) * 2 + s.c)
    for i in range(1, 4):
        hail(lax.rem(s.h + i, 4), s.z * 2 + s.c)
    hail(s.h, s.z * 2 + 1 - s.c)
    pl.semaphore_wait(pltpu.get_barrier_semaphore(), s.nz + 3)


def greet_core(s):
    def signal(i):
        t = lax.rem(s.me + 2 * i, 4 * s.nb)
        hail(t // s.nb, lax.rem(t, s.nb))

    each(2 * s.nb, signal, 1)
    hail(s.h, s.z * 2 + 1 - s.c)
    pl.semaphore_wait(pltpu.get_barrier_semaphore(), 2 * s.nb)


class Scatter:
    def __init__(self, spot, part, twin, diag, near, line, send, recv):
        self.s, self.part, self.t, self.d, self.n, self.l = spot, part, twin, diag, near, line
        self.send, self.recv = send, recv

    def copy(self, src, dst, k, h, z, c, recv_k=None):
        recv_k = k if recv_k is None else recv_k
        return remote(src, dst, self.send.at[k], self.recv.at[recv_k], h, z * 2 + c)

    def mine(self, h, z):
        return h * self.s.nz + z if self.t is None else self.s.index(h, z, self.s.c)

    def to_twin(self, h, z):
        s = self.s
        src = self.part.at[s.index(h, z, 1 - s.c)]
        return self.copy(src, self.t.at[h, z], h * s.nz + z, s.h, s.z, 1 - s.c)

    def to_diag(self, z):
        s = self.s
        src = self.part.at[self.mine(s.diag, z)]
        return self.copy(src, self.d.at[z], 4 * s.nz + z, s.diag, s.z, s.c)

    def to_near(self, w, z):
        s = self.s
        src = self.part.at[self.mine(s.near[w], z)]
        return self.copy(src, self.n.at[w, z], (6 + w) * s.nz + z, s.near[w], s.z, s.c)

    def to_line(self, z):
        s = self.s
        src = self.part.at[self.mine(s.h, z)]
        return self.copy(src, self.l.at[s.z], 8 * s.nz + z, s.h, z, s.c, 8 * s.nz + s.z)

    def from_line(self, z):
        s = self.s
        src = self.part.at[self.mine(s.h, z)]
        return self.copy(src, self.l.at[z], 8 * s.nz + z, s.h, z, s.c)

    def begin(self):
        each(4, lambda h: each(self.s.nz, lambda z: self.to_twin(h, z).start()))

    def pair(self, h, z):
        if self.t is None:
            return self.part[self.mine(h, z)].astype(f32)
        self.to_twin(h, z).wait_recv()
        return self.part[self.mine(h, z)].astype(f32) + self.t[h, z].astype(f32)

    def keep(self, h, z, value):
        self.part[self.mine(h, z)] = value.astype(self.part.dtype)

    def second(self):
        s = self.s

        def go(k):
            z = s.ahead(k)
            for w in range(2):
                if self.t is not None:
                    self.keep(s.near[w], z, self.pair(s.near[w], z))
                self.to_near(w, z).start()
            if self.t is not None:
                self.keep(s.diag, z, self.pair(s.diag, z))
                self.to_diag(z).start()

        each(s.nz + 1, go, 1)

    def joined(self, z):
        value = self.pair(self.s.h, z)
        if self.t is not None:
            self.to_diag(z).wait_recv()
        value = value + self.d[z].astype(f32)
        for w in range(2):
            self.to_near(w, z).wait_recv()
            value = value + self.n[w, z].astype(f32)
        return value

    def third(self):
        s = self.s

        def go(k):
            z = s.ahead(k)
            self.keep(s.h, z, self.joined(z))
            self.to_line(z).start()

        each(s.nz, go, 1)

    def columns(self):
        s = self.s
        self.l[s.z] = self.joined(s.z).astype(self.l.dtype)
        each(s.nz, lambda k: self.from_line(s.ahead(k)).wait_recv(), 1)
        return [self.l[w].astype(f32) + self.l[w + 2].astype(f32) for w in range(2)]

    def total(self):
        s = self.s
        value = self.joined(s.z)

        def go(k, value):
            z = s.ahead(k)
            self.from_line(z).wait_recv()
            return value + self.l[z].astype(f32)

        return lax.fori_loop(1, s.nz, go, value)

    def sent(self):
        s = self.s

        def go(z):
            if self.t is not None:
                each(4, lambda h: self.to_twin(h, z).wait_send())
                self.to_diag(z).wait_send()
            for w in range(2):
                self.to_near(w, z).wait_send()

        each(s.nz, go)
        each(s.nz, lambda k: self.to_line(s.ahead(k)).wait_send(), 1)


class Exchange:
    def __init__(self, spot, src, dst, send, recv, local):
        self.s, self.src, self.dst, self.send, self.recv, self.local = spot, src, dst, send, recv, local
        self.g = spot.me // 2

    def copy(self, i, back=False):
        s = self.s
        to = lax.rem(self.g + i, 16)
        t = to * 2 + s.c
        src = self.src(to)
        dst = self.dst(lax.rem(self.g + 16 - i, 16)) if back else self.dst(self.g)
        return remote(src, dst, self.send.at[i], self.recv.at[i], t // s.nb, lax.rem(t, s.nb))

    def own(self):
        return pltpu.make_async_copy(self.src(self.g), self.dst(self.g), self.local)

    def begin(self):
        self.own().start()
        each(16, lambda i: self.copy(i).start(), 1)

    def arrive(self, i):
        self.copy(i, True).wait_recv()

    def end(self):
        each(16, self.arrive, 1)
        self.sent()

    def sent(self):
        self.own().wait()
        each(16, lambda i: self.copy(i).wait_send(), 1)


class Plane:
    def __init__(self, spot, send, recv):
        self.s, self.send, self.recv = spot, send, recv

    def to(self, k):
        return lax.rem(self.s.h + k, 4)

    def frm(self, k):
        return lax.rem(self.s.h + 4 - k, 4)

    def copy(self, src, dst, j, at_send, at_recv):
        s = self.s
        return remote(src, dst, self.send.at[at_send], self.recv.at[at_recv], j, s.z * 2 + s.c)


def pair_of(g):
    return lax.rem(g, 4) * 4 + g // 4


def weave(left, right):
    kind = left.dtype
    left, right = left.astype(f32), right.astype(f32)
    low = lanes(left.shape) < 64
    first = jnp.where(low, left, pltpu.roll(right, 64, 1)).astype(kind)
    second = jnp.where(low, pltpu.roll(left, 64, 1), right).astype(kind)
    return first, second


def any_specs(count):
    return [pl.BlockSpec(memory_space=pl.ANY)] * count


def copies(pairs, sems):
    jobs = [pltpu.make_async_copy(src, dst, sems.at[k]) for k, (src, dst) in enumerate(pairs)]
    for job in jobs:
        job.start()
    return jobs


def wait_all(jobs):
    for job in jobs:
        job.wait()


def rows_of(shape):
    return lax.broadcasted_iota(jnp.int32, shape, 0)


def spread_row(block, width, each_lane):
    count = block.shape[0]
    pick = (rows_of((128, width)) == lax.rem(lanes((128, width)), each_lane)).astype(f32).astype(bf16)
    wide = dot_n(block.astype(bf16), pick)
    return column_sum(jnp.where(rows_of((count, width)) == lanes((count, width)) // each_lane, wide, 0.0))


def gather_row(row, count, each_lane):
    width = row.shape[1]
    wide = jnp.where(rows_of((count, width)) == lanes((count, width)) // each_lane, row, 0.0)
    pick = (lanes((width, 128)) == lax.rem(rows_of((width, 128)), each_lane)).astype(f32)
    return lax.dot_general(
        wide, pick, (((1,), (0,)), ((), ())), precision=lax.Precision.HIGHEST, preferred_element_type=f32
    )


class Line:
    def __init__(self, spot, shard, full, send, recv, local):
        self.s, self.shard, self.full, self.send, self.recv = spot, shard, full, send, recv
        self.own = pltpu.make_async_copy(shard, full.at[spot.z], local)

    def copy(self, way, t):
        s = self.s
        k = 2 * t + (way + 1) // 2
        src = self.full.at[s.z - way * t] if t else self.shard
        dst = self.full.at[s.z - way * t]
        return remote(src, dst, self.send.at[k], self.recv.at[k], s.h, (s.z + way) * 2 + s.c)

    def inside(self, z):
        return (z >= 0) & (z < self.s.nz)

    def sends(self, t, act):
        for way in (1, -1):
            z = self.s.z

            @pl.when(self.inside(z + way) & self.inside(z - way * t))
            def _():
                act(self.copy(way, t))

    def arrive(self, t):
        for way in (1, -1):
            s = self.s

            @pl.when(self.inside(s.z - way * (t + 1)))
            def _():
                slot = self.full.at[s.z - way * (t + 1)]
                k = 2 * t + (way + 1) // 2
                remote(slot, slot, self.send.at[k], self.recv.at[k], s.h, (s.z - way) * 2 + s.c).wait_recv()

    def begin(self):
        self.own.start()
        self.sends(0, lambda copy: copy.start())

    def onward(self, t):
        self.arrive(t)
        if t + 1 < self.s.nz - 1:
            self.sends(t + 1, lambda copy: copy.start())

    def sent(self):
        self.own.wait()
        for t in range(self.s.nz - 1):
            self.sends(t, lambda copy: copy.wait_send())


def project_kernel(n, nb, *refs):
    x_hbm, wq_hbm, wk_hbm, wv_hbm, wo_hbm, wu_hbm, wd_hbm, seg_hbm = refs[:8]
    smalls = refs[8:16]
    q_out, kv_out, x_out, wa_out, fz_out, par_out, bup_out, segk_out, segq_out = refs[16:25]
    (
        x, wq, wk, wv, wo, wu, wd, seg, *small, bup_small, vec, sa, sb, wa, x_all, kv_send, q_send,
        par, bup, segk, segq,
        in_sem, out_sem, w_send, w_recv, w_local, f_send, f_recv, f_local,
        x_send, x_recv, x_local, ex_send, ex_recv, ex_local, tw_send, tw_recv,
    ) = refs[25:]
    s = Spot(nb)
    loads = copies(
        [(wq_hbm, wq), (wk_hbm, wk), (wv_hbm, wv), (seg_hbm, seg), (smalls[0], bup_small)]
        + [(smalls[k], small[k - 1]) for k in range(1, 8)]
        + [(x_hbm, x), (wo_hbm, wo), (wu_hbm, wu), (wd_hbm, wd)],
        in_sem,
    )
    greet_near(s)

    def pass_x(z, slot):
        return remote(x.at[z // 2], x_all.at[slot], x_send.at[z], x_recv.at[slot], s.h, z * 2 + s.c)

    wait_all(loads[:13])
    vec[...] = jnp.zeros_like(vec)
    vec[0:1, 0:64] = bup_small[...].astype(f32).reshape(1, 64)
    for k in range(7):
        vec[k + 1:k + 2, 0:16] = small[k][...].astype(f32).reshape(1, 16)
    vec[8:10, :] = seg[...].astype(f32)
    for t in range(4):
        tile, at = slice(128 * t, 128 * t + 128), 256 * (t % 2)
        first, second = weave(wk[:, tile], wv[:, tile])
        sa[t // 2, :, at:at + 128] = first
        sa[t // 2, :, at + 128:at + 256] = second
    for w in range(2):
        sa[w, :, 512:768] = wq[:, 256 * w:256 * w + 256]
        sa[w, :, 768:896] = vec[...].astype(bf16)

    def w_line(z, slot):
        return remote(
            sa.at[lax.rem(z, 2)], wa.at[s.h, slot, s.c], w_send.at[z], w_recv.at[slot], s.h, z * 2 + s.c
        )

    def w_plane(j, h):
        slot = wa.at[h, :, s.c]
        return remote(slot, slot, w_send.at[4 + j], w_recv.at[4 + h], j, s.z * 2 + s.c)

    def w_twin(h, c):
        slot = wa.at[h, :, c]
        return remote(slot, slot, w_send.at[8 + h], w_recv.at[8 + h], s.h, s.z * 2 + 1 - s.c)

    each(s.nz, lambda k: w_line(s.ahead(k), s.z).start(), 1)
    own_w = pltpu.make_async_copy(sa.at[lax.rem(s.z, 2)], wa.at[s.h, s.z, s.c], w_local)
    own_w.start()
    each(s.nz, lambda k: pass_x(s.ahead(k), s.z).start(), 1)
    own_x = pltpu.make_async_copy(x.at[s.z // 2], x_all.at[s.z], x_local)
    own_x.start()
    wait_all(loads[13:])
    sb[:, 0:512] = wo[...]
    sb[:, 512:2560] = wu[...]
    for t in range(4):
        sb[:, 2560 + 512 * t:3072 + 512 * t] = wd[16 * t:16 * t + 16, :]
    line = Line(s, sb, fz_out, f_send, f_recv, f_local)
    line.begin()
    own_w.wait()
    each(s.nz, lambda k: w_line(s.ahead(k), s.ahead(k)).wait_recv(), 1)
    each(4, lambda i: w_plane(lax.rem(s.h + i, 4), s.h).start(), 1)
    w_twin(s.h, s.c).start()

    def w_arrive(i):
        h = lax.rem(s.h + 4 - i, 4)
        w_plane(h, h).wait_recv()
        w_twin(h, s.c).start()

    each(4, w_arrive, 1)
    each(4, lambda h: w_twin(h, 1 - s.c).wait_recv())
    outs = copies([(wa, wa_out)], out_sem)
    own_x.wait()
    plane = [Plane(s, ex_send.at[k], ex_recv.at[k]) for k in range(2)]
    kinds = ((kv_send, lambda g: kv_out.at[:, g, s.c]), (q_send, lambda g: q_out.at[:, g]))

    def block(w, j, z):
        src, dst = kinds[w]
        return plane[w].copy(src.at[j, z], dst(s.h * 4 + z), j, j * 4 + z, s.h * 4 + z)

    def from_block(w, j, z):
        src, dst = kinds[w]
        slot = dst(j * 4 + z)
        return plane[w].copy(slot, slot, j, j * 4 + z, j * 4 + z)

    def own_block(w, z):
        src, dst = kinds[w]
        return pltpu.make_async_copy(src.at[s.h, z], dst(s.h * 4 + z), ex_local.at[w, z])

    def twin(src, j, z, c):
        slot = kv_out.at[:, j * 4 + z, c]
        k = j * 4 + z
        return remote(slot if src is None else src, slot, tw_send.at[k], tw_recv.at[k], s.h, s.z * 2 + 1 - s.c)

    def project_rows(k):
        z = s.ahead(k)
        qkv = dot_n(x_all[z], wa[:, :, :, :, 0:768].reshape(512, 768)).astype(bf16)
        for j in range(4):
            kv_send[j, z] = qkv[:, 128 * j:128 * j + 128].reshape(8, 16, 128)
        for t in range(2):
            tile = qkv[:, 512 + 128 * t:640 + 128 * t]
            first, second = weave(tile[0:64], tile[64:128])
            q_send[2 * t, z] = first.reshape(4, 16, 128)
            q_send[2 * t + 1, z] = second.reshape(4, 16, 128)
        for w in range(2):
            each(4, lambda i: block(w, plane[w].to(i), z).start(), 1)
            own_block(w, z).start()
        twin(kv_send.at[s.h, z], s.h, z, s.c).start()

    project_rows(0)

    def project_next(k):
        z = s.ahead(k)
        pass_x(z, z).wait_recv()
        project_rows(k)

    each(s.nz, project_next, 1)
    line.onward(0)
    line.onward(1)
    vecs = wa[:, :, :, :, 768:896].reshape(n, 16, 128).astype(f32)
    outs += copies([(x_all, x_out)], out_sem.at[pl.ds(5, 1)])
    bup[...] = spread_row(vecs[:, 0, :], 2048, 64)
    for k in range(7):
        par[k:k + 1, :] = spread_row(vecs[:, k + 1, :], 512, 16)
    par[7:8, :] = jnp.zeros((1, 512), f32)
    ids = jnp.where(s.z < 2, vecs[:, 8, :], vecs[:, 9, :]).astype(bf16)
    for i in range(8):
        pick = (rows_of((128, 512)) == 16 * i + lax.rem(lanes((128, 512)), 16)).astype(f32).astype(bf16)
        wide = dot_n(ids, pick)
        source = rows_of((n, 512))
        row = jnp.where(source == lanes((n, 512)) // 16, wide, 0.0)
        segk[i:i + 1, :] = column_sum(row).astype(jnp.int32)
        source = rows_of((n, 256))
        own = (source // 2 == lanes((n, 256)) // 16) & (lax.rem(source, 2) == s.c)
        segq[i:i + 1, :] = column_sum(jnp.where(own, wide[:, 0:256], 0.0)).astype(jnp.int32)
    outs += copies([(par, par_out), (bup, bup_out), (segk, segk_out), (segq, segq_out)], out_sem.at[pl.ds(1, 4)])
    def forward(i):
        j = plane[0].frm(i)

        def go(k):
            z = s.ahead(k)
            from_block(0, j, z).wait_recv()
            twin(None, j, z, s.c).start()

        each(s.nz, go)

    each(4, forward, 1)
    line.onward(2)
    each(4, lambda i: each(s.nz, lambda z: from_block(1, plane[1].frm(i), z).wait_recv()), 1)
    each(4, lambda j: each(s.nz, lambda z: twin(None, j, z, 1 - s.c).wait_recv()))
    each(4, lambda j: each(s.nz, lambda z: twin(None, j, z, s.c).wait_send()))
    for w in range(2):
        each(s.nz, lambda z: own_block(w, z).wait())
        each(4, lambda i: each(s.nz, lambda z: block(w, plane[w].to(i), z).wait_send()), 1)
    each(s.nz, lambda k: pass_x(s.ahead(k), s.z).wait_send(), 1)
    each(s.nz, lambda k: w_line(s.ahead(k), s.z).wait_send(), 1)
    each(4, lambda i: w_plane(lax.rem(s.h + i, 4), s.h).wait_send(), 1)
    each(4, lambda h: w_twin(h, s.c).wait_send())
    line.sent()
    wait_all(outs)


def project(n, nb, x, wq, wk, wv, wo, wu, wd, seg, smalls):
    dma = pltpu.SemaphoreType.DMA
    nz = nb // 2
    return pl.pallas_call(
        functools.partial(project_kernel, n, nb),
        out_shape=(
            jax.ShapeDtypeStruct((4, 16, 16, 128), bf16),
            jax.ShapeDtypeStruct((8, 16, 2, 16, 128), bf16),
            jax.ShapeDtypeStruct((nz, 128, 512), bf16),
            jax.ShapeDtypeStruct((4, nz, 2, 16, 896), bf16),
            jax.ShapeDtypeStruct((nz, 16, 4608), bf16),
            jax.ShapeDtypeStruct((8, 512), f32),
            jax.ShapeDtypeStruct((1, 2048), f32),
            jax.ShapeDtypeStruct((8, 512), jnp.int32),
            jax.ShapeDtypeStruct((8, 256), jnp.int32),
        ),
        in_specs=any_specs(16),
        out_specs=any_specs(9),
        scratch_shapes=[
            pltpu.VMEM(x.shape, bf16),
            pltpu.VMEM((16, 512), bf16),
            pltpu.VMEM((16, 512), bf16),
            pltpu.VMEM((16, 512), bf16),
            pltpu.VMEM((16, 512), bf16),
            pltpu.VMEM((16, 2048), bf16),
            pltpu.VMEM((64, 512), bf16),
            pltpu.VMEM((2, 128), jnp.int32),
            *[pltpu.VMEM((16,), bf16)] * 7,
            pltpu.VMEM((64,), bf16),
            pltpu.VMEM((16, 128), f32),
            pltpu.VMEM((2, 16, 896), bf16),
            pltpu.VMEM((16, 4608), bf16),
            pltpu.VMEM((4, nz, 2, 16, 896), bf16),
            pltpu.VMEM((nz, 128, 512), bf16),
            pltpu.VMEM((4, nz, 8, 16, 128), bf16),
            pltpu.VMEM((4, nz, 4, 16, 128), bf16),
            pltpu.VMEM((8, 512), f32),
            pltpu.VMEM((1, 2048), f32),
            pltpu.VMEM((8, 512), jnp.int32),
            pltpu.VMEM((8, 256), jnp.int32),
            dma((16,)),
            dma((6,)),
            dma((12,)),
            dma((12,)),
            dma,
            dma((2 * nz,)),
            dma((2 * nz,)),
            dma,
            dma((nz,)),
            dma((nz,)),
            dma,
            dma((2, 4 * nz)),
            dma((2, 4 * nz)),
            dma((2, nz)),
            dma((4 * nz,)),
            dma((4 * nz,)),
        ],
        compiler_params=pltpu.CompilerParams(
            collective_id=1, has_side_effects=True, vmem_limit_bytes=VMEM_BYTES
        ),
        name="project",
    )(x, wq, wk, wv, wo, wu, wd, seg, *smalls)


def row_norm(v):
    mean = jnp.mean(v, axis=-1, keepdims=True)
    mid = v - mean
    inv = lax.rsqrt(jnp.mean(mid * mid, axis=-1, keepdims=True) + EPSILON)
    return mid * inv, inv


def row_norm_back(grad, normed, inv, gain):
    part = grad * gain
    return inv * (
        part
        - jnp.mean(part, axis=-1, keepdims=True)
        - normed * jnp.mean(part * normed, axis=-1, keepdims=True)
    )


def normal(u):
    bell = jnp.exp(-0.5 * u * u)
    t = 1.0 / (1.0 + (0.3275911 * 0.5**0.5) * jnp.abs(u))
    poly = 0.5 * 1.061405429
    for factor in (-1.453152027, 1.421413741, -0.284496736, 0.254829592):
        poly = poly * t + 0.5 * factor
    tail = poly * t * bell
    return jnp.where(u < 0, tail, 1.0 - tail), bell * ((2.0 * math.pi) ** -0.5)


def column_sum(v):
    return jnp.sum(v, axis=0, keepdims=True)


def middle_kernel(n, nb, *refs):
    o_hbm, x_hbm, y_hbm, g_hbm, fz_hbm, fx_hbm, fy_hbm, par_hbm, bup_hbm = refs[:9]
    outs_hbm = refs[10:17]
    do_out = refs[9]
    (
        o_in, x, y, g_in, wb, wd, par, bup, o_recv, do_send, slope,
        out, dacc_ref, dz1_ref, gvec, sum_b, sum_d, far, bias_up, omix, hid_ref, dur_ref, po, pu, pd, to, tu, td,
        in_sem, out_sem, ex_send, ex_recv, ex_local, f_send, f_recv, p_send, p_recv,
    ) = refs[17:]
    s = Spot(nb)
    loads = copies(
        [
            (o_hbm, o_in), (x_hbm, x), (y_hbm, y), (g_hbm, g_in), (par_hbm, par), (bup_hbm, bup),
            (fz_hbm, wb.at[s.h, :, s.c]), (fx_hbm, wb.at[s.near[0], :, s.c]), (fy_hbm, wb.at[s.near[1], :, s.c]),
        ],
        in_sem,
    )
    greet_core(s)
    loads[0].wait()
    o_ex = Exchange(
        s, lambda g: o_in.at[:, g], lambda g: o_recv.at[pair_of(g)], ex_send.at[0], ex_recv.at[0], ex_local.at[0]
    )
    o_ex.begin()
    cut = [pl.ds(0, 2304), pl.ds(2304, 2304)]
    heads = (s.h, s.near[0], s.near[1], s.diag)

    def onward(w, h, to):
        src = (fx_hbm, fy_hbm)[w].at[:, :, cut[w]]
        return remote(src, wb.at[h, :, s.c, :, cut[w]], f_send.at[4 + w], f_recv.at[4 + w], to, s.z * 2 + s.c)

    def twin(k, c):
        slot = wb.at[heads[k], :, c]
        src = (fz_hbm, fx_hbm, fy_hbm, slot)[k]
        return remote(src, slot, f_send.at[k], f_recv.at[k], s.h, s.z * 2 + 1 - s.c)

    for w in range(2):
        onward(w, s.near[w], s.near[1 - w]).start()
    for k in range(3):
        twin(k, s.c).start()
    for w in range(2):
        onward(w, s.diag, s.near[1 - w]).wait_recv()
    twin(3, s.c).start()
    o_ex.end()
    wait_all(loads[1:])
    for m in range(2):
        for t in range(4):
            first, second = weave(
                o_recv[8 * m + 2 * t].reshape(64, 128), o_recv[8 * m + 2 * t + 1].reshape(64, 128)
            )
            omix[128 * m:128 * m + 64, 128 * t:128 * t + 128] = first
            omix[128 * m + 64:128 * m + 128, 128 * t:128 * t + 128] = second
    gain1, bias1 = par[1:2], par[2:3]
    gain2, bias2 = par[3:4], par[4:5]
    gain3, bias3 = par[5:6], par[6:7]
    for k in range(4):
        twin(k, 1 - s.c).wait_recv()
    for t in range(4):
        for r in range(4):
            wd[t, :, :, r] = wb[t, :, :, :, 2560 + 512 * r:3072 + 512 * r]
    w_out = wb[:, :, :, :, 0:512].reshape(512, 512)
    a = dot_n(omix[...], w_out)
    n1, r1 = row_norm(x[...].astype(f32) + a)
    x1 = n1 * gain1 + bias1
    x1r = x1.astype(bf16)
    feed = jnp.zeros_like(x1)
    for t in range(4):
        cols = slice(512 * t, 512 * t + 512)
        u = dot_n(x1r, wb[:, :, :, :, 512 + 512 * t:1024 + 512 * t].reshape(512, 512)) + bup[:, cols]
        phi, density = normal(u)
        hid = (u * phi).astype(bf16)
        slope[:, cols] = phi + u * density
        hid_ref[:, cols] = hid
        feed = feed + dot_n(hid, wd[t].reshape(512, 512))
    feed = feed + par[0:1]
    n2, r2 = row_norm(x1 + feed)
    n3, r3 = row_norm(y[...].astype(f32) + a + feed)
    out[...] = (n2 * gain2 + bias2 + (n3 * gain3 + bias3)).astype(bf16)
    g = g_in[...].astype(f32)
    dacc = row_norm_back(g, n3, r3, gain3)
    dacc_ref[...] = dacc
    dz2 = row_norm_back(g, n2, r2, gain2)
    df = dz2 + dacc
    dfr = df.astype(bf16)
    swaps = [
        remote(part.at[:, :, 1 - s.c], there, p_send.at[k], p_recv.at[k], s.h, s.z * 2 + 1 - s.c)
        for k, (part, there) in enumerate(((pd, td), (pu, tu), (po, to)))
    ]
    for t in range(4):
        pd[t] = dot_0(hid_ref[:, 512 * t:512 * t + 512], dfr).astype(bf16).reshape(nb // 2, 2, 64, 512)
    swaps[0].start()
    dx1 = dz2
    for t in range(4):
        cols = slice(512 * t, 512 * t + 512)
        du = dot_t(dfr, wd[t].reshape(512, 512)) * slope[:, cols]
        bias_up[:, cols] = column_sum(du)
        dur = du.astype(bf16)
        dur_ref[:, cols] = dur
        dx1 = dx1 + dot_t(dur, wb[:, :, :, :, 512 + 512 * t:1024 + 512 * t].reshape(512, 512))
    dz1 = row_norm_back(dx1, n1, r1, gain1)
    dz1_ref[...] = dz1
    dar = (dz1 + dacc).astype(bf16)
    do = dot_t(dar, w_out).astype(bf16)
    for m in range(2):
        for t in range(4):
            tile = do[128 * m:128 * m + 128, 128 * t:128 * t + 128]
            first, second = weave(tile[0:64], tile[64:128])
            do_send[8 * m + 2 * t] = first.reshape(4, 16, 128)
            do_send[8 * m + 2 * t + 1] = second.reshape(4, 16, 128)
    do_ex = Exchange(
        s, lambda g: do_send.at[pair_of(g)], lambda g: do_out.at[:, g], ex_send.at[1], ex_recv.at[1], ex_local.at[1]
    )
    do_ex.begin()
    stores = copies(zip((out, dacc_ref, dz1_ref), outs_hbm[:3]), out_sem)
    for t in range(4):
        cols = slice(512 * t, 512 * t + 512)
        pu[:, :, :, :, cols] = dot_0(x1r, dur_ref[:, cols]).astype(bf16).reshape(4, nb // 2, 2, 16, 512)
    swaps[1].start()
    po[...] = dot_0(omix[...], dar).astype(bf16).reshape(po.shape)
    swaps[2].start()
    sum_g = column_sum(g)
    sums = (
        column_sum(df), column_sum(dx1 * n1), column_sum(dx1), column_sum(g * n2), sum_g, column_sum(g * n3), sum_g
    )
    gvec[...] = jnp.zeros_like(gvec)
    gvec[:, 0, :] = gather_row(bias_up[...], n, 64)
    for k in range(7):
        gvec[:, k + 1, :] = gather_row(sums[k], n, 16)
    stores += copies([(gvec, outs_hbm[3])], out_sem.at[pl.ds(3, 1)])
    for swap in swaps:
        swap.wait()

    def join(part, there):
        value = part[:, :, s.c].astype(f32) + there[...].astype(f32)
        return value.astype(bf16).reshape(-1, *value.shape[2:])

    sum_d[...] = join(pd, td)
    sum_b[:, :, 512:2560] = join(pu, tu)
    sum_b[:, :, 0:512] = join(po, to)
    stores += copies(zip((sum_b, sum_d), outs_hbm[4:6]), out_sem.at[pl.ds(4, 2)])
    group = pl.ds(s.diag * s.nz, s.nz)
    far[:, :, 0:2560] = sum_b[group]
    for r in range(4):
        far[:, :, 2560 + 512 * r:3072 + 512 * r] = sum_d[group, 16 * r:16 * r + 16, :]
    stores += copies([(far, outs_hbm[6])], out_sem.at[pl.ds(6, 1)])
    do_ex.end()
    for w in range(2):
        onward(w, s.near[w], s.near[1 - w]).wait_send()
    for k in range(4):
        twin(k, s.c).wait_send()
    wait_all(stores)


def middle(n, nb, o, x, y, g, fz, fx, fy, par, bup):
    dma = pltpu.SemaphoreType.DMA
    rows = x.shape[0]
    nz = nb // 2
    saved = [
        ((rows, 512), bf16), ((rows, 512), f32), ((rows, 512), f32), ((n, 16, 128), f32),
        ((4 * nz, 16, 2560), bf16), ((4 * nz, 64, 512), bf16),
    ]
    return pl.pallas_call(
        functools.partial(middle_kernel, n, nb),
        out_shape=[jax.ShapeDtypeStruct((4, 16, 16, 128), bf16)]
        + [jax.ShapeDtypeStruct(shape, kind) for shape, kind in saved]
        + [jax.ShapeDtypeStruct((nz, 16, 4608), bf16)],
        in_specs=any_specs(9),
        out_specs=any_specs(8),
        scratch_shapes=[
            pltpu.VMEM(o.shape, bf16),
            pltpu.VMEM(x.shape, bf16),
            pltpu.VMEM(x.shape, bf16),
            pltpu.VMEM(x.shape, bf16),
            pltpu.VMEM((4, nb // 2, 2, 16, 4608), bf16),
            pltpu.VMEM((4, 4, 2, 4, 16, 512), bf16),
            pltpu.VMEM(par.shape, f32),
            pltpu.VMEM(bup.shape, f32),
            pltpu.VMEM((16, 4, 16, 128), bf16),
            pltpu.VMEM((16, 4, 16, 128), bf16),
            pltpu.VMEM((rows, 2048), f32),
            *[pltpu.VMEM(shape, kind) for shape, kind in saved],
            pltpu.VMEM((nz, 16, 4608), bf16),
            pltpu.VMEM((1, 2048), f32),
            pltpu.VMEM((rows, 512), bf16),
            pltpu.VMEM((rows, 2048), bf16),
            pltpu.VMEM((rows, 2048), bf16),
            *[pltpu.VMEM((4, nz, 2, *tail), bf16) for tail in ((16, 512), (16, 2048), (64, 512))],
            *[pltpu.VMEM((4, nz, *tail), bf16) for tail in ((16, 512), (16, 2048), (64, 512))],
            dma((9,)),
            dma((7,)),
            dma((2, 16)),
            dma((2, 16)),
            dma((2,)),
            dma((6,)),
            dma((6,)),
            dma((3,)),
            dma((3,)),
        ],
        compiler_params=pltpu.CompilerParams(
            collective_id=2, has_side_effects=True, vmem_limit_bytes=VMEM_BYTES
        ),
        name="middle",
    )(o, x, y, g, fz, fx, fy, par, bup)


def finish_kernel(n, nb, *refs):
    ins, far = refs[:8], refs[8]
    outs = refs[9:17]
    (
        dq, dkv, xm, dz1, pb, pd, gvec, wa,
        pa, ta, da, na, la, db, nb_, lb, dd, nd, ld, tv, dv, nv, lv,
        twin_buf, dkv_send, dkv_recv, dq_recv, dqkv, dx_send, dx_recv, gx, gq, gk, gv, go, gu, gd, gs,
        in_sem, far_sem, out_sem, rs_send, rs_recv, ex_send, ex_recv, dx_ssem, dx_rsem, tw_send, tw_recv,
    ) = refs[17:]
    s = Spot(nb)
    order = (1, 0, 4, 5, 6, 7, 2, 3)
    local = (dq, dkv, xm, dz1, pb, pd, gvec, wa)
    loads = copies([(ins[k], local[k]) for k in order], in_sem)
    corners = copies(
        [(far.at[:, :, pl.ds(0, 2560)], db)]
        + [(far.at[:, :, pl.ds(2560 + 512 * r, 512)], dd.at[:, pl.ds(16 * r, 16)]) for r in range(4)],
        far_sem,
    )
    greet_near(s)
    swap = remote(ins[1].at[:, :, 1 - s.c], twin_buf, tw_send, tw_recv, s.h, s.z * 2 + 1 - s.c)
    swap.start()
    jobs = [
        Scatter(s, *bufs, rs_send.at[k], rs_recv.at[k])
        for k, bufs in enumerate(
            ((pb, None, db, nb_, lb), (pd, None, dd, nd, ld), (gvec, tv, dv, nv, lv), (pa, ta, da, na, la))
        )
    ]
    wait_all(loads[:5])
    jobs[2].begin()
    swap.wait()

    def add(g):
        dkv_send[g] = (dkv[:, g, s.c].astype(f32) + twin_buf[:, g].astype(f32)).astype(bf16)

    each(4 * s.nz, add)
    plane = [Plane(s, ex_send.at[k], ex_recv.at[k]) for k in range(2)]

    def block(w, j, z, slot):
        g = j * s.nz + z
        src, dst = ((dkv_send.at[g], dkv_recv.at[slot, z]), (dq.at[:, g], dq_recv.at[slot, z]))[w]
        return plane[w].copy(src, dst, j, g, slot * s.nz + z)

    def pass_on(k):
        z = s.ahead(k)
        for w in range(2):
            each(4, lambda i: block(w, plane[w].to(i), z, s.h).start(), 1)
        dkv_recv[s.h, z] = dkv_send[s.h * s.nz + z]
        dq_recv[s.h, z] = dq[:, s.h * s.nz + z]

    each(s.nz + 1, pass_on, 1)
    wait_all(loads[5:])
    wait_all(corners)

    def back(z, slot):
        return remote(dx_send.at[z], dx_recv.at[slot], dx_ssem.at[z], dx_rsem.at[slot], s.h, z * 2 + s.c)

    def take(k):
        z = s.ahead(k)
        for w in range(2):
            each(4, lambda i: block(w, plane[w].frm(i), z, plane[w].frm(i)).wait_recv(), 1)
        for j in range(4):
            dqkv[z, :, 128 * j:128 * j + 128] = dkv_recv[j, z].reshape(128, 128)
        for t in range(2):
            first, second = weave(dq_recv[2 * t, z].reshape(64, 128), dq_recv[2 * t + 1, z].reshape(64, 128))
            dqkv[z, 0:64, 512 + 128 * t:640 + 128 * t] = first
            dqkv[z, 64:128, 512 + 128 * t:640 + 128 * t] = second
        dx_send[z] = dot_t(dqkv[z], wa[:, :, :, :, 0:768].reshape(512, 768)).astype(bf16)

    def take_and_send(k):
        take(k)
        back(s.ahead(k), s.z).start()

    each(s.nz, take_and_send, 1)
    for job in jobs[:2]:
        job.second()
    take(s.nz)
    dx_recv[s.z] = dx_send[s.z]
    tokens = xm[...].reshape(512, 512)
    pa[...] = dot_0(tokens, dqkv[...].reshape(512, 768)).astype(bf16).reshape(n, 16, 768)
    jobs[3].begin()
    jobs[2].second()
    jobs[3].second()
    for job in jobs:
        job.third()
    each(s.nz, lambda k: back(s.ahead(k), s.ahead(k)).wait_recv(), 1)
    for m in range(2):
        rows = slice(128 * m, 128 * m + 128)
        gx[rows, :] = dz1[rows, :] + (dx_recv[2 * m].astype(f32) + dx_recv[2 * m + 1].astype(f32))
    stores = copies([(gx, outs[0])], out_sem)
    total = jobs[0].total()
    go[...] = total[:, 0:512]
    gu[...] = total[:, 512:2560]
    gd[...] = jobs[1].total()
    gs[...] = jobs[2].total()
    stores += copies(zip((go, gu, gd, gs), outs[4:8]), out_sem.at[pl.ds(1, 4)])
    for w, part in enumerate(jobs[3].columns()):
        gq[:, 256 * w:256 * w + 256] = part[:, 512:768]
        for t in range(2):
            first, second = weave(part[:, 256 * t:256 * t + 128], part[:, 256 * t + 128:256 * t + 256])
            at = 256 * w + 128 * t
            gk[:, at:at + 128] = first
            gv[:, at:at + 128] = second
    stores += copies(zip((gq, gk, gv), outs[1:4]), out_sem.at[pl.ds(5, 3)])
    for w in range(2):
        each(4, lambda i: each(s.nz, lambda z: block(w, plane[w].to(i), z, s.h).wait_send()), 1)
    each(s.nz, lambda k: back(s.ahead(k), s.z).wait_send(), 1)
    for job in jobs:
        job.sent()
    wait_all(stores)


def finish(n, nb, dq, dkv, xm, dz1, pb, pd, gvec, wa, far):
    dma = pltpu.SemaphoreType.DMA
    nz = nb // 2
    rows = dz1.shape[0]

    def buffers(depth, width, kind):
        return [
            pltpu.VMEM((n, depth, width), kind),
            pltpu.VMEM((4, nz, depth, width), kind),
            pltpu.VMEM((nz, depth, width), kind),
            pltpu.VMEM((2, nz, depth, width), kind),
            pltpu.VMEM((nz, depth, width), kind),
        ]

    args = (dq, dkv, xm, dz1, pb, pd, gvec, wa)
    shapes = ((rows, 512), (16, 512), (16, 512), (16, 512), (16, 512), (16, 2048), (64, 512), (16, 128))
    return pl.pallas_call(
        functools.partial(finish_kernel, n, nb),
        out_shape=[jax.ShapeDtypeStruct(shape, f32) for shape in shapes],
        in_specs=any_specs(9),
        out_specs=any_specs(8),
        scratch_shapes=[
            *[pltpu.VMEM(arg.shape, arg.dtype) for arg in args],
            *buffers(16, 768, bf16),
            *buffers(16, 2560, bf16)[2:],
            *buffers(64, 512, bf16)[2:],
            *buffers(16, 128, f32)[1:],
            pltpu.VMEM((8, 16, 16, 128), bf16),
            pltpu.VMEM((16, 8, 16, 128), bf16),
            pltpu.VMEM((4, nz, 8, 16, 128), bf16),
            pltpu.VMEM((4, nz, 4, 16, 128), bf16),
            pltpu.VMEM((nz, 128, 768), bf16),
            pltpu.VMEM((nz, 128, 512), bf16),
            pltpu.VMEM((nz, 128, 512), bf16),
            *[pltpu.VMEM(shape, f32) for shape in shapes],
            dma((8,)),
            dma((5,)),
            dma((8,)),
            dma((4, 9 * nz)),
            dma((4, 9 * nz)),
            dma((2, 4 * nz)),
            dma((2, 4 * nz)),
            dma((nz,)),
            dma((nz,)),
            dma,
            dma,
        ],
        compiler_params=pltpu.CompilerParams(
            collective_id=3, has_side_effects=True, vmem_limit_bytes=VMEM_BYTES
        ),
        name="finish",
    )(*args, far)


def deliver_kernel(count, *refs):
    ins, outs = refs[:count], refs[count:2 * count + 7]
    stage, lines, (in_sem, sems) = refs[2 * count + 7:3 * count + 7], refs[3 * count + 7:3 * count + 15], refs[-2:]
    loads = copies(zip(ins, stage), in_sem)
    jobs = []
    for k in range(count - 1):
        loads[k].wait()
        jobs += copies([(stage[k], outs[k])], sems.at[pl.ds(k, 1)])
    loads[-1].wait()
    vec = stage[-1]
    lines[0][...] = vec[0:1, 0:64].reshape(64)
    for k in range(1, 8):
        lines[k][...] = vec[k:k + 1, 0:16].reshape(16)
    jobs += copies(zip(lines, outs[count - 1:]), sems.at[pl.ds(count - 1, 8)])
    wait_all(jobs)


def deliver(arrays, vec):
    count = len(arrays) + 1
    lines = [(64,)] + [(16,)] * 7
    return pl.pallas_call(
        functools.partial(deliver_kernel, count),
        out_shape=[jax.ShapeDtypeStruct(a.shape, a.dtype) for a in arrays]
        + [jax.ShapeDtypeStruct(shape, f32) for shape in lines],
        in_specs=any_specs(count),
        out_specs=any_specs(count + 7),
        scratch_shapes=[
            *[pltpu.VMEM(a.shape, a.dtype) for a in (*arrays, vec)],
            *[pltpu.VMEM(shape, f32) for shape in lines],
            pltpu.SemaphoreType.DMA((count,)),
            pltpu.SemaphoreType.DMA((count + 7,)),
        ],
        compiler_params=pltpu.CompilerParams(vmem_limit_bytes=VMEM_BYTES),
        name="deliver",
    )(*arrays, vec)


def by_pairs(
    stream, accumulator, upstream, segment_ids, w_query, w_key, w_value, w_out, w_up, b_up, w_down, b_down,
    gain_attn, bias_attn, gain_ffn, bias_ffn, gain_final, bias_final,
):
    nb = lax.axis_size("blk")
    n = 4 * nb
    x = stream.reshape(256, 512)
    y = accumulator.reshape(256, 512)
    g = upstream.reshape(256, 512)
    smalls = (b_up, b_down, gain_attn, bias_attn, gain_ffn, bias_ffn, gain_final, bias_final)
    q, kv, xm, wa, fz, par, bup, seg_k, seg_q = project(
        n, nb, stream.reshape(2, 128, 512), w_query, w_key, w_value, w_out, w_up, w_down, segment_ids.reshape(2, 128), smalls
    )
    fx, fy = (lax.ppermute(fz, "head", [(h, h ^ w) for h in range(4)]) for w in (1, 2))
    o, of, lse, kv2, kvt = attn_fwd(q.reshape(4, 256, 128), kv.reshape(4096, 128), seg_q, seg_k)
    do, out, dacc, dz1, gvec, pb, pd, far = middle(
        n, nb, o.reshape(4, 16, 16, 128), x, y, g, fz, fx, fy, par, bup
    )
    far = lax.ppermute(far, "head", [(h, 3 - h) for h in range(4)])
    dq, dkv, out, dacc = attn_bwd(
        q.reshape(4, 256, 128), do.reshape(4, 256, 128), of, lse, kv2, kvt, seg_q, seg_k, out, dacc
    )
    gx, gq, gk, gv, go, gu, gd, gs = finish(
        n, nb, dq.reshape(4, 16, 16, 128), dkv.reshape(8, 16, 2, 16, 128), xm, dz1, pb, pd, gvec, wa, far
    )
    gx, gq, gk, gv, go, gu, gd, gbu, *small_grads = deliver((gx, gq, gk, gv, go, gu, gd), gs)
    return (
        out.reshape(stream.shape), gx.reshape(stream.shape), dacc.reshape(stream.shape),
        gq, gk, gv, go, gu, gbu, gd, *small_grads,
    )


def pairs_fit(mesh, shape):
    return mesh.shape["head"] == 4 and mesh.shape["blk"] == 8 and shape == (2, 32, 128, 512)


def solution(mesh):
    def step(*args):
        return run(by_pairs if pairs_fit(mesh, args[0].shape) else local, mesh)(*args)

    return step


def run(body, mesh):
    return jax.shard_map(
        body,
        mesh=mesh,
        in_specs=(
            P(None, ("head", "blk"), None, None),
            P(None, ("head", "blk"), None, None),
            P(None, ("head", "blk"), None, None),
            P(None, ("head", "blk"), None),
            P(("head", "blk"), None),
            P(("head", "blk"), None),
            P(("head", "blk"), None),
            P(("head", "blk"), None),
            P(("head", "blk"), None),
            P(("head", "blk")),
            P(("head", "blk"), None),
            P(("head", "blk")),
            P(("head", "blk")),
            P(("head", "blk")),
            P(("head", "blk")),
            P(("head", "blk")),
            P(("head", "blk")),
            P(("head", "blk")),
        ),
        out_specs=(
            P(None, ("head", "blk"), None, None),
            P(None, ("head", "blk"), None, None),
            P(None, ("head", "blk"), None, None),
            P(("head", "blk"), None),
            P(("head", "blk"), None),
            P(("head", "blk"), None),
            P(("head", "blk"), None),
            P(("head", "blk"), None),
            P(("head", "blk")),
            P(("head", "blk"), None),
            P(("head", "blk")),
            P(("head", "blk")),
            P(("head", "blk")),
            P(("head", "blk")),
            P(("head", "blk")),
            P(("head", "blk")),
            P(("head", "blk")),
        ),
        check_vma=False,
    )
```

```python
import functools
import math

import jax
import jax.numpy as jnp
from jax import lax
from jax.experimental import pallas as pl
from jax.experimental.pallas import tpu as pltpu
from jax.sharding import PartitionSpec as P

DH = 64
f32, bf16 = jnp.float32, jnp.bfloat16
MESH = pl.DeviceIdType.MESH
FAR = -1e30
VMEM_BYTES = 60 << 20


EPSILON = 1e-05


def norm_forward(inputs, norm_gain, norm_bias):
    average = jnp.mean(inputs, axis=-1, keepdims=True)
    centered = inputs - average
    inv_std = lax.rsqrt(jnp.mean(centered * centered, axis=-1, keepdims=True) + EPSILON)
    normed = centered * inv_std
    return (normed * norm_gain + norm_bias, normed, inv_std)


def norm_backward(gradient, normed, inv_std, norm_gain):
    scaled = gradient * norm_gain
    projected = (
        scaled
        - jnp.mean(scaled, axis=-1, keepdims=True)
        - normed * jnp.mean(scaled * normed, axis=-1, keepdims=True)
    )
    return (inv_std * projected, jnp.sum(gradient * normed, axis=0), jnp.sum(gradient, axis=0))


def smooth_gate(pre_act):
    return jax.nn.gelu(pre_act, approximate=False)


def split_rows(length):
    block_len = math.gcd(length, 512)
    return (length // block_len, block_len)


def block_scores(queries, query_seg, key_rows, key_seg, scaling):
    scores = (
        jnp.einsum("sgd,kgd->sgk", queries, key_rows, preferred_element_type=jnp.float32) * scaling
    )
    allowed = query_seg[:, None, None] == key_seg[None, None, :]
    return (scores, allowed)


def block_grads(
    queries, query_seg, grad_rows, log_total, row_delta, key_rows, value_rows, key_seg, scaling
):
    scores, allowed = block_scores(queries, query_seg, key_rows, key_seg, scaling)
    attn_prob = jnp.where(allowed, jnp.exp(scores - log_total[:, :, None]), 0.0)
    prob_grad = jnp.einsum(
        "sgd,kgd->sgk", grad_rows, value_rows, preferred_element_type=jnp.float32
    )
    score_grad = (attn_prob * (prob_grad - row_delta[:, :, None]) * scaling).astype(jnp.bfloat16)
    return (attn_prob.astype(jnp.bfloat16), score_grad)


def key_blocks(key_rows, value_rows, key_seg, groups):
    block_num, block_len = split_rows(key_rows.shape[0])
    return (
        key_rows.reshape(block_num, block_len, groups, -1),
        value_rows.reshape(block_num, block_len, groups, -1),
        key_seg.reshape(block_num, block_len),
    )


def attend_fold(queries, query_seg, scaling, carried, portion):
    key_rows, value_rows, key_seg = portion

    def step(running, blocks):
        key_part, value_part, seg_part = blocks
        old_max, old_total, weighted = running
        scores, allowed = block_scores(queries, query_seg, key_part, seg_part, scaling)
        row_max = jnp.maximum(old_max, jnp.max(jnp.where(allowed, scores, -1e30), axis=2))
        exp_scores = jnp.where(allowed, jnp.exp(scores - row_max[:, :, None]), 0.0)
        rescale = jnp.exp(old_max - row_max)
        new_total = old_total * rescale + jnp.sum(exp_scores, axis=2)
        weighted = weighted * rescale[:, :, None] + jnp.einsum(
            "sgk,kgd->sgd",
            exp_scores.astype(jnp.bfloat16),
            value_part,
            preferred_element_type=jnp.float32,
        )
        return ((row_max, new_total, weighted), None)

    running, unused = lax.scan(
        step, carried, key_blocks(key_rows, value_rows, key_seg, queries.shape[1])
    )
    return running


def local(
    stream,
    accumulator,
    upstream,
    segment_ids,
    w_query,
    w_key,
    w_value,
    w_out,
    w_up,
    b_up,
    w_down,
    b_down,
    gain_attn,
    bias_attn,
    gain_ffn,
    bias_ffn,
    gain_final,
    bias_final,
):
    heads_axis = lax.axis_size("head")
    micro = stream.shape[0]
    tokens = stream.shape[2]
    width = stream.shape[3]
    group_width = width // heads_axis
    groups = group_width // DH
    scaling = DH ** (-0.5)
    f32 = jnp.float32
    bf16 = jnp.bfloat16
    out_list = []
    stream_grads = []
    accum_grads = []
    grad_totals = None
    for micro_step in range(micro):
        (
            q_weight,
            k_weight,
            v_weight,
            o_weight,
            up_weight,
            up_bias,
            down_weight,
            down_bias,
            gain_one,
            shift_one,
            gain_two,
            shift_two,
            gain_three,
            shift_three,
        ) = (
            lax.all_gather(w_query, ("head", "blk"), axis=0, tiled=True),
            lax.all_gather(w_key, ("head", "blk"), axis=0, tiled=True),
            lax.all_gather(w_value, ("head", "blk"), axis=0, tiled=True),
            lax.all_gather(w_out, ("head", "blk"), axis=0, tiled=True),
            lax.all_gather(w_up, ("head", "blk"), axis=0, tiled=True),
            lax.all_gather(b_up, ("head", "blk"), axis=0, tiled=True),
            lax.all_gather(w_down, ("head", "blk"), axis=0, tiled=True),
            lax.all_gather(b_down, ("head", "blk"), axis=0, tiled=True),
            lax.all_gather(gain_attn, ("head", "blk"), axis=0, tiled=True),
            lax.all_gather(bias_attn, ("head", "blk"), axis=0, tiled=True),
            lax.all_gather(gain_ffn, ("head", "blk"), axis=0, tiled=True),
            lax.all_gather(bias_ffn, ("head", "blk"), axis=0, tiled=True),
            lax.all_gather(gain_final, ("head", "blk"), axis=0, tiled=True),
            lax.all_gather(bias_final, ("head", "blk"), axis=0, tiled=True),
        )
        inputs = stream[micro_step, 0]
        input_wide = inputs.astype(f32)
        carried = accumulator[micro_step, 0].astype(f32)
        segs = segment_ids[micro_step, 0]
        projections = jnp.stack(
            [
                jnp.dot(inputs, q_weight, preferred_element_type=f32),
                jnp.dot(inputs, k_weight, preferred_element_type=f32),
                jnp.dot(inputs, v_weight, preferred_element_type=f32),
            ]
        ).astype(bf16)
        projections = projections.reshape(3, tokens, heads_axis, group_width)
        seg_wide = jnp.broadcast_to(segs[None, :, None, None], (1, tokens, heads_axis, 1))
        regrouped, seg_group = (
            lax.all_to_all(projections, "head", split_axis=2, concat_axis=1, tiled=True),
            lax.all_to_all(seg_wide, "head", split_axis=2, concat_axis=1, tiled=True),
        )
        rows = regrouped.shape[1]
        query_loc = regrouped[0, :, 0]
        key_loc = regrouped[1, :, 0]
        value_loc = regrouped[2, :, 0]
        seg_loc = seg_group[0, :, 0, 0]
        queries3 = query_loc.reshape(rows, groups, DH)
        start_state = (
            jnp.full((rows, groups), -1e30, f32),
            jnp.zeros((rows, groups), f32),
            jnp.zeros((rows, groups, DH), f32),
        )
        row_max, row_total, weighted = attend_fold(
            queries3,
            seg_loc,
            scaling,
            start_state,
            (
                lax.all_gather(key_loc, "blk", axis=0, tiled=True),
                lax.all_gather(value_loc, "blk", axis=0, tiled=True),
                lax.all_gather(seg_loc, "blk", axis=0, tiled=True),
            ),
        )
        attn_out = weighted / row_total[:, :, None]
        log_total = row_max + jnp.log(row_total)
        attn_send = attn_out.astype(bf16).reshape(rows, 1, group_width)
        mixed = lax.all_to_all(attn_send, "head", split_axis=0, concat_axis=1, tiled=True).reshape(
            tokens, width
        )
        branch = jnp.dot(mixed, o_weight, preferred_element_type=f32)
        first, normed_one, inv_one = norm_forward(
            input_wide + branch, gain_one.astype(f32), shift_one.astype(f32)
        )
        first_low = first.astype(bf16)
        hidden_pre = jnp.dot(first_low, up_weight, preferred_element_type=f32) + up_bias.astype(f32)
        hidden_act, gate_pull = jax.vjp(smooth_gate, hidden_pre)
        hidden = hidden_act.astype(bf16)
        feed = jnp.dot(hidden, down_weight, preferred_element_type=f32) + down_bias.astype(f32)
        second, normed_two, inv_two = norm_forward(
            first + feed, gain_two.astype(f32), shift_two.astype(f32)
        )
        final, normed_three, inv_three = norm_forward(
            carried + branch + feed, gain_three.astype(f32), shift_three.astype(f32)
        )
        out_list.append((second + final).astype(bf16))
        cotangent = upstream[micro_step, 0].astype(f32)
        accum_grad, gain3_grad, shift3_grad = norm_backward(
            cotangent, normed_three, inv_three, gain_three.astype(f32)
        )
        second_grad, gain2_grad, shift2_grad = norm_backward(
            cotangent, normed_two, inv_two, gain_two.astype(f32)
        )
        feed_grad = second_grad + accum_grad
        feed_low = feed_grad.astype(bf16)
        down_grad = jnp.dot(hidden.T, feed_low, preferred_element_type=f32)
        (hidden_grad,) = gate_pull(jnp.dot(feed_low, down_weight.T, preferred_element_type=f32))
        hidden_low = hidden_grad.astype(bf16)
        up_grad = jnp.dot(first_low.T, hidden_low, preferred_element_type=f32)
        first_grad = second_grad + jnp.dot(hidden_low, up_weight.T, preferred_element_type=f32)
        resid_grad, gain1_grad, shift1_grad = norm_backward(
            first_grad, normed_one, inv_one, gain_one.astype(f32)
        )
        branch_low = (resid_grad + accum_grad).astype(bf16)
        out_wgrad = jnp.dot(mixed.T, branch_low, preferred_element_type=f32)
        mixed_grad = jnp.dot(branch_low, o_weight.T, preferred_element_type=f32).astype(bf16)
        mixed_grad = mixed_grad.reshape(tokens, heads_axis, group_width)
        grad_group = lax.all_to_all(mixed_grad, "head", split_axis=1, concat_axis=0, tiled=True)
        grad_loc = grad_group[:, 0]
        grad3 = grad_loc.reshape(rows, groups, DH)
        row_delta = jnp.sum(grad3.astype(f32) * attn_out, axis=2)
        whole_keys, whole_values, whole_seg = (
            lax.all_gather(key_loc, "blk", axis=0, tiled=True),
            lax.all_gather(value_loc, "blk", axis=0, tiled=True),
            lax.all_gather(seg_loc, "blk", axis=0, tiled=True),
        )

        def backward_step(running, blocks):
            key_part, value_part, seg_part = blocks
            attn_prob, score_grad = block_grads(
                queries3,
                seg_loc,
                grad3,
                log_total,
                row_delta,
                key_part,
                value_part,
                seg_part,
                scaling,
            )
            running = running + jnp.einsum(
                "sgk,kgd->sgd", score_grad, key_part, preferred_element_type=f32
            )
            key_term = jnp.einsum("sgk,sgd->kgd", score_grad, queries3, preferred_element_type=f32)
            value_term = jnp.einsum("sgk,sgd->kgd", attn_prob, grad3, preferred_element_type=f32)
            return (running, (key_term, value_term))

        query_grad, (key_terms, value_terms) = lax.scan(
            backward_step,
            jnp.zeros((rows, groups, DH), f32),
            key_blocks(whole_keys, whole_values, whole_seg, groups),
        )
        key_grad, value_grad = (
            lax.psum_scatter(
                key_terms.reshape(-1, group_width), "blk", scatter_dimension=0, tiled=True
            ),
            lax.psum_scatter(
                value_terms.reshape(-1, group_width), "blk", scatter_dimension=0, tiled=True
            ),
        )
        grad_stack = jnp.stack(
            [query_grad.reshape(rows, group_width), key_grad, value_grad]
        ).astype(bf16)
        grad_stack = grad_stack.reshape(3, rows, 1, group_width)
        returned = lax.all_to_all(
            grad_stack, "head", split_axis=1, concat_axis=2, tiled=True
        ).reshape(3, tokens, width)
        query_wgrad = jnp.dot(inputs.T, returned[0], preferred_element_type=f32)
        key_wgrad = jnp.dot(inputs.T, returned[1], preferred_element_type=f32)
        value_wgrad = jnp.dot(inputs.T, returned[2], preferred_element_type=f32)
        input_grad = (
            resid_grad
            + jnp.dot(returned[0], q_weight.T, preferred_element_type=f32)
            + jnp.dot(returned[1], k_weight.T, preferred_element_type=f32)
            + jnp.dot(returned[2], v_weight.T, preferred_element_type=f32)
        )
        stream_grads.append(input_grad)
        accum_grads.append(accum_grad)
        step_grads = (
            query_wgrad,
            key_wgrad,
            value_wgrad,
            out_wgrad,
            up_grad,
            jnp.sum(hidden_grad, axis=0),
            down_grad,
            jnp.sum(feed_grad, axis=0),
            gain1_grad,
            shift1_grad,
            gain2_grad,
            shift2_grad,
            gain3_grad,
            shift3_grad,
        )
        if grad_totals is None:
            grad_totals = step_grads
        else:
            grad_totals = tuple((older + newer for older, newer in zip(grad_totals, step_grads)))
    summed = lax.psum_scatter(grad_totals, ("head", "blk"), scatter_dimension=0, tiled=True)
    layer_out = jnp.stack(out_list)[:, None]
    grad_stream = jnp.stack(stream_grads)[:, None]
    grad_accum = jnp.stack(accum_grads)[:, None]
    return (
        layer_out,
        grad_stream,
        grad_accum,
        summed[0],
        summed[1],
        summed[2],
        summed[3],
        summed[4],
        summed[5],
        summed[6],
        summed[7],
        summed[8],
        summed[9],
        summed[10],
        summed[11],
        summed[12],
        summed[13],
    )


def dot_t(a, b):
    return lax.dot_general(a, b, (((1,), (1,)), ((), ())), preferred_element_type=f32)

def dot_n(a, b):
    return lax.dot_general(a, b, (((1,), (0,)), ((), ())), preferred_element_type=f32)

def dot_0(a, b):
    return lax.dot_general(a, b, (((0,), (0,)), ((), ())), preferred_element_type=f32)

def lanes(shape):
    return lax.broadcasted_iota(jnp.int32, shape, len(shape) - 1)

def query_marks(seg_row):
    wide = jnp.broadcast_to(seg_row, (128, seg_row.shape[1])).T
    return (wide == lanes(wide.shape)).astype(f32).astype(bf16)

def half_lanes(tile, half):
    wide = tile.astype(f32)
    if half:
        wide = pltpu.roll(wide, 64, 1)
    return jnp.where(lanes(wide.shape) < 64, wide, 0.0).astype(bf16)

def key_steps(bounds, low, high):
    chunks, keys = bounds.shape
    first = sum(jnp.where(bounds[t, keys - 1] < low, 1, 0) for t in range(chunks))
    last = sum(jnp.where(bounds[t, 0] <= high, 1, 0) for t in range(chunks))
    pairs = (last - first + 1) // 2
    start = jnp.minimum(first, chunks - 2 * pairs)
    return start, pairs // 2, lax.rem(pairs, 2)


def walk(step, fours, twos, carry):
    carry = lax.fori_loop(0, fours, lambda t, c: step(4, 4 * t, c), carry)
    return lax.fori_loop(0, twos, lambda t, c: step(2, 4 * fours, c), carry)


def attn_fwd_kernel(
    q_hbm, kv_hbm, seg_q_hbm, seg_k_hbm, o_hbm, of_hbm, lse_hbm, kv2_hbm, kvt_hbm,
    q_ref, kv_ref, seg_q_ref, seg_k_ref, bounds, o_ref, of_ref, lse_ref, kv2_ref, kvt_ref, vo_ref, in_sem, out_sem,
):
    loads = copies(
        [(seg_q_hbm, seg_q_ref), (seg_k_hbm, seg_k_ref), (seg_k_hbm, bounds), (kv_hbm, kv_ref), (q_hbm, q_ref)], in_sem
    )
    wait_all(loads)
    chunks, keys = seg_k_ref.shape
    log_scale = math.log2(math.e) * DH ** (-0.5)

    def prepare(t, c):
        rows = pl.ds(pl.multiple_of(t * keys, keys), keys)
        kv = kv_ref[rows, :]
        marks = jnp.where(seg_k_ref[pl.ds(t, 1), :] == rows_of((128, keys)), 0.0, FAR)
        kvt_ref[0:128, rows] = kv.T
        kvt_ref[128:256, rows] = marks.astype(bf16)
        kv2_ref[rows, 0:128] = kv
        kv2_ref[rows, 128:256] = marks.T.astype(bf16)
        vo_ref[rows, :] = jnp.where(lanes(kv.shape) < 64, 1.0, kv.astype(f32)).astype(bf16)
        return c

    lax.fori_loop(0, chunks, prepare, 0)
    stores = copies([(kv2_ref, kv2_hbm), (kvt_ref, kvt_hbm)], out_sem)

    def tile(j, c):
        q_tile = q_ref[j]
        rows = q_tile.shape[0]
        outs = []
        for half in range(2):
            i = half * (chunks // 2) + j
            left = half_lanes(q_tile, half)
            left = jnp.concatenate([left, query_marks(seg_q_ref[pl.ds(i, 1), :])], axis=1)
            low, high = bounds[i, 0], bounds[i, keys - 1]
            start, fours, twos = key_steps(bounds, low, high)

            def step(width, t, carry):
                top, acc = carry
                at = pl.ds(pl.multiple_of((start + t) * keys, keys), width * keys)
                s = dot_n(left, kvt_ref[:, at])
                new = jnp.maximum(top, jnp.max(s, axis=1, keepdims=True))
                p = jnp.exp2((s - new) * log_scale)
                acc = acc * jnp.exp2((top - new) * log_scale) + dot_n(p.astype(bf16), vo_ref[at, :])
                return new, acc

            carry = (jnp.full((rows, 1), FAR, f32), jnp.zeros((rows, 128), f32))
            top, acc = walk(step, fours, twos, carry)
            total = pltpu.roll(acc, 64, 1)
            outs.append(acc / total)
            lse = jnp.broadcast_to(top * log_scale, acc.shape) + jnp.log2(acc)
            lse_ref[pl.ds(i, 1), :] = lse.T[0:1, :]
        o = jnp.where(lanes(outs[0].shape) < 64, pltpu.roll(outs[0], 64, 1), outs[1])
        of_ref[j] = o
        o_ref[j] = o.astype(bf16)
        return c

    lax.fori_loop(0, chunks // 2, tile, 0)
    stores += copies([(o_ref, o_hbm), (of_ref, of_hbm), (lse_ref, lse_hbm)], out_sem.at[pl.ds(2, 3)])
    wait_all(stores)


def attn_fwd(q, kv, seg_q, seg_k):
    chunks, keys = seg_k.shape
    dma = pltpu.SemaphoreType.DMA
    shapes = (
        (q.shape, bf16), (q.shape, f32), (seg_q.shape, f32), ((chunks * keys, 256), bf16), ((256, chunks * keys), bf16)
    )
    return pl.pallas_call(
        attn_fwd_kernel,
        out_shape=[jax.ShapeDtypeStruct(shape, kind) for shape, kind in shapes],
        in_specs=any_specs(4),
        out_specs=any_specs(5),
        scratch_shapes=[
            *[pltpu.VMEM(a.shape, a.dtype) for a in (q, kv, seg_q, seg_k)],
            pltpu.SMEM(seg_k.shape, jnp.int32),
            *[pltpu.VMEM(shape, kind) for shape, kind in shapes],
            pltpu.VMEM((chunks * keys, 128), bf16),
            dma((5,)),
            dma((5,)),
        ],
        compiler_params=pltpu.CompilerParams(vmem_limit_bytes=VMEM_BYTES),
        cost_estimate=pl.CostEstimate(flops=10**10, bytes_accessed=10**7, transcendentals=10**7),
        name="attn_fwd",
    )(q, kv, seg_q, seg_k)


def attn_bwd_kernel(
    q_hbm, do_hbm, of_hbm, lse_hbm, kv2_hbm, kvt_hbm, seg_q_hbm, seg_k_hbm, pass1, pass2, dq_hbm, dkv_hbm, out1, out2,
    q_ref, do_ref, of_ref, lse_ref, kv2_ref, kvt_ref, seg_q_ref, bounds, dq_ref, dkv_low, dkv_ref, hold1, hold2, in_sem, out_sem,
):
    loads = copies(
        [
            (q_hbm, q_ref), (do_hbm, do_ref), (of_hbm, of_ref), (lse_hbm, lse_ref), (kv2_hbm, kv2_ref),
            (seg_q_hbm, seg_q_ref), (seg_k_hbm, bounds),
            (pass1, hold1), (pass2, hold2), (kvt_hbm, kvt_ref),
        ],
        in_sem,
    )
    dkv_ref[...] = jnp.zeros_like(dkv_ref)
    wait_all(loads)
    stores = copies([(hold1, out1), (hold2, out2)], out_sem)
    chunks, keys = bounds.shape
    log_scale = math.log2(math.e) * DH ** (-0.5)

    def tile(j, c):
        q_tile, do_tile = q_ref[j], do_ref[j]
        rows = q_tile.shape[0]
        prod = do_tile.astype(f32) * of_ref[j]
        prod = prod.T
        dqs = []
        for half in range(2):
            i = half * (chunks // 2) + j
            left = half_lanes(q_tile, half)
            grad = do_tile.astype(f32)
            if not half:
                grad = pltpu.roll(grad, 64, 1)
            grad = jnp.where(lanes(grad.shape) < 64, 0.0, grad).astype(bf16)
            delta = jnp.sum(prod[64 * half:64 * half + 64], axis=0, keepdims=True)
            lse = lse_ref[pl.ds(i, 1), :]
            both = jnp.concatenate([left, grad], axis=0)
            marks = query_marks(seg_q_ref[pl.ds(i, 1), :])
            right = jnp.concatenate([both, jnp.concatenate([marks, jnp.zeros_like(marks)], axis=0)], axis=1).T
            low, high = bounds[i, 0], bounds[i, keys - 1]
            start, fours, twos = key_steps(bounds, low, high)

            def step(width, t, dq):
                at = pl.ds(pl.multiple_of((start + t) * keys, keys), width * keys)
                sdp = dot_n(kv2_ref[at, :], right)
                p = jnp.exp2(sdp[:, :rows] * log_scale - lse)
                ds = (p * (sdp[:, rows:] - delta)).astype(bf16)
                dkv_ref[at, :] += dot_n(jnp.concatenate([ds, p.astype(bf16)], axis=1), both)
                return dq + dot_n(kvt_ref[0:128, at], ds)

            dqs.append(walk(step, fours, twos, jnp.zeros((128, rows), f32)).T)
        dq = jnp.where(lanes(dqs[0].shape) < 64, dqs[0], pltpu.roll(dqs[1], 64, 1))
        dq_ref[j] = (dq * DH ** (-0.5)).astype(bf16)
        return c

    lax.fori_loop(0, chunks // 2, tile, 0)
    dkv = dkv_ref[...]
    dkv_low[...] = jnp.where(lanes(dkv.shape) < 64, dkv * DH ** (-0.5), dkv).astype(bf16)
    stores += copies([(dq_ref, dq_hbm), (dkv_low, dkv_hbm)], out_sem.at[pl.ds(2, 2)])
    wait_all(stores)


def attn_bwd(q, do, of, lse, kv2, kvt, seg_q, seg_k, pass1, pass2):
    dma = pltpu.SemaphoreType.DMA
    shapes = ((q.shape, bf16), ((kv2.shape[0], 128), bf16))
    return pl.pallas_call(
        attn_bwd_kernel,
        out_shape=[jax.ShapeDtypeStruct(shape, kind) for shape, kind in shapes]
        + [jax.ShapeDtypeStruct(a.shape, a.dtype) for a in (pass1, pass2)],
        in_specs=any_specs(10),
        out_specs=any_specs(4),
        scratch_shapes=[
            *[pltpu.VMEM(a.shape, a.dtype) for a in (q, do, of, lse, kv2, kvt, seg_q)],
            pltpu.SMEM(seg_k.shape, jnp.int32),
            *[pltpu.VMEM(shape, kind) for shape, kind in shapes],
            pltpu.VMEM((kv2.shape[0], 128), f32),
            *[pltpu.VMEM(a.shape, a.dtype) for a in (pass1, pass2)],
            dma((10,)),
            dma((4,)),
        ],
        compiler_params=pltpu.CompilerParams(vmem_limit_bytes=VMEM_BYTES),
        cost_estimate=pl.CostEstimate(flops=10**10, bytes_accessed=10**7, transcendentals=10**7),
        name="attn_bwd",
    )(q, do, of, lse, kv2, kvt, seg_q, seg_k, pass1, pass2)


class Spot:
    def __init__(self, nb):
        self.nb, self.nz = nb, nb // 2
        self.h, b = lax.axis_index("head"), lax.axis_index("blk")
        self.z, self.c = b // 2, lax.rem(b, 2)
        self.near = (self.h + 1 - 2 * lax.rem(self.h, 2), lax.rem(self.h + 2, 4))
        self.diag = 3 - self.h
        self.me = self.h * nb + b

    def index(self, h, z, c):
        return h * self.nb + z * 2 + c

    def ahead(self, k):
        return lax.rem(self.z + k, self.nz)


def remote(src, dst, send, recv, h, b):
    return pltpu.make_async_remote_copy(
        src_ref=src,
        dst_ref=dst,
        send_sem=send,
        recv_sem=recv,
        device_id={"head": h, "blk": b},
        device_id_type=MESH,
    )


def each(count, body, start=0):
    def run(i, c):
        body(i)
        return c

    lax.fori_loop(start, count, run, 0)


def hail(h, b):
    pl.semaphore_signal(
        pltpu.get_barrier_semaphore(), inc=1, device_id={"head": h, "blk": b}, device_id_type=MESH
    )


def greet_near(s):
    for k in range(1, s.nz):
        hail(s.h, s.ahead(k) * 2 + s.c)
    for i in range(1, 4):
        hail(lax.rem(s.h + i, 4), s.z * 2 + s.c)
    hail(s.h, s.z * 2 + 1 - s.c)
    pl.semaphore_wait(pltpu.get_barrier_semaphore(), s.nz + 3)


def greet_core(s):
    def signal(i):
        t = lax.rem(s.me + 2 * i, 4 * s.nb)
        hail(t // s.nb, lax.rem(t, s.nb))

    each(2 * s.nb, signal, 1)
    hail(s.h, s.z * 2 + 1 - s.c)
    pl.semaphore_wait(pltpu.get_barrier_semaphore(), 2 * s.nb)


class Scatter:
    def __init__(self, spot, part, twin, diag, near, line, send, recv):
        self.s, self.part, self.t, self.d, self.n, self.l = spot, part, twin, diag, near, line
        self.send, self.recv = send, recv

    def copy(self, src, dst, k, h, z, c, recv_k=None):
        recv_k = k if recv_k is None else recv_k
        return remote(src, dst, self.send.at[k], self.recv.at[recv_k], h, z * 2 + c)

    def mine(self, h, z):
        return h * self.s.nz + z if self.t is None else self.s.index(h, z, self.s.c)

    def to_twin(self, h, z):
        s = self.s
        src = self.part.at[s.index(h, z, 1 - s.c)]
        return self.copy(src, self.t.at[h, z], h * s.nz + z, s.h, s.z, 1 - s.c)

    def to_diag(self, z):
        s = self.s
        src = self.part.at[self.mine(s.diag, z)]
        return self.copy(src, self.d.at[z], 4 * s.nz + z, s.diag, s.z, s.c)

    def to_near(self, w, z):
        s = self.s
        src = self.part.at[self.mine(s.near[w], z)]
        return self.copy(src, self.n.at[w, z], (6 + w) * s.nz + z, s.near[w], s.z, s.c)

    def to_line(self, z):
        s = self.s
        src = self.part.at[self.mine(s.h, z)]
        return self.copy(src, self.l.at[s.z], 8 * s.nz + z, s.h, z, s.c, 8 * s.nz + s.z)

    def from_line(self, z):
        s = self.s
        src = self.part.at[self.mine(s.h, z)]
        return self.copy(src, self.l.at[z], 8 * s.nz + z, s.h, z, s.c)

    def begin(self):
        each(4, lambda h: each(self.s.nz, lambda z: self.to_twin(h, z).start()))

    def pair(self, h, z):
        if self.t is None:
            return self.part[self.mine(h, z)].astype(f32)
        self.to_twin(h, z).wait_recv()
        return self.part[self.mine(h, z)].astype(f32) + self.t[h, z].astype(f32)

    def keep(self, h, z, value):
        self.part[self.mine(h, z)] = value.astype(self.part.dtype)

    def second(self):
        s = self.s

        def go(k):
            z = s.ahead(k)
            for w in range(2):
                if self.t is not None:
                    self.keep(s.near[w], z, self.pair(s.near[w], z))
                self.to_near(w, z).start()
            if self.t is not None:
                self.keep(s.diag, z, self.pair(s.diag, z))
                self.to_diag(z).start()

        each(s.nz + 1, go, 1)

    def joined(self, z):
        value = self.pair(self.s.h, z)
        if self.t is not None:
            self.to_diag(z).wait_recv()
        value = value + self.d[z].astype(f32)
        for w in range(2):
            self.to_near(w, z).wait_recv()
            value = value + self.n[w, z].astype(f32)
        return value

    def third(self):
        s = self.s

        def go(k):
            z = s.ahead(k)
            self.keep(s.h, z, self.joined(z))
            self.to_line(z).start()

        each(s.nz, go, 1)

    def columns(self):
        s = self.s
        self.l[s.z] = self.joined(s.z).astype(self.l.dtype)
        each(s.nz, lambda k: self.from_line(s.ahead(k)).wait_recv(), 1)
        return [self.l[w].astype(f32) + self.l[w + 2].astype(f32) for w in range(2)]

    def total(self):
        s = self.s
        value = self.joined(s.z)

        def go(k, value):
            z = s.ahead(k)
            self.from_line(z).wait_recv()
            return value + self.l[z].astype(f32)

        return lax.fori_loop(1, s.nz, go, value)

    def sent(self):
        s = self.s

        def go(z):
            if self.t is not None:
                each(4, lambda h: self.to_twin(h, z).wait_send())
                self.to_diag(z).wait_send()
            for w in range(2):
                self.to_near(w, z).wait_send()

        each(s.nz, go)
        each(s.nz, lambda k: self.to_line(s.ahead(k)).wait_send(), 1)


class Exchange:
    def __init__(self, spot, src, dst, send, recv, local):
        self.s, self.src, self.dst, self.send, self.recv, self.local = spot, src, dst, send, recv, local
        self.g = spot.me // 2

    def copy(self, i, back=False):
        s = self.s
        to = lax.rem(self.g + i, 16)
        t = to * 2 + s.c
        src = self.src(to)
        dst = self.dst(lax.rem(self.g + 16 - i, 16)) if back else self.dst(self.g)
        return remote(src, dst, self.send.at[i], self.recv.at[i], t // s.nb, lax.rem(t, s.nb))

    def own(self):
        return pltpu.make_async_copy(self.src(self.g), self.dst(self.g), self.local)

    def begin(self):
        self.own().start()
        each(16, lambda i: self.copy(i).start(), 1)

    def arrive(self, i):
        self.copy(i, True).wait_recv()

    def end(self):
        each(16, self.arrive, 1)
        self.sent()

    def sent(self):
        self.own().wait()
        each(16, lambda i: self.copy(i).wait_send(), 1)


class Plane:
    def __init__(self, spot, send, recv):
        self.s, self.send, self.recv = spot, send, recv

    def to(self, k):
        return lax.rem(self.s.h + k, 4)

    def frm(self, k):
        return lax.rem(self.s.h + 4 - k, 4)

    def copy(self, src, dst, j, at_send, at_recv):
        s = self.s
        return remote(src, dst, self.send.at[at_send], self.recv.at[at_recv], j, s.z * 2 + s.c)


def pair_of(g):
    return lax.rem(g, 4) * 4 + g // 4


def weave(left, right):
    kind = left.dtype
    left, right = left.astype(f32), right.astype(f32)
    low = lanes(left.shape) < 64
    first = jnp.where(low, left, pltpu.roll(right, 64, 1)).astype(kind)
    second = jnp.where(low, pltpu.roll(left, 64, 1), right).astype(kind)
    return first, second


def any_specs(count):
    return [pl.BlockSpec(memory_space=pl.ANY)] * count


def copies(pairs, sems):
    jobs = [pltpu.make_async_copy(src, dst, sems.at[k]) for k, (src, dst) in enumerate(pairs)]
    for job in jobs:
        job.start()
    return jobs


def wait_all(jobs):
    for job in jobs:
        job.wait()


def rows_of(shape):
    return lax.broadcasted_iota(jnp.int32, shape, 0)


def spread_row(block, width, each_lane):
    count = block.shape[0]
    pick = (rows_of((128, width)) == lax.rem(lanes((128, width)), each_lane)).astype(f32).astype(bf16)
    wide = dot_n(block.astype(bf16), pick)
    return column_sum(jnp.where(rows_of((count, width)) == lanes((count, width)) // each_lane, wide, 0.0))


def gather_row(row, count, each_lane):
    width = row.shape[1]
    wide = jnp.where(rows_of((count, width)) == lanes((count, width)) // each_lane, row, 0.0)
    pick = (lanes((width, 128)) == lax.rem(rows_of((width, 128)), each_lane)).astype(f32)
    return lax.dot_general(
        wide, pick, (((1,), (0,)), ((), ())), precision=lax.Precision.HIGHEST, preferred_element_type=f32
    )


class Line:
    def __init__(self, spot, shard, full, send, recv, local):
        self.s, self.shard, self.full, self.send, self.recv = spot, shard, full, send, recv
        self.own = pltpu.make_async_copy(shard, full.at[spot.z], local)

    def copy(self, way, t):
        s = self.s
        k = 2 * t + (way + 1) // 2
        src = self.full.at[s.z - way * t] if t else self.shard
        dst = self.full.at[s.z - way * t]
        return remote(src, dst, self.send.at[k], self.recv.at[k], s.h, (s.z + way) * 2 + s.c)

    def inside(self, z):
        return (z >= 0) & (z < self.s.nz)

    def sends(self, t, act):
        for way in (1, -1):
            z = self.s.z

            @pl.when(self.inside(z + way) & self.inside(z - way * t))
            def _():
                act(self.copy(way, t))

    def arrive(self, t):
        for way in (1, -1):
            s = self.s

            @pl.when(self.inside(s.z - way * (t + 1)))
            def _():
                slot = self.full.at[s.z - way * (t + 1)]
                k = 2 * t + (way + 1) // 2
                remote(slot, slot, self.send.at[k], self.recv.at[k], s.h, (s.z - way) * 2 + s.c).wait_recv()

    def begin(self):
        self.own.start()
        self.sends(0, lambda copy: copy.start())

    def onward(self, t):
        self.arrive(t)
        if t + 1 < self.s.nz - 1:
            self.sends(t + 1, lambda copy: copy.start())

    def sent(self):
        self.own.wait()
        for t in range(self.s.nz - 1):
            self.sends(t, lambda copy: copy.wait_send())


def project_kernel(n, nb, *refs):
    x_hbm, wq_hbm, wk_hbm, wv_hbm, wo_hbm, wu_hbm, wd_hbm, seg_hbm = refs[:8]
    smalls = refs[8:16]
    q_out, kv_out, x_out, wa_out, fz_out, par_out, bup_out, segk_out, segq_out = refs[16:25]
    (
        x, wq, wk, wv, wo, wu, wd, seg, *small, bup_small, vec, sa, sb, wa, x_all, kv_send, q_send,
        par, bup, segk, segq,
        in_sem, out_sem, w_send, w_recv, w_local, f_send, f_recv, f_local,
        x_send, x_recv, x_local, ex_send, ex_recv, ex_local, tw_send, tw_recv,
    ) = refs[25:]
    s = Spot(nb)
    loads = copies(
        [(wq_hbm, wq), (wk_hbm, wk), (wv_hbm, wv), (seg_hbm, seg), (smalls[0], bup_small)]
        + [(smalls[k], small[k - 1]) for k in range(1, 8)]
        + [(x_hbm, x), (wo_hbm, wo), (wu_hbm, wu), (wd_hbm, wd)],
        in_sem,
    )
    greet_near(s)

    def pass_x(z, slot):
        return remote(x.at[z // 2], x_all.at[slot], x_send.at[z], x_recv.at[slot], s.h, z * 2 + s.c)

    wait_all(loads[:13])
    vec[...] = jnp.zeros_like(vec)
    vec[0:1, 0:64] = bup_small[...].astype(f32).reshape(1, 64)
    for k in range(7):
        vec[k + 1:k + 2, 0:16] = small[k][...].astype(f32).reshape(1, 16)
    vec[8:10, :] = seg[...].astype(f32)
    for t in range(4):
        tile, at = slice(128 * t, 128 * t + 128), 256 * (t % 2)
        first, second = weave(wk[:, tile], wv[:, tile])
        sa[t // 2, :, at:at + 128] = first
        sa[t // 2, :, at + 128:at + 256] = second
    for w in range(2):
        sa[w, :, 512:768] = wq[:, 256 * w:256 * w + 256]
        sa[w, :, 768:896] = vec[...].astype(bf16)

    def w_line(z, slot):
        return remote(
            sa.at[lax.rem(z, 2)], wa.at[s.h, slot, s.c], w_send.at[z], w_recv.at[slot], s.h, z * 2 + s.c
        )

    def w_plane(j, h):
        slot = wa.at[h, :, s.c]
        return remote(slot, slot, w_send.at[4 + j], w_recv.at[4 + h], j, s.z * 2 + s.c)

    def w_twin(h, c):
        slot = wa.at[h, :, c]
        return remote(slot, slot, w_send.at[8 + h], w_recv.at[8 + h], s.h, s.z * 2 + 1 - s.c)

    each(s.nz, lambda k: w_line(s.ahead(k), s.z).start(), 1)
    own_w = pltpu.make_async_copy(sa.at[lax.rem(s.z, 2)], wa.at[s.h, s.z, s.c], w_local)
    own_w.start()
    own_x = pltpu.make_async_copy(x.at[s.z // 2], x_all.at[s.z], x_local)
    own_x.start()
    wait_all(loads[13:])
    sb[:, 0:512] = wo[...]
    sb[:, 512:2560] = wu[...]
    for t in range(4):
        sb[:, 2560 + 512 * t:3072 + 512 * t] = wd[16 * t:16 * t + 16, :]
    line = Line(s, sb, fz_out, f_send, f_recv, f_local)
    own_w.wait()
    each(s.nz, lambda k: w_line(s.ahead(k), s.ahead(k)).wait_recv(), 1)
    each(s.nz, lambda k: pass_x(s.ahead(k), s.z).start(), 1)
    each(4, lambda i: w_plane(lax.rem(s.h + i, 4), s.h).start(), 1)
    w_twin(s.h, s.c).start()

    line.begin()

    def w_arrive(i):
        h = lax.rem(s.h + 4 - i, 4)
        w_plane(h, h).wait_recv()
        w_twin(h, s.c).start()

    each(4, w_arrive, 1)
    each(4, lambda h: w_twin(h, 1 - s.c).wait_recv())
    outs = copies([(wa, wa_out)], out_sem)
    own_x.wait()
    plane = [Plane(s, ex_send.at[k], ex_recv.at[k]) for k in range(2)]
    kinds = ((kv_send, lambda g: kv_out.at[:, g, s.c]), (q_send, lambda g: q_out.at[:, g]))

    def block(w, j, z):
        src, dst = kinds[w]
        return plane[w].copy(src.at[j, z], dst(s.h * 4 + z), j, j * 4 + z, s.h * 4 + z)

    def from_block(w, j, z):
        src, dst = kinds[w]
        slot = dst(j * 4 + z)
        return plane[w].copy(slot, slot, j, j * 4 + z, j * 4 + z)

    def own_block(w, z):
        src, dst = kinds[w]
        return pltpu.make_async_copy(src.at[s.h, z], dst(s.h * 4 + z), ex_local.at[w, z])

    def twin(src, j, z, c):
        slot = kv_out.at[:, j * 4 + z, c]
        k = j * 4 + z
        return remote(slot if src is None else src, slot, tw_send.at[k], tw_recv.at[k], s.h, s.z * 2 + 1 - s.c)

    def project_rows(k):
        z = s.ahead(k)
        qkv = dot_n(x_all[z], wa[:, :, :, :, 0:768].reshape(512, 768)).astype(bf16)
        for j in range(4):
            kv_send[j, z] = qkv[:, 128 * j:128 * j + 128].reshape(8, 16, 128)
        for t in range(2):
            tile = qkv[:, 512 + 128 * t:640 + 128 * t]
            first, second = weave(tile[0:64], tile[64:128])
            q_send[2 * t, z] = first.reshape(4, 16, 128)
            q_send[2 * t + 1, z] = second.reshape(4, 16, 128)
        for w in range(2):
            each(4, lambda i: block(w, plane[w].to(i), z).start(), 1)
            own_block(w, z).start()
        twin(kv_send.at[s.h, z], s.h, z, s.c).start()

    project_rows(0)

    def project_next(k):
        z = s.ahead(k)
        pass_x(z, z).wait_recv()
        project_rows(k)

    each(s.nz, project_next, 1)
    line.onward(0)
    line.onward(1)
    vecs = wa[:, :, :, :, 768:896].reshape(n, 16, 128).astype(f32)
    outs += copies([(x_all, x_out)], out_sem.at[pl.ds(5, 1)])
    bup[...] = spread_row(vecs[:, 0, :], 2048, 64)
    for k in range(7):
        par[k:k + 1, :] = spread_row(vecs[:, k + 1, :], 512, 16)
    par[7:8, :] = jnp.zeros((1, 512), f32)
    ids = jnp.where(s.z < 2, vecs[:, 8, :], vecs[:, 9, :]).astype(bf16)
    for i in range(8):
        pick = (rows_of((128, 512)) == 16 * i + lax.rem(lanes((128, 512)), 16)).astype(f32).astype(bf16)
        wide = dot_n(ids, pick)
        source = rows_of((n, 512))
        row = jnp.where(source == lanes((n, 512)) // 16, wide, 0.0)
        segk[i:i + 1, :] = column_sum(row).astype(jnp.int32)
        source = rows_of((n, 256))
        own = (source // 2 == lanes((n, 256)) // 16) & (lax.rem(source, 2) == s.c)
        segq[i:i + 1, :] = column_sum(jnp.where(own, wide[:, 0:256], 0.0)).astype(jnp.int32)
    outs += copies([(par, par_out), (bup, bup_out), (segk, segk_out), (segq, segq_out)], out_sem.at[pl.ds(1, 4)])
    def forward(i):
        j = plane[0].frm(i)

        def go(k):
            z = s.ahead(k)
            from_block(0, j, z).wait_recv()
            twin(None, j, z, s.c).start()

        each(s.nz, go)

    each(4, forward, 1)
    line.onward(2)
    each(4, lambda i: each(s.nz, lambda z: from_block(1, plane[1].frm(i), z).wait_recv()), 1)
    each(4, lambda j: each(s.nz, lambda z: twin(None, j, z, 1 - s.c).wait_recv()))
    each(4, lambda j: each(s.nz, lambda z: twin(None, j, z, s.c).wait_send()))
    for w in range(2):
        each(s.nz, lambda z: own_block(w, z).wait())
        each(4, lambda i: each(s.nz, lambda z: block(w, plane[w].to(i), z).wait_send()), 1)
    each(s.nz, lambda k: pass_x(s.ahead(k), s.z).wait_send(), 1)
    each(s.nz, lambda k: w_line(s.ahead(k), s.z).wait_send(), 1)
    each(4, lambda i: w_plane(lax.rem(s.h + i, 4), s.h).wait_send(), 1)
    each(4, lambda h: w_twin(h, s.c).wait_send())
    line.sent()
    wait_all(outs)


def project(n, nb, x, wq, wk, wv, wo, wu, wd, seg, smalls):
    dma = pltpu.SemaphoreType.DMA
    nz = nb // 2
    return pl.pallas_call(
        functools.partial(project_kernel, n, nb),
        out_shape=(
            jax.ShapeDtypeStruct((4, 16, 16, 128), bf16),
            jax.ShapeDtypeStruct((8, 16, 2, 16, 128), bf16),
            jax.ShapeDtypeStruct((nz, 128, 512), bf16),
            jax.ShapeDtypeStruct((4, nz, 2, 16, 896), bf16),
            jax.ShapeDtypeStruct((nz, 16, 4608), bf16),
            jax.ShapeDtypeStruct((8, 512), f32),
            jax.ShapeDtypeStruct((1, 2048), f32),
            jax.ShapeDtypeStruct((8, 512), jnp.int32),
            jax.ShapeDtypeStruct((8, 256), jnp.int32),
        ),
        in_specs=any_specs(16),
        out_specs=any_specs(9),
        scratch_shapes=[
            pltpu.VMEM(x.shape, bf16),
            pltpu.VMEM((16, 512), bf16),
            pltpu.VMEM((16, 512), bf16),
            pltpu.VMEM((16, 512), bf16),
            pltpu.VMEM((16, 512), bf16),
            pltpu.VMEM((16, 2048), bf16),
            pltpu.VMEM((64, 512), bf16),
            pltpu.VMEM((2, 128), jnp.int32),
            *[pltpu.VMEM((16,), bf16)] * 7,
            pltpu.VMEM((64,), bf16),
            pltpu.VMEM((16, 128), f32),
            pltpu.VMEM((2, 16, 896), bf16),
            pltpu.VMEM((16, 4608), bf16),
            pltpu.VMEM((4, nz, 2, 16, 896), bf16),
            pltpu.VMEM((nz, 128, 512), bf16),
            pltpu.VMEM((4, nz, 8, 16, 128), bf16),
            pltpu.VMEM((4, nz, 4, 16, 128), bf16),
            pltpu.VMEM((8, 512), f32),
            pltpu.VMEM((1, 2048), f32),
            pltpu.VMEM((8, 512), jnp.int32),
            pltpu.VMEM((8, 256), jnp.int32),
            dma((16,)),
            dma((6,)),
            dma((12,)),
            dma((12,)),
            dma,
            dma((2 * nz,)),
            dma((2 * nz,)),
            dma,
            dma((nz,)),
            dma((nz,)),
            dma,
            dma((2, 4 * nz)),
            dma((2, 4 * nz)),
            dma((2, nz)),
            dma((4 * nz,)),
            dma((4 * nz,)),
        ],
        compiler_params=pltpu.CompilerParams(
            collective_id=1, has_side_effects=True, vmem_limit_bytes=VMEM_BYTES
        ),
        name="project",
    )(x, wq, wk, wv, wo, wu, wd, seg, *smalls)


def row_norm(v):
    mean = jnp.mean(v, axis=-1, keepdims=True)
    mid = v - mean
    inv = lax.rsqrt(jnp.mean(mid * mid, axis=-1, keepdims=True) + EPSILON)
    return mid * inv, inv


def row_norm_back(grad, normed, inv, gain):
    part = grad * gain
    return inv * (
        part
        - jnp.mean(part, axis=-1, keepdims=True)
        - normed * jnp.mean(part * normed, axis=-1, keepdims=True)
    )


def normal(u):
    bell = jnp.exp(-0.5 * u * u)
    t = 1.0 / (1.0 + (0.3275911 * 0.5**0.5) * jnp.abs(u))
    poly = 0.5 * 1.061405429
    for factor in (-1.453152027, 1.421413741, -0.284496736, 0.254829592):
        poly = poly * t + 0.5 * factor
    tail = poly * t * bell
    return jnp.where(u < 0, tail, 1.0 - tail), bell * ((2.0 * math.pi) ** -0.5)


def column_sum(v):
    return jnp.sum(v, axis=0, keepdims=True)


def middle_kernel(n, nb, *refs):
    o_hbm, x_hbm, y_hbm, g_hbm, fz_hbm, fx_hbm, fy_hbm, par_hbm, bup_hbm = refs[:9]
    outs_hbm = refs[10:17]
    do_out = refs[9]
    (
        o_in, x, y, g_in, wb, wd, par, bup, o_recv, do_send, slope,
        out, dacc_ref, dz1_ref, gvec, sum_b, sum_d, far, bias_up, omix, hid_ref, dur_ref, po, pu, pd, to, tu, td,
        in_sem, out_sem, ex_send, ex_recv, ex_local, f_send, f_recv, p_send, p_recv,
    ) = refs[17:]
    s = Spot(nb)
    loads = copies(
        [
            (o_hbm, o_in), (x_hbm, x), (y_hbm, y), (g_hbm, g_in), (par_hbm, par), (bup_hbm, bup),
            (fz_hbm, wb.at[s.h, :, s.c]), (fx_hbm, wb.at[s.near[0], :, s.c]), (fy_hbm, wb.at[s.near[1], :, s.c]),
        ],
        in_sem,
    )
    greet_core(s)
    loads[0].wait()
    o_ex = Exchange(
        s, lambda g: o_in.at[:, g], lambda g: o_recv.at[pair_of(g)], ex_send.at[0], ex_recv.at[0], ex_local.at[0]
    )
    o_ex.begin()
    cut = [pl.ds(0, 2304), pl.ds(2304, 2304)]
    heads = (s.h, s.near[0], s.near[1], s.diag)

    def onward(w, h, to):
        src = (fx_hbm, fy_hbm)[w].at[:, :, cut[w]]
        return remote(src, wb.at[h, :, s.c, :, cut[w]], f_send.at[4 + w], f_recv.at[4 + w], to, s.z * 2 + s.c)

    def twin(k, c):
        slot = wb.at[heads[k], :, c]
        src = (fz_hbm, fx_hbm, fy_hbm, slot)[k]
        return remote(src, slot, f_send.at[k], f_recv.at[k], s.h, s.z * 2 + 1 - s.c)

    for w in range(2):
        onward(w, s.near[w], s.near[1 - w]).start()
    for k in range(3):
        twin(k, s.c).start()
    for w in range(2):
        onward(w, s.diag, s.near[1 - w]).wait_recv()
    twin(3, s.c).start()
    o_ex.end()
    wait_all(loads[1:])
    for m in range(2):
        for t in range(4):
            first, second = weave(
                o_recv[8 * m + 2 * t].reshape(64, 128), o_recv[8 * m + 2 * t + 1].reshape(64, 128)
            )
            omix[128 * m:128 * m + 64, 128 * t:128 * t + 128] = first
            omix[128 * m + 64:128 * m + 128, 128 * t:128 * t + 128] = second
    gain1, bias1 = par[1:2], par[2:3]
    gain2, bias2 = par[3:4], par[4:5]
    gain3, bias3 = par[5:6], par[6:7]
    for k in range(4):
        twin(k, 1 - s.c).wait_recv()
    for t in range(4):
        for r in range(4):
            wd[t, :, :, r] = wb[t, :, :, :, 2560 + 512 * r:3072 + 512 * r]
    w_out = wb[:, :, :, :, 0:512].reshape(512, 512)
    a = dot_n(omix[...], w_out)
    n1, r1 = row_norm(x[...].astype(f32) + a)
    x1 = n1 * gain1 + bias1
    x1r = x1.astype(bf16)
    feed = jnp.zeros_like(x1)
    for t in range(4):
        cols = slice(512 * t, 512 * t + 512)
        u = dot_n(x1r, wb[:, :, :, :, 512 + 512 * t:1024 + 512 * t].reshape(512, 512)) + bup[:, cols]
        phi, density = normal(u)
        hid = (u * phi).astype(bf16)
        slope[:, cols] = phi + u * density
        hid_ref[:, cols] = hid
        feed = feed + dot_n(hid, wd[t].reshape(512, 512))
    feed = feed + par[0:1]
    n2, r2 = row_norm(x1 + feed)
    n3, r3 = row_norm(y[...].astype(f32) + a + feed)
    out[...] = (n2 * gain2 + bias2 + (n3 * gain3 + bias3)).astype(bf16)
    g = g_in[...].astype(f32)
    dacc = row_norm_back(g, n3, r3, gain3)
    dacc_ref[...] = dacc
    dz2 = row_norm_back(g, n2, r2, gain2)
    df = dz2 + dacc
    dfr = df.astype(bf16)
    swaps = [
        remote(part.at[:, :, 1 - s.c], there, p_send.at[k], p_recv.at[k], s.h, s.z * 2 + 1 - s.c)
        for k, (part, there) in enumerate(((pd, td), (pu, tu), (po, to)))
    ]
    for t in range(4):
        pd[t] = dot_0(hid_ref[:, 512 * t:512 * t + 512], dfr).astype(bf16).reshape(nb // 2, 2, 64, 512)
    swaps[0].start()
    dx1 = dz2
    for t in range(4):
        cols = slice(512 * t, 512 * t + 512)
        du = dot_t(dfr, wd[t].reshape(512, 512)) * slope[:, cols]
        bias_up[:, cols] = column_sum(du)
        dur = du.astype(bf16)
        dur_ref[:, cols] = dur
        dx1 = dx1 + dot_t(dur, wb[:, :, :, :, 512 + 512 * t:1024 + 512 * t].reshape(512, 512))
    dz1 = row_norm_back(dx1, n1, r1, gain1)
    dz1_ref[...] = dz1
    dar = (dz1 + dacc).astype(bf16)
    do = dot_t(dar, w_out).astype(bf16)
    for m in range(2):
        for t in range(4):
            tile = do[128 * m:128 * m + 128, 128 * t:128 * t + 128]
            first, second = weave(tile[0:64], tile[64:128])
            do_send[8 * m + 2 * t] = first.reshape(4, 16, 128)
            do_send[8 * m + 2 * t + 1] = second.reshape(4, 16, 128)
    do_ex = Exchange(
        s, lambda g: do_send.at[pair_of(g)], lambda g: do_out.at[:, g], ex_send.at[1], ex_recv.at[1], ex_local.at[1]
    )
    do_ex.begin()
    stores = copies(zip((out, dacc_ref, dz1_ref), outs_hbm[:3]), out_sem)
    for t in range(4):
        cols = slice(512 * t, 512 * t + 512)
        pu[:, :, :, :, cols] = dot_0(x1r, dur_ref[:, cols]).astype(bf16).reshape(4, nb // 2, 2, 16, 512)
    swaps[1].start()
    po[...] = dot_0(omix[...], dar).astype(bf16).reshape(po.shape)
    swaps[2].start()
    sum_g = column_sum(g)
    sums = (
        column_sum(df), column_sum(dx1 * n1), column_sum(dx1), column_sum(g * n2), sum_g, column_sum(g * n3), sum_g
    )
    gvec[...] = jnp.zeros_like(gvec)
    gvec[:, 0, :] = gather_row(bias_up[...], n, 64)
    for k in range(7):
        gvec[:, k + 1, :] = gather_row(sums[k], n, 16)
    stores += copies([(gvec, outs_hbm[3])], out_sem.at[pl.ds(3, 1)])
    for swap in swaps:
        swap.wait()

    def join(part, there):
        value = part[:, :, s.c].astype(f32) + there[...].astype(f32)
        return value.astype(bf16).reshape(-1, *value.shape[2:])

    sum_d[...] = join(pd, td)
    sum_b[:, :, 512:2560] = join(pu, tu)
    sum_b[:, :, 0:512] = join(po, to)
    stores += copies(zip((sum_b, sum_d), outs_hbm[4:6]), out_sem.at[pl.ds(4, 2)])
    group = pl.ds(s.diag * s.nz, s.nz)
    far[:, :, 0:2560] = sum_b[group]
    for r in range(4):
        far[:, :, 2560 + 512 * r:3072 + 512 * r] = sum_d[group, 16 * r:16 * r + 16, :]
    stores += copies([(far, outs_hbm[6])], out_sem.at[pl.ds(6, 1)])
    do_ex.end()
    for w in range(2):
        onward(w, s.near[w], s.near[1 - w]).wait_send()
    for k in range(4):
        twin(k, s.c).wait_send()
    wait_all(stores)


def middle(n, nb, o, x, y, g, fz, fx, fy, par, bup):
    dma = pltpu.SemaphoreType.DMA
    rows = x.shape[0]
    nz = nb // 2
    saved = [
        ((rows, 512), bf16), ((rows, 512), f32), ((rows, 512), f32), ((n, 16, 128), f32),
        ((4 * nz, 16, 2560), bf16), ((4 * nz, 64, 512), bf16),
    ]
    return pl.pallas_call(
        functools.partial(middle_kernel, n, nb),
        out_shape=[jax.ShapeDtypeStruct((4, 16, 16, 128), bf16)]
        + [jax.ShapeDtypeStruct(shape, kind) for shape, kind in saved]
        + [jax.ShapeDtypeStruct((nz, 16, 4608), bf16)],
        in_specs=any_specs(9),
        out_specs=any_specs(8),
        scratch_shapes=[
            pltpu.VMEM(o.shape, bf16),
            pltpu.VMEM(x.shape, bf16),
            pltpu.VMEM(x.shape, bf16),
            pltpu.VMEM(x.shape, bf16),
            pltpu.VMEM((4, nb // 2, 2, 16, 4608), bf16),
            pltpu.VMEM((4, 4, 2, 4, 16, 512), bf16),
            pltpu.VMEM(par.shape, f32),
            pltpu.VMEM(bup.shape, f32),
            pltpu.VMEM((16, 4, 16, 128), bf16),
            pltpu.VMEM((16, 4, 16, 128), bf16),
            pltpu.VMEM((rows, 2048), f32),
            *[pltpu.VMEM(shape, kind) for shape, kind in saved],
            pltpu.VMEM((nz, 16, 4608), bf16),
            pltpu.VMEM((1, 2048), f32),
            pltpu.VMEM((rows, 512), bf16),
            pltpu.VMEM((rows, 2048), bf16),
            pltpu.VMEM((rows, 2048), bf16),
            *[pltpu.VMEM((4, nz, 2, *tail), bf16) for tail in ((16, 512), (16, 2048), (64, 512))],
            *[pltpu.VMEM((4, nz, *tail), bf16) for tail in ((16, 512), (16, 2048), (64, 512))],
            dma((9,)),
            dma((7,)),
            dma((2, 16)),
            dma((2, 16)),
            dma((2,)),
            dma((6,)),
            dma((6,)),
            dma((3,)),
            dma((3,)),
        ],
        compiler_params=pltpu.CompilerParams(
            collective_id=2, has_side_effects=True, vmem_limit_bytes=VMEM_BYTES
        ),
        name="middle",
    )(o, x, y, g, fz, fx, fy, par, bup)


def finish_kernel(n, nb, *refs):
    ins, far = refs[:8], refs[8]
    outs = refs[9:17]
    (
        dq, dkv, xm, dz1, pb, pd, gvec, wa,
        pa, ta, da, na, la, db, nb_, lb, dd, nd, ld, tv, dv, nv, lv,
        twin_buf, dkv_send, dkv_recv, dq_recv, dqkv, dx_send, dx_recv, gx, gq, gk, gv, go, gu, gd, gs,
        in_sem, far_sem, out_sem, rs_send, rs_recv, ex_send, ex_recv, dx_ssem, dx_rsem, tw_send, tw_recv,
    ) = refs[17:]
    s = Spot(nb)
    order = (1, 0, 4, 5, 6, 7, 2, 3)
    local = (dq, dkv, xm, dz1, pb, pd, gvec, wa)
    loads = copies([(ins[k], local[k]) for k in order], in_sem)
    corners = copies(
        [(far.at[:, :, pl.ds(0, 2560)], db)]
        + [(far.at[:, :, pl.ds(2560 + 512 * r, 512)], dd.at[:, pl.ds(16 * r, 16)]) for r in range(4)],
        far_sem,
    )
    greet_near(s)
    swap = remote(ins[1].at[:, :, 1 - s.c], twin_buf, tw_send, tw_recv, s.h, s.z * 2 + 1 - s.c)
    swap.start()
    jobs = [
        Scatter(s, *bufs, rs_send.at[k], rs_recv.at[k])
        for k, bufs in enumerate(
            ((pb, None, db, nb_, lb), (pd, None, dd, nd, ld), (gvec, tv, dv, nv, lv), (pa, ta, da, na, la))
        )
    ]
    wait_all(loads[:5])
    jobs[2].begin()
    swap.wait()

    def add(g):
        dkv_send[g] = (dkv[:, g, s.c].astype(f32) + twin_buf[:, g].astype(f32)).astype(bf16)

    each(4 * s.nz, add)
    plane = [Plane(s, ex_send.at[k], ex_recv.at[k]) for k in range(2)]

    def block(w, j, z, slot):
        g = j * s.nz + z
        src, dst = ((dkv_send.at[g], dkv_recv.at[slot, z]), (dq.at[:, g], dq_recv.at[slot, z]))[w]
        return plane[w].copy(src, dst, j, g, slot * s.nz + z)

    def pass_on(k):
        z = s.ahead(k)
        for w in range(2):
            each(4, lambda i: block(w, plane[w].to(i), z, s.h).start(), 1)
        dkv_recv[s.h, z] = dkv_send[s.h * s.nz + z]
        dq_recv[s.h, z] = dq[:, s.h * s.nz + z]

    each(s.nz + 1, pass_on, 1)
    wait_all(loads[5:])
    wait_all(corners)

    def back(z, slot):
        return remote(dx_send.at[z], dx_recv.at[slot], dx_ssem.at[z], dx_rsem.at[slot], s.h, z * 2 + s.c)

    def take(k):
        z = s.ahead(k)
        for w in range(2):
            each(4, lambda i: block(w, plane[w].frm(i), z, plane[w].frm(i)).wait_recv(), 1)
        for j in range(4):
            dqkv[z, :, 128 * j:128 * j + 128] = dkv_recv[j, z].reshape(128, 128)
        for t in range(2):
            first, second = weave(dq_recv[2 * t, z].reshape(64, 128), dq_recv[2 * t + 1, z].reshape(64, 128))
            dqkv[z, 0:64, 512 + 128 * t:640 + 128 * t] = first
            dqkv[z, 64:128, 512 + 128 * t:640 + 128 * t] = second
        dx_send[z] = dot_t(dqkv[z], wa[:, :, :, :, 0:768].reshape(512, 768)).astype(bf16)

    def take_and_send(k):
        take(k)
        back(s.ahead(k), s.z).start()

    each(s.nz, take_and_send, 1)
    for job in jobs[:2]:
        job.second()
    take(s.nz)
    dx_recv[s.z] = dx_send[s.z]
    tokens = xm[...].reshape(512, 512)
    pa[...] = dot_0(tokens, dqkv[...].reshape(512, 768)).astype(bf16).reshape(n, 16, 768)
    jobs[3].begin()
    jobs[2].second()
    jobs[3].second()
    for job in jobs:
        job.third()
    each(s.nz, lambda k: back(s.ahead(k), s.ahead(k)).wait_recv(), 1)
    for m in range(2):
        rows = slice(128 * m, 128 * m + 128)
        gx[rows, :] = dz1[rows, :] + (dx_recv[2 * m].astype(f32) + dx_recv[2 * m + 1].astype(f32))
    stores = copies([(gx, outs[0])], out_sem)
    total = jobs[0].total()
    go[...] = total[:, 0:512]
    gu[...] = total[:, 512:2560]
    gd[...] = jobs[1].total()
    gs[...] = jobs[2].total()
    stores += copies(zip((go, gu, gd, gs), outs[4:8]), out_sem.at[pl.ds(1, 4)])
    for w, part in enumerate(jobs[3].columns()):
        gq[:, 256 * w:256 * w + 256] = part[:, 512:768]
        for t in range(2):
            first, second = weave(part[:, 256 * t:256 * t + 128], part[:, 256 * t + 128:256 * t + 256])
            at = 256 * w + 128 * t
            gk[:, at:at + 128] = first
            gv[:, at:at + 128] = second
    stores += copies(zip((gq, gk, gv), outs[1:4]), out_sem.at[pl.ds(5, 3)])
    for w in range(2):
        each(4, lambda i: each(s.nz, lambda z: block(w, plane[w].to(i), z, s.h).wait_send()), 1)
    each(s.nz, lambda k: back(s.ahead(k), s.z).wait_send(), 1)
    for job in jobs:
        job.sent()
    wait_all(stores)


def finish(n, nb, dq, dkv, xm, dz1, pb, pd, gvec, wa, far):
    dma = pltpu.SemaphoreType.DMA
    nz = nb // 2
    rows = dz1.shape[0]

    def buffers(depth, width, kind):
        return [
            pltpu.VMEM((n, depth, width), kind),
            pltpu.VMEM((4, nz, depth, width), kind),
            pltpu.VMEM((nz, depth, width), kind),
            pltpu.VMEM((2, nz, depth, width), kind),
            pltpu.VMEM((nz, depth, width), kind),
        ]

    args = (dq, dkv, xm, dz1, pb, pd, gvec, wa)
    shapes = ((rows, 512), (16, 512), (16, 512), (16, 512), (16, 512), (16, 2048), (64, 512), (16, 128))
    return pl.pallas_call(
        functools.partial(finish_kernel, n, nb),
        out_shape=[jax.ShapeDtypeStruct(shape, f32) for shape in shapes],
        in_specs=any_specs(9),
        out_specs=any_specs(8),
        scratch_shapes=[
            *[pltpu.VMEM(arg.shape, arg.dtype) for arg in args],
            *buffers(16, 768, bf16),
            *buffers(16, 2560, bf16)[2:],
            *buffers(64, 512, bf16)[2:],
            *buffers(16, 128, f32)[1:],
            pltpu.VMEM((8, 16, 16, 128), bf16),
            pltpu.VMEM((16, 8, 16, 128), bf16),
            pltpu.VMEM((4, nz, 8, 16, 128), bf16),
            pltpu.VMEM((4, nz, 4, 16, 128), bf16),
            pltpu.VMEM((nz, 128, 768), bf16),
            pltpu.VMEM((nz, 128, 512), bf16),
            pltpu.VMEM((nz, 128, 512), bf16),
            *[pltpu.VMEM(shape, f32) for shape in shapes],
            dma((8,)),
            dma((5,)),
            dma((8,)),
            dma((4, 9 * nz)),
            dma((4, 9 * nz)),
            dma((2, 4 * nz)),
            dma((2, 4 * nz)),
            dma((nz,)),
            dma((nz,)),
            dma,
            dma,
        ],
        compiler_params=pltpu.CompilerParams(
            collective_id=3, has_side_effects=True, vmem_limit_bytes=VMEM_BYTES
        ),
        name="finish",
    )(*args, far)


def deliver_kernel(count, *refs):
    ins, outs = refs[:count], refs[count:2 * count + 7]
    stage, lines, (in_sem, sems) = refs[2 * count + 7:3 * count + 7], refs[3 * count + 7:3 * count + 15], refs[-2:]
    loads = copies(zip(ins, stage), in_sem)
    jobs = []
    for k in range(count - 1):
        loads[k].wait()
        jobs += copies([(stage[k], outs[k])], sems.at[pl.ds(k, 1)])
    loads[-1].wait()
    vec = stage[-1]
    lines[0][...] = vec[0:1, 0:64].reshape(64)
    for k in range(1, 8):
        lines[k][...] = vec[k:k + 1, 0:16].reshape(16)
    jobs += copies(zip(lines, outs[count - 1:]), sems.at[pl.ds(count - 1, 8)])
    wait_all(jobs)


def deliver(arrays, vec):
    count = len(arrays) + 1
    lines = [(64,)] + [(16,)] * 7
    return pl.pallas_call(
        functools.partial(deliver_kernel, count),
        out_shape=[jax.ShapeDtypeStruct(a.shape, a.dtype) for a in arrays]
        + [jax.ShapeDtypeStruct(shape, f32) for shape in lines],
        in_specs=any_specs(count),
        out_specs=any_specs(count + 7),
        scratch_shapes=[
            *[pltpu.VMEM(a.shape, a.dtype) for a in (*arrays, vec)],
            *[pltpu.VMEM(shape, f32) for shape in lines],
            pltpu.SemaphoreType.DMA((count,)),
            pltpu.SemaphoreType.DMA((count + 7,)),
        ],
        compiler_params=pltpu.CompilerParams(vmem_limit_bytes=VMEM_BYTES),
        name="deliver",
    )(*arrays, vec)


def by_pairs(
    stream, accumulator, upstream, segment_ids, w_query, w_key, w_value, w_out, w_up, b_up, w_down, b_down,
    gain_attn, bias_attn, gain_ffn, bias_ffn, gain_final, bias_final,
):
    nb = lax.axis_size("blk")
    n = 4 * nb
    x = stream.reshape(256, 512)
    y = accumulator.reshape(256, 512)
    g = upstream.reshape(256, 512)
    smalls = (b_up, b_down, gain_attn, bias_attn, gain_ffn, bias_ffn, gain_final, bias_final)
    q, kv, xm, wa, fz, par, bup, seg_k, seg_q = project(
        n, nb, stream.reshape(2, 128, 512), w_query, w_key, w_value, w_out, w_up, w_down, segment_ids.reshape(2, 128), smalls
    )
    fx, fy = (lax.ppermute(fz, "head", [(h, h ^ w) for h in range(4)]) for w in (1, 2))
    o, of, lse, kv2, kvt = attn_fwd(q.reshape(4, 256, 128), kv.reshape(4096, 128), seg_q, seg_k)
    do, out, dacc, dz1, gvec, pb, pd, far = middle(
        n, nb, o.reshape(4, 16, 16, 128), x, y, g, fz, fx, fy, par, bup
    )
    far = lax.ppermute(far, "head", [(h, 3 - h) for h in range(4)])
    dq, dkv, out, dacc = attn_bwd(
        q.reshape(4, 256, 128), do.reshape(4, 256, 128), of, lse, kv2, kvt, seg_q, seg_k, out, dacc
    )
    gx, gq, gk, gv, go, gu, gd, gs = finish(
        n, nb, dq.reshape(4, 16, 16, 128), dkv.reshape(8, 16, 2, 16, 128), xm, dz1, pb, pd, gvec, wa, far
    )
    gx, gq, gk, gv, go, gu, gd, gbu, *small_grads = deliver((gx, gq, gk, gv, go, gu, gd), gs)
    return (
        out.reshape(stream.shape), gx.reshape(stream.shape), dacc.reshape(stream.shape),
        gq, gk, gv, go, gu, gbu, gd, *small_grads,
    )


def pairs_fit(mesh, shape):
    return mesh.shape["head"] == 4 and mesh.shape["blk"] == 8 and shape == (2, 32, 128, 512)


def solution(mesh):
    def step(*args):
        return run(by_pairs if pairs_fit(mesh, args[0].shape) else local, mesh)(*args)

    return step


def run(body, mesh):
    return jax.shard_map(
        body,
        mesh=mesh,
        in_specs=(
            P(None, ("head", "blk"), None, None),
            P(None, ("head", "blk"), None, None),
            P(None, ("head", "blk"), None, None),
            P(None, ("head", "blk"), None),
            P(("head", "blk"), None),
            P(("head", "blk"), None),
            P(("head", "blk"), None),
            P(("head", "blk"), None),
            P(("head", "blk"), None),
            P(("head", "blk")),
            P(("head", "blk"), None),
            P(("head", "blk")),
            P(("head", "blk")),
            P(("head", "blk")),
            P(("head", "blk")),
            P(("head", "blk")),
            P(("head", "blk")),
            P(("head", "blk")),
        ),
        out_specs=(
            P(None, ("head", "blk"), None, None),
            P(None, ("head", "blk"), None, None),
            P(None, ("head", "blk"), None, None),
            P(("head", "blk"), None),
            P(("head", "blk"), None),
            P(("head", "blk"), None),
            P(("head", "blk"), None),
            P(("head", "blk"), None),
            P(("head", "blk")),
            P(("head", "blk"), None),
            P(("head", "blk")),
            P(("head", "blk")),
            P(("head", "blk")),
            P(("head", "blk")),
            P(("head", "blk")),
            P(("head", "blk")),
            P(("head", "blk")),
        ),
        check_vma=False,
    )
```

```python
import functools
import math

import jax
import jax.numpy as jnp
from jax import lax
from jax.experimental import pallas as pl
from jax.experimental.pallas import tpu as pltpu
from jax.sharding import PartitionSpec as P

DH = 64
f32, bf16 = jnp.float32, jnp.bfloat16
MESH = pl.DeviceIdType.MESH
FAR = -1e30
VMEM_BYTES = 60 << 20


EPSILON = 1e-05


def norm_forward(inputs, norm_gain, norm_bias):
    average = jnp.mean(inputs, axis=-1, keepdims=True)
    centered = inputs - average
    inv_std = lax.rsqrt(jnp.mean(centered * centered, axis=-1, keepdims=True) + EPSILON)
    normed = centered * inv_std
    return (normed * norm_gain + norm_bias, normed, inv_std)


def norm_backward(gradient, normed, inv_std, norm_gain):
    scaled = gradient * norm_gain
    projected = (
        scaled
        - jnp.mean(scaled, axis=-1, keepdims=True)
        - normed * jnp.mean(scaled * normed, axis=-1, keepdims=True)
    )
    return (inv_std * projected, jnp.sum(gradient * normed, axis=0), jnp.sum(gradient, axis=0))


def smooth_gate(pre_act):
    return jax.nn.gelu(pre_act, approximate=False)


def split_rows(length):
    block_len = math.gcd(length, 512)
    return (length // block_len, block_len)


def block_scores(queries, query_seg, key_rows, key_seg, scaling):
    scores = (
        jnp.einsum("sgd,kgd->sgk", queries, key_rows, preferred_element_type=jnp.float32) * scaling
    )
    allowed = query_seg[:, None, None] == key_seg[None, None, :]
    return (scores, allowed)


def block_grads(
    queries, query_seg, grad_rows, log_total, row_delta, key_rows, value_rows, key_seg, scaling
):
    scores, allowed = block_scores(queries, query_seg, key_rows, key_seg, scaling)
    attn_prob = jnp.where(allowed, jnp.exp(scores - log_total[:, :, None]), 0.0)
    prob_grad = jnp.einsum(
        "sgd,kgd->sgk", grad_rows, value_rows, preferred_element_type=jnp.float32
    )
    score_grad = (attn_prob * (prob_grad - row_delta[:, :, None]) * scaling).astype(jnp.bfloat16)
    return (attn_prob.astype(jnp.bfloat16), score_grad)


def key_blocks(key_rows, value_rows, key_seg, groups):
    block_num, block_len = split_rows(key_rows.shape[0])
    return (
        key_rows.reshape(block_num, block_len, groups, -1),
        value_rows.reshape(block_num, block_len, groups, -1),
        key_seg.reshape(block_num, block_len),
    )


def attend_fold(queries, query_seg, scaling, carried, portion):
    key_rows, value_rows, key_seg = portion

    def step(running, blocks):
        key_part, value_part, seg_part = blocks
        old_max, old_total, weighted = running
        scores, allowed = block_scores(queries, query_seg, key_part, seg_part, scaling)
        row_max = jnp.maximum(old_max, jnp.max(jnp.where(allowed, scores, -1e30), axis=2))
        exp_scores = jnp.where(allowed, jnp.exp(scores - row_max[:, :, None]), 0.0)
        rescale = jnp.exp(old_max - row_max)
        new_total = old_total * rescale + jnp.sum(exp_scores, axis=2)
        weighted = weighted * rescale[:, :, None] + jnp.einsum(
            "sgk,kgd->sgd",
            exp_scores.astype(jnp.bfloat16),
            value_part,
            preferred_element_type=jnp.float32,
        )
        return ((row_max, new_total, weighted), None)

    running, unused = lax.scan(
        step, carried, key_blocks(key_rows, value_rows, key_seg, queries.shape[1])
    )
    return running


def local(
    stream,
    accumulator,
    upstream,
    segment_ids,
    w_query,
    w_key,
    w_value,
    w_out,
    w_up,
    b_up,
    w_down,
    b_down,
    gain_attn,
    bias_attn,
    gain_ffn,
    bias_ffn,
    gain_final,
    bias_final,
):
    heads_axis = lax.axis_size("head")
    micro = stream.shape[0]
    tokens = stream.shape[2]
    width = stream.shape[3]
    group_width = width // heads_axis
    groups = group_width // DH
    scaling = DH ** (-0.5)
    f32 = jnp.float32
    bf16 = jnp.bfloat16
    out_list = []
    stream_grads = []
    accum_grads = []
    grad_totals = None
    for micro_step in range(micro):
        (
            q_weight,
            k_weight,
            v_weight,
            o_weight,
            up_weight,
            up_bias,
            down_weight,
            down_bias,
            gain_one,
            shift_one,
            gain_two,
            shift_two,
            gain_three,
            shift_three,
        ) = (
            lax.all_gather(w_query, ("head", "blk"), axis=0, tiled=True),
            lax.all_gather(w_key, ("head", "blk"), axis=0, tiled=True),
            lax.all_gather(w_value, ("head", "blk"), axis=0, tiled=True),
            lax.all_gather(w_out, ("head", "blk"), axis=0, tiled=True),
            lax.all_gather(w_up, ("head", "blk"), axis=0, tiled=True),
            lax.all_gather(b_up, ("head", "blk"), axis=0, tiled=True),
            lax.all_gather(w_down, ("head", "blk"), axis=0, tiled=True),
            lax.all_gather(b_down, ("head", "blk"), axis=0, tiled=True),
            lax.all_gather(gain_attn, ("head", "blk"), axis=0, tiled=True),
            lax.all_gather(bias_attn, ("head", "blk"), axis=0, tiled=True),
            lax.all_gather(gain_ffn, ("head", "blk"), axis=0, tiled=True),
            lax.all_gather(bias_ffn, ("head", "blk"), axis=0, tiled=True),
            lax.all_gather(gain_final, ("head", "blk"), axis=0, tiled=True),
            lax.all_gather(bias_final, ("head", "blk"), axis=0, tiled=True),
        )
        inputs = stream[micro_step, 0]
        input_wide = inputs.astype(f32)
        carried = accumulator[micro_step, 0].astype(f32)
        segs = segment_ids[micro_step, 0]
        projections = jnp.stack(
            [
                jnp.dot(inputs, q_weight, preferred_element_type=f32),
                jnp.dot(inputs, k_weight, preferred_element_type=f32),
                jnp.dot(inputs, v_weight, preferred_element_type=f32),
            ]
        ).astype(bf16)
        projections = projections.reshape(3, tokens, heads_axis, group_width)
        seg_wide = jnp.broadcast_to(segs[None, :, None, None], (1, tokens, heads_axis, 1))
        regrouped, seg_group = (
            lax.all_to_all(projections, "head", split_axis=2, concat_axis=1, tiled=True),
            lax.all_to_all(seg_wide, "head", split_axis=2, concat_axis=1, tiled=True),
        )
        rows = regrouped.shape[1]
        query_loc = regrouped[0, :, 0]
        key_loc = regrouped[1, :, 0]
        value_loc = regrouped[2, :, 0]
        seg_loc = seg_group[0, :, 0, 0]
        queries3 = query_loc.reshape(rows, groups, DH)
        start_state = (
            jnp.full((rows, groups), -1e30, f32),
            jnp.zeros((rows, groups), f32),
            jnp.zeros((rows, groups, DH), f32),
        )
        row_max, row_total, weighted = attend_fold(
            queries3,
            seg_loc,
            scaling,
            start_state,
            (
                lax.all_gather(key_loc, "blk", axis=0, tiled=True),
                lax.all_gather(value_loc, "blk", axis=0, tiled=True),
                lax.all_gather(seg_loc, "blk", axis=0, tiled=True),
            ),
        )
        attn_out = weighted / row_total[:, :, None]
        log_total = row_max + jnp.log(row_total)
        attn_send = attn_out.astype(bf16).reshape(rows, 1, group_width)
        mixed = lax.all_to_all(attn_send, "head", split_axis=0, concat_axis=1, tiled=True).reshape(
            tokens, width
        )
        branch = jnp.dot(mixed, o_weight, preferred_element_type=f32)
        first, normed_one, inv_one = norm_forward(
            input_wide + branch, gain_one.astype(f32), shift_one.astype(f32)
        )
        first_low = first.astype(bf16)
        hidden_pre = jnp.dot(first_low, up_weight, preferred_element_type=f32) + up_bias.astype(f32)
        hidden_act, gate_pull = jax.vjp(smooth_gate, hidden_pre)
        hidden = hidden_act.astype(bf16)
        feed = jnp.dot(hidden, down_weight, preferred_element_type=f32) + down_bias.astype(f32)
        second, normed_two, inv_two = norm_forward(
            first + feed, gain_two.astype(f32), shift_two.astype(f32)
        )
        final, normed_three, inv_three = norm_forward(
            carried + branch + feed, gain_three.astype(f32), shift_three.astype(f32)
        )
        out_list.append((second + final).astype(bf16))
        cotangent = upstream[micro_step, 0].astype(f32)
        accum_grad, gain3_grad, shift3_grad = norm_backward(
            cotangent, normed_three, inv_three, gain_three.astype(f32)
        )
        second_grad, gain2_grad, shift2_grad = norm_backward(
            cotangent, normed_two, inv_two, gain_two.astype(f32)
        )
        feed_grad = second_grad + accum_grad
        feed_low = feed_grad.astype(bf16)
        down_grad = jnp.dot(hidden.T, feed_low, preferred_element_type=f32)
        (hidden_grad,) = gate_pull(jnp.dot(feed_low, down_weight.T, preferred_element_type=f32))
        hidden_low = hidden_grad.astype(bf16)
        up_grad = jnp.dot(first_low.T, hidden_low, preferred_element_type=f32)
        first_grad = second_grad + jnp.dot(hidden_low, up_weight.T, preferred_element_type=f32)
        resid_grad, gain1_grad, shift1_grad = norm_backward(
            first_grad, normed_one, inv_one, gain_one.astype(f32)
        )
        branch_low = (resid_grad + accum_grad).astype(bf16)
        out_wgrad = jnp.dot(mixed.T, branch_low, preferred_element_type=f32)
        mixed_grad = jnp.dot(branch_low, o_weight.T, preferred_element_type=f32).astype(bf16)
        mixed_grad = mixed_grad.reshape(tokens, heads_axis, group_width)
        grad_group = lax.all_to_all(mixed_grad, "head", split_axis=1, concat_axis=0, tiled=True)
        grad_loc = grad_group[:, 0]
        grad3 = grad_loc.reshape(rows, groups, DH)
        row_delta = jnp.sum(grad3.astype(f32) * attn_out, axis=2)
        whole_keys, whole_values, whole_seg = (
            lax.all_gather(key_loc, "blk", axis=0, tiled=True),
            lax.all_gather(value_loc, "blk", axis=0, tiled=True),
            lax.all_gather(seg_loc, "blk", axis=0, tiled=True),
        )

        def backward_step(running, blocks):
            key_part, value_part, seg_part = blocks
            attn_prob, score_grad = block_grads(
                queries3,
                seg_loc,
                grad3,
                log_total,
                row_delta,
                key_part,
                value_part,
                seg_part,
                scaling,
            )
            running = running + jnp.einsum(
                "sgk,kgd->sgd", score_grad, key_part, preferred_element_type=f32
            )
            key_term = jnp.einsum("sgk,sgd->kgd", score_grad, queries3, preferred_element_type=f32)
            value_term = jnp.einsum("sgk,sgd->kgd", attn_prob, grad3, preferred_element_type=f32)
            return (running, (key_term, value_term))

        query_grad, (key_terms, value_terms) = lax.scan(
            backward_step,
            jnp.zeros((rows, groups, DH), f32),
            key_blocks(whole_keys, whole_values, whole_seg, groups),
        )
        key_grad, value_grad = (
            lax.psum_scatter(
                key_terms.reshape(-1, group_width), "blk", scatter_dimension=0, tiled=True
            ),
            lax.psum_scatter(
                value_terms.reshape(-1, group_width), "blk", scatter_dimension=0, tiled=True
            ),
        )
        grad_stack = jnp.stack(
            [query_grad.reshape(rows, group_width), key_grad, value_grad]
        ).astype(bf16)
        grad_stack = grad_stack.reshape(3, rows, 1, group_width)
        returned = lax.all_to_all(
            grad_stack, "head", split_axis=1, concat_axis=2, tiled=True
        ).reshape(3, tokens, width)
        query_wgrad = jnp.dot(inputs.T, returned[0], preferred_element_type=f32)
        key_wgrad = jnp.dot(inputs.T, returned[1], preferred_element_type=f32)
        value_wgrad = jnp.dot(inputs.T, returned[2], preferred_element_type=f32)
        input_grad = (
            resid_grad
            + jnp.dot(returned[0], q_weight.T, preferred_element_type=f32)
            + jnp.dot(returned[1], k_weight.T, preferred_element_type=f32)
            + jnp.dot(returned[2], v_weight.T, preferred_element_type=f32)
        )
        stream_grads.append(input_grad)
        accum_grads.append(accum_grad)
        step_grads = (
            query_wgrad,
            key_wgrad,
            value_wgrad,
            out_wgrad,
            up_grad,
            jnp.sum(hidden_grad, axis=0),
            down_grad,
            jnp.sum(feed_grad, axis=0),
            gain1_grad,
            shift1_grad,
            gain2_grad,
            shift2_grad,
            gain3_grad,
            shift3_grad,
        )
        if grad_totals is None:
            grad_totals = step_grads
        else:
            grad_totals = tuple((older + newer for older, newer in zip(grad_totals, step_grads)))
    summed = lax.psum_scatter(grad_totals, ("head", "blk"), scatter_dimension=0, tiled=True)
    layer_out = jnp.stack(out_list)[:, None]
    grad_stream = jnp.stack(stream_grads)[:, None]
    grad_accum = jnp.stack(accum_grads)[:, None]
    return (
        layer_out,
        grad_stream,
        grad_accum,
        summed[0],
        summed[1],
        summed[2],
        summed[3],
        summed[4],
        summed[5],
        summed[6],
        summed[7],
        summed[8],
        summed[9],
        summed[10],
        summed[11],
        summed[12],
        summed[13],
    )


def dot_t(a, b):
    return lax.dot_general(a, b, (((1,), (1,)), ((), ())), preferred_element_type=f32)

def dot_n(a, b):
    return lax.dot_general(a, b, (((1,), (0,)), ((), ())), preferred_element_type=f32)

def dot_0(a, b):
    return lax.dot_general(a, b, (((0,), (0,)), ((), ())), preferred_element_type=f32)

def lanes(shape):
    return lax.broadcasted_iota(jnp.int32, shape, len(shape) - 1)

def query_marks(seg_row):
    wide = jnp.broadcast_to(seg_row, (128, seg_row.shape[1])).T
    return (wide == lanes(wide.shape)).astype(f32).astype(bf16)

def half_lanes(tile, half):
    wide = tile.astype(f32)
    if half:
        wide = pltpu.roll(wide, 64, 1)
    return jnp.where(lanes(wide.shape) < 64, wide, 0.0).astype(bf16)

def key_steps(bounds, low, high):
    chunks, keys = bounds.shape
    first = sum(jnp.where(bounds[t, keys - 1] < low, 1, 0) for t in range(chunks))
    last = sum(jnp.where(bounds[t, 0] <= high, 1, 0) for t in range(chunks))
    pairs = (last - first + 1) // 2
    start = jnp.minimum(first, chunks - 2 * pairs)
    return start, pairs // 2, lax.rem(pairs, 2)


def walk(step, fours, twos, carry):
    carry = lax.fori_loop(0, fours, lambda t, c: step(4, 4 * t, c), carry)
    return lax.fori_loop(0, twos, lambda t, c: step(2, 4 * fours, c), carry)


def attn_fwd_kernel(
    q_hbm, kv_hbm, seg_q_hbm, seg_k_hbm, o_hbm, of_hbm, lse_hbm, kv2_hbm, kvt_hbm,
    q_ref, kv_ref, seg_q_ref, seg_k_ref, bounds, o_ref, of_ref, lse_ref, kv2_ref, kvt_ref, vo_ref, in_sem, out_sem,
):
    loads = copies(
        [(seg_q_hbm, seg_q_ref), (seg_k_hbm, seg_k_ref), (seg_k_hbm, bounds), (kv_hbm, kv_ref), (q_hbm, q_ref)], in_sem
    )
    wait_all(loads)
    chunks, keys = seg_k_ref.shape
    log_scale = math.log2(math.e) * DH ** (-0.5)

    def prepare(t, c):
        rows = pl.ds(pl.multiple_of(t * keys, keys), keys)
        kv = kv_ref[rows, :]
        marks = jnp.where(seg_k_ref[pl.ds(t, 1), :] == rows_of((128, keys)), 0.0, FAR)
        kvt_ref[0:128, rows] = kv.T
        kvt_ref[128:256, rows] = marks.astype(bf16)
        kv2_ref[rows, 0:128] = kv
        kv2_ref[rows, 128:256] = marks.T.astype(bf16)
        vo_ref[rows, :] = jnp.where(lanes(kv.shape) < 64, 1.0, kv.astype(f32)).astype(bf16)
        return c

    lax.fori_loop(0, chunks, prepare, 0)
    stores = copies([(kv2_ref, kv2_hbm), (kvt_ref, kvt_hbm)], out_sem)

    def tile(j, c):
        q_tile = q_ref[j]
        rows = q_tile.shape[0]
        outs = []
        for half in range(2):
            i = half * (chunks // 2) + j
            left = half_lanes(q_tile, half)
            left = jnp.concatenate([left, query_marks(seg_q_ref[pl.ds(i, 1), :])], axis=1)
            low, high = bounds[i, 0], bounds[i, keys - 1]
            start, fours, twos = key_steps(bounds, low, high)

            def step(width, t, carry):
                top, acc = carry
                at = pl.ds(pl.multiple_of((start + t) * keys, keys), width * keys)
                s = dot_n(left, kvt_ref[:, at])
                new = jnp.maximum(top, jnp.max(s, axis=1, keepdims=True))
                p = jnp.exp2((s - new) * log_scale)
                acc = acc * jnp.exp2((top - new) * log_scale) + dot_n(p.astype(bf16), vo_ref[at, :])
                return new, acc

            carry = (jnp.full((rows, 1), FAR, f32), jnp.zeros((rows, 128), f32))
            top, acc = walk(step, fours, twos, carry)
            total = pltpu.roll(acc, 64, 1)
            outs.append(acc / total)
            lse = jnp.broadcast_to(top * log_scale, acc.shape) + jnp.log2(acc)
            lse_ref[pl.ds(i, 1), :] = lse.T[0:1, :]
        o = jnp.where(lanes(outs[0].shape) < 64, pltpu.roll(outs[0], 64, 1), outs[1])
        of_ref[j] = o
        o_ref[j] = o.astype(bf16)
        return c

    lax.fori_loop(0, chunks // 2, tile, 0)
    stores += copies([(o_ref, o_hbm), (of_ref, of_hbm), (lse_ref, lse_hbm)], out_sem.at[pl.ds(2, 3)])
    wait_all(stores)


def attn_fwd(q, kv, seg_q, seg_k):
    chunks, keys = seg_k.shape
    dma = pltpu.SemaphoreType.DMA
    shapes = (
        (q.shape, bf16), (q.shape, f32), (seg_q.shape, f32), ((chunks * keys, 256), bf16), ((256, chunks * keys), bf16)
    )
    return pl.pallas_call(
        attn_fwd_kernel,
        out_shape=[jax.ShapeDtypeStruct(shape, kind) for shape, kind in shapes],
        in_specs=any_specs(4),
        out_specs=any_specs(5),
        scratch_shapes=[
            *[pltpu.VMEM(a.shape, a.dtype) for a in (q, kv, seg_q, seg_k)],
            pltpu.SMEM(seg_k.shape, jnp.int32),
            *[pltpu.VMEM(shape, kind) for shape, kind in shapes],
            pltpu.VMEM((chunks * keys, 128), bf16),
            dma((5,)),
            dma((5,)),
        ],
        compiler_params=pltpu.CompilerParams(vmem_limit_bytes=VMEM_BYTES),
        cost_estimate=pl.CostEstimate(flops=10**10, bytes_accessed=10**7, transcendentals=10**7),
        name="attn_fwd",
    )(q, kv, seg_q, seg_k)


def attn_bwd_kernel(
    q_hbm, do_hbm, of_hbm, lse_hbm, kv2_hbm, kvt_hbm, seg_q_hbm, seg_k_hbm, pass1, pass2, dq_hbm, dkv_hbm, out1, out2,
    q_ref, do_ref, of_ref, lse_ref, kv2_ref, kvt_ref, seg_q_ref, bounds, dq_ref, dkv_low, dkv_ref, hold1, hold2, in_sem, out_sem,
):
    loads = copies(
        [
            (q_hbm, q_ref), (do_hbm, do_ref), (of_hbm, of_ref), (lse_hbm, lse_ref), (kv2_hbm, kv2_ref),
            (seg_q_hbm, seg_q_ref), (seg_k_hbm, bounds),
            (pass1, hold1), (pass2, hold2), (kvt_hbm, kvt_ref),
        ],
        in_sem,
    )
    dkv_ref[...] = jnp.zeros_like(dkv_ref)
    wait_all(loads)
    stores = copies([(hold1, out1), (hold2, out2)], out_sem)
    chunks, keys = bounds.shape
    log_scale = math.log2(math.e) * DH ** (-0.5)

    def tile(j, c):
        q_tile, do_tile = q_ref[j], do_ref[j]
        rows = q_tile.shape[0]
        prod = do_tile.astype(f32) * of_ref[j]
        prod = prod.T
        dqs = []
        for half in range(2):
            i = half * (chunks // 2) + j
            left = half_lanes(q_tile, half)
            grad = do_tile.astype(f32)
            if not half:
                grad = pltpu.roll(grad, 64, 1)
            grad = jnp.where(lanes(grad.shape) < 64, 0.0, grad).astype(bf16)
            delta = jnp.sum(prod[64 * half:64 * half + 64], axis=0, keepdims=True)
            lse = lse_ref[pl.ds(i, 1), :]
            both = jnp.concatenate([left, grad], axis=0)
            marks = query_marks(seg_q_ref[pl.ds(i, 1), :])
            right = jnp.concatenate([both, jnp.concatenate([marks, jnp.zeros_like(marks)], axis=0)], axis=1).T
            low, high = bounds[i, 0], bounds[i, keys - 1]
            start, fours, twos = key_steps(bounds, low, high)

            def step(width, t, dq):
                at = pl.ds(pl.multiple_of((start + t) * keys, keys), width * keys)
                sdp = dot_n(kv2_ref[at, :], right)
                p = jnp.exp2(sdp[:, :rows] * log_scale - lse)
                ds = (p * (sdp[:, rows:] - delta)).astype(bf16)
                dkv_ref[at, :] += dot_n(jnp.concatenate([ds, p.astype(bf16)], axis=1), both)
                return dq + dot_n(kvt_ref[0:128, at], ds)

            dqs.append(walk(step, fours, twos, jnp.zeros((128, rows), f32)).T)
        dq = jnp.where(lanes(dqs[0].shape) < 64, dqs[0], pltpu.roll(dqs[1], 64, 1))
        dq_ref[j] = (dq * DH ** (-0.5)).astype(bf16)
        return c

    lax.fori_loop(0, chunks // 2, tile, 0)
    dkv = dkv_ref[...]
    dkv_low[...] = jnp.where(lanes(dkv.shape) < 64, dkv * DH ** (-0.5), dkv).astype(bf16)
    stores += copies([(dq_ref, dq_hbm), (dkv_low, dkv_hbm)], out_sem.at[pl.ds(2, 2)])
    wait_all(stores)


def attn_bwd(q, do, of, lse, kv2, kvt, seg_q, seg_k, pass1, pass2):
    dma = pltpu.SemaphoreType.DMA
    shapes = ((q.shape, bf16), ((kv2.shape[0], 128), bf16))
    return pl.pallas_call(
        attn_bwd_kernel,
        out_shape=[jax.ShapeDtypeStruct(shape, kind) for shape, kind in shapes]
        + [jax.ShapeDtypeStruct(a.shape, a.dtype) for a in (pass1, pass2)],
        in_specs=any_specs(10),
        out_specs=any_specs(4),
        scratch_shapes=[
            *[pltpu.VMEM(a.shape, a.dtype) for a in (q, do, of, lse, kv2, kvt, seg_q)],
            pltpu.SMEM(seg_k.shape, jnp.int32),
            *[pltpu.VMEM(shape, kind) for shape, kind in shapes],
            pltpu.VMEM((kv2.shape[0], 128), f32),
            *[pltpu.VMEM(a.shape, a.dtype) for a in (pass1, pass2)],
            dma((10,)),
            dma((4,)),
        ],
        compiler_params=pltpu.CompilerParams(vmem_limit_bytes=VMEM_BYTES),
        cost_estimate=pl.CostEstimate(flops=10**10, bytes_accessed=10**7, transcendentals=10**7),
        name="attn_bwd",
    )(q, do, of, lse, kv2, kvt, seg_q, seg_k, pass1, pass2)


class Spot:
    def __init__(self, nb):
        self.nb, self.nz = nb, nb // 2
        self.h, b = lax.axis_index("head"), lax.axis_index("blk")
        self.z, self.c = b // 2, lax.rem(b, 2)
        self.near = (self.h + 1 - 2 * lax.rem(self.h, 2), lax.rem(self.h + 2, 4))
        self.diag = 3 - self.h
        self.me = self.h * nb + b

    def index(self, h, z, c):
        return h * self.nb + z * 2 + c

    def ahead(self, k):
        return lax.rem(self.z + k, self.nz)


def remote(src, dst, send, recv, h, b):
    return pltpu.make_async_remote_copy(
        src_ref=src,
        dst_ref=dst,
        send_sem=send,
        recv_sem=recv,
        device_id={"head": h, "blk": b},
        device_id_type=MESH,
    )


def each(count, body, start=0):
    def run(i, c):
        body(i)
        return c

    lax.fori_loop(start, count, run, 0)


def hail(h, b):
    pl.semaphore_signal(
        pltpu.get_barrier_semaphore(), inc=1, device_id={"head": h, "blk": b}, device_id_type=MESH
    )


def greet_near(s):
    for k in range(1, s.nz):
        hail(s.h, s.ahead(k) * 2 + s.c)
    for i in range(1, 4):
        hail(lax.rem(s.h + i, 4), s.z * 2 + s.c)
    hail(s.h, s.z * 2 + 1 - s.c)
    pl.semaphore_wait(pltpu.get_barrier_semaphore(), s.nz + 3)


def greet_core(s):
    def signal(i):
        t = lax.rem(s.me + 2 * i, 4 * s.nb)
        hail(t // s.nb, lax.rem(t, s.nb))

    each(2 * s.nb, signal, 1)
    hail(s.h, s.z * 2 + 1 - s.c)
    pl.semaphore_wait(pltpu.get_barrier_semaphore(), 2 * s.nb)


class Scatter:
    def __init__(self, spot, part, twin, diag, near, line, send, recv):
        self.s, self.part, self.t, self.d, self.n, self.l = spot, part, twin, diag, near, line
        self.send, self.recv = send, recv

    def copy(self, src, dst, k, h, z, c, recv_k=None):
        recv_k = k if recv_k is None else recv_k
        return remote(src, dst, self.send.at[k], self.recv.at[recv_k], h, z * 2 + c)

    def mine(self, h, z):
        return h * self.s.nz + z if self.t is None else self.s.index(h, z, self.s.c)

    def to_twin(self, h, z):
        s = self.s
        src = self.part.at[s.index(h, z, 1 - s.c)]
        return self.copy(src, self.t.at[h, z], h * s.nz + z, s.h, s.z, 1 - s.c)

    def to_diag(self, z):
        s = self.s
        src = self.part.at[self.mine(s.diag, z)]
        return self.copy(src, self.d.at[z], 4 * s.nz + z, s.diag, s.z, s.c)

    def to_near(self, w, z):
        s = self.s
        src = self.part.at[self.mine(s.near[w], z)]
        return self.copy(src, self.n.at[w, z], (6 + w) * s.nz + z, s.near[w], s.z, s.c)

    def to_line(self, z):
        s = self.s
        src = self.part.at[self.mine(s.h, z)]
        return self.copy(src, self.l.at[s.z], 8 * s.nz + z, s.h, z, s.c, 8 * s.nz + s.z)

    def from_line(self, z):
        s = self.s
        src = self.part.at[self.mine(s.h, z)]
        return self.copy(src, self.l.at[z], 8 * s.nz + z, s.h, z, s.c)

    def begin(self):
        each(4, lambda h: each(self.s.nz, lambda z: self.to_twin(h, z).start()))

    def pair(self, h, z):
        if self.t is None:
            return self.part[self.mine(h, z)].astype(f32)
        self.to_twin(h, z).wait_recv()
        return self.part[self.mine(h, z)].astype(f32) + self.t[h, z].astype(f32)

    def keep(self, h, z, value):
        self.part[self.mine(h, z)] = value.astype(self.part.dtype)

    def second(self):
        s = self.s

        def go(k):
            z = s.ahead(k)
            for w in range(2):
                if self.t is not None:
                    self.keep(s.near[w], z, self.pair(s.near[w], z))
                self.to_near(w, z).start()
            if self.t is not None:
                self.keep(s.diag, z, self.pair(s.diag, z))
                self.to_diag(z).start()

        each(s.nz + 1, go, 1)

    def joined(self, z):
        value = self.pair(self.s.h, z)
        if self.t is not None:
            self.to_diag(z).wait_recv()
        value = value + self.d[z].astype(f32)
        for w in range(2):
            self.to_near(w, z).wait_recv()
            value = value + self.n[w, z].astype(f32)
        return value

    def third(self):
        s = self.s

        def go(k):
            z = s.ahead(k)
            self.keep(s.h, z, self.joined(z))
            self.to_line(z).start()

        each(s.nz, go, 1)

    def columns(self):
        s = self.s
        self.l[s.z] = self.joined(s.z).astype(self.l.dtype)
        each(s.nz, lambda k: self.from_line(s.ahead(k)).wait_recv(), 1)
        return [self.l[w].astype(f32) + self.l[w + 2].astype(f32) for w in range(2)]

    def total(self):
        s = self.s
        value = self.joined(s.z)

        def go(k, value):
            z = s.ahead(k)
            self.from_line(z).wait_recv()
            return value + self.l[z].astype(f32)

        return lax.fori_loop(1, s.nz, go, value)

    def sent(self):
        s = self.s

        def go(z):
            if self.t is not None:
                each(4, lambda h: self.to_twin(h, z).wait_send())
                self.to_diag(z).wait_send()
            for w in range(2):
                self.to_near(w, z).wait_send()

        each(s.nz, go)
        each(s.nz, lambda k: self.to_line(s.ahead(k)).wait_send(), 1)


class Exchange:
    def __init__(self, spot, src, dst, send, recv, local):
        self.s, self.src, self.dst, self.send, self.recv, self.local = spot, src, dst, send, recv, local
        self.g = spot.me // 2

    def copy(self, i, back=False):
        s = self.s
        to = lax.rem(self.g + i, 16)
        t = to * 2 + s.c
        src = self.src(to)
        dst = self.dst(lax.rem(self.g + 16 - i, 16)) if back else self.dst(self.g)
        return remote(src, dst, self.send.at[i], self.recv.at[i], t // s.nb, lax.rem(t, s.nb))

    def own(self):
        return pltpu.make_async_copy(self.src(self.g), self.dst(self.g), self.local)

    def begin(self):
        self.own().start()
        each(16, lambda i: self.copy(i).start(), 1)

    def arrive(self, i):
        self.copy(i, True).wait_recv()

    def end(self):
        each(16, self.arrive, 1)
        self.sent()

    def sent(self):
        self.own().wait()
        each(16, lambda i: self.copy(i).wait_send(), 1)


class Plane:
    def __init__(self, spot, send, recv):
        self.s, self.send, self.recv = spot, send, recv

    def to(self, k):
        return lax.rem(self.s.h + k, 4)

    def frm(self, k):
        return lax.rem(self.s.h + 4 - k, 4)

    def copy(self, src, dst, j, at_send, at_recv):
        s = self.s
        return remote(src, dst, self.send.at[at_send], self.recv.at[at_recv], j, s.z * 2 + s.c)


def pair_of(g):
    return lax.rem(g, 4) * 4 + g // 4


def weave(left, right):
    kind = left.dtype
    left, right = left.astype(f32), right.astype(f32)
    low = lanes(left.shape) < 64
    first = jnp.where(low, left, pltpu.roll(right, 64, 1)).astype(kind)
    second = jnp.where(low, pltpu.roll(left, 64, 1), right).astype(kind)
    return first, second


def any_specs(count):
    return [pl.BlockSpec(memory_space=pl.ANY)] * count


def copies(pairs, sems):
    jobs = [pltpu.make_async_copy(src, dst, sems.at[k]) for k, (src, dst) in enumerate(pairs)]
    for job in jobs:
        job.start()
    return jobs


def wait_all(jobs):
    for job in jobs:
        job.wait()


def rows_of(shape):
    return lax.broadcasted_iota(jnp.int32, shape, 0)


def spread_row(block, width, each_lane):
    count = block.shape[0]
    pick = (rows_of((128, width)) == lax.rem(lanes((128, width)), each_lane)).astype(f32).astype(bf16)
    wide = dot_n(block.astype(bf16), pick)
    return column_sum(jnp.where(rows_of((count, width)) == lanes((count, width)) // each_lane, wide, 0.0))


def gather_row(row, count, each_lane):
    width = row.shape[1]
    wide = jnp.where(rows_of((count, width)) == lanes((count, width)) // each_lane, row, 0.0)
    pick = (lanes((width, 128)) == lax.rem(rows_of((width, 128)), each_lane)).astype(f32)
    return lax.dot_general(
        wide, pick, (((1,), (0,)), ((), ())), precision=lax.Precision.HIGHEST, preferred_element_type=f32
    )


class Line:
    def __init__(self, spot, shard, full, send, recv, local):
        self.s, self.shard, self.full, self.send, self.recv = spot, shard, full, send, recv
        self.own = pltpu.make_async_copy(shard, full.at[spot.z], local)

    def copy(self, way, t):
        s = self.s
        k = 2 * t + (way + 1) // 2
        src = self.full.at[s.z - way * t] if t else self.shard
        dst = self.full.at[s.z - way * t]
        return remote(src, dst, self.send.at[k], self.recv.at[k], s.h, (s.z + way) * 2 + s.c)

    def inside(self, z):
        return (z >= 0) & (z < self.s.nz)

    def sends(self, t, act):
        for way in (1, -1):
            z = self.s.z

            @pl.when(self.inside(z + way) & self.inside(z - way * t))
            def _():
                act(self.copy(way, t))

    def arrive(self, t):
        for way in (1, -1):
            s = self.s

            @pl.when(self.inside(s.z - way * (t + 1)))
            def _():
                slot = self.full.at[s.z - way * (t + 1)]
                k = 2 * t + (way + 1) // 2
                remote(slot, slot, self.send.at[k], self.recv.at[k], s.h, (s.z - way) * 2 + s.c).wait_recv()

    def begin(self):
        self.own.start()
        self.sends(0, lambda copy: copy.start())

    def onward(self, t):
        self.arrive(t)
        if t + 1 < self.s.nz - 1:
            self.sends(t + 1, lambda copy: copy.start())

    def sent(self):
        self.own.wait()
        for t in range(self.s.nz - 1):
            self.sends(t, lambda copy: copy.wait_send())


def project_kernel(n, nb, *refs):
    x_hbm, wq_hbm, wk_hbm, wv_hbm, wo_hbm, wu_hbm, wd_hbm, seg_hbm = refs[:8]
    smalls = refs[8:16]
    q_out, kv_out, x_out, wa_out, fz_out, par_out, bup_out, segk_out, segq_out = refs[16:25]
    (
        x, wq, wk, wv, wo, wu, wd, seg, *small, bup_small, vec, sa, sb, wa, x_all, kv_send, q_send,
        par, bup, segk, segq,
        in_sem, out_sem, w_send, w_recv, w_local, f_send, f_recv, f_local,
        x_send, x_recv, x_local, ex_send, ex_recv, ex_local, tw_send, tw_recv,
    ) = refs[25:]
    s = Spot(nb)
    loads = copies(
        [(wq_hbm, wq), (wk_hbm, wk), (wv_hbm, wv), (seg_hbm, seg), (smalls[0], bup_small)]
        + [(smalls[k], small[k - 1]) for k in range(1, 8)]
        + [(x_hbm, x), (wo_hbm, wo), (wu_hbm, wu), (wd_hbm, wd)],
        in_sem,
    )
    greet_near(s)

    def pass_x(z, slot):
        return remote(x.at[z // 2], x_all.at[slot], x_send.at[z], x_recv.at[slot], s.h, z * 2 + s.c)

    wait_all(loads[:13])
    vec[...] = jnp.zeros_like(vec)
    vec[0:1, 0:64] = bup_small[...].astype(f32).reshape(1, 64)
    for k in range(7):
        vec[k + 1:k + 2, 0:16] = small[k][...].astype(f32).reshape(1, 16)
    vec[8:10, :] = seg[...].astype(f32)
    for t in range(4):
        tile, at = slice(128 * t, 128 * t + 128), 256 * (t % 2)
        first, second = weave(wk[:, tile], wv[:, tile])
        sa[t // 2, :, at:at + 128] = first
        sa[t // 2, :, at + 128:at + 256] = second
    for w in range(2):
        sa[w, :, 512:768] = wq[:, 256 * w:256 * w + 256]
        sa[w, :, 768:896] = vec[...].astype(bf16)

    def w_line(z, slot):
        return remote(
            sa.at[lax.rem(z, 2)], wa.at[s.h, slot, s.c], w_send.at[z], w_recv.at[slot], s.h, z * 2 + s.c
        )

    def w_plane(j, h):
        slot = wa.at[h, :, s.c]
        return remote(slot, slot, w_send.at[4 + j], w_recv.at[4 + h], j, s.z * 2 + s.c)

    def w_twin(h, c):
        slot = wa.at[h, :, c]
        return remote(slot, slot, w_send.at[8 + h], w_recv.at[8 + h], s.h, s.z * 2 + 1 - s.c)

    each(s.nz, lambda k: w_line(s.ahead(k), s.z).start(), 1)
    own_w = pltpu.make_async_copy(sa.at[lax.rem(s.z, 2)], wa.at[s.h, s.z, s.c], w_local)
    own_w.start()
    own_x = pltpu.make_async_copy(x.at[s.z // 2], x_all.at[s.z], x_local)
    own_x.start()
    wait_all(loads[13:])
    sb[:, 0:512] = wo[...]
    sb[:, 512:2560] = wu[...]
    for t in range(4):
        sb[:, 2560 + 512 * t:3072 + 512 * t] = wd[16 * t:16 * t + 16, :]
    line = Line(s, sb, fz_out, f_send, f_recv, f_local)
    own_w.wait()
    each(s.nz, lambda k: w_line(s.ahead(k), s.ahead(k)).wait_recv(), 1)
    each(s.nz, lambda k: pass_x(s.ahead(k), s.z).start(), 1)
    each(4, lambda i: w_plane(lax.rem(s.h + i, 4), s.h).start(), 1)
    w_twin(s.h, s.c).start()

    def w_arrive(i):
        h = lax.rem(s.h + 4 - i, 4)
        w_plane(h, h).wait_recv()
        w_twin(h, s.c).start()

    each(4, w_arrive, 1)
    line.begin()
    each(4, lambda h: w_twin(h, 1 - s.c).wait_recv())
    outs = copies([(wa, wa_out)], out_sem)
    own_x.wait()
    plane = [Plane(s, ex_send.at[k], ex_recv.at[k]) for k in range(2)]
    kinds = ((kv_send, lambda g: kv_out.at[:, g, s.c]), (q_send, lambda g: q_out.at[:, g]))

    def block(w, j, z):
        src, dst = kinds[w]
        return plane[w].copy(src.at[j, z], dst(s.h * 4 + z), j, j * 4 + z, s.h * 4 + z)

    def from_block(w, j, z):
        src, dst = kinds[w]
        slot = dst(j * 4 + z)
        return plane[w].copy(slot, slot, j, j * 4 + z, j * 4 + z)

    def own_block(w, z):
        src, dst = kinds[w]
        return pltpu.make_async_copy(src.at[s.h, z], dst(s.h * 4 + z), ex_local.at[w, z])

    def twin(src, j, z, c):
        slot = kv_out.at[:, j * 4 + z, c]
        k = j * 4 + z
        return remote(slot if src is None else src, slot, tw_send.at[k], tw_recv.at[k], s.h, s.z * 2 + 1 - s.c)

    def project_rows(k):
        z = s.ahead(k)
        qkv = dot_n(x_all[z], wa[:, :, :, :, 0:768].reshape(512, 768)).astype(bf16)
        for j in range(4):
            kv_send[j, z] = qkv[:, 128 * j:128 * j + 128].reshape(8, 16, 128)
        for t in range(2):
            tile = qkv[:, 512 + 128 * t:640 + 128 * t]
            first, second = weave(tile[0:64], tile[64:128])
            q_send[2 * t, z] = first.reshape(4, 16, 128)
            q_send[2 * t + 1, z] = second.reshape(4, 16, 128)
        for w in range(2):
            each(4, lambda i: block(w, plane[w].to(i), z).start(), 1)
            own_block(w, z).start()
        twin(kv_send.at[s.h, z], s.h, z, s.c).start()

    project_rows(0)

    def project_next(k):
        z = s.ahead(k)
        pass_x(z, z).wait_recv()
        project_rows(k)

    each(s.nz, project_next, 1)
    line.onward(0)
    line.onward(1)
    vecs = wa[:, :, :, :, 768:896].reshape(n, 16, 128).astype(f32)
    outs += copies([(x_all, x_out)], out_sem.at[pl.ds(5, 1)])
    bup[...] = spread_row(vecs[:, 0, :], 2048, 64)
    for k in range(7):
        par[k:k + 1, :] = spread_row(vecs[:, k + 1, :], 512, 16)
    par[7:8, :] = jnp.zeros((1, 512), f32)
    ids = jnp.where(s.z < 2, vecs[:, 8, :], vecs[:, 9, :]).astype(bf16)
    for i in range(8):
        pick = (rows_of((128, 512)) == 16 * i + lax.rem(lanes((128, 512)), 16)).astype(f32).astype(bf16)
        wide = dot_n(ids, pick)
        source = rows_of((n, 512))
        row = jnp.where(source == lanes((n, 512)) // 16, wide, 0.0)
        segk[i:i + 1, :] = column_sum(row).astype(jnp.int32)
        source = rows_of((n, 256))
        own = (source // 2 == lanes((n, 256)) // 16) & (lax.rem(source, 2) == s.c)
        segq[i:i + 1, :] = column_sum(jnp.where(own, wide[:, 0:256], 0.0)).astype(jnp.int32)
    outs += copies([(par, par_out), (bup, bup_out), (segk, segk_out), (segq, segq_out)], out_sem.at[pl.ds(1, 4)])
    def forward(i):
        j = plane[0].frm(i)

        def go(k):
            z = s.ahead(k)
            from_block(0, j, z).wait_recv()
            twin(None, j, z, s.c).start()

        each(s.nz, go)

    each(4, forward, 1)
    line.onward(2)
    each(4, lambda i: each(s.nz, lambda z: from_block(1, plane[1].frm(i), z).wait_recv()), 1)
    each(4, lambda j: each(s.nz, lambda z: twin(None, j, z, 1 - s.c).wait_recv()))
    each(4, lambda j: each(s.nz, lambda z: twin(None, j, z, s.c).wait_send()))
    for w in range(2):
        each(s.nz, lambda z: own_block(w, z).wait())
        each(4, lambda i: each(s.nz, lambda z: block(w, plane[w].to(i), z).wait_send()), 1)
    each(s.nz, lambda k: pass_x(s.ahead(k), s.z).wait_send(), 1)
    each(s.nz, lambda k: w_line(s.ahead(k), s.z).wait_send(), 1)
    each(4, lambda i: w_plane(lax.rem(s.h + i, 4), s.h).wait_send(), 1)
    each(4, lambda h: w_twin(h, s.c).wait_send())
    line.sent()
    wait_all(outs)


def project(n, nb, x, wq, wk, wv, wo, wu, wd, seg, smalls):
    dma = pltpu.SemaphoreType.DMA
    nz = nb // 2
    return pl.pallas_call(
        functools.partial(project_kernel, n, nb),
        out_shape=(
            jax.ShapeDtypeStruct((4, 16, 16, 128), bf16),
            jax.ShapeDtypeStruct((8, 16, 2, 16, 128), bf16),
            jax.ShapeDtypeStruct((nz, 128, 512), bf16),
            jax.ShapeDtypeStruct((4, nz, 2, 16, 896), bf16),
            jax.ShapeDtypeStruct((nz, 16, 4608), bf16),
            jax.ShapeDtypeStruct((8, 512), f32),
            jax.ShapeDtypeStruct((1, 2048), f32),
            jax.ShapeDtypeStruct((8, 512), jnp.int32),
            jax.ShapeDtypeStruct((8, 256), jnp.int32),
        ),
        in_specs=any_specs(16),
        out_specs=any_specs(9),
        scratch_shapes=[
            pltpu.VMEM(x.shape, bf16),
            pltpu.VMEM((16, 512), bf16),
            pltpu.VMEM((16, 512), bf16),
            pltpu.VMEM((16, 512), bf16),
            pltpu.VMEM((16, 512), bf16),
            pltpu.VMEM((16, 2048), bf16),
            pltpu.VMEM((64, 512), bf16),
            pltpu.VMEM((2, 128), jnp.int32),
            *[pltpu.VMEM((16,), bf16)] * 7,
            pltpu.VMEM((64,), bf16),
            pltpu.VMEM((16, 128), f32),
            pltpu.VMEM((2, 16, 896), bf16),
            pltpu.VMEM((16, 4608), bf16),
            pltpu.VMEM((4, nz, 2, 16, 896), bf16),
            pltpu.VMEM((nz, 128, 512), bf16),
            pltpu.VMEM((4, nz, 8, 16, 128), bf16),
            pltpu.VMEM((4, nz, 4, 16, 128), bf16),
            pltpu.VMEM((8, 512), f32),
            pltpu.VMEM((1, 2048), f32),
            pltpu.VMEM((8, 512), jnp.int32),
            pltpu.VMEM((8, 256), jnp.int32),
            dma((16,)),
            dma((6,)),
            dma((12,)),
            dma((12,)),
            dma,
            dma((2 * nz,)),
            dma((2 * nz,)),
            dma,
            dma((nz,)),
            dma((nz,)),
            dma,
            dma((2, 4 * nz)),
            dma((2, 4 * nz)),
            dma((2, nz)),
            dma((4 * nz,)),
            dma((4 * nz,)),
        ],
        compiler_params=pltpu.CompilerParams(
            collective_id=1, has_side_effects=True, vmem_limit_bytes=VMEM_BYTES
        ),
        name="project",
    )(x, wq, wk, wv, wo, wu, wd, seg, *smalls)


def row_norm(v):
    mean = jnp.mean(v, axis=-1, keepdims=True)
    mid = v - mean
    inv = lax.rsqrt(jnp.mean(mid * mid, axis=-1, keepdims=True) + EPSILON)
    return mid * inv, inv


def row_norm_back(grad, normed, inv, gain):
    part = grad * gain
    return inv * (
        part
        - jnp.mean(part, axis=-1, keepdims=True)
        - normed * jnp.mean(part * normed, axis=-1, keepdims=True)
    )


def normal(u):
    bell = jnp.exp(-0.5 * u * u)
    t = 1.0 / (1.0 + (0.3275911 * 0.5**0.5) * jnp.abs(u))
    poly = 0.5 * 1.061405429
    for factor in (-1.453152027, 1.421413741, -0.284496736, 0.254829592):
        poly = poly * t + 0.5 * factor
    tail = poly * t * bell
    return jnp.where(u < 0, tail, 1.0 - tail), bell * ((2.0 * math.pi) ** -0.5)


def column_sum(v):
    return jnp.sum(v, axis=0, keepdims=True)


def middle_kernel(n, nb, *refs):
    o_hbm, x_hbm, y_hbm, g_hbm, fz_hbm, fx_hbm, fy_hbm, par_hbm, bup_hbm = refs[:9]
    outs_hbm = refs[10:17]
    do_out = refs[9]
    (
        o_in, x, y, g_in, wb, wd, par, bup, o_recv, do_send, slope,
        out, dacc_ref, dz1_ref, gvec, sum_b, sum_d, far, bias_up, omix, hid_ref, dur_ref, po, pu, pd, to, tu, td,
        in_sem, out_sem, ex_send, ex_recv, ex_local, f_send, f_recv, p_send, p_recv,
    ) = refs[17:]
    s = Spot(nb)
    loads = copies(
        [
            (o_hbm, o_in), (x_hbm, x), (y_hbm, y), (g_hbm, g_in), (par_hbm, par), (bup_hbm, bup),
            (fz_hbm, wb.at[s.h, :, s.c]), (fx_hbm, wb.at[s.near[0], :, s.c]), (fy_hbm, wb.at[s.near[1], :, s.c]),
        ],
        in_sem,
    )
    greet_core(s)
    loads[0].wait()
    o_ex = Exchange(
        s, lambda g: o_in.at[:, g], lambda g: o_recv.at[pair_of(g)], ex_send.at[0], ex_recv.at[0], ex_local.at[0]
    )
    o_ex.begin()
    cut = [pl.ds(0, 2304), pl.ds(2304, 2304)]
    heads = (s.h, s.near[0], s.near[1], s.diag)

    def onward(w, h, to):
        src = (fx_hbm, fy_hbm)[w].at[:, :, cut[w]]
        return remote(src, wb.at[h, :, s.c, :, cut[w]], f_send.at[4 + w], f_recv.at[4 + w], to, s.z * 2 + s.c)

    def twin(k, c):
        slot = wb.at[heads[k], :, c]
        src = (fz_hbm, fx_hbm, fy_hbm, slot)[k]
        return remote(src, slot, f_send.at[k], f_recv.at[k], s.h, s.z * 2 + 1 - s.c)

    for w in range(2):
        onward(w, s.near[w], s.near[1 - w]).start()
    for k in range(3):
        twin(k, s.c).start()
    for w in range(2):
        onward(w, s.diag, s.near[1 - w]).wait_recv()
    twin(3, s.c).start()
    o_ex.end()
    wait_all(loads[1:])
    for m in range(2):
        for t in range(4):
            first, second = weave(
                o_recv[8 * m + 2 * t].reshape(64, 128), o_recv[8 * m + 2 * t + 1].reshape(64, 128)
            )
            omix[128 * m:128 * m + 64, 128 * t:128 * t + 128] = first
            omix[128 * m + 64:128 * m + 128, 128 * t:128 * t + 128] = second
    gain1, bias1 = par[1:2], par[2:3]
    gain2, bias2 = par[3:4], par[4:5]
    gain3, bias3 = par[5:6], par[6:7]
    for k in range(4):
        twin(k, 1 - s.c).wait_recv()
    for t in range(4):
        for r in range(4):
            wd[t, :, :, r] = wb[t, :, :, :, 2560 + 512 * r:3072 + 512 * r]
    w_out = wb[:, :, :, :, 0:512].reshape(512, 512)
    a = dot_n(omix[...], w_out)
    n1, r1 = row_norm(x[...].astype(f32) + a)
    x1 = n1 * gain1 + bias1
    x1r = x1.astype(bf16)
    feed = jnp.zeros_like(x1)
    for t in range(4):
        cols = slice(512 * t, 512 * t + 512)
        u = dot_n(x1r, wb[:, :, :, :, 512 + 512 * t:1024 + 512 * t].reshape(512, 512)) + bup[:, cols]
        phi, density = normal(u)
        hid = (u * phi).astype(bf16)
        slope[:, cols] = phi + u * density
        hid_ref[:, cols] = hid
        feed = feed + dot_n(hid, wd[t].reshape(512, 512))
    feed = feed + par[0:1]
    n2, r2 = row_norm(x1 + feed)
    n3, r3 = row_norm(y[...].astype(f32) + a + feed)
    out[...] = (n2 * gain2 + bias2 + (n3 * gain3 + bias3)).astype(bf16)
    g = g_in[...].astype(f32)
    dacc = row_norm_back(g, n3, r3, gain3)
    dacc_ref[...] = dacc
    dz2 = row_norm_back(g, n2, r2, gain2)
    df = dz2 + dacc
    dfr = df.astype(bf16)
    swaps = [
        remote(part.at[:, :, 1 - s.c], there, p_send.at[k], p_recv.at[k], s.h, s.z * 2 + 1 - s.c)
        for k, (part, there) in enumerate(((pd, td), (pu, tu), (po, to)))
    ]
    for t in range(4):
        pd[t] = dot_0(hid_ref[:, 512 * t:512 * t + 512], dfr).astype(bf16).reshape(nb // 2, 2, 64, 512)
    swaps[0].start()
    dx1 = dz2
    for t in range(4):
        cols = slice(512 * t, 512 * t + 512)
        du = dot_t(dfr, wd[t].reshape(512, 512)) * slope[:, cols]
        bias_up[:, cols] = column_sum(du)
        dur = du.astype(bf16)
        dur_ref[:, cols] = dur
        dx1 = dx1 + dot_t(dur, wb[:, :, :, :, 512 + 512 * t:1024 + 512 * t].reshape(512, 512))
    dz1 = row_norm_back(dx1, n1, r1, gain1)
    dz1_ref[...] = dz1
    dar = (dz1 + dacc).astype(bf16)
    do = dot_t(dar, w_out).astype(bf16)
    for m in range(2):
        for t in range(4):
            tile = do[128 * m:128 * m + 128, 128 * t:128 * t + 128]
            first, second = weave(tile[0:64], tile[64:128])
            do_send[8 * m + 2 * t] = first.reshape(4, 16, 128)
            do_send[8 * m + 2 * t + 1] = second.reshape(4, 16, 128)
    do_ex = Exchange(
        s, lambda g: do_send.at[pair_of(g)], lambda g: do_out.at[:, g], ex_send.at[1], ex_recv.at[1], ex_local.at[1]
    )
    do_ex.begin()
    stores = copies(zip((out, dacc_ref, dz1_ref), outs_hbm[:3]), out_sem)
    for t in range(4):
        cols = slice(512 * t, 512 * t + 512)
        pu[:, :, :, :, cols] = dot_0(x1r, dur_ref[:, cols]).astype(bf16).reshape(4, nb // 2, 2, 16, 512)
    swaps[1].start()
    po[...] = dot_0(omix[...], dar).astype(bf16).reshape(po.shape)
    swaps[2].start()
    sum_g = column_sum(g)
    sums = (
        column_sum(df), column_sum(dx1 * n1), column_sum(dx1), column_sum(g * n2), sum_g, column_sum(g * n3), sum_g
    )
    gvec[...] = jnp.zeros_like(gvec)
    gvec[:, 0, :] = gather_row(bias_up[...], n, 64)
    for k in range(7):
        gvec[:, k + 1, :] = gather_row(sums[k], n, 16)
    stores += copies([(gvec, outs_hbm[3])], out_sem.at[pl.ds(3, 1)])
    for swap in swaps:
        swap.wait()

    def join(part, there):
        value = part[:, :, s.c].astype(f32) + there[...].astype(f32)
        return value.astype(bf16).reshape(-1, *value.shape[2:])

    sum_d[...] = join(pd, td)
    sum_b[:, :, 512:2560] = join(pu, tu)
    sum_b[:, :, 0:512] = join(po, to)
    stores += copies(zip((sum_b, sum_d), outs_hbm[4:6]), out_sem.at[pl.ds(4, 2)])
    group = pl.ds(s.diag * s.nz, s.nz)
    far[:, :, 0:2560] = sum_b[group]
    for r in range(4):
        far[:, :, 2560 + 512 * r:3072 + 512 * r] = sum_d[group, 16 * r:16 * r + 16, :]
    stores += copies([(far, outs_hbm[6])], out_sem.at[pl.ds(6, 1)])
    do_ex.end()
    for w in range(2):
        onward(w, s.near[w], s.near[1 - w]).wait_send()
    for k in range(4):
        twin(k, s.c).wait_send()
    wait_all(stores)


def middle(n, nb, o, x, y, g, fz, fx, fy, par, bup):
    dma = pltpu.SemaphoreType.DMA
    rows = x.shape[0]
    nz = nb // 2
    saved = [
        ((rows, 512), bf16), ((rows, 512), f32), ((rows, 512), f32), ((n, 16, 128), f32),
        ((4 * nz, 16, 2560), bf16), ((4 * nz, 64, 512), bf16),
    ]
    return pl.pallas_call(
        functools.partial(middle_kernel, n, nb),
        out_shape=[jax.ShapeDtypeStruct((4, 16, 16, 128), bf16)]
        + [jax.ShapeDtypeStruct(shape, kind) for shape, kind in saved]
        + [jax.ShapeDtypeStruct((nz, 16, 4608), bf16)],
        in_specs=any_specs(9),
        out_specs=any_specs(8),
        scratch_shapes=[
            pltpu.VMEM(o.shape, bf16),
            pltpu.VMEM(x.shape, bf16),
            pltpu.VMEM(x.shape, bf16),
            pltpu.VMEM(x.shape, bf16),
            pltpu.VMEM((4, nb // 2, 2, 16, 4608), bf16),
            pltpu.VMEM((4, 4, 2, 4, 16, 512), bf16),
            pltpu.VMEM(par.shape, f32),
            pltpu.VMEM(bup.shape, f32),
            pltpu.VMEM((16, 4, 16, 128), bf16),
            pltpu.VMEM((16, 4, 16, 128), bf16),
            pltpu.VMEM((rows, 2048), f32),
            *[pltpu.VMEM(shape, kind) for shape, kind in saved],
            pltpu.VMEM((nz, 16, 4608), bf16),
            pltpu.VMEM((1, 2048), f32),
            pltpu.VMEM((rows, 512), bf16),
            pltpu.VMEM((rows, 2048), bf16),
            pltpu.VMEM((rows, 2048), bf16),
            *[pltpu.VMEM((4, nz, 2, *tail), bf16) for tail in ((16, 512), (16, 2048), (64, 512))],
            *[pltpu.VMEM((4, nz, *tail), bf16) for tail in ((16, 512), (16, 2048), (64, 512))],
            dma((9,)),
            dma((7,)),
            dma((2, 16)),
            dma((2, 16)),
            dma((2,)),
            dma((6,)),
            dma((6,)),
            dma((3,)),
            dma((3,)),
        ],
        compiler_params=pltpu.CompilerParams(
            collective_id=2, has_side_effects=True, vmem_limit_bytes=VMEM_BYTES
        ),
        name="middle",
    )(o, x, y, g, fz, fx, fy, par, bup)


def finish_kernel(n, nb, *refs):
    ins, far = refs[:8], refs[8]
    outs = refs[9:17]
    (
        dq, dkv, xm, dz1, pb, pd, gvec, wa,
        pa, ta, da, na, la, db, nb_, lb, dd, nd, ld, tv, dv, nv, lv,
        twin_buf, dkv_send, dkv_recv, dq_recv, dqkv, dx_send, dx_recv, gx, gq, gk, gv, go, gu, gd, gs,
        in_sem, far_sem, out_sem, rs_send, rs_recv, ex_send, ex_recv, dx_ssem, dx_rsem, tw_send, tw_recv,
    ) = refs[17:]
    s = Spot(nb)
    order = (1, 0, 4, 5, 6, 7, 2, 3)
    local = (dq, dkv, xm, dz1, pb, pd, gvec, wa)
    loads = copies([(ins[k], local[k]) for k in order], in_sem)
    corners = copies(
        [(far.at[:, :, pl.ds(0, 2560)], db)]
        + [(far.at[:, :, pl.ds(2560 + 512 * r, 512)], dd.at[:, pl.ds(16 * r, 16)]) for r in range(4)],
        far_sem,
    )
    greet_near(s)
    swap = remote(ins[1].at[:, :, 1 - s.c], twin_buf, tw_send, tw_recv, s.h, s.z * 2 + 1 - s.c)
    swap.start()
    jobs = [
        Scatter(s, *bufs, rs_send.at[k], rs_recv.at[k])
        for k, bufs in enumerate(
            ((pb, None, db, nb_, lb), (pd, None, dd, nd, ld), (gvec, tv, dv, nv, lv), (pa, ta, da, na, la))
        )
    ]
    wait_all(loads[:5])
    jobs[2].begin()
    swap.wait()

    def add(g):
        dkv_send[g] = (dkv[:, g, s.c].astype(f32) + twin_buf[:, g].astype(f32)).astype(bf16)

    each(4 * s.nz, add)
    plane = [Plane(s, ex_send.at[k], ex_recv.at[k]) for k in range(2)]

    def block(w, j, z, slot):
        g = j * s.nz + z
        src, dst = ((dkv_send.at[g], dkv_recv.at[slot, z]), (dq.at[:, g], dq_recv.at[slot, z]))[w]
        return plane[w].copy(src, dst, j, g, slot * s.nz + z)

    def pass_on(k):
        z = s.ahead(k)
        for w in range(2):
            each(4, lambda i: block(w, plane[w].to(i), z, s.h).start(), 1)
        dkv_recv[s.h, z] = dkv_send[s.h * s.nz + z]
        dq_recv[s.h, z] = dq[:, s.h * s.nz + z]

    each(s.nz + 1, pass_on, 1)
    wait_all(loads[5:])
    wait_all(corners)

    def back(z, slot):
        return remote(dx_send.at[z], dx_recv.at[slot], dx_ssem.at[z], dx_rsem.at[slot], s.h, z * 2 + s.c)

    def take(k):
        z = s.ahead(k)
        for w in range(2):
            each(4, lambda i: block(w, plane[w].frm(i), z, plane[w].frm(i)).wait_recv(), 1)
        for j in range(4):
            dqkv[z, :, 128 * j:128 * j + 128] = dkv_recv[j, z].reshape(128, 128)
        for t in range(2):
            first, second = weave(dq_recv[2 * t, z].reshape(64, 128), dq_recv[2 * t + 1, z].reshape(64, 128))
            dqkv[z, 0:64, 512 + 128 * t:640 + 128 * t] = first
            dqkv[z, 64:128, 512 + 128 * t:640 + 128 * t] = second
        dx_send[z] = dot_t(dqkv[z], wa[:, :, :, :, 0:768].reshape(512, 768)).astype(bf16)

    def take_and_send(k):
        take(k)
        back(s.ahead(k), s.z).start()

    each(s.nz, take_and_send, 1)
    for job in jobs[:2]:
        job.second()
    take(s.nz)
    dx_recv[s.z] = dx_send[s.z]
    tokens = xm[...].reshape(512, 512)
    pa[...] = dot_0(tokens, dqkv[...].reshape(512, 768)).astype(bf16).reshape(n, 16, 768)
    jobs[3].begin()
    jobs[2].second()
    jobs[3].second()
    for job in jobs:
        job.third()
    each(s.nz, lambda k: back(s.ahead(k), s.ahead(k)).wait_recv(), 1)
    for m in range(2):
        rows = slice(128 * m, 128 * m + 128)
        gx[rows, :] = dz1[rows, :] + (dx_recv[2 * m].astype(f32) + dx_recv[2 * m + 1].astype(f32))
    stores = copies([(gx, outs[0])], out_sem)
    total = jobs[0].total()
    go[...] = total[:, 0:512]
    gu[...] = total[:, 512:2560]
    gd[...] = jobs[1].total()
    gs[...] = jobs[2].total()
    stores += copies(zip((go, gu, gd, gs), outs[4:8]), out_sem.at[pl.ds(1, 4)])
    for w, part in enumerate(jobs[3].columns()):
        gq[:, 256 * w:256 * w + 256] = part[:, 512:768]
        for t in range(2):
            first, second = weave(part[:, 256 * t:256 * t + 128], part[:, 256 * t + 128:256 * t + 256])
            at = 256 * w + 128 * t
            gk[:, at:at + 128] = first
            gv[:, at:at + 128] = second
    stores += copies(zip((gq, gk, gv), outs[1:4]), out_sem.at[pl.ds(5, 3)])
    for w in range(2):
        each(4, lambda i: each(s.nz, lambda z: block(w, plane[w].to(i), z, s.h).wait_send()), 1)
    each(s.nz, lambda k: back(s.ahead(k), s.z).wait_send(), 1)
    for job in jobs:
        job.sent()
    wait_all(stores)


def finish(n, nb, dq, dkv, xm, dz1, pb, pd, gvec, wa, far):
    dma = pltpu.SemaphoreType.DMA
    nz = nb // 2
    rows = dz1.shape[0]

    def buffers(depth, width, kind):
        return [
            pltpu.VMEM((n, depth, width), kind),
            pltpu.VMEM((4, nz, depth, width), kind),
            pltpu.VMEM((nz, depth, width), kind),
            pltpu.VMEM((2, nz, depth, width), kind),
            pltpu.VMEM((nz, depth, width), kind),
        ]

    args = (dq, dkv, xm, dz1, pb, pd, gvec, wa)
    shapes = ((rows, 512), (16, 512), (16, 512), (16, 512), (16, 512), (16, 2048), (64, 512), (16, 128))
    return pl.pallas_call(
        functools.partial(finish_kernel, n, nb),
        out_shape=[jax.ShapeDtypeStruct(shape, f32) for shape in shapes],
        in_specs=any_specs(9),
        out_specs=any_specs(8),
        scratch_shapes=[
            *[pltpu.VMEM(arg.shape, arg.dtype) for arg in args],
            *buffers(16, 768, bf16),
            *buffers(16, 2560, bf16)[2:],
            *buffers(64, 512, bf16)[2:],
            *buffers(16, 128, f32)[1:],
            pltpu.VMEM((8, 16, 16, 128), bf16),
            pltpu.VMEM((16, 8, 16, 128), bf16),
            pltpu.VMEM((4, nz, 8, 16, 128), bf16),
            pltpu.VMEM((4, nz, 4, 16, 128), bf16),
            pltpu.VMEM((nz, 128, 768), bf16),
            pltpu.VMEM((nz, 128, 512), bf16),
            pltpu.VMEM((nz, 128, 512), bf16),
            *[pltpu.VMEM(shape, f32) for shape in shapes],
            dma((8,)),
            dma((5,)),
            dma((8,)),
            dma((4, 9 * nz)),
            dma((4, 9 * nz)),
            dma((2, 4 * nz)),
            dma((2, 4 * nz)),
            dma((nz,)),
            dma((nz,)),
            dma,
            dma,
        ],
        compiler_params=pltpu.CompilerParams(
            collective_id=3, has_side_effects=True, vmem_limit_bytes=VMEM_BYTES
        ),
        name="finish",
    )(*args, far)


def deliver_kernel(count, *refs):
    ins, outs = refs[:count], refs[count:2 * count + 7]
    stage, lines, (in_sem, sems) = refs[2 * count + 7:3 * count + 7], refs[3 * count + 7:3 * count + 15], refs[-2:]
    loads = copies(zip(ins, stage), in_sem)
    jobs = []
    for k in range(count - 1):
        loads[k].wait()
        jobs += copies([(stage[k], outs[k])], sems.at[pl.ds(k, 1)])
    loads[-1].wait()
    vec = stage[-1]
    lines[0][...] = vec[0:1, 0:64].reshape(64)
    for k in range(1, 8):
        lines[k][...] = vec[k:k + 1, 0:16].reshape(16)
    jobs += copies(zip(lines, outs[count - 1:]), sems.at[pl.ds(count - 1, 8)])
    wait_all(jobs)


def deliver(arrays, vec):
    count = len(arrays) + 1
    lines = [(64,)] + [(16,)] * 7
    return pl.pallas_call(
        functools.partial(deliver_kernel, count),
        out_shape=[jax.ShapeDtypeStruct(a.shape, a.dtype) for a in arrays]
        + [jax.ShapeDtypeStruct(shape, f32) for shape in lines],
        in_specs=any_specs(count),
        out_specs=any_specs(count + 7),
        scratch_shapes=[
            *[pltpu.VMEM(a.shape, a.dtype) for a in (*arrays, vec)],
            *[pltpu.VMEM(shape, f32) for shape in lines],
            pltpu.SemaphoreType.DMA((count,)),
            pltpu.SemaphoreType.DMA((count + 7,)),
        ],
        compiler_params=pltpu.CompilerParams(vmem_limit_bytes=VMEM_BYTES),
        name="deliver",
    )(*arrays, vec)


def by_pairs(
    stream, accumulator, upstream, segment_ids, w_query, w_key, w_value, w_out, w_up, b_up, w_down, b_down,
    gain_attn, bias_attn, gain_ffn, bias_ffn, gain_final, bias_final,
):
    nb = lax.axis_size("blk")
    n = 4 * nb
    x = stream.reshape(256, 512)
    y = accumulator.reshape(256, 512)
    g = upstream.reshape(256, 512)
    smalls = (b_up, b_down, gain_attn, bias_attn, gain_ffn, bias_ffn, gain_final, bias_final)
    q, kv, xm, wa, fz, par, bup, seg_k, seg_q = project(
        n, nb, stream.reshape(2, 128, 512), w_query, w_key, w_value, w_out, w_up, w_down, segment_ids.reshape(2, 128), smalls
    )
    fx, fy = (lax.ppermute(fz, "head", [(h, h ^ w) for h in range(4)]) for w in (1, 2))
    o, of, lse, kv2, kvt = attn_fwd(q.reshape(4, 256, 128), kv.reshape(4096, 128), seg_q, seg_k)
    do, out, dacc, dz1, gvec, pb, pd, far = middle(
        n, nb, o.reshape(4, 16, 16, 128), x, y, g, fz, fx, fy, par, bup
    )
    far = lax.ppermute(far, "head", [(h, 3 - h) for h in range(4)])
    dq, dkv, out, dacc = attn_bwd(
        q.reshape(4, 256, 128), do.reshape(4, 256, 128), of, lse, kv2, kvt, seg_q, seg_k, out, dacc
    )
    gx, gq, gk, gv, go, gu, gd, gs = finish(
        n, nb, dq.reshape(4, 16, 16, 128), dkv.reshape(8, 16, 2, 16, 128), xm, dz1, pb, pd, gvec, wa, far
    )
    gx, gq, gk, gv, go, gu, gd, gbu, *small_grads = deliver((gx, gq, gk, gv, go, gu, gd), gs)
    return (
        out.reshape(stream.shape), gx.reshape(stream.shape), dacc.reshape(stream.shape),
        gq, gk, gv, go, gu, gbu, gd, *small_grads,
    )


def pairs_fit(mesh, shape):
    return mesh.shape["head"] == 4 and mesh.shape["blk"] == 8 and shape == (2, 32, 128, 512)


def solution(mesh):
    def step(*args):
        return run(by_pairs if pairs_fit(mesh, args[0].shape) else local, mesh)(*args)

    return step


def run(body, mesh):
    return jax.shard_map(
        body,
        mesh=mesh,
        in_specs=(
            P(None, ("head", "blk"), None, None),
            P(None, ("head", "blk"), None, None),
            P(None, ("head", "blk"), None, None),
            P(None, ("head", "blk"), None),
            P(("head", "blk"), None),
            P(("head", "blk"), None),
            P(("head", "blk"), None),
            P(("head", "blk"), None),
            P(("head", "blk"), None),
            P(("head", "blk")),
            P(("head", "blk"), None),
            P(("head", "blk")),
            P(("head", "blk")),
            P(("head", "blk")),
            P(("head", "blk")),
            P(("head", "blk")),
            P(("head", "blk")),
            P(("head", "blk")),
        ),
        out_specs=(
            P(None, ("head", "blk"), None, None),
            P(None, ("head", "blk"), None, None),
            P(None, ("head", "blk"), None, None),
            P(("head", "blk"), None),
            P(("head", "blk"), None),
            P(("head", "blk"), None),
            P(("head", "blk"), None),
            P(("head", "blk"), None),
            P(("head", "blk")),
            P(("head", "blk"), None),
            P(("head", "blk")),
            P(("head", "blk")),
            P(("head", "blk")),
            P(("head", "blk")),
            P(("head", "blk")),
            P(("head", "blk")),
            P(("head", "blk")),
        ),
        check_vma=False,
    )
```
